128 devices in a mesh: tok: 8 (over z, core), narrow: 2 (over x_lo), wide: 8 (over y, x_hi).
Axes of the slice: x: 4 (x_hi: 2, x_lo: 2; x = x_hi * 2 + x_lo), y: 4, z: 4, core: 2. Of those that a mesh axis runs over, the one named last changes fastest.
Arguments:
- layer_input: bfloat16 [12288, 2048], P('tok', ('narrow', 'wide')), may hold values from -6 to 6
- doc_lengths: int32 [8, 2], P('tok'), may hold values from 256 to 1024, as said below
- attn_gain: float32 [2048], replicated, may hold values from 0.1 to 1.9
- w_query: bfloat16 [2048, 2048], P(None, ('narrow', 'wide')), may hold values from -0.25 to 0.25
- w_key: bfloat16 [2048, 512], P(None, 'narrow'), may hold values from -0.125 to 0.125
- w_value: bfloat16 [2048, 512], P(None, 'narrow'), may hold values from -0.125 to 0.125
- w_output: bfloat16 [2048, 2048], P(None, ('narrow', 'wide')), may hold values from -0.75 to 0.75
- ffn_gain: float32 [2048], P(('narrow', 'wide')), may hold values from 0.1 to 1.9
- w_gate: bfloat16 [2048, 8192], P('narrow', 'wide'), may hold values from -0.125 to 0.125
- w_up: bfloat16 [2048, 8192], P('narrow', 'wide'), may hold values from -0.125 to 0.125
- w_down: bfloat16 [8192, 2048], P('wide', 'narrow'), may hold values from -0.125 to 0.125
- output_grad: bfloat16 [12288, 2048], P('tok', ('narrow', 'wide')), may hold values from -6 to 6
Outputs:
- layer_output: bfloat16 [12288, 2048], P('tok', ('narrow', 'wide'))
- input_grad: bfloat16 [12288, 2048], P('tok', ('narrow', 'wide'))
- attn_gain_grad: float32 [16, 128], P(('narrow', 'wide'), 'tok')
- query_grad: float32 [2048, 2048], P('tok', ('narrow', 'wide'))
- key_grad: float32 [2048, 512], P(('tok', 'wide'), 'narrow')
- value_grad: float32 [2048, 512], P(('tok', 'wide'), 'narrow')
- output_proj_grad: float32 [2048, 2048], P('tok', ('narrow', 'wide'))
- ffn_gain_grad: float32 [16, 128], P(('narrow', 'wide'), 'tok')
- gate_grad: float32 [16, 128, 8192], P('narrow', 'tok', 'wide')
- up_grad: float32 [16, 128, 8192], P('narrow', 'tok', 'wide')
- down_grad: float32 [64, 128, 2048], P('wide', 'tok', 'narrow')
The draws below stay inside these ranges and needn't reach their ends.
Inputs may be any that keep to these rules, and one draw needn't show every extreme that they name: `doc_lengths`: each row lists the lengths of the 2 documents packed in order into one index of tok; a row sums to 1536, and in every row exactly one document has 1024 tokens, the most.
All inputs are finite; a program needn't handle non-finite values.
Results may differ from the reference program's by a relative error of at most 0.024.
Values may be sent and summed in bfloat16 or wider, within the bound.
A program may use at most 192 MiB of HBM per device.

```python
import math
import jax
import jax.numpy as jnp
from jax import lax

D = 2048
HEADS = 32
KV_HEADS = 8
HEAD_DIM = 64
FF = 8192
GROUP = 128
TOK_DEV = 1536
DOC_LEN = 1024
DOCS = 2
TOKENS = 12288
HQ_DEV = 2
N_TOK = 8


def draw_doc_lengths(key, part):
    key = jax.random.fold_in(key, 11)
    key_moves, key_spot = jax.random.split(key)
    rest = TOK_DEV - DOC_LEN
    pieces = DOCS - 1
    base = rest // pieces
    extra = rest - base * pieces
    pairs = pieces // 2
    shifted = jax.random.randint(key_moves, (N_TOK, pairs), -(base // 2), base // 2 + 1, dtype=jnp.int32)
    moves = jnp.stack([-shifted, shifted], axis=2).reshape(N_TOK, 2 * pairs)
    if pieces > 2 * pairs:
        moves = jnp.concatenate([moves, jnp.zeros((N_TOK, 1), jnp.int32)], axis=1)
    lengths_rest = (base + moves).astype(jnp.int32)
    lengths_rest = lengths_rest.at[:, pieces - 1].add(extra)
    spot = jax.random.randint(key_spot, (N_TOK, 1), 0, DOCS, dtype=jnp.int32)
    slots = jnp.arange(DOCS, dtype=jnp.int32)[None, :]
    source = jnp.clip(slots - (slots > spot).astype(jnp.int32), 0, pieces - 1)
    source = jnp.broadcast_to(source, (N_TOK, DOCS)).astype(jnp.int32)
    taken = jnp.take_along_axis(lengths_rest, source, axis=1)
    return jnp.where(slots == spot, DOC_LEN, taken).astype(jnp.int32)


def level_of(rng, dims, shards, least, high):
    loudness, own = 1.0, jax.random.fold_in(rng, 6)
    for dim, blocks in shards:
        draws = jnp.exp(jax.random.uniform(jax.random.fold_in(own, dim), (blocks,), jnp.float32, least / len(shards), high / len(shards)))
        loudness = loudness * jnp.repeat(draws, dims[dim] // blocks).reshape([-1 if axis == dim else 1 for axis in range(len(dims))])
    return loudness


def scatter_about(rng, dims, width, bound, cuts=(), kind=jnp.bfloat16):
    entries = jax.random.normal(rng, dims, jnp.float32) * width
    if len(cuts) > 0:
        entries = level_of(rng, dims, cuts, -0.22, 0.18) * entries
    return jnp.clip(entries, min=-bound, max=bound).astype(kind)


def setup_inputs(seed: int = 0) -> dict:
    seeds = jax.random.split(jax.random.key(seed), 13)
    return {
        "layer_input": scatter_about(seeds[0], (TOKENS, D), 1.0, 6.0, ((0, 8), (1, 16))),
        "doc_lengths": draw_doc_lengths(jax.random.fold_in(seeds[12], 71), 0),
        "attn_gain": jnp.clip(1.0 + 0.18 * jax.random.normal(seeds[2], (D,), jnp.float32), 0.1, 1.9),
        "w_query": scatter_about(seeds[3], (D, HEADS * HEAD_DIM), (D // 4) ** -0.5, 0.25, ((1, 16),)),
        "w_key": scatter_about(seeds[4], (D, KV_HEADS * HEAD_DIM), D ** -0.5, 0.125, ((1, 2),)),
        "w_value": scatter_about(seeds[5], (D, KV_HEADS * HEAD_DIM), D ** -0.5, 0.125, ((1, 2),)),
        "w_output": scatter_about(seeds[6], (D, HEADS * HEAD_DIM), (HEADS * HEAD_DIM // 32) ** -0.5, 0.75, ((1, 16),)),
        "ffn_gain": jnp.clip(1.0 + 0.18 * jax.random.normal(seeds[7], (D,), jnp.float32), 0.1, 1.9),
        "w_gate": scatter_about(seeds[8], (D, FF), D ** -0.5, 0.125, ((0, 2), (1, 8))),
        "w_up": scatter_about(seeds[9], (D, FF), D ** -0.5, 0.125, ((0, 2), (1, 8))),
        "w_down": scatter_about(seeds[10], (FF, D), (FF // 4) ** -0.5, 0.125, ((0, 8), (1, 2))),
        "output_grad": scatter_about(seeds[11], (TOKENS, D), 1.0, 6.0, ((0, 8), (1, 16))),
    }


EPS = 1e-05
THETA = 500000.0
FACTOR = 32.0
LOW_FACTOR = 1.0
HIGH_FACTOR = 4.0
INITIAL = 8192.0
NEG = -1e+30
HIGH = lax.Precision.HIGHEST

@jax.custom_vjp
def low(v):
    return lax.optimization_barrier(v.astype(jnp.bfloat16)).astype(jnp.float32)

@jax.custom_vjp
def low_back(v):
    return v

def low_keep(v):
    return (low(v), None)

def low_pass(kept, grad):
    return (grad,)

def back_keep(v):
    return (v, None)

def back_low(kept, grad):
    return (low(grad),)
low.defvjp(low_keep, low_pass)
low_back.defvjp(back_keep, back_low)

def rope_tables(positions, head_size):
    halfway = head_size // 2
    position_k = jnp.arange(halfway, dtype=jnp.float32)
    inverse = jnp.exp(-2.0 * position_k / head_size * math.log(THETA))
    wavelen = 2.0 * math.pi / inverse
    scaled = inverse / FACTOR
    smooth = (INITIAL / wavelen - LOW_FACTOR) / (HIGH_FACTOR - LOW_FACTOR)
    middle = (1.0 - smooth) * scaled + smooth * inverse
    frequency = jnp.where(wavelen < INITIAL / HIGH_FACTOR, inverse, jnp.where(wavelen > INITIAL / LOW_FACTOR, scaled, middle))
    angles = positions[:, None] * frequency[None, :]
    return (jnp.cos(angles), jnp.sin(angles))

def rotate(tensor, cosine, sine_table):
    halfway = tensor.shape[-1] // 2
    front = tensor[..., :halfway]
    behind = tensor[..., halfway:]
    cos_rows = cosine[:, None, :]
    sin_rows = sine_table[:, None, :]
    return jnp.concatenate([front * cos_rows - behind * sin_rows, behind * cos_rows + front * sin_rows], axis=-1)

def doc_layout(lengths, length_all):
    finish = jnp.cumsum(lengths).astype(jnp.int32)
    starts = finish - lengths.astype(jnp.int32)
    row_ids = jnp.arange(length_all, dtype=jnp.int32)
    inside = (row_ids[:, None] >= starts[None, :]) & (row_ids[:, None] < finish[None, :])
    doc_first = lax.optimization_barrier(jnp.sum(jnp.where(inside, starts[None, :], 0), axis=1)).astype(jnp.int32)
    return (doc_first, (row_ids - doc_first).astype(jnp.float32))

def expand(stacked):
    moved = jnp.transpose(stacked, (1, 2, 0, 3))
    spread = jnp.broadcast_to(moved[:, :, :, None, :], moved.shape[:3] + (HQ_DEV,) + moved.shape[3:])
    return spread.reshape(moved.shape[0], HEADS, HEAD_DIM)

def shard_forward(weights, shard_rows, lengths):
    attn_gain, w_query, w_key, w_value, w_output, ffn_gain, w_gate, w_up, w_down = weights
    length_all = shard_rows.shape[0]
    doc_first, positions = doc_layout(lengths, length_all)
    cosine, sine_table = rope_tables(positions, HEAD_DIM)
    scale_one = lax.rsqrt(lax.optimization_barrier(jnp.mean(shard_rows * shard_rows, axis=1, keepdims=True)) + EPS)
    normed = low(shard_rows * scale_one * attn_gain)
    query_lin = low_back(jnp.dot(normed, w_query, precision=HIGH))
    queries = low(rotate(query_lin.reshape(length_all, HEADS, HEAD_DIM), cosine, sine_table))
    key_lin = jnp.dot(normed, w_key, precision=HIGH)
    value_lin = jnp.dot(normed, w_value, precision=HIGH)
    key_list = []
    value_list = []
    for copy_index in range(HEADS // KV_HEADS // HQ_DEV):
        key_list.append(low(rotate(low_back(key_lin).reshape(length_all, KV_HEADS, HEAD_DIM), cosine, sine_table)))
        value_list.append(low(low_back(value_lin)).reshape(length_all, KV_HEADS, HEAD_DIM))
    keys_all = expand(jnp.stack(key_list, 0))
    values_all = expand(jnp.stack(value_list, 0))
    block_rows = min(512, length_all)
    key_index = jnp.arange(length_all, dtype=jnp.int32)

    def attend(block_start):
        query_block = lax.dynamic_slice_in_dim(queries, block_start, block_rows, 0)
        first_block = lax.dynamic_slice_in_dim(doc_first, block_start, block_rows, 0)
        query_index = block_start + jnp.arange(block_rows, dtype=jnp.int32)
        scores = jnp.einsum('qhd,khd->hqk', query_block, keys_all, precision=HIGH) * HEAD_DIM ** (-0.5)
        allowed = (key_index[None, :] <= query_index[:, None]) & (key_index[None, :] >= first_block[:, None])
        scores = low_back(jnp.where(allowed[None], scores, NEG))
        highest = lax.optimization_barrier(jnp.max(scores, axis=2, keepdims=True))
        raised = jnp.exp(scores - highest)
        soft = low(raised / lax.optimization_barrier(jnp.sum(raised, axis=2, keepdims=True)))
        return jnp.einsum('hqk,khd->qhd', soft, values_all, precision=HIGH)
    block_starts = jnp.arange(length_all // block_rows, dtype=jnp.int32) * block_rows
    heads_out = lax.map(jax.checkpoint(attend), block_starts)
    heads_out = low(low_back(heads_out.reshape(length_all, HEADS * HEAD_DIM)))
    attn_term = low_back(jnp.dot(heads_out, w_output.T, precision=HIGH))
    resid = shard_rows + attn_term
    scale_two = lax.rsqrt(lax.optimization_barrier(jnp.mean(resid * resid, axis=1, keepdims=True)) + EPS)
    ffn_input = low(resid * scale_two * ffn_gain)
    gate_lin = low_back(jnp.dot(ffn_input, w_gate, precision=HIGH))
    up_lin = low_back(jnp.dot(ffn_input, w_up, precision=HIGH))
    activation = low(jax.nn.silu(gate_lin) * up_lin)
    return resid + jnp.dot(activation, w_down, precision=HIGH)

def reference(layer_input, doc_lengths, attn_gain, w_query, w_key, w_value, w_output, ffn_gain, w_gate, w_up, w_down, output_grad):
    floats = [item.astype(jnp.float32) for item in (layer_input, attn_gain, w_query, w_key, w_value, w_output, ffn_gain, w_gate, w_up, w_down)]

    def forward(rows_all, *weights):
        stacked = rows_all.reshape(N_TOK, TOK_DEV, D)

        def shard_step(carry, items):
            return (carry, shard_forward(weights, items[0], items[1]))
        unused, outputs = lax.scan(jax.checkpoint(shard_step), jnp.zeros((), jnp.float32), (stacked, doc_lengths))
        return outputs.reshape(N_TOK * TOK_DEV, D)
    result, pullback = jax.vjp(forward, *floats)
    grads = pullback(output_grad.astype(jnp.float32))
    return (result.astype(jnp.bfloat16), grads[0].astype(jnp.bfloat16), grads[1].reshape(D // GROUP, GROUP), grads[2], grads[3], grads[4], grads[5], grads[6].reshape(D // GROUP, GROUP), grads[7].reshape(D // GROUP, GROUP, FF), grads[8].reshape(D // GROUP, GROUP, FF), grads[9].reshape(FF // GROUP, GROUP, D))
```

```python
import functools
import math

import jax
import jax.numpy as jnp
import numpy as np
from jax import lax
from jax.experimental import pallas as pl
from jax.experimental.pallas import tpu as pltpu
from jax.sharding import PartitionSpec as P

HEADS = 32
KV_HEADS = 8
HEAD_DIM = 64
GROUP = 128
EPS = 1e-05
THETA = 500000.0
FACTOR = 32.0
LOW_FACTOR = 1.0
HIGH_FACTOR = 4.0
INITIAL = 8192.0
NEG = -1e30

D = 2048
ROWS = 1536
CHUNK = 384
SUB = 96
SHORT = 512
BF = jnp.bfloat16
F32 = jnp.float32
MESH = pl.DeviceIdType.MESH
SDS = jax.ShapeDtypeStruct

HERE = (0, 0, 0, 0, 0)
XOFF = [(0, 0, 0, 0, 0), (0, 0, 1, 0, 0), (0, 0, 0, 0, 1), (0, 0, 1, 0, 1)]
YOFF = [(0, 0, 0, d, 0) for d in range(4)]
PLANE = [(0, 0, a, b, e) for b in range(4) for a in range(2) for e in range(2)]
SIBLING = (1, 0, 0, 0, 0)
TOKS = [(a, b, 0, 0, 0) for b in range(4) for a in range(2)]


class Place:
    def __init__(self, core, z, xl, y, xh):
        self.core, self.z, self.xl, self.y, self.xh = core, z, xl, y, xh
        self.tok = z * 2 + core
        self.wide = y * 2 + xh
        self.block = xl * 8 + self.wide
        self.chunk = xl * 2 + xh

    def at(self, off):
        return Place(
            (self.core + off[0]) % 2,
            (self.z + off[1]) % 4,
            (self.xl + off[2]) % 2,
            (self.y + off[3]) % 4,
            (self.xh + off[4]) % 2,
        )

    def device(self):
        return (self.tok, self.xl, self.wide)


def whereami():
    tok = lax.axis_index("tok")
    wide = lax.axis_index("wide")
    return Place(tok % 2, tok // 2, lax.axis_index("narrow"), wide // 2, wide % 2)


def rows(start, size):
    return pl.ds(pl.multiple_of(start, size), size)


def exchange(name, number, plan, ins, outs):
    n_in, n_out = len(ins), len(outs)

    def count():
        fake = Place(0, 0, 0, 0, 0)
        probe = [_Any() for _ in range(n_in)], [_Any() for _ in range(n_out)]
        local, sends = plan(fake, *probe)
        return len(local), sum(1 + len(s[3]) for s in sends)

    n_local, n_send = count()

    def body(*refs):
        sources, targets = refs[:n_in], refs[n_in : n_in + n_out]
        send_sem, recv_sem, local_sem = refs[n_in + n_out :]
        me = whereami()
        local, sends = plan(me, sources, targets)
        offsets = []
        for off, _, _, forwards in sends:
            for o in [off] + [f[0] for f in forwards]:
                if o not in offsets:
                    offsets.append(o)
        barrier = pltpu.get_barrier_semaphore()
        for off in offsets:
            back = tuple(-v for v in off)
            pl.semaphore_signal(
                barrier, inc=1, device_id=me.at(back).device(), device_id_type=MESH
            )
        near = []
        for i, (src, dst) in enumerate(local):
            near.append(pltpu.make_async_copy(src, dst, local_sem.at[i]))
            near[-1].start()
        pl.semaphore_wait(barrier, len(offsets))
        slot = 0

        def launch(off, src, dst):
            nonlocal slot
            copy = pltpu.make_async_remote_copy(
                src_ref=src,
                dst_ref=dst,
                send_sem=send_sem.at[slot],
                recv_sem=recv_sem.at[slot],
                device_id=me.at(off).device(),
                device_id_type=MESH,
            )
            copy.start()
            slot += 1
            return copy

        first = [(launch(off, src, dst), forwards) for off, src, dst, forwards in sends]
        second = []
        for copy, forwards in first:
            if forwards:
                copy.wait_recv()
                second += [launch(*f) for f in forwards]
        for copy, forwards in first:
            copy.wait_send()
            if not forwards:
                copy.wait_recv()
        for copy in second:
            copy.wait()
        for copy in near:
            copy.wait()

    return pl.pallas_call(
        body,
        name=name,
        out_shape=outs,
        in_specs=[pl.BlockSpec(memory_space=pl.ANY)] * n_in,
        out_specs=[pl.BlockSpec(memory_space=pltpu.VMEM)] * n_out,
        scratch_shapes=[
            pltpu.SemaphoreType.DMA((n_send,)),
            pltpu.SemaphoreType.DMA((n_send,)),
            pltpu.SemaphoreType.DMA((max(n_local, 1),)),
        ],
        compiler_params=pltpu.CompilerParams(
            collective_id=number, has_side_effects=True, vmem_limit_bytes=40 * 2**20
        ),
    )(*ins)


class _Any:
    @property
    def at(self):
        return self

    def __getitem__(self, key):
        return self


def lanes(index, size=128):
    return pl.ds(pl.multiple_of(index * size, size), size)


def spread_plan(me, src, dst):
    local = [(src.at[rows(me.chunk * CHUNK, CHUNK), :], dst.at[:, lanes(me.block)])]
    sends = [
        (off, src.at[rows(me.at(off).chunk * CHUNK, CHUNK), :], dst.at[:, lanes(me.block)], [])
        for off in PLANE[1:]
    ]
    return local, sends


def enter_plan(me, ins, outs):
    hidden, w_q, w_kv, gain = ins
    full, w_attn, gains = outs
    half = rows(me.core * 1024, 1024)
    local, sends = spread_plan(me, hidden, full)
    local += [
        (w_q, w_attn.at[:, 0:128]),
        (w_kv, w_attn.at[:, 512:640]),
        (gain, gains.at[me.block]),
    ]
    head = []
    for k in (1, 2, 3):
        cols = slice(k * 128, k * 128 + 128)
        block = w_attn.at[half, cols]
        head.append((XOFF[k], w_q.at[half, :], block, [(SIBLING, block, block)]))
    block = w_attn.at[half, 640:768]
    head.append((XOFF[1], w_kv.at[half, :], block, [(SIBLING, block, block)]))
    sends = head + sends
    sends += [(off, gain, gains.at[me.block], []) for off in PLANE[1:]]
    return local, sends


def to_heads_plan(me, ins, outs):
    (lin,) = ins
    q, kv = outs
    mine = rows(me.chunk * CHUNK, CHUNK)
    local, sends = [], []
    for k, off in enumerate(XOFF):
        kv_col = 512 + 128 * off[2]
        pairs = [
            (lin.at[:, k * 128 : k * 128 + 128], q.at[mine, :]),
            (lin.at[:, kv_col : kv_col + 128], kv.at[mine, :]),
        ]
        if k == 0:
            local += pairs
        else:
            sends += [(off, s, d, []) for s, d in pairs]
    return local, sends


def from_heads_moves(me, src, dst, first_col=0):
    local, sends = [], []
    for k, off in enumerate(XOFF):
        col = first_col + k * 128
        pair = (src.at[rows(me.at(off).chunk * CHUNK, CHUNK), :], dst.at[:, col : col + 128])
        if k == 0:
            local.append(pair)
        else:
            sends.append((off, *pair, []))
    return local, sends


def heads_out_plan(me, ins, outs):
    heads, w_out, half1, half2, half3 = ins
    cat, w_cat = outs
    local, sends = from_heads_moves(me, heads, cat)
    half = rows(me.core * 1024, 1024)
    local.append((w_out, w_cat.at[:, 0:128]))
    for k, part in ((1, half1), (2, half2), (3, half3)):
        block = w_cat.at[half, k * 128 : k * 128 + 128]
        local.append((part, block))
        sends.append((SIBLING, part, block, []))
    return local, sends


def heads_back_plan(me, ins, outs):
    (cat,) = ins
    (heads,) = outs
    mine = rows(me.chunk * CHUNK, CHUNK)
    local, sends = [], []
    for k, off in enumerate(XOFF):
        pair = (cat.at[:, k * 128 : k * 128 + 128], heads.at[mine, :])
        if k == 0:
            local.append(pair)
        else:
            sends.append((off, *pair, []))
    return local, sends


def grads_out_plan(me, ins, outs):
    q, kv = ins
    (cat,) = outs
    local, sends = from_heads_moves(me, q, cat)
    local2, sends2 = from_heads_moves(me, kv, cat, 512)
    return local + local2, sends + sends2


def scatter_moves(me, src, dst):
    local = [(src.at[rows(me.y * SUB, SUB), :], dst.at[me.y])]
    sends = [(off, src.at[rows(me.at(off).y * SUB, SUB), :], dst.at[me.y], []) for off in YOFF[1:]]
    return local, sends


def out_sum_plan(me, ins, outs):
    local, sends = scatter_moves(me, ins[0], outs[0])
    local2, sends2 = spread_plan(me, ins[1], outs[1])
    return local + local2, sends + sends2


def sum_plan(me, ins, outs):
    local, sends = [], []
    for src, dst in zip(ins, outs):
        a, b = scatter_moves(me, src, dst)
        local, sends = local + a, sends + b
    return local, sends


def gather_moves(me, src, dst):
    block = dst.at[rows(me.y * SUB, SUB), :]
    return [(src, block)], [(off, src, block, []) for off in YOFF[1:]]


def gather_plan(me, ins, outs):
    return gather_moves(me, ins[0], outs[0])


def weight_moves(me, own, parts, dst):
    local = [(own, dst.at[rows(me.xl * 1024, 1024), lanes(me.xh, 1024)])]
    sends = []
    for off, part in zip(XOFF[1:], parts):
        there = me.at(off)
        block = dst.at[rows(there.xl * 1024 + me.core * 512, 512), lanes(there.xh, 1024)]
        local.append((part, block))
        sends.append((SIBLING, part, block, []))
    return local, sends


def weight_moves_t(me, own, parts, dst):
    local = [(own, dst.at[rows(me.xh * 1024, 1024), lanes(me.xl, 1024)])]
    sends = []
    for off, part in zip(XOFF[1:], parts):
        there = me.at(off)
        block = dst.at[rows(there.xh * 1024 + me.core * 512, 512), lanes(there.xl, 1024)]
        local.append((part, block))
        sends.append((SIBLING, part, block, []))
    return local, sends


def ffn_enter_plan(me, ins, outs):
    hidden, gate, up, p1, p2, p3 = ins
    full, w_gate, w_up = outs
    local, sends = gather_moves(me, hidden, full)
    for j, (own, dst) in enumerate(((gate, w_gate), (up, w_up))):
        a, b = weight_moves(me, own, [p.at[j] for p in (p1, p2, p3)], dst)
        local, sends = local + a, sends + b
    return local, sends


def down_plan(me, ins, outs):
    return weight_moves_t(me, ins[0], ins[1:], outs[0])


def leave_plan(me, ins, outs):
    local, sends = [], []
    mine = rows(me.chunk * CHUNK + me.y * SUB, SUB)
    for k, off in enumerate(PLANE):
        there = me.at(off)
        pairs = [(src.at[:, lanes(there.block)], dst.at[mine, :]) for src, dst in zip(ins[:2], outs[:2])]
        pairs.append((ins[2].at[:, lanes(there.block)], outs[2].at[me.block]))
        if k == 0:
            local += pairs
        else:
            sends += [(off, s, d, []) for s, d in pairs]
    return local, sends


def gains_plan(me, ins, outs):
    local = [(ins[0], outs[0].at[me.tok])]
    sends = [(off, ins[0], outs[0].at[me.tok], []) for off in TOKS[1:]]
    return local, sends


def block_probs(q_ref, kv_ref, start, i, stack):
    n = 256 * (i + 1)
    keys = kv_ref[rows_256(start, n), 0:64]
    scores = lax.dot_general(
        keys, stack, (((1,), (1,)), ((), ())), preferred_element_type=F32
    ) * (HEAD_DIM**-0.5)
    last = scores[n - 256 :, :]
    key_id = lax.broadcasted_iota(jnp.int32, (256, 512), 0)
    query_id = lax.broadcasted_iota(jnp.int32, (256, 512), 1) % 256
    last = jnp.where(key_id <= query_id, last, NEG)
    if n > 256:
        scores = jnp.concatenate([scores[: n - 256, :], last], axis=0)
    else:
        scores = last
    raised = jnp.exp(scores - jnp.max(scores, axis=0, keepdims=True))
    return keys, raised, jnp.sum(raised, axis=0, keepdims=True)


def rows_256(start, size):
    return pl.ds(pl.multiple_of(start, 256), size)


def starts_of(len_ref):
    long_first = len_ref[0, 0] > SHORT
    long_start = jnp.where(long_first, 0, SHORT)
    short_start = jnp.where(long_first, 2 * SHORT, 0)
    return ((long_start, 4), (short_start, 2))


def both(block):
    return jnp.concatenate([block[:, 0:64], block[:, 64:128]], axis=0)


def attend_body(len_ref, q_ref, kv_ref, out_ref):
    for start, blocks in starts_of(len_ref):
        for i in range(blocks):
            mine = rows_256(start + 256 * i, 256)
            stack = both(q_ref[mine, :])
            keys, raised, mass = block_probs(q_ref, kv_ref, start, i, stack)
            soft = (raised * (1.0 / mass)).astype(BF)
            values = kv_ref[rows_256(start, 256 * (i + 1)), 64:128]
            mixed = lax.dot_general(
                soft, values, (((0,), (0,)), ((), ())), preferred_element_type=F32
            )
            out_ref[mine, :] = jnp.concatenate([mixed[:256], mixed[256:]], axis=1).astype(BF)


def unrope(tensor, cosine, sine):
    lane = lax.broadcasted_iota(jnp.int32, tensor.shape, 1)
    first = (lane % 64) < 32
    swapped = jnp.where(first, pltpu.roll(tensor, 96, 1), -pltpu.roll(tensor, 32, 1))
    return tensor * cosine + swapped * sine


def attend_back_body(len_ref, q_ref, kv_ref, back_ref, cos_ref, sin_ref, dq_ref, dkv_ref, acc_ref):
    for start, blocks in starts_of(len_ref):
        acc_ref[...] = jnp.zeros(acc_ref.shape, F32)
        for i in range(blocks):
            n = 256 * (i + 1)
            mine = rows_256(start + 256 * i, 256)
            stack = both(q_ref[mine, :])
            keys, raised, mass = block_probs(q_ref, kv_ref, start, i, stack)
            soft = raised * (1.0 / mass)
            values = kv_ref[rows_256(start, n), 64:128]
            backs = both(back_ref[mine, :])
            prob_back = lax.dot_general(
                values, backs, (((1,), (1,)), ((), ())), preferred_element_type=F32
            )
            inner = jnp.sum(soft * prob_back, axis=0, keepdims=True)
            score_back = (soft * (prob_back - inner)).astype(BF)
            dq = lax.dot_general(
                score_back, keys, (((0,), (0,)), ((), ())), preferred_element_type=F32
            ) * (HEAD_DIM**-0.5)
            dq = jnp.concatenate([dq[:256], dq[256:]], axis=1)
            pos = slice(256 * i, 256 * i + 256)
            dq_ref[mine, :] = unrope(dq, cos_ref[pos, :], sin_ref[pos, :]).astype(BF)
            dk = jnp.dot(score_back, stack, preferred_element_type=F32) * (HEAD_DIM**-0.5)
            dv = jnp.dot(soft.astype(BF), backs, preferred_element_type=F32)
            acc_ref[0:n, :] += jnp.concatenate([dk, dv], axis=1)
        m = 256 * blocks
        acc = acc_ref[0:m, :]
        lane = lax.broadcasted_iota(jnp.int32, acc.shape, 1)
        turned = unrope(acc, cos_ref[0:m, :], sin_ref[0:m, :])
        dkv_ref[rows_256(start, m), :] = jnp.where(lane < 64, turned, acc).astype(BF)


def vmem_call(name, body, ins, outs, scratch=(), flops=0):
    return pl.pallas_call(
        body,
        name=name,
        out_shape=outs,
        in_specs=[pl.BlockSpec(memory_space=pltpu.SMEM)]
        + [pl.BlockSpec(memory_space=pltpu.VMEM)] * (len(ins) - 1),
        out_specs=[pl.BlockSpec(memory_space=pltpu.VMEM)] * len(outs),
        scratch_shapes=list(scratch),
        compiler_params=pltpu.CompilerParams(vmem_limit_bytes=48 * 2**20),
        cost_estimate=pl.CostEstimate(flops=flops, bytes_accessed=2**20, transcendentals=0),
    )(*ins)


def rope_table():
    halfway = HEAD_DIM // 2
    k = np.arange(halfway, dtype=np.float32)
    inverse = np.exp(-2.0 * k / HEAD_DIM * math.log(THETA)).astype(np.float32)
    wavelen = (2.0 * math.pi / inverse).astype(np.float32)
    scaled = inverse / np.float32(FACTOR)
    smooth = (INITIAL / wavelen - LOW_FACTOR) / (HIGH_FACTOR - LOW_FACTOR)
    middle = (1.0 - smooth) * scaled + smooth * inverse
    frequency = np.where(
        wavelen < INITIAL / HIGH_FACTOR,
        inverse,
        np.where(wavelen > INITIAL / LOW_FACTOR, scaled, middle),
    ).astype(np.float32)
    positions = np.concatenate([np.arange(512), np.arange(1024), np.arange(512)]).astype(np.float32)
    angles = (positions[:, None] * frequency[None, :]).astype(np.float32).astype(np.float64)
    return (
        np.tile(np.cos(angles).astype(np.float32), (1, 4)),
        np.tile(np.sin(angles).astype(np.float32), (1, 4)),
    )


def x_permute(value, k):
    if k == 1:
        return lax.ppermute(value, "narrow", [(0, 1), (1, 0)])
    if k == 2:
        return lax.ppermute(value, "wide", [(i, i ^ 1) for i in range(8)])
    return lax.ppermute(value, ("narrow", "wide"), [(i, i ^ 9) for i in range(16)])


def z_permute(value, d):
    return lax.ppermute(value, "tok", [(i, (i + 2 * d) % 8) for i in range(8)])


def y_permute(value, d):
    return lax.ppermute(value, "wide", [(i, (i + 2 * d) % 8) for i in range(8)])


def core_permute(value):
    return lax.ppermute(value, "tok", [(i, i ^ 1) for i in range(8)])


def pick(array, index, axis):
    return lax.dynamic_index_in_dim(array, index, axis, keepdims=False)


def part(array, start, size, axis):
    return lax.dynamic_slice_in_dim(array, start, size, axis)


def total(terms):
    out = terms[0].astype(F32)
    for term in terms[1:]:
        out = out + term.astype(F32)
    return out


def reduce_ffn(me, partial, rows_by_xl):
    view = partial.reshape(2, 8, 4, 2, 16, 2048)
    mine = pick(view, me.core, 3)
    came = core_permute(pick(view, 1 - me.core, 3))

    def quarter(k):
        there = me.at(XOFF[k])
        r, c = (there.xl, there.xh) if rows_by_xl else (there.xh, there.xl)
        return total([part(pick(a, r, 0), c * 1024, 1024, 3) for a in (mine, came)])

    own = quarter(0)
    got = [x_permute(quarter(k).astype(BF), k) for k in (1, 2, 3)]
    summed = total([own] + got).astype(BF)
    own = pick(summed, me.z, 1)
    got = [z_permute(pick(summed, (me.z + d) % 4, 1), d) for d in (1, 2, 3)]
    return total([own] + got)


def reduce_core(me, partial):
    view = partial.reshape(4, 2, 256, partial.shape[1])
    return pick(view, me.core, 1), core_permute(pick(view, 1 - me.core, 1))


def reduce_z(me, summed):
    own = pick(summed, me.z, 0)
    got = [z_permute(pick(summed, (me.z + d) % 4, 0), d) for d in (1, 2, 3)]
    return total([own] + got)


def reduce_heads(me, pair):
    pieces = [total([a[:, :, k * 128 : k * 128 + 128] for a in pair]) for k in range(4)]
    got = [x_permute(pieces[k].astype(BF), k) for k in (1, 2, 3)]
    return reduce_z(me, total([pieces[0]] + got).astype(BF))


def contract_rows(left_side, right_side):
    return lax.dot_general(
        left_side, right_side, (((0,), (0,)), ((), ())), preferred_element_type=F32
    )


def contract_cols(left_side, right_side):
    return lax.dot_general(
        left_side, right_side, (((1,), (1,)), ((), ())), preferred_element_type=F32
    )


def multiply(left_side, right_side):
    return jnp.dot(left_side, right_side, preferred_element_type=F32)


def per_device(
    layer_input,
    doc_lengths,
    attn_gain,
    w_query,
    w_key,
    w_value,
    w_output,
    ffn_gain,
    w_gate,
    w_up,
    w_down,
    output_grad,
):
    me = whereami()
    cos_np, sin_np = rope_table()
    cos_all, sin_all = jnp.asarray(cos_np), jnp.asarray(sin_np)
    long_first = doc_lengths[0, 0] > SHORT
    table_start = jnp.where(long_first, SHORT, 0) + me.chunk * CHUNK
    cos_here = part(cos_all, table_start, CHUNK, 0)
    sin_here = part(sin_all, table_start, CHUNK, 0)
    cos_doc, sin_doc = cos_all[512:1536], sin_all[512:1536]

    w_kv = jnp.concatenate(
        [part(w_key, me.y * 64, 64, 1), part(w_value, me.y * 64, 64, 1)], axis=1
    )
    full_in, w_attn, gains = exchange(
        "enter",
        0,
        enter_plan,
        [layer_input, w_query, w_kv, jnp.broadcast_to(ffn_gain[None, :], (8, 128))],
        [SDS((CHUNK, D), BF), SDS((D, 768), BF), SDS((16, 8, 128), F32)],
    )
    ffn_gain_all = gains[:, 0, :].reshape(1, D)

    half_out = part(w_output, me.core * 1024, 1024, 0)
    half_gu = jnp.stack([part(w_gate, me.core * 512, 512, 0), part(w_up, me.core * 512, 512, 0)])
    half_down = part(w_down, me.core * 512, 512, 0)
    full_in, half_out, half_gu, half_down = lax.optimization_barrier(
        (full_in, half_out, half_gu, half_down)
    )
    got_out = [x_permute(half_out, k) for k in (1, 2, 3)]
    got_gu = [x_permute(half_gu, k) for k in (1, 2, 3)]
    got_down = [x_permute(half_down, k) for k in (1, 2, 3)]

    in_f = full_in.astype(F32)
    scale_one = lax.rsqrt(jnp.mean(in_f * in_f, axis=1, keepdims=True) + EPS)
    normed = (in_f * scale_one * attn_gain[None, :]).astype(BF)
    lin = multiply(normed, w_attn)

    def turn(block):
        lane = lax.broadcasted_iota(jnp.int32, block.shape, 1)
        swapped = jnp.where(
            (lane % 64) < 32, -jnp.roll(block, -32, axis=1), jnp.roll(block, 32, axis=1)
        )
        return block * cos_here + swapped * sin_here

    turned = [turn(lin[:, k * 128 : k * 128 + 128]) for k in range(6)]
    for k in (4, 5):
        turned[k] = jnp.concatenate(
            [turned[k][:, :64], lin[:, k * 128 + 64 : k * 128 + 128]], axis=1
        )
    lin = jnp.concatenate(turned, axis=1).astype(BF)
    queries, kv = exchange(
        "to_heads", 1, to_heads_plan, [lin], [SDS((ROWS, 128), BF), SDS((ROWS, 128), BF)]
    )
    (heads_out,) = vmem_call(
        "attend", attend_body, [doc_lengths, queries, kv], [SDS((ROWS, 128), BF)], flops=2 * 10**9
    )
    heads_cat, w_out = exchange(
        "heads_out",
        2,
        heads_out_plan,
        [heads_out, w_output] + got_out,
        [SDS((CHUNK, 512), BF), SDS((D, 512), BF)],
    )
    attn_term = contract_cols(heads_cat, w_out).astype(BF)
    attn_terms, grad_full = exchange(
        "out_sum",
        3,
        out_sum_plan,
        [attn_term, output_grad],
        [SDS((4, SUB, D), BF), SDS((CHUNK, D), BF)],
    )
    in_mine = part(full_in, me.y * SUB, SUB, 0).astype(F32)
    resid = in_mine + jnp.sum(attn_terms.astype(F32), axis=0)
    scale_two = lax.rsqrt(jnp.mean(resid * resid, axis=1, keepdims=True) + EPS)
    ffn_mine = (resid * scale_two * ffn_gain_all).astype(BF)
    ffn_input, wg, wu = exchange(
        "ffn_enter",
        4,
        ffn_enter_plan,
        [ffn_mine, w_gate, w_up] + got_gu,
        [SDS((CHUNK, D), BF), SDS((D, D), BF), SDS((D, D), BF)],
    )
    gate_lin = multiply(ffn_input, wg)
    up_lin = multiply(ffn_input, wu)
    sigmoid_gate = jax.nn.sigmoid(gate_lin)
    act = (gate_lin * sigmoid_gate * up_lin).astype(BF)
    (wd,) = exchange("down_weight", 5, down_plan, [w_down] + got_down, [SDS((D, D), BF)])
    down_term = multiply(act, wd).astype(BF)
    act_back = contract_cols(grad_full, wd)
    gate_back = (act_back * up_lin * sigmoid_gate * (1.0 + gate_lin * (1.0 - sigmoid_gate))).astype(
        BF
    )
    up_back = (act_back * gate_lin * sigmoid_gate).astype(BF)
    ffn_term = (contract_cols(gate_back, wg) + contract_cols(up_back, wu)).astype(BF)
    down_terms, ffn_terms = exchange(
        "ffn_sum",
        6,
        sum_plan,
        [down_term, ffn_term],
        [SDS((4, SUB, D), BF), SDS((4, SUB, D), BF)],
    )
    out_mine = (resid + jnp.sum(down_terms.astype(F32), axis=0)).astype(BF)
    ffn_input_back = jnp.sum(ffn_terms.astype(F32), axis=0)
    grad_mine = part(grad_full, me.y * SUB, SUB, 0).astype(F32)
    scaled_back = ffn_input_back * ffn_gain_all
    inner_two = jnp.sum(scaled_back * resid, axis=1, keepdims=True)
    resid_back = grad_mine + scale_two * scaled_back - resid * scale_two**3 * inner_two / D
    ffn_gain_part = jnp.sum(ffn_input_back * resid * scale_two, axis=0, keepdims=True)
    (mix_full,) = exchange(
        "mix_gather", 7, gather_plan, [resid_back.astype(BF)], [SDS((CHUNK, D), BF)]
    )
    back_cat = multiply(mix_full, w_out).astype(BF)
    (heads_back,) = exchange("heads_back", 8, heads_back_plan, [back_cat], [SDS((ROWS, 128), BF)])

    down_grad = reduce_ffn(me, contract_rows(act, grad_full).astype(BF), False)
    gate_grad = reduce_ffn(me, contract_rows(ffn_input, gate_back).astype(BF), True)
    up_grad = reduce_ffn(me, contract_rows(ffn_input, up_back).astype(BF), True)
    out_pair = reduce_core(me, contract_rows(mix_full, heads_cat).astype(BF))
    output_proj_grad = reduce_heads(me, out_pair)

    query_back, kv_back = vmem_call(
        "attend_back",
        attend_back_body,
        [doc_lengths, queries, kv, heads_back, cos_doc, sin_doc],
        [SDS((ROWS, 128), BF), SDS((ROWS, 128), BF)],
        scratch=[pltpu.VMEM((1024, 128), F32)],
        flops=5 * 10**9,
    )
    (cat_back,) = exchange(
        "grads_out", 9, grads_out_plan, [query_back, kv_back], [SDS((CHUNK, 1024), BF)]
    )
    normed_term = (
        contract_cols(cat_back[:, :768], w_attn) + contract_cols(cat_back[:, 768:], w_attn[:, 512:])
    ).astype(BF)
    (normed_terms,) = exchange(
        "normed_sum", 10, sum_plan, [normed_term], [SDS((4, SUB, D), BF)]
    )
    attn_partial = contract_rows(normed, cat_back)
    kv_partial = attn_partial[:, 512:768] + attn_partial[:, 768:]
    query_grad = reduce_heads(me, reduce_core(me, attn_partial[:, :512].astype(BF)))

    kv_pair = reduce_core(me, kv_partial.astype(BF))
    kv_pair = [a.reshape(4, 4, 2, 32, 256) for a in kv_pair]

    def kv_piece(k):
        return total([pick(a, me.at(XOFF[k]).xh, 2)[..., 128 * XOFF[k][2] : 128 * XOFF[k][2] + 128] for a in kv_pair])

    got = [x_permute(kv_piece(k).astype(BF), k) for k in (1, 2, 3)]
    kv_sum = reduce_z(me, total([kv_piece(0)] + got).astype(BF))
    kv_cols = jnp.stack(
        [pick(kv_sum, me.y, 0)] + [y_permute(pick(kv_sum, (me.y + d) % 4, 0), d) for d in (1, 2, 3)]
    )
    kv_cols = jnp.concatenate([pick(kv_cols, (me.y - h) % 4, 0) for h in range(4)], axis=1)
    kv_cols = kv_cols.reshape(32, 4, 2, 64)
    key_grad = kv_cols[:, :, 0, :].reshape(32, 256)
    value_grad = kv_cols[:, :, 1, :].reshape(32, 256)

    normed_back = jnp.sum(normed_terms.astype(F32), axis=0)
    scale_mine = part(scale_one, me.y * SUB, SUB, 0)
    scaled_back = normed_back * attn_gain[None, :]
    inner_one = jnp.sum(scaled_back * in_mine, axis=1, keepdims=True)
    in_grad_mine = (
        resid_back + scale_mine * scaled_back - in_mine * scale_mine**3 * inner_one / D
    ).astype(BF)
    attn_gain_part = jnp.sum(normed_back * in_mine * scale_mine, axis=0, keepdims=True)
    gain_parts = jnp.concatenate([attn_gain_part, ffn_gain_part, jnp.zeros((6, D), F32)], axis=0)
    layer_output, input_grad, gain_terms = exchange(
        "leave",
        11,
        leave_plan,
        [out_mine, in_grad_mine, gain_parts],
        [SDS((ROWS, 128), BF), SDS((ROWS, 128), BF), SDS((16, 8, 128), F32)],
    )
    (gain_toks,) = exchange(
        "gains", 12, gains_plan, [jnp.sum(gain_terms, axis=0)], [SDS((8, 8, 128), F32)]
    )
    gain_grads = part(jnp.sum(gain_toks, axis=0), me.tok * 16, 16, 1)
    return (
        layer_output,
        input_grad,
        gain_grads[0:1],
        query_grad,
        key_grad,
        value_grad,
        output_proj_grad,
        gain_grads[1:2],
        gate_grad,
        up_grad,
        down_grad,
    )


def solution(mesh):
    in_specs = (
        P("tok", ("narrow", "wide")),
        P("tok", None),
        P(),
        P(None, ("narrow", "wide")),
        P(None, "narrow"),
        P(None, "narrow"),
        P(None, ("narrow", "wide")),
        P(("narrow", "wide")),
        P("narrow", "wide"),
        P("narrow", "wide"),
        P("wide", "narrow"),
        P("tok", ("narrow", "wide")),
    )
    out_specs = (
        P("tok", ("narrow", "wide")),
        P("tok", ("narrow", "wide")),
        P(("narrow", "wide"), "tok"),
        P("tok", ("narrow", "wide")),
        P(("tok", "wide"), "narrow"),
        P(("tok", "wide"), "narrow"),
        P("tok", ("narrow", "wide")),
        P(("narrow", "wide"), "tok"),
        P("narrow", "tok", "wide"),
        P("narrow", "tok", "wide"),
        P("wide", "tok", "narrow"),
    )
    return jax.shard_map(
        per_device, mesh=mesh, in_specs=in_specs, out_specs=out_specs, check_vma=False
    )
```

```python
import functools
import math

import jax
import jax.numpy as jnp
import numpy as np
from jax import lax
from jax.experimental import pallas as pl
from jax.experimental.pallas import tpu as pltpu
from jax.sharding import PartitionSpec as P

HEADS = 32
KV_HEADS = 8
HEAD_DIM = 64
GROUP = 128
EPS = 1e-05
THETA = 500000.0
FACTOR = 32.0
LOW_FACTOR = 1.0
HIGH_FACTOR = 4.0
INITIAL = 8192.0
NEG = -1e30

D = 2048
ROWS = 1536
CHUNK = 384
SUB = 96
SHORT = 512
BF = jnp.bfloat16
F32 = jnp.float32
MESH = pl.DeviceIdType.MESH
SDS = jax.ShapeDtypeStruct

HERE = (0, 0, 0, 0, 0)
XOFF = [(0, 0, 0, 0, 0), (0, 0, 1, 0, 0), (0, 0, 0, 0, 1), (0, 0, 1, 0, 1)]
YOFF = [(0, 0, 0, d, 0) for d in range(4)]
PLANE = [(0, 0, a, b, e) for b in range(4) for a in range(2) for e in range(2)]
SIBLING = (1, 0, 0, 0, 0)
TOKS = [(a, b, 0, 0, 0) for b in range(4) for a in range(2)]


class Place:
    def __init__(self, core, z, xl, y, xh):
        self.core, self.z, self.xl, self.y, self.xh = core, z, xl, y, xh
        self.tok = z * 2 + core
        self.wide = y * 2 + xh
        self.block = xl * 8 + self.wide
        self.chunk = xl * 2 + xh

    def at(self, off):
        return Place(
            (self.core + off[0]) % 2,
            (self.z + off[1]) % 4,
            (self.xl + off[2]) % 2,
            (self.y + off[3]) % 4,
            (self.xh + off[4]) % 2,
        )

    def device(self):
        return (self.tok, self.xl, self.wide)


def whereami():
    tok = lax.axis_index("tok")
    wide = lax.axis_index("wide")
    return Place(tok % 2, tok // 2, lax.axis_index("narrow"), wide // 2, wide % 2)


def rows(start, size):
    return pl.ds(pl.multiple_of(start, size), size)


def exchange(name, number, plan, ins, outs):
    n_in, n_out = len(ins), len(outs)

    def count():
        fake = Place(0, 0, 0, 0, 0)
        probe = [_Any() for _ in range(n_in)], [_Any() for _ in range(n_out)]
        local, sends = plan(fake, *probe)
        return len(local), sum(1 + len(s[3]) for s in sends)

    n_local, n_send = count()

    def body(*refs):
        sources, targets = refs[:n_in], refs[n_in : n_in + n_out]
        send_sem, recv_sem, local_sem = refs[n_in + n_out :]
        me = whereami()
        local, sends = plan(me, sources, targets)
        offsets = []
        for off, _, _, forwards in sends:
            for o in [off] + [f[0] for f in forwards]:
                if o not in offsets:
                    offsets.append(o)
        barrier = pltpu.get_barrier_semaphore()
        for off in offsets:
            back = tuple(-v for v in off)
            pl.semaphore_signal(
                barrier, inc=1, device_id=me.at(back).device(), device_id_type=MESH
            )
        near = []
        for i, (src, dst) in enumerate(local):
            near.append(pltpu.make_async_copy(src, dst, local_sem.at[i]))
            near[-1].start()
        pl.semaphore_wait(barrier, len(offsets))
        slot = 0

        def launch(off, src, dst):
            nonlocal slot
            copy = pltpu.make_async_remote_copy(
                src_ref=src,
                dst_ref=dst,
                send_sem=send_sem.at[slot],
                recv_sem=recv_sem.at[slot],
                device_id=me.at(off).device(),
                device_id_type=MESH,
            )
            copy.start()
            slot += 1
            return copy

        first = [(launch(off, src, dst), forwards) for off, src, dst, forwards in sends]
        second = []
        for copy, forwards in first:
            if forwards:
                copy.wait_recv()
                second += [launch(*f) for f in forwards]
        for copy, forwards in first:
            copy.wait_send()
            if not forwards:
                copy.wait_recv()
        for copy in second:
            copy.wait()
        for copy in near:
            copy.wait()

    return pl.pallas_call(
        body,
        name=name,
        out_shape=outs,
        in_specs=[pl.BlockSpec(memory_space=pl.ANY)] * n_in,
        out_specs=[pl.BlockSpec(memory_space=pltpu.VMEM)] * n_out,
        scratch_shapes=[
            pltpu.SemaphoreType.DMA((n_send,)),
            pltpu.SemaphoreType.DMA((n_send,)),
            pltpu.SemaphoreType.DMA((max(n_local, 1),)),
        ],
        compiler_params=pltpu.CompilerParams(
            collective_id=number, has_side_effects=True, vmem_limit_bytes=40 * 2**20
        ),
    )(*ins)


class _Any:
    @property
    def at(self):
        return self

    def __getitem__(self, key):
        return self


def lanes(index, size=128):
    return pl.ds(pl.multiple_of(index * size, size), size)


def spread_plan(me, src, dst, own_first=False):
    def block(off):
        return lanes(off[2] * 8 + me.wide if own_first else me.block)

    local = [(src.at[rows(me.chunk * CHUNK, CHUNK), :], dst.at[:, block(HERE)])]
    sends = [
        (off, src.at[rows(me.at(off).chunk * CHUNK, CHUNK), :], dst.at[:, block(off)], [])
        for off in PLANE[1:]
    ]
    return local, sends


def enter_plan(me, ins, outs):
    hidden, w_q, w_kv, gain = ins
    full, w_attn, gains = outs
    half = rows(me.core * 1024, 1024)
    local, sends = spread_plan(me, hidden, full)
    local += [
        (w_q, w_attn.at[:, 0:128]),
        (w_kv, w_attn.at[:, 512:640]),
        (gain, gains.at[me.block]),
    ]
    head = []
    for k in (1, 2, 3):
        cols = slice(k * 128, k * 128 + 128)
        block = w_attn.at[half, cols]
        head.append((XOFF[k], w_q.at[half, :], block, [(SIBLING, block, block)]))
    block = w_attn.at[half, 640:768]
    head.append((XOFF[1], w_kv.at[half, :], block, [(SIBLING, block, block)]))
    sends = head + sends
    sends += [(off, gain, gains.at[me.block], []) for off in PLANE[1:]]
    return local, sends


def to_heads_plan(me, ins, outs):
    (lin,) = ins
    q, kv = outs
    mine = rows(me.chunk * CHUNK, CHUNK)
    local, sends = [], []
    for k, off in enumerate(XOFF):
        kv_col = 512 + 128 * off[2]
        pairs = [
            (lin.at[:, k * 128 : k * 128 + 128], q.at[mine, :]),
            (lin.at[:, kv_col : kv_col + 128], kv.at[mine, :]),
        ]
        if k == 0:
            local += pairs
        else:
            sends += [(off, s, d, []) for s, d in pairs]
    return local, sends


def from_heads_moves(me, src, dst, first_col=0):
    local, sends = [], []
    for k, off in enumerate(XOFF):
        col = first_col + k * 128
        pair = (src.at[rows(me.at(off).chunk * CHUNK, CHUNK), :], dst.at[:, col : col + 128])
        if k == 0:
            local.append(pair)
        else:
            sends.append((off, *pair, []))
    return local, sends


def heads_out_plan(me, ins, outs):
    heads, w_out, half1, half2, half3 = ins
    cat, w_cat = outs
    local, sends = from_heads_moves(me, heads, cat)
    half = rows(me.core * 1024, 1024)
    local.append((w_out, w_cat.at[:, 0:128]))
    for k, part in ((1, half1), (2, half2), (3, half3)):
        block = w_cat.at[half, k * 128 : k * 128 + 128]
        local.append((part, block))
        sends.append((SIBLING, part, block, []))
    return local, sends


def heads_back_plan(me, ins, outs):
    (cat,) = ins
    (heads,) = outs
    mine = rows(me.chunk * CHUNK, CHUNK)
    local, sends = [], []
    for k, off in enumerate(XOFF):
        pair = (cat.at[:, k * 128 : k * 128 + 128], heads.at[mine, :])
        if k == 0:
            local.append(pair)
        else:
            sends.append((off, *pair, []))
    return local, sends


def grads_out_plan(me, ins, outs):
    q, kv = ins
    (cat,) = outs
    local, sends = from_heads_moves(me, q, cat)
    local2, sends2 = from_heads_moves(me, kv, cat, 512)
    return local + local2, sends + sends2


def scatter_moves(me, src, dst):
    local = [(src.at[rows(me.y * SUB, SUB), :], dst.at[me.y])]
    sends = [(off, src.at[rows(me.at(off).y * SUB, SUB), :], dst.at[me.y], []) for off in YOFF[1:]]
    return local, sends


def out_sum_plan(me, ins, outs):
    local, sends = scatter_moves(me, ins[0], outs[0])
    local2, sends2 = spread_plan(me, ins[1], outs[1], True)
    return local + local2, sends + sends2


def sum_plan(me, ins, outs):
    local, sends = [], []
    for src, dst in zip(ins, outs):
        a, b = scatter_moves(me, src, dst)
        local, sends = local + a, sends + b
    return local, sends


def gather_moves(me, src, dst):
    block = dst.at[rows(me.y * SUB, SUB), :]
    return [(src, block)], [(off, src, block, []) for off in YOFF[1:]]


def gather_plan(me, ins, outs):
    return gather_moves(me, ins[0], outs[0])


def weight_moves(me, own, parts, dst):
    local = [(own, dst.at[rows(me.xl * 1024, 1024), lanes(me.xh, 1024)])]
    sends = []
    for off, part in zip(XOFF[1:], parts):
        there = me.at(off)
        block = dst.at[rows(there.xl * 1024 + me.core * 512, 512), lanes(there.xh, 1024)]
        local.append((part, block))
        sends.append((SIBLING, part, block, []))
    return local, sends


def weight_moves_t(me, own, parts, dst):
    local = [(own, dst.at[rows(me.xh * 1024, 1024), lanes(me.xl, 1024)])]
    sends = []
    for off, part in zip(XOFF[1:], parts):
        there = me.at(off)
        block = dst.at[rows(there.xh * 1024 + me.core * 512, 512), lanes(there.xl, 1024)]
        local.append((part, block))
        sends.append((SIBLING, part, block, []))
    return local, sends


def ffn_enter_plan(me, ins, outs):
    hidden, gate, up, p1, p2, p3 = ins
    full, w_gate, w_up = outs
    local, sends = gather_moves(me, hidden, full)
    for j, (own, dst) in enumerate(((gate, w_gate), (up, w_up))):
        a, b = weight_moves(me, own, [p.at[j] for p in (p1, p2, p3)], dst)
        local, sends = local + a, sends + b
    return local, sends


def down_plan(me, ins, outs):
    return weight_moves_t(me, ins[0], ins[1:], outs[0])


def leave_plan(me, ins, outs):
    local, sends = [], []
    mine = rows(me.chunk * CHUNK + me.y * SUB, SUB)
    for k, off in enumerate(PLANE):
        there = me.at(off)
        pairs = [(src.at[:, lanes(there.block)], dst.at[mine, :]) for src, dst in zip(ins[:2], outs[:2])]
        pairs.append((ins[2].at[:, lanes(there.block)], outs[2].at[me.block]))
        if k == 0:
            local += pairs
        else:
            sends += [(off, s, d, []) for s, d in pairs]
    return local, sends


def gains_plan(me, ins, outs):
    local = [(ins[0], outs[0].at[me.tok])]
    sends = [(off, ins[0], outs[0].at[me.tok], []) for off in TOKS[1:]]
    return local, sends


def block_probs(q_ref, kv_ref, start, i, stack):
    n = 256 * (i + 1)
    keys = kv_ref[rows_256(start, n), 0:64]
    scores = lax.dot_general(
        keys, stack, (((1,), (1,)), ((), ())), preferred_element_type=F32
    ) * (HEAD_DIM**-0.5)
    last = scores[n - 256 :, :]
    key_id = lax.broadcasted_iota(jnp.int32, (256, 512), 0)
    query_id = lax.broadcasted_iota(jnp.int32, (256, 512), 1) % 256
    last = jnp.where(key_id <= query_id, last, NEG)
    if n > 256:
        scores = jnp.concatenate([scores[: n - 256, :], last], axis=0)
    else:
        scores = last
    raised = jnp.exp(scores - jnp.max(scores, axis=0, keepdims=True))
    return keys, raised, jnp.sum(raised, axis=0, keepdims=True)


def rows_256(start, size):
    return pl.ds(pl.multiple_of(start, 256), size)


def starts_of(len_ref):
    long_first = len_ref[0, 0] > SHORT
    long_start = jnp.where(long_first, 0, SHORT)
    short_start = jnp.where(long_first, 2 * SHORT, 0)
    return ((long_start, 4), (short_start, 2))


def both(block):
    return jnp.concatenate([block[:, 0:64], block[:, 64:128]], axis=0)


def attend_body(len_ref, q_ref, kv_ref, out_ref):
    for start, blocks in starts_of(len_ref):
        for i in range(blocks):
            mine = rows_256(start + 256 * i, 256)
            stack = both(q_ref[mine, :])
            keys, raised, mass = block_probs(q_ref, kv_ref, start, i, stack)
            soft = (raised * (1.0 / mass)).astype(BF)
            values = kv_ref[rows_256(start, 256 * (i + 1)), 64:128]
            mixed = lax.dot_general(
                soft, values, (((0,), (0,)), ((), ())), preferred_element_type=F32
            )
            out_ref[mine, :] = jnp.concatenate([mixed[:256], mixed[256:]], axis=1).astype(BF)


def unrope(tensor, cosine, sine):
    lane = lax.broadcasted_iota(jnp.int32, tensor.shape, 1)
    first = (lane % 64) < 32
    swapped = jnp.where(first, pltpu.roll(tensor, 96, 1), -pltpu.roll(tensor, 32, 1))
    return tensor * cosine + swapped * sine


def attend_back_body(len_ref, q_ref, kv_ref, back_ref, cos_ref, sin_ref, dq_ref, dkv_ref, acc_ref):
    for start, blocks in starts_of(len_ref):
        acc_ref[...] = jnp.zeros(acc_ref.shape, F32)
        for i in range(blocks):
            n = 256 * (i + 1)
            mine = rows_256(start + 256 * i, 256)
            stack = both(q_ref[mine, :])
            keys, raised, mass = block_probs(q_ref, kv_ref, start, i, stack)
            soft = raised * (1.0 / mass)
            values = kv_ref[rows_256(start, n), 64:128]
            backs = both(back_ref[mine, :])
            prob_back = lax.dot_general(
                values, backs, (((1,), (1,)), ((), ())), preferred_element_type=F32
            )
            inner = jnp.sum(soft * prob_back, axis=0, keepdims=True)
            score_back = (soft * (prob_back - inner)).astype(BF)
            dq = lax.dot_general(
                score_back, keys, (((0,), (0,)), ((), ())), preferred_element_type=F32
            ) * (HEAD_DIM**-0.5)
            dq = jnp.concatenate([dq[:256], dq[256:]], axis=1)
            pos = slice(256 * i, 256 * i + 256)
            dq_ref[mine, :] = unrope(dq, cos_ref[pos, :], sin_ref[pos, :]).astype(BF)
            dk = jnp.dot(score_back, stack, preferred_element_type=F32) * (HEAD_DIM**-0.5)
            dv = jnp.dot(soft.astype(BF), backs, preferred_element_type=F32)
            acc_ref[0:n, :] += jnp.concatenate([dk, dv], axis=1)
        m = 256 * blocks
        acc = acc_ref[0:m, :]
        lane = lax.broadcasted_iota(jnp.int32, acc.shape, 1)
        turned = unrope(acc, cos_ref[0:m, :], sin_ref[0:m, :])
        dkv_ref[rows_256(start, m), :] = jnp.where(lane < 64, turned, acc).astype(BF)


def vmem_call(name, body, ins, outs, scratch=(), flops=0):
    return pl.pallas_call(
        body,
        name=name,
        out_shape=outs,
        in_specs=[pl.BlockSpec(memory_space=pltpu.SMEM)]
        + [pl.BlockSpec(memory_space=pltpu.VMEM)] * (len(ins) - 1),
        out_specs=[pl.BlockSpec(memory_space=pltpu.VMEM)] * len(outs),
        scratch_shapes=list(scratch),
        compiler_params=pltpu.CompilerParams(vmem_limit_bytes=48 * 2**20),
        cost_estimate=pl.CostEstimate(flops=flops, bytes_accessed=2**20, transcendentals=0),
    )(*ins)


def rope_table():
    halfway = HEAD_DIM // 2
    k = np.arange(halfway, dtype=np.float32)
    inverse = np.exp(-2.0 * k / HEAD_DIM * math.log(THETA)).astype(np.float32)
    wavelen = (2.0 * math.pi / inverse).astype(np.float32)
    scaled = inverse / np.float32(FACTOR)
    smooth = (INITIAL / wavelen - LOW_FACTOR) / (HIGH_FACTOR - LOW_FACTOR)
    middle = (1.0 - smooth) * scaled + smooth * inverse
    frequency = np.where(
        wavelen < INITIAL / HIGH_FACTOR,
        inverse,
        np.where(wavelen > INITIAL / LOW_FACTOR, scaled, middle),
    ).astype(np.float32)
    positions = np.concatenate([np.arange(512), np.arange(1024), np.arange(512)]).astype(np.float32)
    angles = (positions[:, None] * frequency[None, :]).astype(np.float32).astype(np.float64)
    return (
        np.tile(np.cos(angles).astype(np.float32), (1, 4)),
        np.tile(np.sin(angles).astype(np.float32), (1, 4)),
    )


def x_permute(value, k):
    if k == 1:
        return lax.ppermute(value, "narrow", [(0, 1), (1, 0)])
    if k == 2:
        return lax.ppermute(value, "wide", [(i, i ^ 1) for i in range(8)])
    return lax.ppermute(value, ("narrow", "wide"), [(i, i ^ 9) for i in range(16)])


def z_permute(value, d):
    return lax.ppermute(value, "tok", [(i, (i + 2 * d) % 8) for i in range(8)])


def y_permute(value, d):
    return lax.ppermute(value, "wide", [(i, (i + 2 * d) % 8) for i in range(8)])


def core_permute(value):
    return lax.ppermute(value, "tok", [(i, i ^ 1) for i in range(8)])


def pick(array, index, axis):
    return lax.dynamic_index_in_dim(array, index, axis, keepdims=False)


def part(array, start, size, axis):
    return lax.dynamic_slice_in_dim(array, start, size, axis)


def total(terms):
    out = terms[0].astype(F32)
    for term in terms[1:]:
        out = out + term.astype(F32)
    return out


def reduce_ffn(me, partial):
    view = partial.reshape(2, 8, 4, 2, 16, 2048)
    mine = pick(view, me.core, 3)
    came = core_permute(pick(view, 1 - me.core, 3))

    def quarter(k):
        r, c = XOFF[k][2], XOFF[k][4]
        return total([a[r, ..., c * 1024 : c * 1024 + 1024] for a in (mine, came)])

    own = quarter(0)
    got = [x_permute(quarter(k).astype(BF), k) for k in (1, 2, 3)]
    summed = total([own] + got).astype(BF)
    own = pick(summed, me.z, 1)
    got = [z_permute(pick(summed, (me.z + d) % 4, 1), d) for d in (1, 2, 3)]
    return total([own] + got)


def reduce_core(me, partial):
    view = partial.reshape(4, 2, 256, partial.shape[1])
    return pick(view, me.core, 1), core_permute(pick(view, 1 - me.core, 1))


def reduce_z(me, summed):
    own = pick(summed, me.z, 0)
    got = [z_permute(pick(summed, (me.z + d) % 4, 0), d) for d in (1, 2, 3)]
    return total([own] + got)


def reduce_heads(me, pair):
    pieces = [total([a[:, :, k * 128 : k * 128 + 128] for a in pair]) for k in range(4)]
    got = [x_permute(pieces[k].astype(BF), k) for k in (1, 2, 3)]
    return reduce_z(me, total([pieces[0]] + got).astype(BF))


def contract_rows(left_side, right_side):
    return lax.dot_general(
        left_side, right_side, (((0,), (0,)), ((), ())), preferred_element_type=F32
    )


def contract_cols(left_side, right_side):
    return lax.dot_general(
        left_side, right_side, (((1,), (1,)), ((), ())), preferred_element_type=F32
    )


def multiply(left_side, right_side):
    return jnp.dot(left_side, right_side, preferred_element_type=F32)


class Wire:
    def __init__(self, me, send_sem, recv_sem):
        self.me, self.send_sem, self.recv_sem, self.used = me, send_sem, recv_sem, 0

    def send(self, off, src, dst):
        copy = pltpu.make_async_remote_copy(
            src_ref=src,
            dst_ref=dst,
            send_sem=self.send_sem.at[self.used],
            recv_sem=self.recv_sem.at[self.used],
            device_id=self.me.at(off).device(),
            device_id_type=MESH,
        )
        copy.start()
        self.used += 1
        return copy


def meet(me, offsets):
    barrier = pltpu.get_barrier_semaphore()
    for off in offsets:
        back = tuple(-v for v in off)
        pl.semaphore_signal(barrier, inc=1, device_id=me.at(back).device(), device_id_type=MESH)
    pl.semaphore_wait(barrier, len(offsets))


def finish(copies):
    for copy in copies:
        copy.wait()


ZOFF = [(0, d, 0, 0, 0) for d in range(4)]


def weights_body(pieces, whole, send_sem, recv_sem):
    me = whereami()
    wire = Wire(me, send_sem, recv_sem)
    meet(me, XOFF[1:] + ZOFF[1:] + [SIBLING])
    over_x = [wire.send(XOFF[k], pieces, whole.at[k - 1, :, me.tok]) for k in (1, 2, 3)]
    over_z, over_core = [], []
    for k in (1, 2, 3):
        over_x[k - 1].wait_recv()
        block = whole.at[k - 1, :, me.tok]
        over_core.append(wire.send(SIBLING, block, block))
        over_z.append([wire.send(ZOFF[d], block, block) for d in (1, 2, 3)])
    for k in (1, 2, 3):
        for d in (1, 2, 3):
            over_z[k - 1][d - 1].wait_recv()
            block = whole.at[k - 1, :, (me.z - d + 4) % 4 * 2 + me.core]
            over_core.append(wire.send(SIBLING, block, block))
    for copy in over_x:
        copy.wait_send()
    for copies in over_z:
        for copy in copies:
            copy.wait_send()
    finish(over_core)


def gather_weights(pieces):
    return pl.pallas_call(
        weights_body,
        name="weights",
        out_shape=SDS((3, 3, 8, 128, 1024), BF),
        in_specs=[pl.BlockSpec(memory_space=pl.ANY)],
        out_specs=pl.BlockSpec(memory_space=pl.ANY),
        scratch_shapes=[pltpu.SemaphoreType.DMA((24,)), pltpu.SemaphoreType.DMA((24,))],
        compiler_params=pltpu.CompilerParams(collective_id=13, has_side_effects=True),
    )(pieces)


class PairSum:
    def __init__(self, me, left, right, terms, came, send_sem, recv_sem):
        self.me, self.left, self.right, self.terms, self.came = me, left, right, terms, came
        self.send_sem, self.recv_sem = send_sem, recv_sem

    def copy(self, i):
        return pltpu.make_async_remote_copy(
            src_ref=self.terms.at[i, :, :, 1 - self.me.core],
            dst_ref=self.came.at[i],
            send_sem=self.send_sem.at[i],
            recv_sem=self.recv_sem.at[i],
            device_id=self.me.at(SIBLING).device(),
            device_id_type=MESH,
        )

    def multiply(self, first, last):
        def step(i, _):
            cols = pl.ds(pl.multiple_of(i * 256, 256), 256)
            block = contract_rows(self.left[:, cols], self.right[...])
            self.terms[i] = block.astype(BF).reshape(2, 4, 2, 16, 2048)
            self.copy(i).start()
            return 0

        lax.fori_loop(first, last, step, 0)

    def add(self, first, last):
        def step(i, _):
            copy = self.copy(i)
            copy.wait_recv()
            mine = self.terms[i, :, :, self.me.core].astype(F32) + self.came[i].astype(F32)
            self.terms[i, :, :, self.me.core] = mine.astype(BF)
            return 0

        lax.fori_loop(first, last, step, 0)

    def sent(self):
        def step(i, _):
            self.copy(i).wait_send()
            return 0

        lax.fori_loop(0, 8, step, 0)


def ffn_body(
    mine_ref,
    grad_ref,
    resid_ref,
    scale_ref,
    gain_ref,
    w_out_ref,
    own_gate,
    own_up,
    own_down,
    whole,
    out_mine,
    resid_back,
    gain_part,
    mix_full,
    heads_back,
    ffn_in,
    up_back,
    down_own,
    down_came,
    gate_own,
    gate_came,
    turned,
    act,
    gate_back,
    gate_tile,
    up_tile,
    down_tile,
    down_acc,
    ffn_acc,
    down_send,
    ffn_send,
    down_recv,
    ffn_recv,
    mix_mine,
    back_cat,
    down_terms,
    gate_terms,
    came,
    send_sem,
    recv_sem,
    core_send,
    core_recv,
    tile_sem,
    local_sem,
    ack,
):
    me = whereami()
    wire = Wire(me, send_sem, recv_sem)
    half = [lanes(me.xl, 1024), lanes(1 - me.xl, 1024)]
    here = rows(me.y * SUB, SUB)

    def tile_copies(e, q, slot):
        copies = []
        cols = pl.ds(pl.multiple_of(q * 256, 256), 256)
        for dxl in range(2):
            k = e * 2 + dxl
            for j, (own, tile) in enumerate(
                ((own_gate, gate_tile), (own_up, up_tile), (own_down, down_tile))
            ):
                block = own if k == 0 else whole.at[k - 1, j]
                if j < 2:
                    src, dst = block.at[:, :, cols], tile.at[slot, dxl]
                else:
                    src = block.at[pl.ds(q * 2, 2)]
                    dst = tile.at[slot, :, :, dxl * 1024 : dxl * 1024 + 1024]
                copies.append(pltpu.make_async_copy(src, dst, tile_sem.at[slot, dxl * 3 + j]))
        return copies

    def fetch(e, q, slot):
        for copy in tile_copies(e, q, slot):
            copy.start()

    meet(me, YOFF[1:] + XOFF[1:] + ZOFF[1:] + [SIBLING])
    for h in range(2):
        turned[:, h * 1024 : h * 1024 + 1024] = mine_ref[:, half[h]]
    gathers = [wire.send(off, turned, ffn_in.at[here, :]) for off in YOFF[1:]]
    fetch(0, 0, 0)
    ffn_in[here, :] = turned[...]
    down_acc[...] = jnp.zeros(down_acc.shape, F32)
    ffn_acc[...] = jnp.zeros(ffn_acc.shape, F32)
    finish(gathers)

    down_sum = PairSum(me, act, grad_ref, down_terms, came, core_send.at[0], core_recv.at[0])
    gate_sum = PairSum(me, ffn_in, gate_back, gate_terms, came, core_send.at[1], core_recv.at[1])

    for e in range(2):

        def step(q, _, e=e):
            slot = q % 2

            @pl.when(q < 3)
            def _():
                fetch(e, q + 1, 1 - slot)

            if e == 0:

                @pl.when(q == 3)
                def _():
                    fetch(1, 0, 0)

            for copy in tile_copies(e, q, slot):
                copy.wait()
            cols = pl.ds(pl.multiple_of(e * 1024 + q * 256, 256), 256)
            w_g = gate_tile[slot].reshape(2048, 256)
            w_u = up_tile[slot].reshape(2048, 256)
            w_d = down_tile[slot].reshape(256, 2048)
            gate = multiply(ffn_in[...], w_g)
            up = multiply(ffn_in[...], w_u)
            act_back = contract_cols(grad_ref[...], w_d)
            sigmoid = jax.nn.sigmoid(gate)
            silu = gate * sigmoid
            act_here = (silu * up).astype(BF)
            act[:, cols] = act_here
            down_acc[...] += multiply(act_here, w_d)
            g_back = (act_back * up * sigmoid * (1.0 + gate * (1.0 - sigmoid))).astype(BF)
            u_back = (act_back * silu).astype(BF)
            gate_back[:, cols] = g_back
            up_back[:, cols] = u_back
            ffn_acc[...] += contract_cols(g_back, w_g) + contract_cols(u_back, w_u)
            return 0

        lax.fori_loop(0, 4, step, 0)
        if e == 0:
            down_sum.multiply(0, 4)

    ffn_send[...] = ffn_acc[...].astype(BF)
    ffn_moves = [
        wire.send(YOFF[d], ffn_send.at[rows(me.at(YOFF[d]).y * SUB, SUB), :], ffn_recv.at[d - 1])
        for d in (1, 2, 3)
    ]
    down_sum.multiply(4, 8)
    down_send[...] = down_acc[...].astype(BF)
    down_moves = [
        wire.send(YOFF[d], down_send.at[rows(me.at(YOFF[d]).y * SUB, SUB), :], down_recv.at[d - 1])
        for d in (1, 2, 3)
    ]

    def down_block(k):
        e, dxl = XOFF[k][4], XOFF[k][2]
        return down_terms.at[e * 4 : e * 4 + 4, :, :, me.core, :, dxl * 1024 : dxl * 1024 + 1024]

    down_sum.add(0, 4)
    x_moves = [wire.send(XOFF[1], down_block(1), down_came.at[0])]
    down_sum.add(4, 8)
    x_moves += [wire.send(XOFF[k], down_block(k), down_came.at[k - 1]) for k in (2, 3)]
    near = [pltpu.make_async_copy(down_block(0), down_own, local_sem.at[0])]
    near[0].start()
    pl.semaphore_signal(ack, inc=1, device_id=me.at(SIBLING).device(), device_id_type=MESH)

    finish(ffn_moves)

    def summed(send, recv, h):
        cols = slice(h * 1024, h * 1024 + 1024)
        out = send[here, cols].astype(F32)
        for d in range(3):
            out = out + recv[d, :, cols].astype(F32)
        return out

    scale = scale_ref[...]
    inner = jnp.zeros((SUB, 1), F32)
    for h in range(2):
        back = summed(ffn_send, ffn_recv, h)
        weighed = back * resid_ref[:, half[h]]
        inner = inner + jnp.sum(weighed * gain_ref[:, half[h]], axis=1, keepdims=True)
        gain_part[:, half[h]] = jnp.sum(weighed * scale, axis=0, keepdims=True)
    pull = scale * scale * scale * inner / D
    for h in range(2):
        back = summed(ffn_send, ffn_recv, h)
        grad = grad_ref[here, h * 1024 : h * 1024 + 1024].astype(F32)
        total_back = grad + scale * gain_ref[:, half[h]] * back - resid_ref[:, half[h]] * pull
        resid_back[:, half[h]] = total_back
        mix_mine[:, half[h]] = total_back.astype(BF)
    mix_full[here, :] = mix_mine[...]
    mix_moves = [wire.send(off, mix_mine, mix_full.at[here, :]) for off in YOFF[1:]]

    pl.semaphore_wait(ack, 1)
    gate_sum.multiply(0, 8)
    finish(down_moves)
    for h in range(2):
        out_mine[:, half[h]] = (resid_ref[:, half[h]] + summed(down_send, down_recv, h)).astype(BF)
    gate_sum.add(0, 8)

    def gate_block(z):
        return gate_terms.at[:, :, z, me.core]

    z_moves = [
        wire.send(ZOFF[d], gate_block((me.z + d) % 4), gate_came.at[d - 1]) for d in (1, 2, 3)
    ]
    near.append(pltpu.make_async_copy(gate_block(me.z), gate_own, local_sem.at[1]))
    near[1].start()

    finish(mix_moves)
    back_cat[...] = multiply(mix_full[...], w_out_ref[...]).astype(BF)
    spot = rows(me.chunk * CHUNK, CHUNK)
    head_moves = [
        wire.send(XOFF[k], back_cat.at[:, k * 128 : k * 128 + 128], heads_back.at[spot, :])
        for k in (1, 2, 3)
    ]
    heads_back[spot, :] = back_cat[:, 0:128]
    finish(head_moves + x_moves + z_moves)
    for copy in near:
        copy.wait()
    down_sum.sent()
    gate_sum.sent()


def ffn(ffn_mine, grad_full, resid, scale_two, gain, w_out, w_gate, w_up, w_down, whole):
    vm = pl.BlockSpec(memory_space=pltpu.VMEM)
    hbm = pl.BlockSpec(memory_space=pl.ANY)
    return pl.pallas_call(
        ffn_body,
        name="ffn",
        out_shape=[
            SDS((SUB, D), BF),
            SDS((SUB, D), F32),
            SDS((1, D), F32),
            SDS((CHUNK, D), BF),
            SDS((ROWS, 128), BF),
            SDS((CHUNK, D), BF),
            SDS((CHUNK, D), BF),
            SDS((4, 2, 4, 16, 1024), BF),
            SDS((3, 4, 2, 4, 16, 1024), BF),
            SDS((8, 2, 16, 2048), BF),
            SDS((3, 8, 2, 16, 2048), BF),
        ],
        in_specs=[vm] * 6 + [hbm] * 4,
        out_specs=[vm] * 7 + [hbm] * 4,
        scratch_shapes=[
            pltpu.VMEM((SUB, D), BF),
            pltpu.VMEM((CHUNK, D), BF),
            pltpu.VMEM((CHUNK, D), BF),
            pltpu.VMEM((2, 2, 8, 128, 256), BF),
            pltpu.VMEM((2, 2, 8, 128, 256), BF),
            pltpu.VMEM((2, 2, 128, 2048), BF),
            pltpu.VMEM((CHUNK, D), F32),
            pltpu.VMEM((CHUNK, D), F32),
            pltpu.VMEM((CHUNK, D), BF),
            pltpu.VMEM((CHUNK, D), BF),
            pltpu.VMEM((3, SUB, D), BF),
            pltpu.VMEM((3, SUB, D), BF),
            pltpu.VMEM((SUB, D), BF),
            pltpu.VMEM((CHUNK, 512), BF),
            pltpu.VMEM((8, 2, 4, 2, 16, 2048), BF),
            pltpu.VMEM((8, 2, 4, 2, 16, 2048), BF),
            pltpu.VMEM((8, 2, 4, 16, 2048), BF),
            pltpu.SemaphoreType.DMA((24,)),
            pltpu.SemaphoreType.DMA((24,)),
            pltpu.SemaphoreType.DMA((2, 8)),
            pltpu.SemaphoreType.DMA((2, 8)),
            pltpu.SemaphoreType.DMA((2, 6)),
            pltpu.SemaphoreType.DMA((2,)),
            pltpu.SemaphoreType.REGULAR,
        ],
        compiler_params=pltpu.CompilerParams(
            collective_id=14, has_side_effects=True, vmem_limit_bytes=60 * 2**20
        ),
        cost_estimate=pl.CostEstimate(flops=26 * 10**9, bytes_accessed=40 * 2**20, transcendentals=0),
    )(
        ffn_mine,
        grad_full,
        resid,
        scale_two,
        gain,
        w_out,
        w_gate.reshape(8, 128, 1024),
        w_up.reshape(8, 128, 1024),
        w_down.reshape(8, 128, 1024),
        whole,
    )


def per_device(
    layer_input,
    doc_lengths,
    attn_gain,
    w_query,
    w_key,
    w_value,
    w_output,
    ffn_gain,
    w_gate,
    w_up,
    w_down,
    output_grad,
):
    me = whereami()
    cos_np, sin_np = rope_table()
    cos_all, sin_all = jnp.asarray(cos_np), jnp.asarray(sin_np)
    long_first = doc_lengths[0, 0] > SHORT
    table_start = jnp.where(long_first, SHORT, 0) + me.chunk * CHUNK
    cos_here = part(cos_all, table_start, CHUNK, 0)
    sin_here = part(sin_all, table_start, CHUNK, 0)
    cos_doc, sin_doc = cos_all[512:1536], sin_all[512:1536]

    w_kv = jnp.concatenate(
        [part(w_key, me.y * 64, 64, 1), part(w_value, me.y * 64, 64, 1)], axis=1
    )
    full_in, w_attn, gains = exchange(
        "enter",
        0,
        enter_plan,
        [layer_input, w_query, w_kv, jnp.broadcast_to(ffn_gain[None, :], (8, 128))],
        [SDS((CHUNK, D), BF), SDS((D, 768), BF), SDS((16, 8, 128), F32)],
    )
    ffn_gain_all = gains[:, 0, :].reshape(1, D)

    half_out = part(w_output, me.core * 1024, 1024, 0)
    pieces = jnp.stack([part(w, me.tok * 128, 128, 0) for w in (w_gate, w_up, w_down)])
    full_in, half_out, pieces = lax.optimization_barrier((full_in, half_out, pieces))
    whole = gather_weights(pieces)
    got_out = [x_permute(half_out, k) for k in (1, 2, 3)]

    in_f = full_in.astype(F32)
    scale_one = lax.rsqrt(jnp.mean(in_f * in_f, axis=1, keepdims=True) + EPS)
    normed = (in_f * scale_one * attn_gain[None, :]).astype(BF)
    lin = multiply(normed, w_attn)

    def turn(block):
        lane = lax.broadcasted_iota(jnp.int32, block.shape, 1)
        swapped = jnp.where(
            (lane % 64) < 32, -jnp.roll(block, -32, axis=1), jnp.roll(block, 32, axis=1)
        )
        return block * cos_here + swapped * sin_here

    turned = [turn(lin[:, k * 128 : k * 128 + 128]) for k in range(6)]
    for k in (4, 5):
        turned[k] = jnp.concatenate(
            [turned[k][:, :64], lin[:, k * 128 + 64 : k * 128 + 128]], axis=1
        )
    lin = jnp.concatenate(turned, axis=1).astype(BF)
    queries, kv = exchange(
        "to_heads", 1, to_heads_plan, [lin], [SDS((ROWS, 128), BF), SDS((ROWS, 128), BF)]
    )
    (heads_out,) = vmem_call(
        "attend", attend_body, [doc_lengths, queries, kv], [SDS((ROWS, 128), BF)], flops=2 * 10**9
    )
    heads_cat, w_out = exchange(
        "heads_out",
        2,
        heads_out_plan,
        [heads_out, w_output] + got_out,
        [SDS((CHUNK, 512), BF), SDS((D, 512), BF)],
    )
    attn_term = contract_cols(heads_cat, w_out).astype(BF)
    attn_terms, grad_full = exchange(
        "out_sum",
        3,
        out_sum_plan,
        [attn_term, output_grad],
        [SDS((4, SUB, D), BF), SDS((CHUNK, D), BF)],
    )
    in_mine = part(full_in, me.y * SUB, SUB, 0).astype(F32)
    resid = in_mine + jnp.sum(attn_terms.astype(F32), axis=0)
    scale_two = lax.rsqrt(jnp.mean(resid * resid, axis=1, keepdims=True) + EPS)
    ffn_mine = (resid * scale_two * ffn_gain_all).astype(BF)
    (
        out_mine,
        resid_back,
        ffn_gain_part,
        mix_full,
        heads_back,
        ffn_input,
        up_back,
        down_own,
        down_came,
        gate_own,
        gate_came,
    ) = ffn(
        ffn_mine, grad_full, resid, scale_two, ffn_gain_all, w_out, w_gate, w_up, w_down, whole
    )

    down_sum = (down_own.astype(F32) + total(list(down_came))).astype(BF).reshape(8, 4, 16, 1024)
    down_grad = reduce_z(me, jnp.moveaxis(down_sum, 1, 0))
    gate_sum = (gate_own.astype(F32) + total(list(gate_came))).astype(BF)
    gate_sum = gate_sum.reshape(2, 8, 16, 2, 1024)

    def gate_piece(k):
        return gate_sum[XOFF[k][2], :, :, XOFF[k][4], :]

    gate_grad = total([gate_piece(0)] + [x_permute(gate_piece(k), k) for k in (1, 2, 3)])
    up_partial = contract_rows(ffn_input, up_back).astype(BF)
    up_grad = reduce_ffn(me, up_partial)
    out_pair = reduce_core(me, contract_rows(mix_full, heads_cat).astype(BF))
    output_proj_grad = reduce_heads(me, out_pair)

    query_back, kv_back = vmem_call(
        "attend_back",
        attend_back_body,
        [doc_lengths, queries, kv, heads_back, cos_doc, sin_doc],
        [SDS((ROWS, 128), BF), SDS((ROWS, 128), BF)],
        scratch=[pltpu.VMEM((1024, 128), F32)],
        flops=5 * 10**9,
    )
    (cat_back,) = exchange(
        "grads_out", 9, grads_out_plan, [query_back, kv_back], [SDS((CHUNK, 1024), BF)]
    )
    normed_term = (
        contract_cols(cat_back[:, :768], w_attn) + contract_cols(cat_back[:, 768:], w_attn[:, 512:])
    ).astype(BF)
    (normed_terms,) = exchange(
        "normed_sum", 10, sum_plan, [normed_term], [SDS((4, SUB, D), BF)]
    )
    attn_partial = contract_rows(normed, cat_back)
    kv_partial = attn_partial[:, 512:768] + attn_partial[:, 768:]
    query_grad = reduce_heads(me, reduce_core(me, attn_partial[:, :512].astype(BF)))

    kv_pair = reduce_core(me, kv_partial.astype(BF))
    kv_pair = [a.reshape(4, 4, 2, 32, 256) for a in kv_pair]

    def kv_piece(k):
        return total([pick(a, me.at(XOFF[k]).xh, 2)[..., 128 * XOFF[k][2] : 128 * XOFF[k][2] + 128] for a in kv_pair])

    got = [x_permute(kv_piece(k).astype(BF), k) for k in (1, 2, 3)]
    kv_sum = reduce_z(me, total([kv_piece(0)] + got).astype(BF))
    kv_cols = jnp.stack(
        [pick(kv_sum, me.y, 0)] + [y_permute(pick(kv_sum, (me.y + d) % 4, 0), d) for d in (1, 2, 3)]
    )
    kv_cols = jnp.concatenate([pick(kv_cols, (me.y - h) % 4, 0) for h in range(4)], axis=1)
    kv_cols = kv_cols.reshape(32, 4, 2, 64)
    key_grad = kv_cols[:, :, 0, :].reshape(32, 256)
    value_grad = kv_cols[:, :, 1, :].reshape(32, 256)

    normed_back = jnp.sum(normed_terms.astype(F32), axis=0)
    scale_mine = part(scale_one, me.y * SUB, SUB, 0)
    scaled_back = normed_back * attn_gain[None, :]
    inner_one = jnp.sum(scaled_back * in_mine, axis=1, keepdims=True)
    in_grad_mine = (
        resid_back + scale_mine * scaled_back - in_mine * scale_mine**3 * inner_one / D
    ).astype(BF)
    attn_gain_part = jnp.sum(normed_back * in_mine * scale_mine, axis=0, keepdims=True)
    gain_parts = jnp.concatenate([attn_gain_part, ffn_gain_part, jnp.zeros((6, D), F32)], axis=0)
    layer_output, input_grad, gain_terms = exchange(
        "leave",
        11,
        leave_plan,
        [out_mine, in_grad_mine, gain_parts],
        [SDS((ROWS, 128), BF), SDS((ROWS, 128), BF), SDS((16, 8, 128), F32)],
    )
    (gain_toks,) = exchange(
        "gains", 12, gains_plan, [jnp.sum(gain_terms, axis=0)], [SDS((8, 8, 128), F32)]
    )
    gain_grads = part(jnp.sum(gain_toks, axis=0), me.tok * 16, 16, 1)
    return (
        layer_output,
        input_grad,
        gain_grads[0:1],
        query_grad,
        key_grad,
        value_grad,
        output_proj_grad,
        gain_grads[1:2],
        gate_grad,
        up_grad,
        down_grad,
    )


def solution(mesh):
    in_specs = (
        P("tok", ("narrow", "wide")),
        P("tok", None),
        P(),
        P(None, ("narrow", "wide")),
        P(None, "narrow"),
        P(None, "narrow"),
        P(None, ("narrow", "wide")),
        P(("narrow", "wide")),
        P("narrow", "wide"),
        P("narrow", "wide"),
        P("wide", "narrow"),
        P("tok", ("narrow", "wide")),
    )
    out_specs = (
        P("tok", ("narrow", "wide")),
        P("tok", ("narrow", "wide")),
        P(("narrow", "wide"), "tok"),
        P("tok", ("narrow", "wide")),
        P(("tok", "wide"), "narrow"),
        P(("tok", "wide"), "narrow"),
        P("tok", ("narrow", "wide")),
        P(("narrow", "wide"), "tok"),
        P("narrow", "tok", "wide"),
        P("narrow", "tok", "wide"),
        P("wide", "tok", "narrow"),
    )
    return jax.shard_map(
        per_device, mesh=mesh, in_specs=in_specs, out_specs=out_specs, check_vma=False
    )
```

```python
import functools
import math

import jax
import jax.numpy as jnp
import numpy as np
from jax import lax
from jax.experimental import pallas as pl
from jax.experimental.pallas import tpu as pltpu
from jax.sharding import PartitionSpec as P

HEADS = 32
KV_HEADS = 8
HEAD_DIM = 64
GROUP = 128
EPS = 1e-05
THETA = 500000.0
FACTOR = 32.0
LOW_FACTOR = 1.0
HIGH_FACTOR = 4.0
INITIAL = 8192.0
NEG = -1e30

D = 2048
ROWS = 1536
CHUNK = 384
SUB = 96
SHORT = 512
BF = jnp.bfloat16
F32 = jnp.float32
MESH = pl.DeviceIdType.MESH
SDS = jax.ShapeDtypeStruct

HERE = (0, 0, 0, 0, 0)
XOFF = [(0, 0, 0, 0, 0), (0, 0, 1, 0, 0), (0, 0, 0, 0, 1), (0, 0, 1, 0, 1)]
YOFF = [(0, 0, 0, d, 0) for d in range(4)]
PLANE = [(0, 0, a, b, e) for b in range(4) for a in range(2) for e in range(2)]
SIBLING = (1, 0, 0, 0, 0)
TOKS = [(a, b, 0, 0, 0) for b in range(4) for a in range(2)]


class Place:
    def __init__(self, core, z, xl, y, xh):
        self.core, self.z, self.xl, self.y, self.xh = core, z, xl, y, xh
        self.tok = z * 2 + core
        self.wide = y * 2 + xh
        self.block = xl * 8 + self.wide
        self.chunk = xl * 2 + xh

    def at(self, off):
        return Place(
            (self.core + off[0]) % 2,
            (self.z + off[1]) % 4,
            (self.xl + off[2]) % 2,
            (self.y + off[3]) % 4,
            (self.xh + off[4]) % 2,
        )

    def device(self):
        return (self.tok, self.xl, self.wide)


def whereami():
    tok = lax.axis_index("tok")
    wide = lax.axis_index("wide")
    return Place(tok % 2, tok // 2, lax.axis_index("narrow"), wide // 2, wide % 2)


def rows(start, size):
    return pl.ds(pl.multiple_of(start, size), size)


def exchange(name, number, plan, ins, outs):
    n_in, n_out = len(ins), len(outs)

    def count():
        fake = Place(0, 0, 0, 0, 0)
        probe = [_Any() for _ in range(n_in)], [_Any() for _ in range(n_out)]
        local, sends = plan(fake, *probe)
        return len(local), sum(1 + len(s[3]) for s in sends)

    n_local, n_send = count()

    def body(*refs):
        sources, targets = refs[:n_in], refs[n_in : n_in + n_out]
        send_sem, recv_sem, local_sem = refs[n_in + n_out :]
        me = whereami()
        local, sends = plan(me, sources, targets)
        offsets = []
        for off, _, _, forwards in sends:
            for o in [off] + [f[0] for f in forwards]:
                if o not in offsets:
                    offsets.append(o)
        barrier = pltpu.get_barrier_semaphore()
        for off in offsets:
            back = tuple(-v for v in off)
            pl.semaphore_signal(
                barrier, inc=1, device_id=me.at(back).device(), device_id_type=MESH
            )
        near = []
        for i, (src, dst) in enumerate(local):
            near.append(pltpu.make_async_copy(src, dst, local_sem.at[i]))
            near[-1].start()
        pl.semaphore_wait(barrier, len(offsets))
        slot = 0

        def launch(off, src, dst):
            nonlocal slot
            copy = pltpu.make_async_remote_copy(
                src_ref=src,
                dst_ref=dst,
                send_sem=send_sem.at[slot],
                recv_sem=recv_sem.at[slot],
                device_id=me.at(off).device(),
                device_id_type=MESH,
            )
            copy.start()
            slot += 1
            return copy

        first = [(launch(off, src, dst), forwards) for off, src, dst, forwards in sends]
        second = []
        for copy, forwards in first:
            if forwards:
                copy.wait_recv()
                second += [launch(*f) for f in forwards]
        for copy, forwards in first:
            copy.wait_send()
            if not forwards:
                copy.wait_recv()
        for copy in second:
            copy.wait()
        for copy in near:
            copy.wait()

    return pl.pallas_call(
        body,
        name=name,
        out_shape=outs,
        in_specs=[pl.BlockSpec(memory_space=pl.ANY)] * n_in,
        out_specs=[pl.BlockSpec(memory_space=pltpu.VMEM)] * n_out,
        scratch_shapes=[
            pltpu.SemaphoreType.DMA((n_send,)),
            pltpu.SemaphoreType.DMA((n_send,)),
            pltpu.SemaphoreType.DMA((max(n_local, 1),)),
        ],
        compiler_params=pltpu.CompilerParams(
            collective_id=number, has_side_effects=True, vmem_limit_bytes=40 * 2**20
        ),
    )(*ins)


class _Any:
    @property
    def at(self):
        return self

    def __getitem__(self, key):
        return self


def lanes(index, size=128):
    return pl.ds(pl.multiple_of(index * size, size), size)


def spread_plan(me, src, dst, own_first=False):
    def block(off):
        return lanes(off[2] * 8 + me.wide if own_first else me.block)

    local = [(src.at[rows(me.chunk * CHUNK, CHUNK), :], dst.at[:, block(HERE)])]
    sends = [
        (off, src.at[rows(me.at(off).chunk * CHUNK, CHUNK), :], dst.at[:, block(off)], [])
        for off in PLANE[1:]
    ]
    return local, sends


def enter_plan(me, ins, outs):
    hidden, w_q, w_kv, gain = ins
    full, w_attn, gains = outs
    half = rows(me.core * 1024, 1024)
    local, sends = spread_plan(me, hidden, full)
    local += [
        (w_q, w_attn.at[:, 0:128]),
        (w_kv, w_attn.at[:, 512:640]),
        (gain, gains.at[me.block]),
    ]
    head = []
    for k in (1, 2, 3):
        cols = slice(k * 128, k * 128 + 128)
        block = w_attn.at[half, cols]
        head.append((XOFF[k], w_q.at[half, :], block, [(SIBLING, block, block)]))
    block = w_attn.at[half, 640:768]
    head.append((XOFF[1], w_kv.at[half, :], block, [(SIBLING, block, block)]))
    sends = head + sends
    sends += [(off, gain, gains.at[me.block], []) for off in PLANE[1:]]
    return local, sends


def to_heads_plan(me, ins, outs):
    (lin,) = ins
    q, kv = outs
    mine = rows(me.chunk * CHUNK, CHUNK)
    local, sends = [], []
    for k, off in enumerate(XOFF):
        kv_col = 512 + 128 * off[2]
        pairs = [
            (lin.at[:, k * 128 : k * 128 + 128], q.at[mine, :]),
            (lin.at[:, kv_col : kv_col + 128], kv.at[mine, :]),
        ]
        if k == 0:
            local += pairs
        else:
            sends += [(off, s, d, []) for s, d in pairs]
    return local, sends


def from_heads_moves(me, src, dst, first_col=0):
    local, sends = [], []
    for k, off in enumerate(XOFF):
        col = first_col + k * 128
        pair = (src.at[rows(me.at(off).chunk * CHUNK, CHUNK), :], dst.at[:, col : col + 128])
        if k == 0:
            local.append(pair)
        else:
            sends.append((off, *pair, []))
    return local, sends


def heads_out_plan(me, ins, outs):
    heads, w_out, half1, half2, half3 = ins
    cat, w_cat = outs
    local, sends = from_heads_moves(me, heads, cat)
    half = rows(me.core * 1024, 1024)
    local.append((w_out, w_cat.at[:, 0:128]))
    for k, part in ((1, half1), (2, half2), (3, half3)):
        block = w_cat.at[half, k * 128 : k * 128 + 128]
        local.append((part, block))
        sends.append((SIBLING, part, block, []))
    return local, sends


def heads_back_plan(me, ins, outs):
    (cat,) = ins
    (heads,) = outs
    mine = rows(me.chunk * CHUNK, CHUNK)
    local, sends = [], []
    for k, off in enumerate(XOFF):
        pair = (cat.at[:, k * 128 : k * 128 + 128], heads.at[mine, :])
        if k == 0:
            local.append(pair)
        else:
            sends.append((off, *pair, []))
    return local, sends


def grads_out_plan(me, ins, outs):
    q, kv = ins
    (cat,) = outs
    local, sends = from_heads_moves(me, q, cat)
    local2, sends2 = from_heads_moves(me, kv, cat, 512)
    return local + local2, sends + sends2


def scatter_moves(me, src, dst):
    local = [(src.at[rows(me.y * SUB, SUB), :], dst.at[me.y])]
    sends = [(off, src.at[rows(me.at(off).y * SUB, SUB), :], dst.at[me.y], []) for off in YOFF[1:]]
    return local, sends


def out_sum_plan(me, ins, outs):
    local, sends = scatter_moves(me, ins[0], outs[0])
    local2, sends2 = spread_plan(me, ins[1], outs[1], True)
    return local + local2, sends + sends2


def sum_plan(me, ins, outs):
    local, sends = [], []
    for src, dst in zip(ins, outs):
        a, b = scatter_moves(me, src, dst)
        local, sends = local + a, sends + b
    return local, sends


def gather_moves(me, src, dst):
    block = dst.at[rows(me.y * SUB, SUB), :]
    return [(src, block)], [(off, src, block, []) for off in YOFF[1:]]


def gather_plan(me, ins, outs):
    return gather_moves(me, ins[0], outs[0])


def weight_moves(me, own, parts, dst):
    local = [(own, dst.at[rows(me.xl * 1024, 1024), lanes(me.xh, 1024)])]
    sends = []
    for off, part in zip(XOFF[1:], parts):
        there = me.at(off)
        block = dst.at[rows(there.xl * 1024 + me.core * 512, 512), lanes(there.xh, 1024)]
        local.append((part, block))
        sends.append((SIBLING, part, block, []))
    return local, sends


def weight_moves_t(me, own, parts, dst):
    local = [(own, dst.at[rows(me.xh * 1024, 1024), lanes(me.xl, 1024)])]
    sends = []
    for off, part in zip(XOFF[1:], parts):
        there = me.at(off)
        block = dst.at[rows(there.xh * 1024 + me.core * 512, 512), lanes(there.xl, 1024)]
        local.append((part, block))
        sends.append((SIBLING, part, block, []))
    return local, sends


def ffn_enter_plan(me, ins, outs):
    hidden, gate, up, p1, p2, p3 = ins
    full, w_gate, w_up = outs
    local, sends = gather_moves(me, hidden, full)
    for j, (own, dst) in enumerate(((gate, w_gate), (up, w_up))):
        a, b = weight_moves(me, own, [p.at[j] for p in (p1, p2, p3)], dst)
        local, sends = local + a, sends + b
    return local, sends


def down_plan(me, ins, outs):
    return weight_moves_t(me, ins[0], ins[1:], outs[0])


def leave_plan(me, ins, outs):
    local, sends = [], []
    mine = rows(me.chunk * CHUNK + me.y * SUB, SUB)
    for k, off in enumerate(PLANE):
        there = me.at(off)
        pairs = [(src.at[:, lanes(there.block)], dst.at[mine, :]) for src, dst in zip(ins[:2], outs[:2])]
        pairs.append((ins[2].at[:, lanes(there.block)], outs[2].at[me.block]))
        if k == 0:
            local += pairs
        else:
            sends += [(off, s, d, []) for s, d in pairs]
    return local, sends


def gains_plan(me, ins, outs):
    local = [(ins[0], outs[0].at[me.tok])]
    sends = [(off, ins[0], outs[0].at[me.tok], []) for off in TOKS[1:]]
    return local, sends


def block_probs(q_ref, kv_ref, start, i, stack):
    n = 256 * (i + 1)
    keys = kv_ref[rows_256(start, n), 0:64]
    scores = lax.dot_general(
        keys, stack, (((1,), (1,)), ((), ())), preferred_element_type=F32
    ) * (HEAD_DIM**-0.5)
    last = scores[n - 256 :, :]
    key_id = lax.broadcasted_iota(jnp.int32, (256, 512), 0)
    query_id = lax.broadcasted_iota(jnp.int32, (256, 512), 1) % 256
    last = jnp.where(key_id <= query_id, last, NEG)
    if n > 256:
        scores = jnp.concatenate([scores[: n - 256, :], last], axis=0)
    else:
        scores = last
    raised = jnp.exp(scores - jnp.max(scores, axis=0, keepdims=True))
    return keys, raised, jnp.sum(raised, axis=0, keepdims=True)


def rows_256(start, size):
    return pl.ds(pl.multiple_of(start, 256), size)


def starts_of(len_ref):
    long_first = len_ref[0, 0] > SHORT
    long_start = jnp.where(long_first, 0, SHORT)
    short_start = jnp.where(long_first, 2 * SHORT, 0)
    return ((long_start, 4), (short_start, 2))


def both(block):
    return jnp.concatenate([block[:, 0:64], block[:, 64:128]], axis=0)


def attend_body(len_ref, q_ref, kv_ref, out_ref):
    for start, blocks in starts_of(len_ref):
        for i in range(blocks):
            mine = rows_256(start + 256 * i, 256)
            stack = both(q_ref[mine, :])
            keys, raised, mass = block_probs(q_ref, kv_ref, start, i, stack)
            soft = (raised * (1.0 / mass)).astype(BF)
            values = kv_ref[rows_256(start, 256 * (i + 1)), 64:128]
            mixed = lax.dot_general(
                soft, values, (((0,), (0,)), ((), ())), preferred_element_type=F32
            )
            out_ref[mine, :] = jnp.concatenate([mixed[:256], mixed[256:]], axis=1).astype(BF)


def unrope(tensor, cosine, sine):
    lane = lax.broadcasted_iota(jnp.int32, tensor.shape, 1)
    first = (lane % 64) < 32
    swapped = jnp.where(first, pltpu.roll(tensor, 96, 1), -pltpu.roll(tensor, 32, 1))
    return tensor * cosine + swapped * sine


def attend_back_body(len_ref, q_ref, kv_ref, back_ref, cos_ref, sin_ref, dq_ref, dkv_ref, acc_ref):
    for start, blocks in starts_of(len_ref):
        acc_ref[...] = jnp.zeros(acc_ref.shape, F32)
        for i in range(blocks):
            n = 256 * (i + 1)
            mine = rows_256(start + 256 * i, 256)
            stack = both(q_ref[mine, :])
            keys, raised, mass = block_probs(q_ref, kv_ref, start, i, stack)
            soft = raised * (1.0 / mass)
            values = kv_ref[rows_256(start, n), 64:128]
            backs = both(back_ref[mine, :])
            prob_back = lax.dot_general(
                values, backs, (((1,), (1,)), ((), ())), preferred_element_type=F32
            )
            inner = jnp.sum(soft * prob_back, axis=0, keepdims=True)
            score_back = (soft * (prob_back - inner)).astype(BF)
            dq = lax.dot_general(
                score_back, keys, (((0,), (0,)), ((), ())), preferred_element_type=F32
            ) * (HEAD_DIM**-0.5)
            dq = jnp.concatenate([dq[:256], dq[256:]], axis=1)
            pos = slice(256 * i, 256 * i + 256)
            dq_ref[mine, :] = unrope(dq, cos_ref[pos, :], sin_ref[pos, :]).astype(BF)
            dk = jnp.dot(score_back, stack, preferred_element_type=F32) * (HEAD_DIM**-0.5)
            dv = jnp.dot(soft.astype(BF), backs, preferred_element_type=F32)
            acc_ref[0:n, :] += jnp.concatenate([dk, dv], axis=1)
        m = 256 * blocks
        acc = acc_ref[0:m, :]
        lane = lax.broadcasted_iota(jnp.int32, acc.shape, 1)
        turned = unrope(acc, cos_ref[0:m, :], sin_ref[0:m, :])
        dkv_ref[rows_256(start, m), :] = jnp.where(lane < 64, turned, acc).astype(BF)


def vmem_call(name, body, ins, outs, scratch=(), flops=0):
    return pl.pallas_call(
        body,
        name=name,
        out_shape=outs,
        in_specs=[pl.BlockSpec(memory_space=pltpu.SMEM)]
        + [pl.BlockSpec(memory_space=pltpu.VMEM)] * (len(ins) - 1),
        out_specs=[pl.BlockSpec(memory_space=pltpu.VMEM)] * len(outs),
        scratch_shapes=list(scratch),
        compiler_params=pltpu.CompilerParams(vmem_limit_bytes=48 * 2**20),
        cost_estimate=pl.CostEstimate(flops=flops, bytes_accessed=2**20, transcendentals=0),
    )(*ins)


def back_body(
    dq_ref,
    dkv_ref,
    w_attn,
    heads_cat,
    out_mine,
    in_mine,
    resid_back,
    scale_ref,
    gain_ref,
    ffn_gain_part,
    normed_in,
    mix_in,
    ffn_in,
    up_in,
    down_own,
    down_came,
    gate_own,
    gate_came,
    layer_output,
    input_grad,
    query_grad,
    kv_grad,
    out_grad,
    gate_grad,
    up_grad,
    down_grad,
    gain_grad,
    left_buf,
    right_buf,
    down_in,
    gate_in,
    down_sum,
    gate_sum,
    down_z,
    gate_x,
    up_terms,
    up_core,
    up_z,
    up_sum,
    up_x,
    cat_back,
    norm_send,
    norm_recv,
    in_grad,
    gain_parts,
    gain_plane,
    gain_mine,
    gain_toks,
    o_terms,
    o_core,
    o_x,
    o_sum,
    o_z,
    q_terms,
    q_core,
    q_x,
    q_sum,
    q_z,
    k_terms,
    k_core,
    k_x,
    k_sum,
    k_z,
    k_last,
    send_sem,
    recv_sem,
    core_send,
    core_recv,
    local_sem,
):
    me = whereami()
    wire = Wire(me, send_sem, recv_sem)
    load_left = pltpu.make_async_copy(ffn_in, left_buf, local_sem.at[0])
    load_right = pltpu.make_async_copy(up_in, right_buf, local_sem.at[1])
    load_left.start()
    load_right.start()

    def halves(own, came, buf, h, sem):
        part_of = pl.ds(h * (own.shape[0] // 2), own.shape[0] // 2)
        return [
            pltpu.make_async_copy(own.at[part_of], buf.at[0], local_sem.at[sem]),
            pltpu.make_async_copy(came.at[:, part_of], buf.at[1:4], local_sem.at[sem + 1]),
        ]

    def start(copies):
        for copy in copies:
            copy.start()

    start(halves(gate_own, gate_came, gate_in, 0, 2))
    start(halves(down_own, down_came, down_in, 0, 4))
    meet(me, PLANE[1:] + TOKS[1:])
    sent = []

    spot = rows(me.chunk * CHUNK, CHUNK)
    moves = []
    for k in (1, 2, 3):
        there = rows(me.at(XOFF[k]).chunk * CHUNK, CHUNK)
        for ref, col in ((dq_ref, 0), (dkv_ref, 512)):
            moves.append(
                wire.send(
                    XOFF[k], ref.at[there, :], cat_back.at[:, col + k * 128 : col + k * 128 + 128]
                )
            )
    cat_back[:, 0:128] = dq_ref[spot, :]
    cat_back[:, 512:640] = dkv_ref[spot, :]

    mine = rows(me.chunk * CHUNK + me.y * SUB, SUB)
    leaving = [
        wire.send(off, out_mine.at[:, lanes(me.at(off).block)], layer_output.at[mine, :])
        for off in PLANE[1:]
    ]
    layer_output[mine, :] = out_mine[:, lanes(me.block)]

    load_left.wait()
    load_right.wait()
    up_pair = PairSum(me, left_buf, right_buf, up_terms, up_core, core_send, core_recv)
    up_pair.multiply(0, 8)
    load_left = pltpu.make_async_copy(normed_in, left_buf, local_sem.at[0])
    load_right = pltpu.make_async_copy(mix_in, right_buf, local_sem.at[1])
    load_left.start()
    load_right.start()
    up_pair.add(0, 8)
    up_moves = [
        wire.send(ZOFF[d], up_terms.at[:, :, (me.z + d) % 4, me.core], up_z.at[d - 1])
        for d in (1, 2, 3)
    ]

    finish(moves)
    for h in range(4):
        cols = slice(h * 512, h * 512 + 512)
        term = contract_cols(cat_back[:, 0:768], w_attn[cols, :]) + contract_cols(
            cat_back[:, 768:1024], w_attn[cols, 512:768]
        )
        norm_send[:, cols] = term.astype(BF)
    norm_moves = [
        wire.send(YOFF[d], norm_send.at[rows(me.at(YOFF[d]).y * SUB, SUB), :], norm_recv.at[d - 1])
        for d in (1, 2, 3)
    ]

    load_left.wait()
    load_right.wait()
    for z in range(4):
        block = contract_rows(left_buf[:, z * 512 : z * 512 + 512], cat_back[:, 0:512])
        q_terms[z] = block.astype(BF).reshape(2, 256, 512)
    q_pair = wire.send(SIBLING, q_terms.at[:, 1 - me.core], q_core)
    for z in range(4):
        left = left_buf[:, z * 512 : z * 512 + 512]
        block = contract_rows(left, cat_back[:, 512:768]) + contract_rows(
            left, cat_back[:, 768:1024]
        )
        k_terms[z] = block.astype(BF).reshape(2, 4, 2, 32, 256)
    k_pair = wire.send(SIBLING, k_terms.at[:, 1 - me.core], k_core)
    for z in range(4):
        block = contract_rows(right_buf[:, z * 512 : z * 512 + 512], heads_cat[...])
        o_terms[z] = block.astype(BF).reshape(2, 256, 512)
    o_pair = wire.send(SIBLING, o_terms.at[:, 1 - me.core], o_core)

    def fold(own, came, buf, out, sem):
        size = buf.shape[1]
        for h in range(2):
            copies = halves(own, came, buf, h, sem)
            for copy in copies:
                copy.wait()

            def step(i, _, h=h):
                value = buf[0, i].astype(F32)
                for k in (1, 2, 3):
                    value = value + buf[k, i].astype(F32)
                out[h * size + i] = value.astype(BF)
                return 0

            lax.fori_loop(0, size, step, 0)
            if h == 0:
                start(halves(own, came, buf, 1, sem))

    def gate_block(k):
        e, dxl = XOFF[k][4], XOFF[k][2]
        return gate_sum.at[dxl * 4 : dxl * 4 + 4, :, :, e * 1024 : e * 1024 + 1024]

    fold(gate_own, gate_came, gate_in, gate_sum, 2)
    gate_moves = [wire.send(XOFF[k], gate_block(k), gate_x.at[k - 1]) for k in (1, 2, 3)]
    fold(down_own, down_came, down_in, down_sum, 4)
    down_moves = [
        wire.send(ZOFF[d], down_sum.at[:, :, (me.z + d) % 4], down_z.at[d - 1]) for d in (1, 2, 3)
    ]

    def add_core(copy, terms, came):
        copy.wait_recv()
        terms[:, me.core] = (terms[:, me.core].astype(F32) + came[...].astype(F32)).astype(BF)

    def kv_block(k):
        e, dxl = XOFF[k][4], XOFF[k][2]
        return k_terms.at[:, me.core, :, (me.xh + e) % 2, :, dxl * 128 : dxl * 128 + 128]

    add_core(k_pair, k_terms, k_core)
    k_moves = [wire.send(XOFF[k], kv_block(k), k_x.at[k - 1]) for k in (1, 2, 3)]
    add_core(q_pair, q_terms, q_core)
    q_moves = [
        wire.send(XOFF[k], q_terms.at[:, me.core, :, k * 128 : k * 128 + 128], q_x.at[k - 1])
        for k in (1, 2, 3)
    ]
    add_core(o_pair, o_terms, o_core)
    o_moves = [
        wire.send(XOFF[k], o_terms.at[:, me.core, :, k * 128 : k * 128 + 128], o_x.at[k - 1])
        for k in (1, 2, 3)
    ]

    finish(norm_moves)
    here = rows(me.y * SUB, SUB)
    back = norm_send[here, :].astype(F32)
    for d in range(3):
        back = back + norm_recv[d].astype(F32)
    scale = scale_ref[...]
    enter = in_mine[...].astype(F32)
    weighed = back * enter
    inner = jnp.sum(weighed * gain_ref[...], axis=1, keepdims=True)
    gain_parts[0:1, :] = jnp.sum(weighed * scale, axis=0, keepdims=True)
    gain_parts[1:2, :] = ffn_gain_part[...]
    gain_parts[2:8, :] = jnp.zeros((6, D), F32)
    pull = scale * scale * scale * inner / D
    in_grad[...] = (resid_back[...] + scale * gain_ref[...] * back - enter * pull).astype(BF)
    for off in PLANE[1:]:
        there = lanes(me.at(off).block)
        leaving.append(wire.send(off, in_grad.at[:, there], input_grad.at[mine, :]))
        leaving.append(wire.send(off, gain_parts.at[:, there], gain_plane.at[me.block]))
    input_grad[mine, :] = in_grad[:, lanes(me.block)]
    gain_plane[me.block] = gain_parts[:, lanes(me.block)]

    def over_x(moves, own, came, out):
        for copy in moves:
            copy.wait_recv()
        value = own.astype(F32)
        for k in range(3):
            value = value + came[k].astype(F32)
        out[...] = value.astype(BF)
        sent.extend(moves)

    over_x(o_moves, o_terms[:, me.core, :, 0:128], o_x, o_sum)
    over_x(q_moves, q_terms[:, me.core, :, 0:128], q_x, q_sum)
    over_x(k_moves, k_terms[:, me.core, :, me.xh, :, 0:128], k_x, k_sum)
    late = []
    for summed, came in ((o_sum, o_z), (q_sum, q_z), (k_sum, k_z)):
        late.append(
            [wire.send(ZOFF[d], summed.at[(me.z + d) % 4], came.at[d - 1]) for d in (1, 2, 3)]
        )

    def over_z(moves, own, came):
        for copy in moves:
            copy.wait_recv()
        sent.extend(moves)
        value = own.astype(F32)
        for d in range(3):
            value = value + came[d].astype(F32)
        return value

    down_grad[...] = over_z(down_moves, down_sum[:, :, me.z].reshape(8, 16, 1024), down_z.reshape(3, 8, 16, 1024))
    gate_grad[...] = over_z(gate_moves, gate_sum[0:4, :, :, 0:1024].reshape(8, 16, 1024), gate_x.reshape(3, 8, 16, 1024))
    for copy in up_moves:
        copy.wait_recv()
    sent.extend(up_moves)

    def up_step(i, _):
        value = up_terms[i, :, me.z, me.core].astype(F32)
        for d in range(3):
            value = value + up_z[d, i].astype(F32)
        up_sum[i] = value.astype(BF)
        return 0

    lax.fori_loop(0, 8, up_step, 0)

    def up_block(k):
        e, dxl = XOFF[k][4], XOFF[k][2]
        return up_sum.at[dxl * 4 : dxl * 4 + 4, :, :, e * 1024 : e * 1024 + 1024]

    up_moves = [wire.send(XOFF[k], up_block(k), up_x.at[k - 1]) for k in (1, 2, 3)]

    out_grad[...] = over_z(late[0], o_sum[me.z], o_z)
    query_grad[...] = over_z(late[1], q_sum[me.z], q_z)
    k_last[...] = over_z(late[2], k_sum[me.z], k_z)
    y_moves = [wire.send(YOFF[d], k_last.at[me.at(YOFF[d]).y], kv_grad.at[me.y]) for d in (1, 2, 3)]
    kv_grad[me.y] = k_last[me.y]
    for copy in leaving:
        copy.wait_recv()
    sent.extend(leaving)
    gain_mine[...] = jnp.sum(gain_plane[...], axis=0)
    tok_moves = [wire.send(off, gain_mine, gain_toks.at[me.tok]) for off in TOKS[1:]]
    gain_toks[me.tok] = gain_mine[...]
    up_grad[...] = over_z(up_moves, up_sum[0:4, :, :, 0:1024].reshape(8, 16, 1024), up_x.reshape(3, 8, 16, 1024))
    finish(y_moves + tok_moves)
    gain_grad[...] = jnp.sum(gain_toks[...], axis=0)
    for copy in sent:
        copy.wait_send()
    up_pair.sent()
    o_pair.wait_send()
    q_pair.wait_send()
    k_pair.wait_send()


def back(vmem_ins, hbm_ins):
    vm = pl.BlockSpec(memory_space=pltpu.VMEM)
    hbm = pl.BlockSpec(memory_space=pl.ANY)
    outs = [
        SDS((ROWS, 128), BF),
        SDS((ROWS, 128), BF),
        SDS((256, 128), F32),
        SDS((4, 32, 128), F32),
        SDS((256, 128), F32),
        SDS((8, 16, 1024), F32),
        SDS((8, 16, 1024), F32),
        SDS((8, 16, 1024), F32),
        SDS((8, 128), F32),
    ]
    v = pltpu.VMEM
    heads_sum = [
        v((4, 2, 256, 512), BF),
        v((4, 256, 512), BF),
        v((3, 4, 256, 128), BF),
        v((4, 256, 128), BF),
        v((3, 256, 128), BF),
    ]
    return pl.pallas_call(
        back_body,
        name="back",
        out_shape=outs,
        in_specs=[vm] * len(vmem_ins) + [hbm] * len(hbm_ins),
        out_specs=[vm] * len(outs),
        scratch_shapes=[
            v((CHUNK, D), BF),
            v((CHUNK, D), BF),
            v((4, 2, 2, 4, 16, 1024), BF),
            v((4, 4, 2, 16, 2048), BF),
            v((4, 2, 4, 16, 1024), BF),
            v((8, 2, 16, 2048), BF),
            v((3, 4, 2, 16, 1024), BF),
            v((3, 4, 2, 16, 1024), BF),
            v((8, 2, 4, 2, 16, 2048), BF),
            v((8, 2, 4, 16, 2048), BF),
            v((3, 8, 2, 16, 2048), BF),
            v((8, 2, 16, 2048), BF),
            v((3, 4, 2, 16, 1024), BF),
            v((CHUNK, 1024), BF),
            v((CHUNK, D), BF),
            v((3, SUB, D), BF),
            v((SUB, D), BF),
            v((8, D), F32),
            v((16, 8, 128), F32),
            v((8, 128), F32),
            v((8, 8, 128), F32),
        ]
        + heads_sum
        + heads_sum
        + [
            v((4, 2, 4, 2, 32, 256), BF),
            v((4, 4, 2, 32, 256), BF),
            v((3, 4, 4, 32, 128), BF),
            v((4, 4, 32, 128), BF),
            v((3, 4, 32, 128), BF),
            v((4, 32, 128), F32),
            pltpu.SemaphoreType.DMA((104,)),
            pltpu.SemaphoreType.DMA((104,)),
            pltpu.SemaphoreType.DMA((8,)),
            pltpu.SemaphoreType.DMA((8,)),
            pltpu.SemaphoreType.DMA((6,)),
        ],
        compiler_params=pltpu.CompilerParams(
            collective_id=15, has_side_effects=True, vmem_limit_bytes=56 * 2**20
        ),
        cost_estimate=pl.CostEstimate(flops=10**10, bytes_accessed=30 * 2**20, transcendentals=0),
    )(*vmem_ins, *hbm_ins)


def rope_table():
    halfway = HEAD_DIM // 2
    k = np.arange(halfway, dtype=np.float32)
    inverse = np.exp(-2.0 * k / HEAD_DIM * math.log(THETA)).astype(np.float32)
    wavelen = (2.0 * math.pi / inverse).astype(np.float32)
    scaled = inverse / np.float32(FACTOR)
    smooth = (INITIAL / wavelen - LOW_FACTOR) / (HIGH_FACTOR - LOW_FACTOR)
    middle = (1.0 - smooth) * scaled + smooth * inverse
    frequency = np.where(
        wavelen < INITIAL / HIGH_FACTOR,
        inverse,
        np.where(wavelen > INITIAL / LOW_FACTOR, scaled, middle),
    ).astype(np.float32)
    positions = np.concatenate([np.arange(512), np.arange(1024), np.arange(512)]).astype(np.float32)
    angles = (positions[:, None] * frequency[None, :]).astype(np.float32).astype(np.float64)
    return (
        np.tile(np.cos(angles).astype(np.float32), (1, 4)),
        np.tile(np.sin(angles).astype(np.float32), (1, 4)),
    )


def x_permute(value, k):
    if k == 1:
        return lax.ppermute(value, "narrow", [(0, 1), (1, 0)])
    if k == 2:
        return lax.ppermute(value, "wide", [(i, i ^ 1) for i in range(8)])
    return lax.ppermute(value, ("narrow", "wide"), [(i, i ^ 9) for i in range(16)])


def z_permute(value, d):
    return lax.ppermute(value, "tok", [(i, (i + 2 * d) % 8) for i in range(8)])


def y_permute(value, d):
    return lax.ppermute(value, "wide", [(i, (i + 2 * d) % 8) for i in range(8)])


def core_permute(value):
    return lax.ppermute(value, "tok", [(i, i ^ 1) for i in range(8)])


def pick(array, index, axis):
    return lax.dynamic_index_in_dim(array, index, axis, keepdims=False)


def part(array, start, size, axis):
    return lax.dynamic_slice_in_dim(array, start, size, axis)


def total(terms):
    out = terms[0].astype(F32)
    for term in terms[1:]:
        out = out + term.astype(F32)
    return out


def contract_rows(left_side, right_side):
    return lax.dot_general(
        left_side, right_side, (((0,), (0,)), ((), ())), preferred_element_type=F32
    )


def contract_cols(left_side, right_side):
    return lax.dot_general(
        left_side, right_side, (((1,), (1,)), ((), ())), preferred_element_type=F32
    )


def multiply(left_side, right_side):
    return jnp.dot(left_side, right_side, preferred_element_type=F32)


class Wire:
    def __init__(self, me, send_sem, recv_sem):
        self.me, self.send_sem, self.recv_sem, self.used = me, send_sem, recv_sem, 0

    def send(self, off, src, dst):
        copy = pltpu.make_async_remote_copy(
            src_ref=src,
            dst_ref=dst,
            send_sem=self.send_sem.at[self.used],
            recv_sem=self.recv_sem.at[self.used],
            device_id=self.me.at(off).device(),
            device_id_type=MESH,
        )
        copy.start()
        self.used += 1
        return copy


def meet(me, offsets):
    barrier = pltpu.get_barrier_semaphore()
    for off in offsets:
        back = tuple(-v for v in off)
        pl.semaphore_signal(barrier, inc=1, device_id=me.at(back).device(), device_id_type=MESH)
    pl.semaphore_wait(barrier, len(offsets))


def finish(copies):
    for copy in copies:
        copy.wait()


ZOFF = [(0, d, 0, 0, 0) for d in range(4)]


def weights_body(pieces, whole, send_sem, recv_sem):
    me = whereami()
    wire = Wire(me, send_sem, recv_sem)
    meet(me, XOFF[1:] + ZOFF[1:] + [SIBLING])
    over_x = [wire.send(XOFF[k], pieces, whole.at[k - 1, :, me.tok]) for k in (1, 2, 3)]
    over_z, over_core = [], []
    for k in (1, 2, 3):
        over_x[k - 1].wait_recv()
        block = whole.at[k - 1, :, me.tok]
        over_core.append(wire.send(SIBLING, block, block))
        over_z.append([wire.send(ZOFF[d], block, block) for d in (1, 2, 3)])
    for k in (1, 2, 3):
        for d in (1, 2, 3):
            over_z[k - 1][d - 1].wait_recv()
            block = whole.at[k - 1, :, (me.z - d + 4) % 4 * 2 + me.core]
            over_core.append(wire.send(SIBLING, block, block))
    for copy in over_x:
        copy.wait_send()
    for copies in over_z:
        for copy in copies:
            copy.wait_send()
    finish(over_core)


def gather_weights(pieces):
    return pl.pallas_call(
        weights_body,
        name="weights",
        out_shape=SDS((3, 3, 8, 128, 1024), BF),
        in_specs=[pl.BlockSpec(memory_space=pl.ANY)],
        out_specs=pl.BlockSpec(memory_space=pl.ANY),
        scratch_shapes=[pltpu.SemaphoreType.DMA((24,)), pltpu.SemaphoreType.DMA((24,))],
        compiler_params=pltpu.CompilerParams(collective_id=13, has_side_effects=True),
    )(pieces)


class PairSum:
    def __init__(self, me, left, right, terms, came, send_sem, recv_sem):
        self.me, self.left, self.right, self.terms, self.came = me, left, right, terms, came
        self.send_sem, self.recv_sem = send_sem, recv_sem

    def copy(self, i):
        return pltpu.make_async_remote_copy(
            src_ref=self.terms.at[i, :, :, 1 - self.me.core],
            dst_ref=self.came.at[i],
            send_sem=self.send_sem.at[i],
            recv_sem=self.recv_sem.at[i],
            device_id=self.me.at(SIBLING).device(),
            device_id_type=MESH,
        )

    def multiply(self, first, last):
        def step(i, _):
            cols = pl.ds(pl.multiple_of(i * 256, 256), 256)
            block = contract_rows(self.left[:, cols], self.right[...])
            self.terms[i] = block.astype(BF).reshape(2, 4, 2, 16, 2048)
            self.copy(i).start()
            return 0

        lax.fori_loop(first, last, step, 0)

    def add(self, first, last):
        def step(i, _):
            copy = self.copy(i)
            copy.wait_recv()
            mine = self.terms[i, :, :, self.me.core].astype(F32) + self.came[i].astype(F32)
            self.terms[i, :, :, self.me.core] = mine.astype(BF)
            return 0

        lax.fori_loop(first, last, step, 0)

    def sent(self):
        def step(i, _):
            self.copy(i).wait_send()
            return 0

        lax.fori_loop(0, 8, step, 0)


def ffn_body(
    mine_ref,
    grad_ref,
    resid_ref,
    scale_ref,
    gain_ref,
    w_out_ref,
    own_gate,
    own_up,
    own_down,
    whole,
    out_mine,
    resid_back,
    gain_part,
    mix_full,
    heads_back,
    ffn_in,
    up_back,
    down_own,
    down_came,
    gate_own,
    gate_came,
    turned,
    act,
    gate_back,
    gate_tile,
    up_tile,
    down_tile,
    down_acc,
    ffn_acc,
    down_send,
    ffn_send,
    down_recv,
    ffn_recv,
    mix_mine,
    back_cat,
    down_terms,
    gate_terms,
    came,
    send_sem,
    recv_sem,
    core_send,
    core_recv,
    tile_sem,
    local_sem,
    ack,
):
    me = whereami()
    wire = Wire(me, send_sem, recv_sem)
    half = [lanes(me.xl, 1024), lanes(1 - me.xl, 1024)]
    here = rows(me.y * SUB, SUB)

    def tile_copies(e, q, slot):
        copies = []
        cols = pl.ds(pl.multiple_of(q * 256, 256), 256)
        for dxl in range(2):
            k = e * 2 + dxl
            for j, (own, tile) in enumerate(
                ((own_gate, gate_tile), (own_up, up_tile), (own_down, down_tile))
            ):
                block = own if k == 0 else whole.at[k - 1, j]
                if j < 2:
                    src, dst = block.at[:, :, cols], tile.at[slot, dxl]
                else:
                    src = block.at[pl.ds(q * 2, 2)]
                    dst = tile.at[slot, :, :, dxl * 1024 : dxl * 1024 + 1024]
                copies.append(pltpu.make_async_copy(src, dst, tile_sem.at[slot, dxl * 3 + j]))
        return copies

    def fetch(e, q, slot):
        for copy in tile_copies(e, q, slot):
            copy.start()

    meet(me, YOFF[1:] + XOFF[1:] + ZOFF[1:] + [SIBLING])
    for h in range(2):
        turned[:, h * 1024 : h * 1024 + 1024] = mine_ref[:, half[h]]
    gathers = [wire.send(off, turned, ffn_in.at[here, :]) for off in YOFF[1:]]
    fetch(0, 0, 0)
    ffn_in[here, :] = turned[...]
    down_acc[...] = jnp.zeros(down_acc.shape, F32)
    ffn_acc[...] = jnp.zeros(ffn_acc.shape, F32)
    finish(gathers)

    down_sum = PairSum(me, act, grad_ref, down_terms, came, core_send.at[0], core_recv.at[0])
    gate_sum = PairSum(me, ffn_in, gate_back, gate_terms, came, core_send.at[1], core_recv.at[1])

    for e in range(2):

        def step(q, _, e=e):
            slot = q % 2

            @pl.when(q < 3)
            def _():
                fetch(e, q + 1, 1 - slot)

            if e == 0:

                @pl.when(q == 3)
                def _():
                    fetch(1, 0, 0)

            for copy in tile_copies(e, q, slot):
                copy.wait()
            cols = pl.ds(pl.multiple_of(e * 1024 + q * 256, 256), 256)
            w_g = gate_tile[slot].reshape(2048, 256)
            w_u = up_tile[slot].reshape(2048, 256)
            w_d = down_tile[slot].reshape(256, 2048)
            gate = multiply(ffn_in[...], w_g)
            up = multiply(ffn_in[...], w_u)
            act_back = contract_cols(grad_ref[...], w_d)
            sigmoid = jax.nn.sigmoid(gate)
            silu = gate * sigmoid
            act_here = (silu * up).astype(BF)
            act[:, cols] = act_here
            down_acc[...] += multiply(act_here, w_d)
            g_back = (act_back * up * sigmoid * (1.0 + gate * (1.0 - sigmoid))).astype(BF)
            u_back = (act_back * silu).astype(BF)
            gate_back[:, cols] = g_back
            up_back[:, cols] = u_back
            ffn_acc[...] += contract_cols(g_back, w_g) + contract_cols(u_back, w_u)
            return 0

        lax.fori_loop(0, 4, step, 0)
        if e == 0:
            down_sum.multiply(0, 4)

    ffn_send[...] = ffn_acc[...].astype(BF)
    ffn_moves = [
        wire.send(YOFF[d], ffn_send.at[rows(me.at(YOFF[d]).y * SUB, SUB), :], ffn_recv.at[d - 1])
        for d in (1, 2, 3)
    ]
    down_sum.multiply(4, 8)
    down_send[...] = down_acc[...].astype(BF)
    down_moves = [
        wire.send(YOFF[d], down_send.at[rows(me.at(YOFF[d]).y * SUB, SUB), :], down_recv.at[d - 1])
        for d in (1, 2, 3)
    ]

    def down_block(k):
        e, dxl = XOFF[k][4], XOFF[k][2]
        return down_terms.at[e * 4 : e * 4 + 4, :, :, me.core, :, dxl * 1024 : dxl * 1024 + 1024]

    down_sum.add(0, 4)
    x_moves = [wire.send(XOFF[1], down_block(1), down_came.at[0])]
    down_sum.add(4, 8)
    x_moves += [wire.send(XOFF[k], down_block(k), down_came.at[k - 1]) for k in (2, 3)]
    near = [pltpu.make_async_copy(down_block(0), down_own, local_sem.at[0])]
    near[0].start()
    pl.semaphore_signal(ack, inc=1, device_id=me.at(SIBLING).device(), device_id_type=MESH)

    finish(ffn_moves)

    def summed(send, recv, h):
        cols = slice(h * 1024, h * 1024 + 1024)
        out = send[here, cols].astype(F32)
        for d in range(3):
            out = out + recv[d, :, cols].astype(F32)
        return out

    scale = scale_ref[...]
    inner = jnp.zeros((SUB, 1), F32)
    for h in range(2):
        back = summed(ffn_send, ffn_recv, h)
        weighed = back * resid_ref[:, half[h]]
        inner = inner + jnp.sum(weighed * gain_ref[:, half[h]], axis=1, keepdims=True)
        gain_part[:, half[h]] = jnp.sum(weighed * scale, axis=0, keepdims=True)
    pull = scale * scale * scale * inner / D
    for h in range(2):
        back = summed(ffn_send, ffn_recv, h)
        grad = grad_ref[here, h * 1024 : h * 1024 + 1024].astype(F32)
        total_back = grad + scale * gain_ref[:, half[h]] * back - resid_ref[:, half[h]] * pull
        resid_back[:, half[h]] = total_back
        mix_mine[:, half[h]] = total_back.astype(BF)
    mix_full[here, :] = mix_mine[...]
    mix_moves = [wire.send(off, mix_mine, mix_full.at[here, :]) for off in YOFF[1:]]

    pl.semaphore_wait(ack, 1)
    gate_sum.multiply(0, 8)
    finish(down_moves)
    for h in range(2):
        out_mine[:, half[h]] = (resid_ref[:, half[h]] + summed(down_send, down_recv, h)).astype(BF)
    gate_sum.add(0, 8)

    def gate_block(z):
        return gate_terms.at[:, :, z, me.core]

    z_moves = [
        wire.send(ZOFF[d], gate_block((me.z + d) % 4), gate_came.at[d - 1]) for d in (1, 2, 3)
    ]
    near.append(pltpu.make_async_copy(gate_block(me.z), gate_own, local_sem.at[1]))
    near[1].start()

    finish(mix_moves)
    back_cat[...] = multiply(mix_full[...], w_out_ref[...]).astype(BF)
    spot = rows(me.chunk * CHUNK, CHUNK)
    head_moves = [
        wire.send(XOFF[k], back_cat.at[:, k * 128 : k * 128 + 128], heads_back.at[spot, :])
        for k in (1, 2, 3)
    ]
    heads_back[spot, :] = back_cat[:, 0:128]
    finish(head_moves + x_moves + z_moves)
    for copy in near:
        copy.wait()
    down_sum.sent()
    gate_sum.sent()


def ffn(ffn_mine, grad_full, resid, scale_two, gain, w_out, w_gate, w_up, w_down, whole):
    vm = pl.BlockSpec(memory_space=pltpu.VMEM)
    hbm = pl.BlockSpec(memory_space=pl.ANY)
    return pl.pallas_call(
        ffn_body,
        name="ffn",
        out_shape=[
            SDS((SUB, D), BF),
            SDS((SUB, D), F32),
            SDS((1, D), F32),
            SDS((CHUNK, D), BF),
            SDS((ROWS, 128), BF),
            SDS((CHUNK, D), BF),
            SDS((CHUNK, D), BF),
            SDS((4, 2, 4, 16, 1024), BF),
            SDS((3, 4, 2, 4, 16, 1024), BF),
            SDS((8, 2, 16, 2048), BF),
            SDS((3, 8, 2, 16, 2048), BF),
        ],
        in_specs=[vm] * 6 + [hbm] * 4,
        out_specs=[vm] * 7 + [hbm] * 4,
        scratch_shapes=[
            pltpu.VMEM((SUB, D), BF),
            pltpu.VMEM((CHUNK, D), BF),
            pltpu.VMEM((CHUNK, D), BF),
            pltpu.VMEM((2, 2, 8, 128, 256), BF),
            pltpu.VMEM((2, 2, 8, 128, 256), BF),
            pltpu.VMEM((2, 2, 128, 2048), BF),
            pltpu.VMEM((CHUNK, D), F32),
            pltpu.VMEM((CHUNK, D), F32),
            pltpu.VMEM((CHUNK, D), BF),
            pltpu.VMEM((CHUNK, D), BF),
            pltpu.VMEM((3, SUB, D), BF),
            pltpu.VMEM((3, SUB, D), BF),
            pltpu.VMEM((SUB, D), BF),
            pltpu.VMEM((CHUNK, 512), BF),
            pltpu.VMEM((8, 2, 4, 2, 16, 2048), BF),
            pltpu.VMEM((8, 2, 4, 2, 16, 2048), BF),
            pltpu.VMEM((8, 2, 4, 16, 2048), BF),
            pltpu.SemaphoreType.DMA((24,)),
            pltpu.SemaphoreType.DMA((24,)),
            pltpu.SemaphoreType.DMA((2, 8)),
            pltpu.SemaphoreType.DMA((2, 8)),
            pltpu.SemaphoreType.DMA((2, 6)),
            pltpu.SemaphoreType.DMA((2,)),
            pltpu.SemaphoreType.REGULAR,
        ],
        compiler_params=pltpu.CompilerParams(
            collective_id=14, has_side_effects=True, vmem_limit_bytes=60 * 2**20
        ),
        cost_estimate=pl.CostEstimate(flops=26 * 10**9, bytes_accessed=40 * 2**20, transcendentals=0),
    )(
        ffn_mine,
        grad_full,
        resid,
        scale_two,
        gain,
        w_out,
        w_gate.reshape(8, 128, 1024),
        w_up.reshape(8, 128, 1024),
        w_down.reshape(8, 128, 1024),
        whole,
    )


def per_device(
    layer_input,
    doc_lengths,
    attn_gain,
    w_query,
    w_key,
    w_value,
    w_output,
    ffn_gain,
    w_gate,
    w_up,
    w_down,
    output_grad,
):
    me = whereami()
    cos_np, sin_np = rope_table()
    cos_all, sin_all = jnp.asarray(cos_np), jnp.asarray(sin_np)
    long_first = doc_lengths[0, 0] > SHORT
    table_start = jnp.where(long_first, SHORT, 0) + me.chunk * CHUNK
    cos_here = part(cos_all, table_start, CHUNK, 0)
    sin_here = part(sin_all, table_start, CHUNK, 0)

    w_kv = jnp.concatenate(
        [part(w_key, me.y * 64, 64, 1), part(w_value, me.y * 64, 64, 1)], axis=1
    )
    full_in, w_attn, gains = exchange(
        "enter",
        0,
        enter_plan,
        [layer_input, w_query, w_kv, jnp.broadcast_to(ffn_gain[None, :], (8, 128))],
        [SDS((CHUNK, D), BF), SDS((D, 768), BF), SDS((16, 8, 128), F32)],
    )
    ffn_gain_all = gains[:, 0, :].reshape(1, D)

    half_out = part(w_output, me.core * 1024, 1024, 0)
    pieces = jnp.stack([part(w, me.tok * 128, 128, 0) for w in (w_gate, w_up, w_down)])
    full_in, half_out, pieces = lax.optimization_barrier((full_in, half_out, pieces))
    whole = gather_weights(pieces)
    got_out = [x_permute(half_out, k) for k in (1, 2, 3)]

    in_f = full_in.astype(F32)
    scale_one = lax.rsqrt(jnp.mean(in_f * in_f, axis=1, keepdims=True) + EPS)
    normed = (in_f * scale_one * attn_gain[None, :]).astype(BF)
    lin = multiply(normed, w_attn)

    def turn(block):
        lane = lax.broadcasted_iota(jnp.int32, block.shape, 1)
        swapped = jnp.where(
            (lane % 64) < 32, -jnp.roll(block, -32, axis=1), jnp.roll(block, 32, axis=1)
        )
        return block * cos_here + swapped * sin_here

    turned = [turn(lin[:, k * 128 : k * 128 + 128]) for k in range(6)]
    for k in (4, 5):
        turned[k] = jnp.concatenate(
            [turned[k][:, :64], lin[:, k * 128 + 64 : k * 128 + 128]], axis=1
        )
    lin = jnp.concatenate(turned, axis=1).astype(BF)
    queries, kv = exchange(
        "to_heads", 1, to_heads_plan, [lin], [SDS((ROWS, 128), BF), SDS((ROWS, 128), BF)]
    )
    (heads_out,) = vmem_call(
        "attend", attend_body, [doc_lengths, queries, kv], [SDS((ROWS, 128), BF)], flops=2 * 10**9
    )
    heads_cat, w_out = exchange(
        "heads_out",
        2,
        heads_out_plan,
        [heads_out, w_output] + got_out,
        [SDS((CHUNK, 512), BF), SDS((D, 512), BF)],
    )
    attn_term = contract_cols(heads_cat, w_out).astype(BF)
    attn_terms, grad_full = exchange(
        "out_sum",
        3,
        out_sum_plan,
        [attn_term, output_grad],
        [SDS((4, SUB, D), BF), SDS((CHUNK, D), BF)],
    )
    in_mine = part(full_in, me.y * SUB, SUB, 0).astype(F32)
    resid = in_mine + jnp.sum(attn_terms.astype(F32), axis=0)
    scale_two = lax.rsqrt(jnp.mean(resid * resid, axis=1, keepdims=True) + EPS)
    ffn_mine = (resid * scale_two * ffn_gain_all).astype(BF)
    (
        out_mine,
        resid_back,
        ffn_gain_part,
        mix_full,
        heads_back,
        ffn_input,
        up_back,
        down_own,
        down_came,
        gate_own,
        gate_came,
    ) = ffn(
        ffn_mine, grad_full, resid, scale_two, ffn_gain_all, w_out, w_gate, w_up, w_down, whole
    )

    query_back, kv_back = vmem_call(
        "attend_back",
        attend_back_body,
        [doc_lengths, queries, kv, heads_back, cos_all[512:1536], sin_all[512:1536]],
        [SDS((ROWS, 128), BF), SDS((ROWS, 128), BF)],
        scratch=[pltpu.VMEM((1024, 128), F32)],
        flops=5 * 10**9,
    )
    (
        layer_output,
        input_grad,
        query_grad,
        kv_grad,
        output_proj_grad,
        gate_grad,
        up_grad,
        down_grad,
        gain_grads,
    ) = back(
        [
            query_back,
            kv_back,
            w_attn,
            heads_cat,
            out_mine,
            part(full_in, me.y * SUB, SUB, 0),
            resid_back,
            part(scale_one, me.y * SUB, SUB, 0),
            attn_gain[None, :],
            ffn_gain_part,
        ],
        [normed, mix_full, ffn_input, up_back, down_own, down_came, gate_own, gate_came],
    )
    kv_cols = jnp.moveaxis(kv_grad, 0, 1).reshape(32, 4, 2, 64)
    key_grad = kv_cols[:, :, 0, :].reshape(32, 256)
    value_grad = kv_cols[:, :, 1, :].reshape(32, 256)
    gain_grads = part(gain_grads, me.tok * 16, 16, 1)
    return (
        layer_output,
        input_grad,
        gain_grads[0:1],
        query_grad,
        key_grad,
        value_grad,
        output_proj_grad,
        gain_grads[1:2],
        gate_grad,
        up_grad,
        down_grad,
    )


def solution(mesh):
    in_specs = (
        P("tok", ("narrow", "wide")),
        P("tok", None),
        P(),
        P(None, ("narrow", "wide")),
        P(None, "narrow"),
        P(None, "narrow"),
        P(None, ("narrow", "wide")),
        P(("narrow", "wide")),
        P("narrow", "wide"),
        P("narrow", "wide"),
        P("wide", "narrow"),
        P("tok", ("narrow", "wide")),
    )
    out_specs = (
        P("tok", ("narrow", "wide")),
        P("tok", ("narrow", "wide")),
        P(("narrow", "wide"), "tok"),
        P("tok", ("narrow", "wide")),
        P(("tok", "wide"), "narrow"),
        P(("tok", "wide"), "narrow"),
        P("tok", ("narrow", "wide")),
        P(("narrow", "wide"), "tok"),
        P("narrow", "tok", "wide"),
        P("narrow", "tok", "wide"),
        P("wide", "tok", "narrow"),
    )
    return jax.shard_map(
        per_device, mesh=mesh, in_specs=in_specs, out_specs=out_specs, check_vma=False
    )
```

```python
import functools
import math

import jax
import jax.numpy as jnp
import numpy as np
from jax import lax
from jax.experimental import pallas as pl
from jax.experimental.pallas import tpu as pltpu
from jax.sharding import PartitionSpec as P

HEADS = 32
KV_HEADS = 8
HEAD_DIM = 64
GROUP = 128
EPS = 1e-05
THETA = 500000.0
FACTOR = 32.0
LOW_FACTOR = 1.0
HIGH_FACTOR = 4.0
INITIAL = 8192.0
NEG = -1e30

D = 2048
ROWS = 1536
CHUNK = 384
SUB = 96
SHORT = 512
BF = jnp.bfloat16
F32 = jnp.float32
MESH = pl.DeviceIdType.MESH
SDS = jax.ShapeDtypeStruct

HERE = (0, 0, 0, 0, 0)
XOFF = [(0, 0, 0, 0, 0), (0, 0, 1, 0, 0), (0, 0, 0, 0, 1), (0, 0, 1, 0, 1)]
YOFF = [(0, 0, 0, d, 0) for d in range(4)]
PLANE = [(0, 0, a, b, e) for b in range(4) for a in range(2) for e in range(2)]
SIBLING = (1, 0, 0, 0, 0)
TOKS = [(a, b, 0, 0, 0) for b in range(4) for a in range(2)]


class Place:
    def __init__(self, core, z, xl, y, xh):
        self.core, self.z, self.xl, self.y, self.xh = core, z, xl, y, xh
        self.tok = z * 2 + core
        self.wide = y * 2 + xh
        self.block = xl * 8 + self.wide
        self.chunk = xl * 2 + xh

    def at(self, off):
        return Place(
            (self.core + off[0]) % 2,
            (self.z + off[1]) % 4,
            (self.xl + off[2]) % 2,
            (self.y + off[3]) % 4,
            (self.xh + off[4]) % 2,
        )

    def device(self):
        return (self.tok, self.xl, self.wide)


def whereami():
    tok = lax.axis_index("tok")
    wide = lax.axis_index("wide")
    return Place(tok % 2, tok // 2, lax.axis_index("narrow"), wide // 2, wide % 2)


def rows(start, size):
    return pl.ds(pl.multiple_of(start, size), size)


def lanes(index, size=128):
    return pl.ds(pl.multiple_of(index * size, size), size)


def block_probs(q_ref, kv_ref, start, i, stack):
    n = 256 * (i + 1)
    keys = kv_ref[rows_256(start, n), 0:64]
    scores = lax.dot_general(
        keys, stack, (((1,), (1,)), ((), ())), preferred_element_type=F32
    ) * (HEAD_DIM**-0.5)
    last = scores[n - 256 :, :]
    key_id = lax.broadcasted_iota(jnp.int32, (256, 512), 0)
    query_id = lax.broadcasted_iota(jnp.int32, (256, 512), 1) % 256
    last = jnp.where(key_id <= query_id, last, NEG)
    if n > 256:
        scores = jnp.concatenate([scores[: n - 256, :], last], axis=0)
    else:
        scores = last
    raised = jnp.exp(scores - jnp.max(scores, axis=0, keepdims=True))
    return keys, raised, jnp.sum(raised, axis=0, keepdims=True)


def rows_256(start, size):
    return pl.ds(pl.multiple_of(start, 256), size)


def starts_of(len_ref):
    long_first = len_ref[0, 0] > SHORT
    long_start = jnp.where(long_first, 0, SHORT)
    short_start = jnp.where(long_first, 2 * SHORT, 0)
    return ((long_start, 4), (short_start, 2))


def both(block):
    return jnp.concatenate([block[:, 0:64], block[:, 64:128]], axis=0)


def attend_body(len_ref, q_ref, kv_ref, out_ref):
    for start, blocks in starts_of(len_ref):
        for i in range(blocks):
            mine = rows_256(start + 256 * i, 256)
            stack = both(q_ref[mine, :])
            keys, raised, mass = block_probs(q_ref, kv_ref, start, i, stack)
            soft = (raised * (1.0 / mass)).astype(BF)
            values = kv_ref[rows_256(start, 256 * (i + 1)), 64:128]
            mixed = lax.dot_general(
                soft, values, (((0,), (0,)), ((), ())), preferred_element_type=F32
            )
            out_ref[mine, :] = jnp.concatenate([mixed[:256], mixed[256:]], axis=1).astype(BF)


def unrope(tensor, cosine, sine):
    lane = lax.broadcasted_iota(jnp.int32, tensor.shape, 1)
    first = (lane % 64) < 32
    swapped = jnp.where(first, pltpu.roll(tensor, 96, 1), -pltpu.roll(tensor, 32, 1))
    return tensor * cosine + swapped * sine


def attend_back_body(len_ref, q_ref, kv_ref, back_ref, cos_ref, sin_ref, dq_ref, dkv_ref, acc_ref):
    for start, blocks in starts_of(len_ref):
        acc_ref[...] = jnp.zeros(acc_ref.shape, F32)
        for i in range(blocks):
            n = 256 * (i + 1)
            mine = rows_256(start + 256 * i, 256)
            stack = both(q_ref[mine, :])
            keys, raised, mass = block_probs(q_ref, kv_ref, start, i, stack)
            soft = raised * (1.0 / mass)
            values = kv_ref[rows_256(start, n), 64:128]
            backs = both(back_ref[mine, :])
            prob_back = lax.dot_general(
                values, backs, (((1,), (1,)), ((), ())), preferred_element_type=F32
            )
            inner = jnp.sum(soft * prob_back, axis=0, keepdims=True)
            score_back = (soft * (prob_back - inner)).astype(BF)
            dq = lax.dot_general(
                score_back, keys, (((0,), (0,)), ((), ())), preferred_element_type=F32
            ) * (HEAD_DIM**-0.5)
            dq = jnp.concatenate([dq[:256], dq[256:]], axis=1)
            pos = slice(256 * i, 256 * i + 256)
            dq_ref[mine, :] = unrope(dq, cos_ref[pos, :], sin_ref[pos, :]).astype(BF)
            dk = jnp.dot(score_back, stack, preferred_element_type=F32) * (HEAD_DIM**-0.5)
            dv = jnp.dot(soft.astype(BF), backs, preferred_element_type=F32)
            acc_ref[0:n, :] += jnp.concatenate([dk, dv], axis=1)
        m = 256 * blocks
        acc = acc_ref[0:m, :]
        lane = lax.broadcasted_iota(jnp.int32, acc.shape, 1)
        turned = unrope(acc, cos_ref[0:m, :], sin_ref[0:m, :])
        dkv_ref[rows_256(start, m), :] = jnp.where(lane < 64, turned, acc).astype(BF)


def vmem_call(name, body, ins, outs, scratch=(), flops=0):
    return pl.pallas_call(
        body,
        name=name,
        out_shape=outs,
        in_specs=[pl.BlockSpec(memory_space=pltpu.SMEM)]
        + [pl.BlockSpec(memory_space=pltpu.VMEM)] * (len(ins) - 1),
        out_specs=[pl.BlockSpec(memory_space=pltpu.VMEM)] * len(outs),
        scratch_shapes=list(scratch),
        compiler_params=pltpu.CompilerParams(vmem_limit_bytes=48 * 2**20),
        cost_estimate=pl.CostEstimate(flops=flops, bytes_accessed=2**20, transcendentals=0),
    )(*ins)


def back_body(
    dq_ref,
    dkv_ref,
    w_attn,
    heads_cat,
    out_mine,
    in_mine,
    resid_back,
    scale_ref,
    gain_ref,
    ffn_gain_part,
    normed_in,
    mix_in,
    ffn_in,
    up_in,
    down_own,
    down_came,
    gate_own,
    gate_came,
    layer_output,
    input_grad,
    query_grad,
    kv_grad,
    out_grad,
    gate_grad,
    up_grad,
    down_grad,
    gain_grad,
    left_buf,
    right_buf,
    down_in,
    gate_in,
    down_sum,
    gate_sum,
    down_z,
    gate_x,
    up_terms,
    up_core,
    up_z,
    up_sum,
    up_x,
    cat_back,
    norm_send,
    norm_recv,
    in_grad,
    gain_parts,
    gain_plane,
    gain_mine,
    gain_toks,
    o_terms,
    o_core,
    o_x,
    o_sum,
    o_z,
    q_terms,
    q_core,
    q_x,
    q_sum,
    q_z,
    k_terms,
    k_core,
    k_x,
    k_sum,
    k_z,
    k_last,
    send_sem,
    recv_sem,
    core_send,
    core_recv,
    local_sem,
):
    me = whereami()
    wire = Wire(me, send_sem, recv_sem)
    load_left = pltpu.make_async_copy(ffn_in, left_buf, local_sem.at[0])
    load_right = pltpu.make_async_copy(up_in, right_buf, local_sem.at[1])
    load_left.start()
    load_right.start()

    def halves(own, came, buf, h, sem):
        part_of = pl.ds(h * (own.shape[0] // 2), own.shape[0] // 2)
        return [
            pltpu.make_async_copy(own.at[part_of], buf.at[0], local_sem.at[sem]),
            pltpu.make_async_copy(came.at[:, part_of], buf.at[1:4], local_sem.at[sem + 1]),
        ]

    def start(copies):
        for copy in copies:
            copy.start()

    start(halves(gate_own, gate_came, gate_in, 0, 2))
    start(halves(down_own, down_came, down_in, 0, 4))
    meet(me, PLANE[1:] + TOKS[1:])
    sent = []

    spot = rows(me.chunk * CHUNK, CHUNK)
    moves = []
    for k in (1, 2, 3):
        there = rows(me.at(XOFF[k]).chunk * CHUNK, CHUNK)
        for ref, col in ((dq_ref, 0), (dkv_ref, 512)):
            moves.append(
                wire.send(
                    XOFF[k], ref.at[there, :], cat_back.at[:, col + k * 128 : col + k * 128 + 128]
                )
            )
    cat_back[:, 0:128] = dq_ref[spot, :]
    cat_back[:, 512:640] = dkv_ref[spot, :]

    mine = rows(me.chunk * CHUNK + me.y * SUB, SUB)
    leaving = [
        wire.send(off, out_mine.at[:, lanes(me.at(off).block)], layer_output.at[mine, :])
        for off in PLANE[1:]
    ]
    layer_output[mine, :] = out_mine[:, lanes(me.block)]

    load_left.wait()
    load_right.wait()
    up_pair = PairSum(me, left_buf, right_buf, up_terms, up_core, core_send, core_recv)
    up_pair.multiply(0, 8)
    load_left = pltpu.make_async_copy(normed_in, left_buf, local_sem.at[0])
    load_right = pltpu.make_async_copy(mix_in, right_buf, local_sem.at[1])
    load_left.start()
    load_right.start()
    up_pair.add(0, 8)
    up_moves = [
        wire.send(ZOFF[d], up_terms.at[:, :, (me.z + d) % 4, me.core], up_z.at[d - 1])
        for d in (1, 2, 3)
    ]

    finish(moves)
    for h in range(4):
        cols = slice(h * 512, h * 512 + 512)
        term = contract_cols(cat_back[:, 0:768], w_attn[cols, :]) + contract_cols(
            cat_back[:, 768:1024], w_attn[cols, 512:768]
        )
        norm_send[:, cols] = term.astype(BF)
    norm_moves = [
        wire.send(YOFF[d], norm_send.at[rows(me.at(YOFF[d]).y * SUB, SUB), :], norm_recv.at[d - 1])
        for d in (1, 2, 3)
    ]

    load_left.wait()
    load_right.wait()
    for z in range(4):
        block = contract_rows(left_buf[:, z * 512 : z * 512 + 512], cat_back[:, 0:512])
        q_terms[z] = block.astype(BF).reshape(2, 256, 512)
    q_pair = wire.send(SIBLING, q_terms.at[:, 1 - me.core], q_core)
    for z in range(4):
        left = left_buf[:, z * 512 : z * 512 + 512]
        block = contract_rows(left, cat_back[:, 512:768]) + contract_rows(
            left, cat_back[:, 768:1024]
        )
        k_terms[z] = block.astype(BF).reshape(2, 4, 2, 32, 256)
    k_pair = wire.send(SIBLING, k_terms.at[:, 1 - me.core], k_core)
    for z in range(4):
        block = contract_rows(right_buf[:, z * 512 : z * 512 + 512], heads_cat[...])
        o_terms[z] = block.astype(BF).reshape(2, 256, 512)
    o_pair = wire.send(SIBLING, o_terms.at[:, 1 - me.core], o_core)

    def fold(own, came, buf, out, sem):
        size = buf.shape[1]
        for h in range(2):
            copies = halves(own, came, buf, h, sem)
            for copy in copies:
                copy.wait()

            def step(i, _, h=h):
                value = buf[0, i].astype(F32)
                for k in (1, 2, 3):
                    value = value + buf[k, i].astype(F32)
                out[h * size + i] = value.astype(BF)
                return 0

            lax.fori_loop(0, size, step, 0)
            if h == 0:
                start(halves(own, came, buf, 1, sem))

    def gate_block(k):
        e, dxl = XOFF[k][4], XOFF[k][2]
        return gate_sum.at[dxl * 4 : dxl * 4 + 4, :, :, e * 1024 : e * 1024 + 1024]

    fold(gate_own, gate_came, gate_in, gate_sum, 2)
    gate_moves = [wire.send(XOFF[k], gate_block(k), gate_x.at[k - 1]) for k in (1, 2, 3)]
    fold(down_own, down_came, down_in, down_sum, 4)
    down_moves = [
        wire.send(ZOFF[d], down_sum.at[:, :, (me.z + d) % 4], down_z.at[d - 1]) for d in (1, 2, 3)
    ]

    def add_core(copy, terms, came):
        copy.wait_recv()
        terms[:, me.core] = (terms[:, me.core].astype(F32) + came[...].astype(F32)).astype(BF)

    def kv_block(k):
        e, dxl = XOFF[k][4], XOFF[k][2]
        return k_terms.at[:, me.core, :, (me.xh + e) % 2, :, dxl * 128 : dxl * 128 + 128]

    add_core(k_pair, k_terms, k_core)
    k_moves = [wire.send(XOFF[k], kv_block(k), k_x.at[k - 1]) for k in (1, 2, 3)]
    add_core(q_pair, q_terms, q_core)
    q_moves = [
        wire.send(XOFF[k], q_terms.at[:, me.core, :, k * 128 : k * 128 + 128], q_x.at[k - 1])
        for k in (1, 2, 3)
    ]
    add_core(o_pair, o_terms, o_core)
    o_moves = [
        wire.send(XOFF[k], o_terms.at[:, me.core, :, k * 128 : k * 128 + 128], o_x.at[k - 1])
        for k in (1, 2, 3)
    ]

    finish(norm_moves)
    here = rows(me.y * SUB, SUB)
    back = norm_send[here, :].astype(F32)
    for d in range(3):
        back = back + norm_recv[d].astype(F32)
    scale = scale_ref[...]
    enter = in_mine[...].astype(F32)
    weighed = back * enter
    inner = jnp.sum(weighed * gain_ref[...], axis=1, keepdims=True)
    gain_parts[0:1, :] = jnp.sum(weighed * scale, axis=0, keepdims=True)
    gain_parts[1:2, :] = ffn_gain_part[...]
    gain_parts[2:8, :] = jnp.zeros((6, D), F32)
    pull = scale * scale * scale * inner / D
    in_grad[...] = (resid_back[...] + scale * gain_ref[...] * back - enter * pull).astype(BF)
    for off in PLANE[1:]:
        there = lanes(me.at(off).block)
        leaving.append(wire.send(off, in_grad.at[:, there], input_grad.at[mine, :]))
        leaving.append(wire.send(off, gain_parts.at[:, there], gain_plane.at[me.block]))
    input_grad[mine, :] = in_grad[:, lanes(me.block)]
    gain_plane[me.block] = gain_parts[:, lanes(me.block)]

    def over_x(moves, own, came, out):
        for copy in moves:
            copy.wait_recv()
        value = own.astype(F32)
        for k in range(3):
            value = value + came[k].astype(F32)
        out[...] = value.astype(BF)
        sent.extend(moves)

    over_x(o_moves, o_terms[:, me.core, :, 0:128], o_x, o_sum)
    over_x(q_moves, q_terms[:, me.core, :, 0:128], q_x, q_sum)
    over_x(k_moves, k_terms[:, me.core, :, me.xh, :, 0:128], k_x, k_sum)
    late = []
    for summed, came in ((o_sum, o_z), (q_sum, q_z), (k_sum, k_z)):
        late.append(
            [wire.send(ZOFF[d], summed.at[(me.z + d) % 4], came.at[d - 1]) for d in (1, 2, 3)]
        )

    def over_z(moves, own, came):
        for copy in moves:
            copy.wait_recv()
        sent.extend(moves)
        value = own.astype(F32)
        for d in range(3):
            value = value + came[d].astype(F32)
        return value

    down_grad[...] = over_z(down_moves, down_sum[:, :, me.z].reshape(8, 16, 1024), down_z.reshape(3, 8, 16, 1024))
    gate_grad[...] = over_z(gate_moves, gate_sum[0:4, :, :, 0:1024].reshape(8, 16, 1024), gate_x.reshape(3, 8, 16, 1024))
    for copy in up_moves:
        copy.wait_recv()
    sent.extend(up_moves)

    def up_step(i, _):
        value = up_terms[i, :, me.z, me.core].astype(F32)
        for d in range(3):
            value = value + up_z[d, i].astype(F32)
        up_sum[i] = value.astype(BF)
        return 0

    lax.fori_loop(0, 8, up_step, 0)

    def up_block(k):
        e, dxl = XOFF[k][4], XOFF[k][2]
        return up_sum.at[dxl * 4 : dxl * 4 + 4, :, :, e * 1024 : e * 1024 + 1024]

    up_moves = [wire.send(XOFF[k], up_block(k), up_x.at[k - 1]) for k in (1, 2, 3)]

    out_grad[...] = over_z(late[0], o_sum[me.z], o_z)
    query_grad[...] = over_z(late[1], q_sum[me.z], q_z)
    k_last[...] = over_z(late[2], k_sum[me.z], k_z)
    y_moves = [wire.send(YOFF[d], k_last.at[me.at(YOFF[d]).y], kv_grad.at[me.y]) for d in (1, 2, 3)]
    kv_grad[me.y] = k_last[me.y]
    for copy in leaving:
        copy.wait_recv()
    sent.extend(leaving)
    gain_mine[...] = jnp.sum(gain_plane[...], axis=0)
    tok_moves = [wire.send(off, gain_mine, gain_toks.at[me.tok]) for off in TOKS[1:]]
    gain_toks[me.tok] = gain_mine[...]
    up_grad[...] = over_z(up_moves, up_sum[0:4, :, :, 0:1024].reshape(8, 16, 1024), up_x.reshape(3, 8, 16, 1024))
    finish(y_moves + tok_moves)
    gain_grad[...] = jnp.sum(gain_toks[...], axis=0)
    for copy in sent:
        copy.wait_send()
    up_pair.sent()
    o_pair.wait_send()
    q_pair.wait_send()
    k_pair.wait_send()


def back(vmem_ins, hbm_ins):
    vm = pl.BlockSpec(memory_space=pltpu.VMEM)
    hbm = pl.BlockSpec(memory_space=pl.ANY)
    outs = [
        SDS((ROWS, 128), BF),
        SDS((ROWS, 128), BF),
        SDS((256, 128), F32),
        SDS((4, 32, 128), F32),
        SDS((256, 128), F32),
        SDS((8, 16, 1024), F32),
        SDS((8, 16, 1024), F32),
        SDS((8, 16, 1024), F32),
        SDS((8, 128), F32),
    ]
    v = pltpu.VMEM
    heads_sum = [
        v((4, 2, 256, 512), BF),
        v((4, 256, 512), BF),
        v((3, 4, 256, 128), BF),
        v((4, 256, 128), BF),
        v((3, 256, 128), BF),
    ]
    return pl.pallas_call(
        back_body,
        name="back",
        out_shape=outs,
        in_specs=[vm] * len(vmem_ins) + [hbm] * len(hbm_ins),
        out_specs=[vm] * len(outs),
        scratch_shapes=[
            v((CHUNK, D), BF),
            v((CHUNK, D), BF),
            v((4, 2, 2, 4, 16, 1024), BF),
            v((4, 4, 2, 16, 2048), BF),
            v((4, 2, 4, 16, 1024), BF),
            v((8, 2, 16, 2048), BF),
            v((3, 4, 2, 16, 1024), BF),
            v((3, 4, 2, 16, 1024), BF),
            v((8, 2, 4, 2, 16, 2048), BF),
            v((8, 2, 4, 16, 2048), BF),
            v((3, 8, 2, 16, 2048), BF),
            v((8, 2, 16, 2048), BF),
            v((3, 4, 2, 16, 1024), BF),
            v((CHUNK, 1024), BF),
            v((CHUNK, D), BF),
            v((3, SUB, D), BF),
            v((SUB, D), BF),
            v((8, D), F32),
            v((16, 8, 128), F32),
            v((8, 128), F32),
            v((8, 8, 128), F32),
        ]
        + heads_sum
        + heads_sum
        + [
            v((4, 2, 4, 2, 32, 256), BF),
            v((4, 4, 2, 32, 256), BF),
            v((3, 4, 4, 32, 128), BF),
            v((4, 4, 32, 128), BF),
            v((3, 4, 32, 128), BF),
            v((4, 32, 128), F32),
            pltpu.SemaphoreType.DMA((104,)),
            pltpu.SemaphoreType.DMA((104,)),
            pltpu.SemaphoreType.DMA((8,)),
            pltpu.SemaphoreType.DMA((8,)),
            pltpu.SemaphoreType.DMA((6,)),
        ],
        compiler_params=pltpu.CompilerParams(
            collective_id=15, has_side_effects=True, vmem_limit_bytes=56 * 2**20
        ),
        cost_estimate=pl.CostEstimate(flops=10**10, bytes_accessed=30 * 2**20, transcendentals=0),
    )(*vmem_ins, *hbm_ins)


def rope_table():
    halfway = HEAD_DIM // 2
    k = np.arange(halfway, dtype=np.float32)
    inverse = np.exp(-2.0 * k / HEAD_DIM * math.log(THETA)).astype(np.float32)
    wavelen = (2.0 * math.pi / inverse).astype(np.float32)
    scaled = inverse / np.float32(FACTOR)
    smooth = (INITIAL / wavelen - LOW_FACTOR) / (HIGH_FACTOR - LOW_FACTOR)
    middle = (1.0 - smooth) * scaled + smooth * inverse
    frequency = np.where(
        wavelen < INITIAL / HIGH_FACTOR,
        inverse,
        np.where(wavelen > INITIAL / LOW_FACTOR, scaled, middle),
    ).astype(np.float32)
    positions = np.concatenate([np.arange(512), np.arange(1024), np.arange(512)]).astype(np.float32)
    angles = (positions[:, None] * frequency[None, :]).astype(np.float32).astype(np.float64)
    return (
        np.tile(np.cos(angles).astype(np.float32), (1, 4)),
        np.tile(np.sin(angles).astype(np.float32), (1, 4)),
    )


def x_permute(value, k):
    if k == 1:
        return lax.ppermute(value, "narrow", [(0, 1), (1, 0)])
    if k == 2:
        return lax.ppermute(value, "wide", [(i, i ^ 1) for i in range(8)])
    return lax.ppermute(value, ("narrow", "wide"), [(i, i ^ 9) for i in range(16)])


def z_permute(value, d):
    return lax.ppermute(value, "tok", [(i, (i + 2 * d) % 8) for i in range(8)])


def part(array, start, size, axis):
    return lax.dynamic_slice_in_dim(array, start, size, axis)


def contract_rows(left_side, right_side):
    return lax.dot_general(
        left_side, right_side, (((0,), (0,)), ((), ())), preferred_element_type=F32
    )


def contract_cols(left_side, right_side):
    return lax.dot_general(
        left_side, right_side, (((1,), (1,)), ((), ())), preferred_element_type=F32
    )


def multiply(left_side, right_side):
    return jnp.dot(left_side, right_side, preferred_element_type=F32)


class Wire:
    def __init__(self, me, send_sem, recv_sem):
        self.me, self.send_sem, self.recv_sem, self.used = me, send_sem, recv_sem, 0

    def send(self, off, src, dst):
        copy = pltpu.make_async_remote_copy(
            src_ref=src,
            dst_ref=dst,
            send_sem=self.send_sem.at[self.used],
            recv_sem=self.recv_sem.at[self.used],
            device_id=self.me.at(off).device(),
            device_id_type=MESH,
        )
        copy.start()
        self.used += 1
        return copy


def meet(me, offsets):
    barrier = pltpu.get_barrier_semaphore()
    for off in offsets:
        back = tuple(-v for v in off)
        pl.semaphore_signal(barrier, inc=1, device_id=me.at(back).device(), device_id_type=MESH)
    pl.semaphore_wait(barrier, len(offsets))


def finish(copies):
    for copy in copies:
        copy.wait()


ZOFF = [(0, d, 0, 0, 0) for d in range(4)]


def weights_body(pieces, came, send_sem, recv_sem):
    me = whereami()
    wire = Wire(me, send_sem, recv_sem)
    meet(me, XOFF[1:])
    finish([wire.send(XOFF[k], pieces, came.at[k - 1]) for k in (1, 2, 3)])


def weights_over_x(pieces):
    return pl.pallas_call(
        weights_body,
        name="weights",
        out_shape=SDS((3, 3, 128, 1024), BF),
        in_specs=[pl.BlockSpec(memory_space=pl.ANY)],
        out_specs=pl.BlockSpec(memory_space=pl.ANY),
        scratch_shapes=[pltpu.SemaphoreType.DMA((3,)), pltpu.SemaphoreType.DMA((3,))],
        compiler_params=pltpu.CompilerParams(collective_id=13, has_side_effects=True),
    )(pieces)


def split_rows(count, size):
    return [slice(i * size, i * size + size) for i in range(count)]


def front_body(
    gain_row,
    attn_gain,
    cos_ref,
    sin_ref,
    hidden,
    w_q,
    w_kv,
    out_grad,
    q,
    kv,
    w_attn,
    normed,
    in_mine,
    scale_mine,
    gains,
    grad_full,
    full,
    lin,
    scales,
    send_sem,
    recv_sem,
    local_sem,
):
    me = whereami()
    wire = Wire(me, send_sem, recv_sem)
    chunk = rows(me.chunk * CHUNK, CHUNK)
    near = []

    def take(src, dst):
        near.append(pltpu.make_async_copy(src, dst, local_sem.at[len(near)]))
        near[-1].start()

    take(w_q, w_attn.at[:, 0:128])
    take(w_kv, w_attn.at[:, 512:640])
    take(hidden.at[chunk, :], full.at[:, lanes(me.block)])
    take(out_grad.at[chunk, :], grad_full.at[:, lanes(me.wide)])
    gains[me.block] = gain_row[...]
    meet(me, PLANE[1:] + [SIBLING])

    half = rows(me.core * 1024, 1024)
    blocks = [w_attn.at[half, k * 128 : k * 128 + 128] for k in (1, 2, 3)]
    over_x = [wire.send(XOFF[k], w_q.at[half, :], blocks[k - 1]) for k in (1, 2, 3)]
    blocks.append(w_attn.at[half, 640:768])
    over_x.append(wire.send(XOFF[1], w_kv.at[half, :], blocks[3]))

    def chunk_of(off):
        return rows(me.at(off).chunk * CHUNK, CHUNK)

    enter = [
        wire.send(off, hidden.at[chunk_of(off), :], full.at[:, lanes(me.block)])
        for off in PLANE[1:]
    ]
    others = [wire.send(off, gain_row, gains.at[me.block]) for off in PLANE[1:]]
    others += [
        wire.send(off, out_grad.at[chunk_of(off), :], grad_full.at[:, lanes(off[2] * 8 + me.wide)])
        for off in PLANE[1:]
    ]
    over_core = []
    for copy, block in zip(over_x, blocks):
        copy.wait_recv()
        over_core.append(wire.send(SIBLING, block, block))
    for copy in enter:
        copy.wait_recv()
    for copy in near:
        copy.wait()
    for part_rows in split_rows(4, SUB):
        value = full[part_rows, :].astype(F32)
        scale = lax.rsqrt(jnp.mean(value * value, axis=1, keepdims=True) + EPS)
        scales[part_rows, :] = scale
        normed[part_rows, :] = (value * scale * attn_gain[...]).astype(BF)
    for copy in over_core:
        copy.wait_recv()
    lane = lax.broadcasted_iota(jnp.int32, (CHUNK, 128), 1)
    for k in range(6):
        cols = slice(k * 128, k * 128 + 128)
        block = multiply(normed[...], w_attn[:, cols])
        swapped = jnp.where(
            (lane % 64) < 32, -pltpu.roll(block, 96, 1), pltpu.roll(block, 32, 1)
        )
        turned = block * cos_ref[...] + swapped * sin_ref[...]
        if k >= 4:
            turned = jnp.where(lane < 64, turned, block)
        lin[:, cols] = turned.astype(BF)
    moves = []
    for k in (1, 2, 3):
        kv_col = 512 + 128 * XOFF[k][2]
        moves.append(wire.send(XOFF[k], lin.at[:, k * 128 : k * 128 + 128], q.at[chunk, :]))
        moves.append(wire.send(XOFF[k], lin.at[:, kv_col : kv_col + 128], kv.at[chunk, :]))
    q[chunk, :] = lin[:, 0:128]
    kv[chunk, :] = lin[:, 512:640]
    here = rows(me.y * SUB, SUB)
    in_mine[...] = full[here, :]
    scale_mine[...] = scales[here, :]
    for copy in over_x + enter:
        copy.wait_send()
    for copy in over_core:
        copy.wait_send()
    finish(others + moves)


def front(gain_row, attn_gain, cos_here, sin_here, hidden, w_q, w_kv, out_grad):
    vm = pl.BlockSpec(memory_space=pltpu.VMEM)
    hbm = pl.BlockSpec(memory_space=pl.ANY)
    outs = [
        SDS((ROWS, 128), BF),
        SDS((ROWS, 128), BF),
        SDS((D, 768), BF),
        SDS((CHUNK, D), BF),
        SDS((SUB, D), BF),
        SDS((SUB, 1), F32),
        SDS((16, 8, 128), F32),
        SDS((CHUNK, D), BF),
    ]
    return pl.pallas_call(
        front_body,
        name="front",
        out_shape=outs,
        in_specs=[vm] * 4 + [hbm] * 4,
        out_specs=[vm] * len(outs),
        scratch_shapes=[
            pltpu.VMEM((CHUNK, D), BF),
            pltpu.VMEM((CHUNK, 768), BF),
            pltpu.VMEM((CHUNK, 1), F32),
            pltpu.SemaphoreType.DMA((60,)),
            pltpu.SemaphoreType.DMA((60,)),
            pltpu.SemaphoreType.DMA((4,)),
        ],
        compiler_params=pltpu.CompilerParams(
            collective_id=0, has_side_effects=True, vmem_limit_bytes=40 * 2**20
        ),
        cost_estimate=pl.CostEstimate(flops=2 * 10**9, bytes_accessed=2**23, transcendentals=0),
    )(gain_row, attn_gain, cos_here, sin_here, hidden, w_q, w_kv, out_grad)


def middle_body(
    heads,
    in_mine,
    gain,
    w_out,
    half1,
    half2,
    half3,
    heads_cat,
    w_cat,
    resid,
    scale_out,
    ffn_mine,
    term_send,
    term_recv,
    send_sem,
    recv_sem,
    local_sem,
):
    me = whereami()
    wire = Wire(me, send_sem, recv_sem)
    half = rows(me.core * 1024, 1024)
    blocks = [w_cat.at[half, k * 128 : k * 128 + 128] for k in (1, 2, 3)]
    pairs = [(w_out, w_cat.at[:, 0:128])] + list(zip((half1, half2, half3), blocks))
    near = []
    for src, dst in pairs:
        near.append(pltpu.make_async_copy(src, dst, local_sem.at[len(near)]))
        near[-1].start()
    meet(me, XOFF[1:] + YOFF[1:] + [SIBLING])
    moves = [
        wire.send(
            XOFF[k],
            heads.at[rows(me.at(XOFF[k]).chunk * CHUNK, CHUNK), :],
            heads_cat.at[:, k * 128 : k * 128 + 128],
        )
        for k in (1, 2, 3)
    ]
    moves += [wire.send(SIBLING, src, dst) for src, dst in pairs[1:]]
    heads_cat[:, 0:128] = heads[rows(me.chunk * CHUNK, CHUNK), :]
    for copy in near:
        copy.wait()
    finish(moves)
    sums = []
    for h in range(2):
        for p in range(2):
            cols = slice(h * 1024 + p * 512, h * 1024 + p * 512 + 512)
            term_send[:, cols] = contract_cols(heads_cat[...], w_cat[cols, :]).astype(BF)
        cols = slice(h * 1024, h * 1024 + 1024)
        for d in (1, 2, 3):
            there = rows(me.at(YOFF[d]).y * SUB, SUB)
            sums.append(
                wire.send(YOFF[d], term_send.at[there, cols], term_recv.at[d - 1, :, cols])
            )
    finish(sums)
    value = in_mine[...].astype(F32) + term_send[rows(me.y * SUB, SUB), :].astype(F32)
    for d in range(3):
        value = value + term_recv[d].astype(F32)
    resid[...] = value
    scale = lax.rsqrt(jnp.mean(value * value, axis=1, keepdims=True) + EPS)
    scale_out[...] = scale
    ffn_mine[...] = (value * scale * gain[...]).astype(BF)


def middle(heads, in_mine, gain, w_out, halves):
    vm = pl.BlockSpec(memory_space=pltpu.VMEM)
    hbm = pl.BlockSpec(memory_space=pl.ANY)
    outs = [
        SDS((CHUNK, 512), BF),
        SDS((D, 512), BF),
        SDS((SUB, D), F32),
        SDS((SUB, 1), F32),
        SDS((SUB, D), BF),
    ]
    return pl.pallas_call(
        middle_body,
        name="middle",
        out_shape=outs,
        in_specs=[vm] * 3 + [hbm] * 4,
        out_specs=[vm] * len(outs),
        scratch_shapes=[
            pltpu.VMEM((CHUNK, D), BF),
            pltpu.VMEM((3, SUB, D), BF),
            pltpu.SemaphoreType.DMA((12,)),
            pltpu.SemaphoreType.DMA((12,)),
            pltpu.SemaphoreType.DMA((4,)),
        ],
        compiler_params=pltpu.CompilerParams(
            collective_id=1, has_side_effects=True, vmem_limit_bytes=32 * 2**20
        ),
        cost_estimate=pl.CostEstimate(flops=10**9, bytes_accessed=2**23, transcendentals=0),
    )(heads, in_mine, gain, w_out, *halves)


class PairSum:
    def __init__(self, me, left, right, terms, came, send_sem, recv_sem):
        self.me, self.left, self.right, self.terms, self.came = me, left, right, terms, came
        self.send_sem, self.recv_sem = send_sem, recv_sem

    def copy(self, i):
        return pltpu.make_async_remote_copy(
            src_ref=self.terms.at[i, :, :, 1 - self.me.core],
            dst_ref=self.came.at[i],
            send_sem=self.send_sem.at[i],
            recv_sem=self.recv_sem.at[i],
            device_id=self.me.at(SIBLING).device(),
            device_id_type=MESH,
        )

    def multiply(self, first, last):
        def step(i, _):
            cols = pl.ds(pl.multiple_of(i * 256, 256), 256)
            block = contract_rows(self.left[:, cols], self.right[...])
            self.terms[i] = block.astype(BF).reshape(2, 4, 2, 16, 2048)
            self.copy(i).start()
            return 0

        lax.fori_loop(first, last, step, 0)

    def add(self, first, last):
        def step(i, _):
            copy = self.copy(i)
            copy.wait_recv()
            mine = self.terms[i, :, :, self.me.core].astype(F32) + self.came[i].astype(F32)
            self.terms[i, :, :, self.me.core] = mine.astype(BF)
            return 0

        lax.fori_loop(first, last, step, 0)

    def sent(self):
        def step(i, _):
            self.copy(i).wait_send()
            return 0

        lax.fori_loop(0, 8, step, 0)


def ffn_body(
    mine_ref,
    grad_ref,
    resid_ref,
    scale_ref,
    gain_ref,
    w_out_ref,
    own_gate,
    own_up,
    own_down,
    piece0,
    piece1,
    piece2,
    piece3,
    out_mine,
    resid_back,
    gain_part,
    mix_full,
    heads_back,
    ffn_in,
    up_back,
    down_own,
    down_came,
    gate_own,
    gate_came,
    other_core,
    turned,
    act,
    gate_back,
    gate_tile,
    up_tile,
    down_tile,
    down_acc,
    ffn_acc,
    down_send,
    ffn_send,
    down_recv,
    ffn_recv,
    mix_mine,
    back_cat,
    down_terms,
    gate_terms,
    came,
    send_sem,
    recv_sem,
    core_send,
    core_recv,
    tile_sem,
    local_sem,
    ack,
):
    me = whereami()
    wire = Wire(me, send_sem, recv_sem)
    half = [lanes(me.xl, 1024), lanes(1 - me.xl, 1024)]
    here = rows(me.y * SUB, SUB)

    pieces = (piece0, piece1, piece2, piece3)

    def tile_copies(e, q, slot):
        copies, groups = [], []
        cols = pl.ds(pl.multiple_of(q * 256, 256), 256)

        def copy(src, dst):
            sem = tile_sem.at[slot, len(copies) + len(groups)]
            return pltpu.make_async_copy(src, dst, sem)

        for dxl in range(2):
            k = e * 2 + dxl
            for j, (own, tile) in enumerate(((own_gate, gate_tile), (own_up, up_tile))):
                if k == 0:
                    copies.append(copy(own.at[:, :, :, cols], tile.at[slot, dxl]))
                    continue
                for d, piece in enumerate(pieces):
                    spot = tile.at[slot, dxl, (me.z - d + 4) % 4, me.core]
                    copies.append(copy(piece.at[k - 1, j, :, cols], spot))
                spot = tile.at[slot, dxl, :, 1 - me.core]
                copies.append(copy(other_core.at[:, k - 1, j, :, cols], spot))
            here = slice(dxl * 1024, dxl * 1024 + 1024)
            if k == 0:
                copies.append(copy(own_down.at[q], down_tile.at[slot, :, :, here]))
                continue
            spot = down_tile.at[slot, 1 - me.core, :, here]
            copies.append(copy(other_core.at[q, k - 1, 2], spot))
            spot = down_tile.at[slot, me.core, :, here]
            groups.append([copy(piece.at[k - 1, 2], spot) for piece in pieces])
        return copies, groups

    def fetch(e, q, slot):
        copies, groups = tile_copies(e, q, slot)
        for copy in copies:
            copy.start()
        for group in groups:
            for d, copy in enumerate(group):
                pl.when((me.z - q + 4) % 4 == d)(copy.start)

    def arrive(e, q, slot):
        copies, groups = tile_copies(e, q, slot)
        for copy in copies + [group[0] for group in groups]:
            copy.wait()

    meet(me, YOFF[1:] + XOFF[1:] + ZOFF[1:] + [SIBLING])
    for h in range(2):
        turned[:, h * 1024 : h * 1024 + 1024] = mine_ref[:, half[h]]
    gathers = [wire.send(off, turned, ffn_in.at[here, :]) for off in YOFF[1:]]
    shares = [
        [
            wire.send(SIBLING, piece.at[k], other_core.at[(me.z - d + 4) % 4, k])
            for d, piece in enumerate(pieces)
        ]
        for k in range(3)
    ]
    ffn_in[here, :] = turned[...]
    down_acc[...] = jnp.zeros(down_acc.shape, F32)
    ffn_acc[...] = jnp.zeros(ffn_acc.shape, F32)
    finish(shares[0])
    fetch(0, 0, 0)
    finish(gathers)

    down_sum = PairSum(me, act, grad_ref, down_terms, came, core_send.at[0], core_recv.at[0])
    gate_sum = PairSum(me, ffn_in, gate_back, gate_terms, came, core_send.at[1], core_recv.at[1])

    for e in range(2):

        if e == 0:
            finish(shares[1] + shares[2])

        def step(q, _, e=e):
            slot = q % 2

            @pl.when(q < 3)
            def _():
                fetch(e, q + 1, 1 - slot)

            if e == 0:

                @pl.when(q == 3)
                def _():
                    fetch(1, 0, 0)

            arrive(e, q, slot)
            cols = pl.ds(pl.multiple_of(e * 1024 + q * 256, 256), 256)
            w_g = gate_tile[slot].reshape(2048, 256)
            w_u = up_tile[slot].reshape(2048, 256)
            w_d = down_tile[slot].reshape(256, 2048)
            gate = multiply(ffn_in[...], w_g)
            up = multiply(ffn_in[...], w_u)
            act_back = contract_cols(grad_ref[...], w_d)
            sigmoid = jax.nn.sigmoid(gate)
            silu = gate * sigmoid
            act_here = (silu * up).astype(BF)
            act[:, cols] = act_here
            down_acc[...] += multiply(act_here, w_d)
            g_back = (act_back * up * sigmoid * (1.0 + gate * (1.0 - sigmoid))).astype(BF)
            u_back = (act_back * silu).astype(BF)
            gate_back[:, cols] = g_back
            up_back[:, cols] = u_back
            ffn_acc[...] += contract_cols(g_back, w_g) + contract_cols(u_back, w_u)
            return 0

        lax.fori_loop(0, 4, step, 0)
        if e == 0:
            down_sum.multiply(0, 4)

    ffn_send[...] = ffn_acc[...].astype(BF)
    ffn_moves = [
        wire.send(YOFF[d], ffn_send.at[rows(me.at(YOFF[d]).y * SUB, SUB), :], ffn_recv.at[d - 1])
        for d in (1, 2, 3)
    ]
    down_sum.multiply(4, 8)
    down_send[...] = down_acc[...].astype(BF)
    down_moves = [
        wire.send(YOFF[d], down_send.at[rows(me.at(YOFF[d]).y * SUB, SUB), :], down_recv.at[d - 1])
        for d in (1, 2, 3)
    ]

    def down_block(k):
        e, dxl = XOFF[k][4], XOFF[k][2]
        return down_terms.at[e * 4 : e * 4 + 4, :, :, me.core, :, dxl * 1024 : dxl * 1024 + 1024]

    down_sum.add(0, 4)
    x_moves = [wire.send(XOFF[1], down_block(1), down_came.at[0])]
    down_sum.add(4, 8)
    x_moves += [wire.send(XOFF[k], down_block(k), down_came.at[k - 1]) for k in (2, 3)]
    near = [pltpu.make_async_copy(down_block(0), down_own, local_sem.at[0])]
    near[0].start()
    pl.semaphore_signal(ack, inc=1, device_id=me.at(SIBLING).device(), device_id_type=MESH)

    finish(ffn_moves)

    def summed(send, recv, h):
        cols = slice(h * 1024, h * 1024 + 1024)
        out = send[here, cols].astype(F32)
        for d in range(3):
            out = out + recv[d, :, cols].astype(F32)
        return out

    scale = scale_ref[...]
    inner = jnp.zeros((SUB, 1), F32)
    for h in range(2):
        back = summed(ffn_send, ffn_recv, h)
        weighed = back * resid_ref[:, half[h]]
        inner = inner + jnp.sum(weighed * gain_ref[:, half[h]], axis=1, keepdims=True)
        gain_part[:, half[h]] = jnp.sum(weighed * scale, axis=0, keepdims=True)
    pull = scale * scale * scale * inner / D
    for h in range(2):
        back = summed(ffn_send, ffn_recv, h)
        grad = grad_ref[here, h * 1024 : h * 1024 + 1024].astype(F32)
        total_back = grad + scale * gain_ref[:, half[h]] * back - resid_ref[:, half[h]] * pull
        resid_back[:, half[h]] = total_back
        mix_mine[:, half[h]] = total_back.astype(BF)
    mix_full[here, :] = mix_mine[...]
    mix_moves = [wire.send(off, mix_mine, mix_full.at[here, :]) for off in YOFF[1:]]

    pl.semaphore_wait(ack, 1)
    gate_sum.multiply(0, 8)
    finish(down_moves)
    for h in range(2):
        out_mine[:, half[h]] = (resid_ref[:, half[h]] + summed(down_send, down_recv, h)).astype(BF)
    gate_sum.add(0, 8)

    def gate_block(z):
        return gate_terms.at[:, :, z, me.core]

    z_moves = [
        wire.send(ZOFF[d], gate_block((me.z + d) % 4), gate_came.at[d - 1]) for d in (1, 2, 3)
    ]
    near.append(pltpu.make_async_copy(gate_block(me.z), gate_own, local_sem.at[1]))
    near[1].start()

    finish(mix_moves)
    back_cat[...] = multiply(mix_full[...], w_out_ref[...]).astype(BF)
    spot = rows(me.chunk * CHUNK, CHUNK)
    head_moves = [
        wire.send(XOFF[k], back_cat.at[:, k * 128 : k * 128 + 128], heads_back.at[spot, :])
        for k in (1, 2, 3)
    ]
    heads_back[spot, :] = back_cat[:, 0:128]
    finish(head_moves + x_moves + z_moves)
    for copy in near:
        copy.wait()
    down_sum.sent()
    gate_sum.sent()


def ffn(ffn_mine, grad_full, resid, scale_two, gain, w_out, w_gate, w_up, w_down, pieces):
    vm = pl.BlockSpec(memory_space=pltpu.VMEM)
    hbm = pl.BlockSpec(memory_space=pl.ANY)
    return pl.pallas_call(
        ffn_body,
        name="ffn",
        out_shape=[
            SDS((SUB, D), BF),
            SDS((SUB, D), F32),
            SDS((1, D), F32),
            SDS((CHUNK, D), BF),
            SDS((ROWS, 128), BF),
            SDS((CHUNK, D), BF),
            SDS((CHUNK, D), BF),
            SDS((4, 2, 4, 16, 1024), BF),
            SDS((3, 4, 2, 4, 16, 1024), BF),
            SDS((8, 2, 16, 2048), BF),
            SDS((3, 8, 2, 16, 2048), BF),
            SDS((4, 3, 3, 128, 1024), BF),
        ],
        in_specs=[vm] * 6 + [hbm] * 7,
        out_specs=[vm] * 7 + [hbm] * 5,
        scratch_shapes=[
            pltpu.VMEM((SUB, D), BF),
            pltpu.VMEM((CHUNK, D), BF),
            pltpu.VMEM((CHUNK, D), BF),
            pltpu.VMEM((2, 2, 4, 2, 128, 256), BF),
            pltpu.VMEM((2, 2, 4, 2, 128, 256), BF),
            pltpu.VMEM((2, 2, 128, 2048), BF),
            pltpu.VMEM((CHUNK, D), F32),
            pltpu.VMEM((CHUNK, D), F32),
            pltpu.VMEM((CHUNK, D), BF),
            pltpu.VMEM((CHUNK, D), BF),
            pltpu.VMEM((3, SUB, D), BF),
            pltpu.VMEM((3, SUB, D), BF),
            pltpu.VMEM((SUB, D), BF),
            pltpu.VMEM((CHUNK, 512), BF),
            pltpu.VMEM((8, 2, 4, 2, 16, 2048), BF),
            pltpu.VMEM((8, 2, 4, 2, 16, 2048), BF),
            pltpu.VMEM((8, 2, 4, 16, 2048), BF),
            pltpu.SemaphoreType.DMA((36,)),
            pltpu.SemaphoreType.DMA((36,)),
            pltpu.SemaphoreType.DMA((2, 8)),
            pltpu.SemaphoreType.DMA((2, 8)),
            pltpu.SemaphoreType.DMA((2, 24)),
            pltpu.SemaphoreType.DMA((2,)),
            pltpu.SemaphoreType.REGULAR,
        ],
        compiler_params=pltpu.CompilerParams(
            collective_id=14, has_side_effects=True, vmem_limit_bytes=60 * 2**20
        ),
        cost_estimate=pl.CostEstimate(flops=26 * 10**9, bytes_accessed=40 * 2**20, transcendentals=0),
    )(
        ffn_mine,
        grad_full,
        resid,
        scale_two,
        gain,
        w_out,
        w_gate.reshape(4, 2, 128, 1024),
        w_up.reshape(4, 2, 128, 1024),
        w_down.reshape(4, 2, 128, 1024),
        *pieces,
    )


def per_device(
    layer_input,
    doc_lengths,
    attn_gain,
    w_query,
    w_key,
    w_value,
    w_output,
    ffn_gain,
    w_gate,
    w_up,
    w_down,
    output_grad,
):
    me = whereami()
    cos_np, sin_np = rope_table()
    cos_all, sin_all = jnp.asarray(cos_np), jnp.asarray(sin_np)
    long_first = doc_lengths[0, 0] > SHORT
    table_start = jnp.where(long_first, SHORT, 0) + me.chunk * CHUNK
    cos_here = part(cos_all, table_start, CHUNK, 0)
    sin_here = part(sin_all, table_start, CHUNK, 0)

    w_kv = jnp.concatenate(
        [part(w_key, me.y * 64, 64, 1), part(w_value, me.y * 64, 64, 1)], axis=1
    )
    pieces = jnp.stack([part(w, me.tok * 128, 128, 0) for w in (w_gate, w_up, w_down)])
    pieces = [weights_over_x(pieces)]
    pieces += [z_permute(pieces[0], d) for d in (1, 2, 3)]
    queries, kv, w_attn, normed, in_mine, scale_mine, gains, grad_full = front(
        jnp.broadcast_to(ffn_gain[None, :], (8, 128)),
        attn_gain[None, :],
        cos_here,
        sin_here,
        layer_input,
        w_query,
        w_kv,
        output_grad,
    )
    ffn_gain_all = gains[:, 0, :].reshape(1, D)
    half_out = part(w_output, me.core * 1024, 1024, 0)
    queries, half_out = lax.optimization_barrier((queries, half_out))
    got_out = [x_permute(half_out, k) for k in (1, 2, 3)]
    (heads_out,) = vmem_call(
        "attend", attend_body, [doc_lengths, queries, kv], [SDS((ROWS, 128), BF)], flops=2 * 10**9
    )
    heads_cat, w_out, resid, scale_two, ffn_mine = middle(
        heads_out, in_mine, ffn_gain_all, w_output, got_out
    )
    (
        out_mine,
        resid_back,
        ffn_gain_part,
        mix_full,
        heads_back,
        ffn_input,
        up_back,
        down_own,
        down_came,
        gate_own,
        gate_came,
        _,
    ) = ffn(
        ffn_mine, grad_full, resid, scale_two, ffn_gain_all, w_out, w_gate, w_up, w_down, pieces
    )

    query_back, kv_back = vmem_call(
        "attend_back",
        attend_back_body,
        [doc_lengths, queries, kv, heads_back, cos_all[512:1536], sin_all[512:1536]],
        [SDS((ROWS, 128), BF), SDS((ROWS, 128), BF)],
        scratch=[pltpu.VMEM((1024, 128), F32)],
        flops=5 * 10**9,
    )
    (
        layer_output,
        input_grad,
        query_grad,
        kv_grad,
        output_proj_grad,
        gate_grad,
        up_grad,
        down_grad,
        gain_grads,
    ) = back(
        [
            query_back,
            kv_back,
            w_attn,
            heads_cat,
            out_mine,
            in_mine,
            resid_back,
            scale_mine,
            attn_gain[None, :],
            ffn_gain_part,
        ],
        [normed, mix_full, ffn_input, up_back, down_own, down_came, gate_own, gate_came],
    )
    kv_cols = jnp.moveaxis(kv_grad, 0, 1).reshape(32, 4, 2, 64)
    key_grad = kv_cols[:, :, 0, :].reshape(32, 256)
    value_grad = kv_cols[:, :, 1, :].reshape(32, 256)
    gain_grads = part(gain_grads, me.tok * 16, 16, 1)
    return (
        layer_output,
        input_grad,
        gain_grads[0:1],
        query_grad,
        key_grad,
        value_grad,
        output_proj_grad,
        gain_grads[1:2],
        gate_grad,
        up_grad,
        down_grad,
    )


def solution(mesh):
    in_specs = (
        P("tok", ("narrow", "wide")),
        P("tok", None),
        P(),
        P(None, ("narrow", "wide")),
        P(None, "narrow"),
        P(None, "narrow"),
        P(None, ("narrow", "wide")),
        P(("narrow", "wide")),
        P("narrow", "wide"),
        P("narrow", "wide"),
        P("wide", "narrow"),
        P("tok", ("narrow", "wide")),
    )
    out_specs = (
        P("tok", ("narrow", "wide")),
        P("tok", ("narrow", "wide")),
        P(("narrow", "wide"), "tok"),
        P("tok", ("narrow", "wide")),
        P(("tok", "wide"), "narrow"),
        P(("tok", "wide"), "narrow"),
        P("tok", ("narrow", "wide")),
        P(("narrow", "wide"), "tok"),
        P("narrow", "tok", "wide"),
        P("narrow", "tok", "wide"),
        P("wide", "tok", "narrow"),
    )
    return jax.shard_map(
        per_device, mesh=mesh, in_specs=in_specs, out_specs=out_specs, check_vma=False
    )
```

```python
import functools
import math

import jax
import jax.numpy as jnp
import numpy as np
from jax import lax
from jax.experimental import pallas as pl
from jax.experimental.pallas import tpu as pltpu
from jax.sharding import PartitionSpec as P

HEADS = 32
KV_HEADS = 8
HEAD_DIM = 64
GROUP = 128
EPS = 1e-05
THETA = 500000.0
FACTOR = 32.0
LOW_FACTOR = 1.0
HIGH_FACTOR = 4.0
INITIAL = 8192.0
NEG = -1e30

D = 2048
ROWS = 1536
CHUNK = 384
SUB = 96
SHORT = 512
BF = jnp.bfloat16
F32 = jnp.float32
MESH = pl.DeviceIdType.MESH
SDS = jax.ShapeDtypeStruct

HERE = (0, 0, 0, 0, 0)
XOFF = [(0, 0, 0, 0, 0), (0, 0, 1, 0, 0), (0, 0, 0, 0, 1), (0, 0, 1, 0, 1)]
YOFF = [(0, 0, 0, d, 0) for d in range(4)]
PLANE = [(0, 0, a, b, e) for b in range(4) for a in range(2) for e in range(2)]
SIBLING = (1, 0, 0, 0, 0)
TOKS = [(a, b, 0, 0, 0) for b in range(4) for a in range(2)]


class Place:
    def __init__(self, core, z, xl, y, xh):
        self.core, self.z, self.xl, self.y, self.xh = core, z, xl, y, xh
        self.tok = z * 2 + core
        self.wide = y * 2 + xh
        self.block = xl * 8 + self.wide
        self.chunk = xl * 2 + xh

    def at(self, off):
        return Place(
            (self.core + off[0]) % 2,
            (self.z + off[1]) % 4,
            (self.xl + off[2]) % 2,
            (self.y + off[3]) % 4,
            (self.xh + off[4]) % 2,
        )

    def device(self):
        return (self.tok, self.xl, self.wide)


def whereami():
    tok = lax.axis_index("tok")
    wide = lax.axis_index("wide")
    return Place(tok % 2, tok // 2, lax.axis_index("narrow"), wide // 2, wide % 2)


def rows(start, size):
    return pl.ds(pl.multiple_of(start, size), size)


def lanes(index, size=128):
    return pl.ds(pl.multiple_of(index * size, size), size)


def block_probs(q_ref, kv_ref, start, i, stack):
    n = 256 * (i + 1)
    keys = kv_ref[rows_256(start, n), 0:64]
    scores = lax.dot_general(
        keys, stack, (((1,), (1,)), ((), ())), preferred_element_type=F32
    ) * (HEAD_DIM**-0.5)
    last = scores[n - 256 :, :]
    key_id = lax.broadcasted_iota(jnp.int32, (256, 512), 0)
    query_id = lax.broadcasted_iota(jnp.int32, (256, 512), 1) % 256
    last = jnp.where(key_id <= query_id, last, NEG)
    if n > 256:
        scores = jnp.concatenate([scores[: n - 256, :], last], axis=0)
    else:
        scores = last
    raised = jnp.exp(scores - jnp.max(scores, axis=0, keepdims=True))
    return keys, raised, jnp.sum(raised, axis=0, keepdims=True)


def rows_256(start, size):
    return pl.ds(pl.multiple_of(start, 256), size)


def starts_of(len_ref):
    long_first = len_ref[0, 0] > SHORT
    long_start = jnp.where(long_first, 0, SHORT)
    short_start = jnp.where(long_first, 2 * SHORT, 0)
    return ((long_start, 4), (short_start, 2))


def both(block):
    return jnp.concatenate([block[:, 0:64], block[:, 64:128]], axis=0)


def attend_body(len_ref, q_ref, kv_ref, out_ref):
    for start, blocks in starts_of(len_ref):
        for i in range(blocks):
            mine = rows_256(start + 256 * i, 256)
            stack = both(q_ref[mine, :])
            keys, raised, mass = block_probs(q_ref, kv_ref, start, i, stack)
            soft = (raised * (1.0 / mass)).astype(BF)
            values = kv_ref[rows_256(start, 256 * (i + 1)), 64:128]
            mixed = lax.dot_general(
                soft, values, (((0,), (0,)), ((), ())), preferred_element_type=F32
            )
            out_ref[mine, :] = jnp.concatenate([mixed[:256], mixed[256:]], axis=1).astype(BF)


def unrope(tensor, cosine, sine):
    lane = lax.broadcasted_iota(jnp.int32, tensor.shape, 1)
    first = (lane % 64) < 32
    swapped = jnp.where(first, pltpu.roll(tensor, 96, 1), -pltpu.roll(tensor, 32, 1))
    return tensor * cosine + swapped * sine


def attend_back_body(len_ref, q_ref, kv_ref, back_ref, cos_ref, sin_ref, dq_ref, dkv_ref, acc_ref):
    for start, blocks in starts_of(len_ref):
        acc_ref[...] = jnp.zeros(acc_ref.shape, F32)
        for i in range(blocks):
            n = 256 * (i + 1)
            mine = rows_256(start + 256 * i, 256)
            stack = both(q_ref[mine, :])
            keys, raised, mass = block_probs(q_ref, kv_ref, start, i, stack)
            soft = raised * (1.0 / mass)
            values = kv_ref[rows_256(start, n), 64:128]
            backs = both(back_ref[mine, :])
            prob_back = lax.dot_general(
                values, backs, (((1,), (1,)), ((), ())), preferred_element_type=F32
            )
            inner = jnp.sum(soft * prob_back, axis=0, keepdims=True)
            score_back = (soft * (prob_back - inner)).astype(BF)
            dq = lax.dot_general(
                score_back, keys, (((0,), (0,)), ((), ())), preferred_element_type=F32
            ) * (HEAD_DIM**-0.5)
            dq = jnp.concatenate([dq[:256], dq[256:]], axis=1)
            pos = slice(256 * i, 256 * i + 256)
            dq_ref[mine, :] = unrope(dq, cos_ref[pos, :], sin_ref[pos, :]).astype(BF)
            dk = jnp.dot(score_back, stack, preferred_element_type=F32) * (HEAD_DIM**-0.5)
            dv = jnp.dot(soft.astype(BF), backs, preferred_element_type=F32)
            acc_ref[0:n, :] += jnp.concatenate([dk, dv], axis=1)
        m = 256 * blocks
        acc = acc_ref[0:m, :]
        lane = lax.broadcasted_iota(jnp.int32, acc.shape, 1)
        turned = unrope(acc, cos_ref[0:m, :], sin_ref[0:m, :])
        dkv_ref[rows_256(start, m), :] = jnp.where(lane < 64, turned, acc).astype(BF)


def vmem_call(name, body, ins, outs, scratch=(), flops=0):
    return pl.pallas_call(
        body,
        name=name,
        out_shape=outs,
        in_specs=[pl.BlockSpec(memory_space=pltpu.SMEM)]
        + [pl.BlockSpec(memory_space=pltpu.VMEM)] * (len(ins) - 1),
        out_specs=[pl.BlockSpec(memory_space=pltpu.VMEM)] * len(outs),
        scratch_shapes=list(scratch),
        compiler_params=pltpu.CompilerParams(vmem_limit_bytes=48 * 2**20),
        cost_estimate=pl.CostEstimate(flops=flops, bytes_accessed=2**20, transcendentals=0),
    )(*ins)


def back_body(
    dq_ref,
    dkv_ref,
    w_attn,
    heads_cat,
    out_mine,
    in_mine,
    resid_back,
    scale_ref,
    gain_ref,
    ffn_gain_part,
    normed_in,
    mix_in,
    ffn_in,
    up_in,
    down_own,
    down_came,
    gate_own,
    gate_came,
    layer_output,
    input_grad,
    query_grad,
    kv_grad,
    out_grad,
    gate_grad,
    up_grad,
    down_grad,
    gain_grad,
    left_buf,
    right_buf,
    down_in,
    gate_in,
    down_sum,
    gate_sum,
    down_z,
    gate_x,
    up_terms,
    up_core,
    up_z,
    up_sum,
    up_x,
    cat_back,
    norm_send,
    norm_recv,
    in_grad,
    gain_parts,
    gain_plane,
    gain_mine,
    gain_toks,
    o_terms,
    o_core,
    o_x,
    o_sum,
    o_z,
    q_terms,
    q_core,
    q_x,
    q_sum,
    q_z,
    k_terms,
    k_core,
    k_x,
    k_sum,
    k_z,
    k_last,
    send_sem,
    recv_sem,
    core_send,
    core_recv,
    local_sem,
):
    me = whereami()
    wire = Wire(me, send_sem, recv_sem)
    load_left = pltpu.make_async_copy(ffn_in, left_buf, local_sem.at[0])
    load_right = pltpu.make_async_copy(up_in, right_buf, local_sem.at[1])
    load_left.start()
    load_right.start()

    def halves(own, came, buf, h, sem):
        part_of = pl.ds(h * (own.shape[0] // 2), own.shape[0] // 2)
        return [
            pltpu.make_async_copy(own.at[part_of], buf.at[0], local_sem.at[sem]),
            pltpu.make_async_copy(came.at[:, part_of], buf.at[1:4], local_sem.at[sem + 1]),
        ]

    def start(copies):
        for copy in copies:
            copy.start()

    start(halves(gate_own, gate_came, gate_in, 0, 2))
    start(halves(down_own, down_came, down_in, 0, 4))
    meet(me, PLANE[1:] + TOKS[1:])
    sent = []

    spot = rows(me.chunk * CHUNK, CHUNK)
    moves = []
    for k in (1, 2, 3):
        there = rows(me.at(XOFF[k]).chunk * CHUNK, CHUNK)
        for ref, col in ((dq_ref, 0), (dkv_ref, 512)):
            moves.append(
                wire.send(
                    XOFF[k], ref.at[there, :], cat_back.at[:, col + k * 128 : col + k * 128 + 128]
                )
            )
    cat_back[:, 0:128] = dq_ref[spot, :]
    cat_back[:, 512:640] = dkv_ref[spot, :]

    mine = rows(me.chunk * CHUNK + me.y * SUB, SUB)
    leaving = [
        wire.send(off, out_mine.at[:, lanes(me.at(off).block)], layer_output.at[mine, :])
        for off in PLANE[1:]
    ]
    layer_output[mine, :] = out_mine[:, lanes(me.block)]

    load_left.wait()
    load_right.wait()
    up_pair = PairSum(me, left_buf, right_buf, up_terms, up_core, core_send, core_recv)
    up_pair.multiply(0, 8)
    load_left = pltpu.make_async_copy(mix_in, left_buf, local_sem.at[0])
    load_left.start()
    load_left.wait()
    for z in range(4):
        block = contract_rows(left_buf[:, z * 512 : z * 512 + 512], heads_cat[...])
        o_terms[z] = block.astype(BF).reshape(2, 256, 512)
    o_pair = wire.send(SIBLING, o_terms.at[:, 1 - me.core], o_core)
    load_right = pltpu.make_async_copy(normed_in, right_buf, local_sem.at[1])
    load_right.start()
    up_pair.add(0, 8)
    up_moves = [
        wire.send(ZOFF[d], up_terms.at[:, :, (me.z + d) % 4, me.core], up_z.at[d - 1])
        for d in (1, 2, 3)
    ]

    finish(moves)
    for h in range(4):
        cols = slice(h * 512, h * 512 + 512)
        term = contract_cols(cat_back[:, 0:768], w_attn[cols, :]) + contract_cols(
            cat_back[:, 768:1024], w_attn[cols, 512:768]
        )
        norm_send[:, cols] = term.astype(BF)
    norm_moves = [
        wire.send(YOFF[d], norm_send.at[rows(me.at(YOFF[d]).y * SUB, SUB), :], norm_recv.at[d - 1])
        for d in (1, 2, 3)
    ]

    def add_core(copy, terms, came):
        copy.wait_recv()
        terms[:, me.core] = (terms[:, me.core].astype(F32) + came[...].astype(F32)).astype(BF)

    add_core(o_pair, o_terms, o_core)
    o_moves = [
        wire.send(XOFF[k], o_terms.at[:, me.core, :, k * 128 : k * 128 + 128], o_x.at[k - 1])
        for k in (1, 2, 3)
    ]

    load_right.wait()
    for z in range(4):
        block = contract_rows(right_buf[:, z * 512 : z * 512 + 512], cat_back[:, 0:512])
        q_terms[z] = block.astype(BF).reshape(2, 256, 512)
    q_pair = wire.send(SIBLING, q_terms.at[:, 1 - me.core], q_core)
    for z in range(4):
        left = right_buf[:, z * 512 : z * 512 + 512]
        block = contract_rows(left, cat_back[:, 512:768]) + contract_rows(
            left, cat_back[:, 768:1024]
        )
        k_terms[z] = block.astype(BF).reshape(2, 4, 2, 32, 256)
    k_pair = wire.send(SIBLING, k_terms.at[:, 1 - me.core], k_core)

    def fold(own, came, buf, out, sem):
        size = buf.shape[1]
        for h in range(2):
            copies = halves(own, came, buf, h, sem)
            for copy in copies:
                copy.wait()

            def step(i, _, h=h):
                value = buf[0, i].astype(F32)
                for k in (1, 2, 3):
                    value = value + buf[k, i].astype(F32)
                out[h * size + i] = value.astype(BF)
                return 0

            lax.fori_loop(0, size, step, 0)
            if h == 0:
                start(halves(own, came, buf, 1, sem))

    def gate_block(k):
        e, dxl = XOFF[k][4], XOFF[k][2]
        return gate_sum.at[dxl * 4 : dxl * 4 + 4, :, :, e * 1024 : e * 1024 + 1024]

    fold(gate_own, gate_came, gate_in, gate_sum, 2)
    gate_moves = [wire.send(XOFF[k], gate_block(k), gate_x.at[k - 1]) for k in (1, 2, 3)]
    fold(down_own, down_came, down_in, down_sum, 4)
    down_moves = [
        wire.send(ZOFF[d], down_sum.at[:, :, (me.z + d) % 4], down_z.at[d - 1]) for d in (1, 2, 3)
    ]

    def kv_block(k):
        e, dxl = XOFF[k][4], XOFF[k][2]
        return k_terms.at[:, me.core, :, (me.xh + e) % 2, :, dxl * 128 : dxl * 128 + 128]

    add_core(k_pair, k_terms, k_core)
    k_moves = [wire.send(XOFF[k], kv_block(k), k_x.at[k - 1]) for k in (1, 2, 3)]
    add_core(q_pair, q_terms, q_core)
    q_moves = [
        wire.send(XOFF[k], q_terms.at[:, me.core, :, k * 128 : k * 128 + 128], q_x.at[k - 1])
        for k in (1, 2, 3)
    ]

    finish(norm_moves)
    here = rows(me.y * SUB, SUB)
    back = norm_send[here, :].astype(F32)
    for d in range(3):
        back = back + norm_recv[d].astype(F32)
    scale = scale_ref[...]
    enter = in_mine[...].astype(F32)
    weighed = back * enter
    inner = jnp.sum(weighed * gain_ref[...], axis=1, keepdims=True)
    gain_parts[0:1, :] = jnp.sum(weighed * scale, axis=0, keepdims=True)
    gain_parts[1:2, :] = ffn_gain_part[...]
    gain_parts[2:8, :] = jnp.zeros((6, D), F32)
    pull = scale * scale * scale * inner / D
    in_grad[...] = (resid_back[...] + scale * gain_ref[...] * back - enter * pull).astype(BF)
    for off in PLANE[1:]:
        there = lanes(me.at(off).block)
        leaving.append(wire.send(off, in_grad.at[:, there], input_grad.at[mine, :]))
        leaving.append(wire.send(off, gain_parts.at[:, there], gain_plane.at[me.block]))
    input_grad[mine, :] = in_grad[:, lanes(me.block)]
    gain_plane[me.block] = gain_parts[:, lanes(me.block)]

    def over_x(moves, own, came, out):
        for copy in moves:
            copy.wait_recv()
        value = own.astype(F32)
        for k in range(3):
            value = value + came[k].astype(F32)
        out[...] = value.astype(BF)
        sent.extend(moves)

    over_x(o_moves, o_terms[:, me.core, :, 0:128], o_x, o_sum)
    over_x(q_moves, q_terms[:, me.core, :, 0:128], q_x, q_sum)
    over_x(k_moves, k_terms[:, me.core, :, me.xh, :, 0:128], k_x, k_sum)
    late = []
    for summed, came in ((o_sum, o_z), (q_sum, q_z), (k_sum, k_z)):
        late.append(
            [wire.send(ZOFF[d], summed.at[(me.z + d) % 4], came.at[d - 1]) for d in (1, 2, 3)]
        )

    def over_z(moves, own, came):
        for copy in moves:
            copy.wait_recv()
        sent.extend(moves)
        value = own.astype(F32)
        for d in range(3):
            value = value + came[d].astype(F32)
        return value

    down_grad[...] = over_z(down_moves, down_sum[:, :, me.z].reshape(8, 16, 1024), down_z.reshape(3, 8, 16, 1024))
    gate_grad[...] = over_z(gate_moves, gate_sum[0:4, :, :, 0:1024].reshape(8, 16, 1024), gate_x.reshape(3, 8, 16, 1024))
    for copy in up_moves:
        copy.wait_recv()
    sent.extend(up_moves)

    def up_step(i, _):
        value = up_terms[i, :, me.z, me.core].astype(F32)
        for d in range(3):
            value = value + up_z[d, i].astype(F32)
        up_sum[i] = value.astype(BF)
        return 0

    lax.fori_loop(0, 8, up_step, 0)

    def up_block(k):
        e, dxl = XOFF[k][4], XOFF[k][2]
        return up_sum.at[dxl * 4 : dxl * 4 + 4, :, :, e * 1024 : e * 1024 + 1024]

    up_moves = [wire.send(XOFF[k], up_block(k), up_x.at[k - 1]) for k in (1, 2, 3)]

    out_grad[...] = over_z(late[0], o_sum[me.z], o_z)
    query_grad[...] = over_z(late[1], q_sum[me.z], q_z)
    k_last[...] = over_z(late[2], k_sum[me.z], k_z)
    y_moves = [wire.send(YOFF[d], k_last.at[me.at(YOFF[d]).y], kv_grad.at[me.y]) for d in (1, 2, 3)]
    kv_grad[me.y] = k_last[me.y]
    for copy in leaving:
        copy.wait_recv()
    sent.extend(leaving)
    gain_mine[...] = jnp.sum(gain_plane[...], axis=0)
    tok_moves = [wire.send(off, gain_mine, gain_toks.at[me.tok]) for off in TOKS[1:]]
    gain_toks[me.tok] = gain_mine[...]
    up_grad[...] = over_z(up_moves, up_sum[0:4, :, :, 0:1024].reshape(8, 16, 1024), up_x.reshape(3, 8, 16, 1024))
    finish(y_moves + tok_moves)
    gain_grad[...] = jnp.sum(gain_toks[...], axis=0)
    for copy in sent:
        copy.wait_send()
    up_pair.sent()
    o_pair.wait_send()
    q_pair.wait_send()
    k_pair.wait_send()


def back(vmem_ins, hbm_ins):
    vm = pl.BlockSpec(memory_space=pltpu.VMEM)
    hbm = pl.BlockSpec(memory_space=pl.ANY)
    outs = [
        SDS((ROWS, 128), BF),
        SDS((ROWS, 128), BF),
        SDS((256, 128), F32),
        SDS((4, 32, 128), F32),
        SDS((256, 128), F32),
        SDS((8, 16, 1024), F32),
        SDS((8, 16, 1024), F32),
        SDS((8, 16, 1024), F32),
        SDS((8, 128), F32),
    ]
    v = pltpu.VMEM
    heads_sum = [
        v((4, 2, 256, 512), BF),
        v((4, 256, 512), BF),
        v((3, 4, 256, 128), BF),
        v((4, 256, 128), BF),
        v((3, 256, 128), BF),
    ]
    return pl.pallas_call(
        back_body,
        name="back",
        out_shape=outs,
        in_specs=[vm] * len(vmem_ins) + [hbm] * len(hbm_ins),
        out_specs=[vm] * len(outs),
        scratch_shapes=[
            v((CHUNK, D), BF),
            v((CHUNK, D), BF),
            v((4, 2, 2, 4, 16, 1024), BF),
            v((4, 4, 2, 16, 2048), BF),
            v((4, 2, 4, 16, 1024), BF),
            v((8, 2, 16, 2048), BF),
            v((3, 4, 2, 16, 1024), BF),
            v((3, 4, 2, 16, 1024), BF),
            v((8, 2, 4, 2, 16, 2048), BF),
            v((8, 2, 4, 16, 2048), BF),
            v((3, 8, 2, 16, 2048), BF),
            v((8, 2, 16, 2048), BF),
            v((3, 4, 2, 16, 1024), BF),
            v((CHUNK, 1024), BF),
            v((CHUNK, D), BF),
            v((3, SUB, D), BF),
            v((SUB, D), BF),
            v((8, D), F32),
            v((16, 8, 128), F32),
            v((8, 128), F32),
            v((8, 8, 128), F32),
        ]
        + heads_sum
        + heads_sum
        + [
            v((4, 2, 4, 2, 32, 256), BF),
            v((4, 4, 2, 32, 256), BF),
            v((3, 4, 4, 32, 128), BF),
            v((4, 4, 32, 128), BF),
            v((3, 4, 32, 128), BF),
            v((4, 32, 128), F32),
            pltpu.SemaphoreType.DMA((104,)),
            pltpu.SemaphoreType.DMA((104,)),
            pltpu.SemaphoreType.DMA((8,)),
            pltpu.SemaphoreType.DMA((8,)),
            pltpu.SemaphoreType.DMA((6,)),
        ],
        compiler_params=pltpu.CompilerParams(
            collective_id=15, has_side_effects=True, vmem_limit_bytes=56 * 2**20
        ),
        cost_estimate=pl.CostEstimate(flops=10**10, bytes_accessed=30 * 2**20, transcendentals=0),
    )(*vmem_ins, *hbm_ins)


def rope_table():
    halfway = HEAD_DIM // 2
    k = np.arange(halfway, dtype=np.float32)
    inverse = np.exp(-2.0 * k / HEAD_DIM * math.log(THETA)).astype(np.float32)
    wavelen = (2.0 * math.pi / inverse).astype(np.float32)
    scaled = inverse / np.float32(FACTOR)
    smooth = (INITIAL / wavelen - LOW_FACTOR) / (HIGH_FACTOR - LOW_FACTOR)
    middle = (1.0 - smooth) * scaled + smooth * inverse
    frequency = np.where(
        wavelen < INITIAL / HIGH_FACTOR,
        inverse,
        np.where(wavelen > INITIAL / LOW_FACTOR, scaled, middle),
    ).astype(np.float32)
    positions = np.concatenate([np.arange(512), np.arange(1024), np.arange(512)]).astype(np.float32)
    angles = (positions[:, None] * frequency[None, :]).astype(np.float32).astype(np.float64)
    return (
        np.tile(np.cos(angles).astype(np.float32), (1, 4)),
        np.tile(np.sin(angles).astype(np.float32), (1, 4)),
    )


def z_permute(value, d):
    return lax.ppermute(value, "tok", [(i, (i + 2 * d) % 8) for i in range(8)])


def part(array, start, size, axis):
    return lax.dynamic_slice_in_dim(array, start, size, axis)


def contract_rows(left_side, right_side):
    return lax.dot_general(
        left_side, right_side, (((0,), (0,)), ((), ())), preferred_element_type=F32
    )


def contract_cols(left_side, right_side):
    return lax.dot_general(
        left_side, right_side, (((1,), (1,)), ((), ())), preferred_element_type=F32
    )


def multiply(left_side, right_side):
    return jnp.dot(left_side, right_side, preferred_element_type=F32)


class Wire:
    def __init__(self, me, send_sem, recv_sem):
        self.me, self.send_sem, self.recv_sem, self.used = me, send_sem, recv_sem, 0

    def send(self, off, src, dst):
        copy = pltpu.make_async_remote_copy(
            src_ref=src,
            dst_ref=dst,
            send_sem=self.send_sem.at[self.used],
            recv_sem=self.recv_sem.at[self.used],
            device_id=self.me.at(off).device(),
            device_id_type=MESH,
        )
        copy.start()
        self.used += 1
        return copy


def meet(me, offsets):
    barrier = pltpu.get_barrier_semaphore()
    for off in offsets:
        back = tuple(-v for v in off)
        pl.semaphore_signal(barrier, inc=1, device_id=me.at(back).device(), device_id_type=MESH)
    pl.semaphore_wait(barrier, len(offsets))


def finish(copies):
    for copy in copies:
        copy.wait()


ZOFF = [(0, d, 0, 0, 0) for d in range(4)]


def weights_body(pieces, came, send_sem, recv_sem):
    me = whereami()
    wire = Wire(me, send_sem, recv_sem)
    meet(me, [XOFF[1], XOFF[3]])
    first = [wire.send(XOFF[k], pieces, came.at[:, k - 1]) for k in (1, 3)]
    first[0].wait_recv()
    second = [wire.send(XOFF[3], came.at[0, 0], came.at[0, 1])]
    first[1].wait_recv()
    second.append(wire.send(XOFF[1], came.at[1, 2], came.at[1, 1]))
    for copy in first:
        copy.wait_send()
    finish(second)


def weights_over_x(pieces):
    return pl.pallas_call(
        weights_body,
        name="weights",
        out_shape=SDS((2, 3, 3, 64, 1024), BF),
        in_specs=[pl.BlockSpec(memory_space=pl.ANY)],
        out_specs=pl.BlockSpec(memory_space=pl.ANY),
        scratch_shapes=[pltpu.SemaphoreType.DMA((4,)), pltpu.SemaphoreType.DMA((4,))],
        compiler_params=pltpu.CompilerParams(collective_id=13, has_side_effects=True),
    )(pieces)


def split_rows(count, size):
    return [slice(i * size, i * size + size) for i in range(count)]


def front_body(
    gain_row,
    attn_gain,
    cos_ref,
    sin_ref,
    hidden,
    w_q,
    w_kv,
    out_grad,
    w_o,
    q,
    kv,
    w_attn,
    normed,
    in_mine,
    scale_mine,
    gains,
    grad_full,
    w_cat,
    full,
    lin,
    scales,
    send_sem,
    recv_sem,
    local_sem,
):
    me = whereami()
    wire = Wire(me, send_sem, recv_sem)
    chunk = rows(me.chunk * CHUNK, CHUNK)
    near = []

    def take(src, dst):
        near.append(pltpu.make_async_copy(src, dst, local_sem.at[len(near)]))
        near[-1].start()

    take(w_q, w_attn.at[:, 0:128])
    take(w_kv, w_attn.at[:, 512:640])
    take(w_o, w_cat.at[:, 0:128])
    take(hidden.at[chunk, :], full.at[:, lanes(me.block)])
    take(out_grad.at[chunk, :], grad_full.at[:, lanes(me.wide)])
    gains[me.block] = gain_row[...]
    meet(me, PLANE[1:] + [SIBLING])

    def chunk_of(off):
        return rows(me.at(off).chunk * CHUNK, CHUNK)

    def spread(src, dst, column):
        return [wire.send(XOFF[k], src.at[chunk_of(XOFF[k]), :], dst.at[:, column(k)]) for k in (1, 2, 3)]

    enter = spread(hidden, full, lambda k: lanes(me.block))
    half = rows(me.core * 1024, 1024)
    blocks = [w_attn.at[half, k * 128 : k * 128 + 128] for k in (1, 2, 3)]
    over_x = [wire.send(XOFF[k], w_q.at[half, :], blocks[k - 1]) for k in (1, 2, 3)]
    blocks.append(w_attn.at[half, 640:768])
    over_x.append(wire.send(XOFF[1], w_kv.at[half, :], blocks[3]))
    others = [wire.send(off, gain_row, gains.at[me.block]) for off in PLANE[1:]]
    grads = spread(out_grad, grad_full, lambda k: lanes(XOFF[k][2] * 8 + me.wide))
    out_blocks = [w_cat.at[half, k * 128 : k * 128 + 128] for k in (1, 2, 3)]
    out_x = [wire.send(XOFF[k], w_o.at[half, :], out_blocks[k - 1]) for k in (1, 2, 3)]

    def pass_on(ref):
        out = []
        for h in range(2):
            cols = lanes(h * 4 + me.y, 256)
            out += [wire.send(off, ref.at[:, cols], ref.at[:, cols]) for off in YOFF[1:]]
        return out

    for copy in near:
        copy.wait()
    for copy in enter:
        copy.wait_recv()
    over_y = pass_on(full)
    over_core = []
    for copy, block in zip(over_x, blocks):
        copy.wait_recv()
        over_core.append(wire.send(SIBLING, block, block))
    for copy in grads:
        copy.wait_recv()
    others += pass_on(grad_full)
    for copy in over_y:
        copy.wait_recv()
    for part_rows in split_rows(4, SUB):
        value = full[part_rows, :].astype(F32)
        scale = lax.rsqrt(jnp.mean(value * value, axis=1, keepdims=True) + EPS)
        scales[part_rows, :] = scale
        normed[part_rows, :] = (value * scale * attn_gain[...]).astype(BF)
    for copy in over_core:
        copy.wait_recv()
    lane = lax.broadcasted_iota(jnp.int32, (CHUNK, 128), 1)
    for k in range(6):
        cols = slice(k * 128, k * 128 + 128)
        block = multiply(normed[...], w_attn[:, cols])
        swapped = jnp.where(
            (lane % 64) < 32, -pltpu.roll(block, 96, 1), pltpu.roll(block, 32, 1)
        )
        turned = block * cos_ref[...] + swapped * sin_ref[...]
        if k >= 4:
            turned = jnp.where(lane < 64, turned, block)
        lin[:, cols] = turned.astype(BF)
    moves = []
    for k in (1, 2, 3):
        kv_col = 512 + 128 * XOFF[k][2]
        moves.append(wire.send(XOFF[k], lin.at[:, k * 128 : k * 128 + 128], q.at[chunk, :]))
        moves.append(wire.send(XOFF[k], lin.at[:, kv_col : kv_col + 128], kv.at[chunk, :]))
    q[chunk, :] = lin[:, 0:128]
    kv[chunk, :] = lin[:, 512:640]
    for copy, block in zip(out_x, out_blocks):
        copy.wait_recv()
        over_core.append(wire.send(SIBLING, block, block))
        others.append(over_core[-1])
    here = rows(me.y * SUB, SUB)
    in_mine[...] = full[here, :]
    scale_mine[...] = scales[here, :]
    for copy in over_x + enter + grads + over_y + out_x + over_core[:4]:
        copy.wait_send()
    finish(others + moves)


def front(gain_row, attn_gain, cos_here, sin_here, hidden, w_q, w_kv, out_grad, w_o):
    vm = pl.BlockSpec(memory_space=pltpu.VMEM)
    hbm = pl.BlockSpec(memory_space=pl.ANY)
    outs = [
        SDS((ROWS, 128), BF),
        SDS((ROWS, 128), BF),
        SDS((D, 768), BF),
        SDS((CHUNK, D), BF),
        SDS((SUB, D), BF),
        SDS((SUB, 1), F32),
        SDS((16, 8, 128), F32),
        SDS((CHUNK, D), BF),
        SDS((D, 512), BF),
    ]
    return pl.pallas_call(
        front_body,
        name="front",
        out_shape=outs,
        in_specs=[vm] * 4 + [hbm] * 5,
        out_specs=[vm] * len(outs),
        scratch_shapes=[
            pltpu.VMEM((CHUNK, D), BF),
            pltpu.VMEM((CHUNK, 768), BF),
            pltpu.VMEM((CHUNK, 1), F32),
            pltpu.SemaphoreType.DMA((64,)),
            pltpu.SemaphoreType.DMA((64,)),
            pltpu.SemaphoreType.DMA((5,)),
        ],
        compiler_params=pltpu.CompilerParams(
            collective_id=0, has_side_effects=True, vmem_limit_bytes=40 * 2**20
        ),
        cost_estimate=pl.CostEstimate(flops=2 * 10**9, bytes_accessed=2**23, transcendentals=0),
    )(gain_row, attn_gain, cos_here, sin_here, hidden, w_q, w_kv, out_grad, w_o)


def middle_body(
    heads,
    in_mine,
    gain,
    w_cat,
    heads_cat,
    resid,
    scale_out,
    ffn_mine,
    term_send,
    term_recv,
    send_sem,
    recv_sem,
):
    me = whereami()
    wire = Wire(me, send_sem, recv_sem)
    meet(me, XOFF[1:] + YOFF[1:])
    moves = [
        wire.send(
            XOFF[k],
            heads.at[rows(me.at(XOFF[k]).chunk * CHUNK, CHUNK), :],
            heads_cat.at[:, k * 128 : k * 128 + 128],
        )
        for k in (1, 2, 3)
    ]
    heads_cat[:, 0:128] = heads[rows(me.chunk * CHUNK, CHUNK), :]
    finish(moves)
    sums = []
    for h in range(2):
        for p in range(2):
            cols = slice(h * 1024 + p * 512, h * 1024 + p * 512 + 512)
            term_send[:, cols] = contract_cols(heads_cat[...], w_cat[cols, :]).astype(BF)
        cols = slice(h * 1024, h * 1024 + 1024)
        for d in (1, 2, 3):
            there = rows(me.at(YOFF[d]).y * SUB, SUB)
            sums.append(
                wire.send(YOFF[d], term_send.at[there, cols], term_recv.at[d - 1, :, cols])
            )
    finish(sums)
    value = in_mine[...].astype(F32) + term_send[rows(me.y * SUB, SUB), :].astype(F32)
    for d in range(3):
        value = value + term_recv[d].astype(F32)
    resid[...] = value
    scale = lax.rsqrt(jnp.mean(value * value, axis=1, keepdims=True) + EPS)
    scale_out[...] = scale
    ffn_mine[...] = (value * scale * gain[...]).astype(BF)


def middle(heads, in_mine, gain, w_cat):
    vm = pl.BlockSpec(memory_space=pltpu.VMEM)
    outs = [SDS((CHUNK, 512), BF), SDS((SUB, D), F32), SDS((SUB, 1), F32), SDS((SUB, D), BF)]
    return pl.pallas_call(
        middle_body,
        name="middle",
        out_shape=outs,
        in_specs=[vm] * 4,
        out_specs=[vm] * len(outs),
        scratch_shapes=[
            pltpu.VMEM((CHUNK, D), BF),
            pltpu.VMEM((3, SUB, D), BF),
            pltpu.SemaphoreType.DMA((9,)),
            pltpu.SemaphoreType.DMA((9,)),
        ],
        compiler_params=pltpu.CompilerParams(
            collective_id=1, has_side_effects=True, vmem_limit_bytes=32 * 2**20
        ),
        cost_estimate=pl.CostEstimate(flops=10**9, bytes_accessed=2**23, transcendentals=0),
    )(heads, in_mine, gain, w_cat)


class PairSum:
    def __init__(self, me, left, right, terms, came, send_sem, recv_sem):
        self.me, self.left, self.right, self.terms, self.came = me, left, right, terms, came
        self.send_sem, self.recv_sem = send_sem, recv_sem

    def copy(self, i):
        return pltpu.make_async_remote_copy(
            src_ref=self.terms.at[i, :, :, 1 - self.me.core],
            dst_ref=self.came.at[i],
            send_sem=self.send_sem.at[i],
            recv_sem=self.recv_sem.at[i],
            device_id=self.me.at(SIBLING).device(),
            device_id_type=MESH,
        )

    def multiply(self, first, last):
        def step(i, _):
            cols = pl.ds(pl.multiple_of(i * 256, 256), 256)
            block = contract_rows(self.left[:, cols], self.right[...])
            self.terms[i] = block.astype(BF).reshape(2, 4, 2, 16, 2048)
            self.copy(i).start()
            return 0

        lax.fori_loop(first, last, step, 0)

    def add(self, first, last):
        def step(i, _):
            copy = self.copy(i)
            copy.wait_recv()
            mine = self.terms[i, :, :, self.me.core].astype(F32) + self.came[i].astype(F32)
            self.terms[i, :, :, self.me.core] = mine.astype(BF)
            return 0

        lax.fori_loop(first, last, step, 0)

    def sent(self):
        def step(i, _):
            self.copy(i).wait_send()
            return 0

        lax.fori_loop(0, 8, step, 0)


def ffn_body(
    mine_ref,
    grad_ref,
    resid_ref,
    scale_ref,
    gain_ref,
    w_out_ref,
    own_gate,
    own_up,
    own_down,
    piece0,
    piece1,
    piece2_first,
    piece2_second,
    piece3,
    out_mine,
    resid_back,
    gain_part,
    mix_full,
    heads_back,
    ffn_in,
    up_back,
    down_own,
    down_came,
    gate_own,
    gate_came,
    other_core,
    turned,
    act,
    gate_back,
    gate_tile,
    up_tile,
    down_tile,
    down_acc,
    ffn_acc,
    down_send,
    ffn_send,
    down_recv,
    ffn_recv,
    mix_mine,
    back_cat,
    down_terms,
    gate_terms,
    came,
    send_sem,
    recv_sem,
    core_send,
    core_recv,
    tile_sem,
    local_sem,
    ack,
):
    me = whereami()
    wire = Wire(me, send_sem, recv_sem)
    half = [lanes(me.xl, 1024), lanes(1 - me.xl, 1024)]
    here = rows(me.y * SUB, SUB)

    pieces = (piece0, piece1, None, piece3)
    opposite = (piece2_first, piece2_second)

    def tile_copies(e, q, slot):
        copies, groups = [], []
        cols = pl.ds(pl.multiple_of(q * 256, 256), 256)

        def copy(src, dst):
            sem = tile_sem.at[slot, len(copies) + len(groups)]
            return pltpu.make_async_copy(src, dst, sem)

        for dxl in range(2):
            k = e * 2 + dxl
            for j, (own, tile) in enumerate(((own_gate, gate_tile), (own_up, up_tile))):
                if k == 0:
                    copies.append(copy(own.at[:, :, :, :, cols], tile.at[slot, dxl]))
                    continue
                for d, piece in enumerate(pieces):
                    spot = tile.at[slot, dxl, (me.z - d + 4) % 4, me.core]
                    if piece is not None:
                        copies.append(copy(piece.at[:, k - 1, j, :, cols], spot))
                        continue
                    for h in range(2):
                        copies.append(copy(opposite[h].at[k - 1, j, :, cols], spot.at[h]))
                spot = tile.at[slot, dxl, :, 1 - me.core]
                copies.append(copy(other_core.at[:, :, k - 1, j, :, cols], spot))
            here = slice(dxl * 1024, dxl * 1024 + 1024)
            if k == 0:
                copies.append(copy(own_down.at[q], down_tile.at[slot, :, :, :, here]))
                continue
            spot = down_tile.at[slot, 1 - me.core, :, :, here]
            copies.append(copy(other_core.at[q, :, k - 1, 2], spot))
            for h in range(2):
                spot = down_tile.at[slot, me.core, h, :, here]
                groups.append(
                    [
                        copy(opposite[h].at[k - 1, 2] if p is None else p.at[h, k - 1, 2], spot)
                        for p in pieces
                    ]
                )
        return copies, groups

    def fetch(e, q, slot):
        copies, groups = tile_copies(e, q, slot)
        for copy in copies:
            copy.start()
        for group in groups:
            for d, copy in enumerate(group):
                pl.when((me.z - q + 4) % 4 == d)(copy.start)

    def arrive(e, q, slot):
        copies, groups = tile_copies(e, q, slot)
        for copy in copies + [group[0] for group in groups]:
            copy.wait()

    meet(me, YOFF[1:] + XOFF[1:] + ZOFF[1:] + [SIBLING])
    for h in range(2):
        turned[:, h * 1024 : h * 1024 + 1024] = mine_ref[:, half[h]]
    gathers = [wire.send(off, turned, ffn_in.at[here, :]) for off in YOFF[1:]]
    shares = []
    for k in range(3):
        shares.append([])
        for d, piece in enumerate(pieces):
            spot = other_core.at[(me.z - d + 4) % 4, :, k]
            if piece is not None:
                shares[k].append(wire.send(SIBLING, piece.at[:, k], spot))
                continue
            for h in range(2):
                shares[k].append(wire.send(SIBLING, opposite[h].at[k], spot.at[h]))
    ffn_in[here, :] = turned[...]
    down_acc[...] = jnp.zeros(down_acc.shape, F32)
    ffn_acc[...] = jnp.zeros(ffn_acc.shape, F32)
    finish(shares[0])
    fetch(0, 0, 0)
    finish(gathers)

    down_sum = PairSum(me, act, grad_ref, down_terms, came, core_send.at[0], core_recv.at[0])
    gate_sum = PairSum(me, ffn_in, gate_back, gate_terms, came, core_send.at[1], core_recv.at[1])

    for e in range(2):

        if e == 0:
            finish(shares[1] + shares[2])

        def step(q, _, e=e):
            slot = q % 2

            @pl.when(q < 3)
            def _():
                fetch(e, q + 1, 1 - slot)

            if e == 0:

                @pl.when(q == 3)
                def _():
                    fetch(1, 0, 0)

            arrive(e, q, slot)
            cols = pl.ds(pl.multiple_of(e * 1024 + q * 256, 256), 256)
            w_g = gate_tile[slot].reshape(2048, 256)
            w_u = up_tile[slot].reshape(2048, 256)
            w_d = down_tile[slot].reshape(256, 2048)
            gate = multiply(ffn_in[...], w_g)
            up = multiply(ffn_in[...], w_u)
            act_back = contract_cols(grad_ref[...], w_d)
            sigmoid = jax.nn.sigmoid(gate)
            silu = gate * sigmoid
            act_here = (silu * up).astype(BF)
            act[:, cols] = act_here
            down_acc[...] += multiply(act_here, w_d)
            g_back = (act_back * up * sigmoid * (1.0 + gate * (1.0 - sigmoid))).astype(BF)
            u_back = (act_back * silu).astype(BF)
            gate_back[:, cols] = g_back
            up_back[:, cols] = u_back
            ffn_acc[...] += contract_cols(g_back, w_g) + contract_cols(u_back, w_u)
            return 0

        lax.fori_loop(0, 4, step, 0)
        if e == 0:
            down_sum.multiply(0, 4)

    ffn_send[...] = ffn_acc[...].astype(BF)
    ffn_moves = [
        wire.send(YOFF[d], ffn_send.at[rows(me.at(YOFF[d]).y * SUB, SUB), :], ffn_recv.at[d - 1])
        for d in (1, 2, 3)
    ]
    down_sum.multiply(4, 8)

    def down_block(k):
        e, dxl = XOFF[k][4], XOFF[k][2]
        here = slice(dxl * 1024, dxl * 1024 + 1024)
        return down_terms.at[e * 4 : e * 4 + 4, :, :, me.core, :, here]

    down_sum.add(0, 4)
    x_moves = [wire.send(XOFF[1], down_block(1), down_came.at[0])]
    down_sum.add(4, 8)
    x_moves += [wire.send(XOFF[k], down_block(k), down_came.at[k - 1]) for k in (2, 3)]
    near = [pltpu.make_async_copy(down_block(0), down_own, local_sem.at[0])]
    near[0].start()

    pl.semaphore_signal(ack, inc=1, device_id=me.at(SIBLING).device(), device_id_type=MESH)
    pl.semaphore_wait(ack, 1)
    gate_sum.multiply(0, 8)
    gate_sum.add(0, 8)

    def gate_block(z):
        return gate_terms.at[:, :, z, me.core]

    z_moves = [
        wire.send(ZOFF[d], gate_block((me.z + d) % 4), gate_came.at[d - 1]) for d in (1, 2, 3)
    ]
    near.append(pltpu.make_async_copy(gate_block(me.z), gate_own, local_sem.at[1]))
    near[1].start()

    finish(ffn_moves)

    def summed(send, recv, h):
        cols = slice(h * 1024, h * 1024 + 1024)
        out = send[here, cols].astype(F32)
        for d in range(3):
            out = out + recv[d, :, cols].astype(F32)
        return out

    scale = scale_ref[...]
    inner = jnp.zeros((SUB, 1), F32)
    for h in range(2):
        back = summed(ffn_send, ffn_recv, h)
        weighed = back * resid_ref[:, half[h]]
        inner = inner + jnp.sum(weighed * gain_ref[:, half[h]], axis=1, keepdims=True)
        gain_part[:, half[h]] = jnp.sum(weighed * scale, axis=0, keepdims=True)
    pull = scale * scale * scale * inner / D
    for h in range(2):
        back = summed(ffn_send, ffn_recv, h)
        grad = grad_ref[here, h * 1024 : h * 1024 + 1024].astype(F32)
        total_back = grad + scale * gain_ref[:, half[h]] * back - resid_ref[:, half[h]] * pull
        resid_back[:, half[h]] = total_back
        mix_mine[:, half[h]] = total_back.astype(BF)
    mix_full[here, :] = mix_mine[...]
    mix_moves = [wire.send(off, mix_mine, mix_full.at[here, :]) for off in YOFF[1:]]

    down_send[...] = down_acc[...].astype(BF)
    down_moves = [
        wire.send(YOFF[d], down_send.at[rows(me.at(YOFF[d]).y * SUB, SUB), :], down_recv.at[d - 1])
        for d in (1, 2, 3)
    ]
    finish(mix_moves)
    back_cat[...] = multiply(mix_full[...], w_out_ref[...]).astype(BF)
    spot = rows(me.chunk * CHUNK, CHUNK)
    head_moves = [
        wire.send(XOFF[k], back_cat.at[:, k * 128 : k * 128 + 128], heads_back.at[spot, :])
        for k in (1, 2, 3)
    ]
    heads_back[spot, :] = back_cat[:, 0:128]
    finish(down_moves)
    for h in range(2):
        out_mine[:, half[h]] = (resid_ref[:, half[h]] + summed(down_send, down_recv, h)).astype(BF)
    finish(head_moves + x_moves + z_moves)
    for copy in near:
        copy.wait()
    down_sum.sent()
    gate_sum.sent()


def ffn(ffn_mine, grad_full, resid, scale_two, gain, w_out, w_gate, w_up, w_down, pieces):
    vm = pl.BlockSpec(memory_space=pltpu.VMEM)
    hbm = pl.BlockSpec(memory_space=pl.ANY)
    return pl.pallas_call(
        ffn_body,
        name="ffn",
        out_shape=[
            SDS((SUB, D), BF),
            SDS((SUB, D), F32),
            SDS((1, D), F32),
            SDS((CHUNK, D), BF),
            SDS((ROWS, 128), BF),
            SDS((CHUNK, D), BF),
            SDS((CHUNK, D), BF),
            SDS((4, 2, 4, 16, 1024), BF),
            SDS((3, 4, 2, 4, 16, 1024), BF),
            SDS((8, 2, 16, 2048), BF),
            SDS((3, 8, 2, 16, 2048), BF),
            SDS((4, 2, 3, 3, 64, 1024), BF),
        ],
        in_specs=[vm] * 6 + [hbm] * 8,
        out_specs=[vm] * 7 + [hbm] * 5,
        scratch_shapes=[
            pltpu.VMEM((SUB, D), BF),
            pltpu.VMEM((CHUNK, D), BF),
            pltpu.VMEM((CHUNK, D), BF),
            pltpu.VMEM((2, 2, 4, 2, 2, 64, 256), BF),
            pltpu.VMEM((2, 2, 4, 2, 2, 64, 256), BF),
            pltpu.VMEM((2, 2, 2, 64, 2048), BF),
            pltpu.VMEM((CHUNK, D), F32),
            pltpu.VMEM((CHUNK, D), F32),
            pltpu.VMEM((CHUNK, D), BF),
            pltpu.VMEM((CHUNK, D), BF),
            pltpu.VMEM((3, SUB, D), BF),
            pltpu.VMEM((3, SUB, D), BF),
            pltpu.VMEM((SUB, D), BF),
            pltpu.VMEM((CHUNK, 512), BF),
            pltpu.VMEM((8, 2, 4, 2, 16, 2048), BF),
            pltpu.VMEM((8, 2, 4, 2, 16, 2048), BF),
            pltpu.VMEM((8, 2, 4, 16, 2048), BF),
            pltpu.SemaphoreType.DMA((36,)),
            pltpu.SemaphoreType.DMA((36,)),
            pltpu.SemaphoreType.DMA((2, 8)),
            pltpu.SemaphoreType.DMA((2, 8)),
            pltpu.SemaphoreType.DMA((2, 32)),
            pltpu.SemaphoreType.DMA((2,)),
            pltpu.SemaphoreType.REGULAR,
        ],
        compiler_params=pltpu.CompilerParams(
            collective_id=14, has_side_effects=True, vmem_limit_bytes=60 * 2**20
        ),
        cost_estimate=pl.CostEstimate(flops=26 * 10**9, bytes_accessed=40 * 2**20, transcendentals=0),
    )(
        ffn_mine,
        grad_full,
        resid,
        scale_two,
        gain,
        w_out,
        w_gate.reshape(4, 2, 2, 64, 1024),
        w_up.reshape(4, 2, 2, 64, 1024),
        w_down.reshape(4, 2, 2, 64, 1024),
        *pieces,
    )


def per_device(
    layer_input,
    doc_lengths,
    attn_gain,
    w_query,
    w_key,
    w_value,
    w_output,
    ffn_gain,
    w_gate,
    w_up,
    w_down,
    output_grad,
):
    me = whereami()
    cos_np, sin_np = rope_table()
    cos_all, sin_all = jnp.asarray(cos_np), jnp.asarray(sin_np)
    long_first = doc_lengths[0, 0] > SHORT
    table_start = jnp.where(long_first, SHORT, 0) + me.chunk * CHUNK
    cos_here = part(cos_all, table_start, CHUNK, 0)
    sin_here = part(sin_all, table_start, CHUNK, 0)

    w_kv = jnp.concatenate(
        [part(w_key, me.y * 64, 64, 1), part(w_value, me.y * 64, 64, 1)], axis=1
    )
    pieces = jnp.stack([part(w, me.tok * 128, 128, 0) for w in (w_gate, w_up, w_down)])
    piece0 = weights_over_x(jnp.moveaxis(pieces.reshape(3, 2, 64, 1024), 1, 0))
    piece1, piece3 = z_permute(piece0, 1), z_permute(piece0, 3)
    queries, kv, w_attn, normed, in_mine, scale_mine, gains, grad_full, w_out = front(
        jnp.broadcast_to(ffn_gain[None, :], (8, 128)),
        attn_gain[None, :],
        cos_here,
        sin_here,
        layer_input,
        w_query,
        w_kv,
        output_grad,
        w_output,
    )
    ffn_gain_all = gains[:, 0, :].reshape(1, D)
    queries, second, first = lax.optimization_barrier((queries, piece1[0], piece3[1]))
    pieces = [piece0, piece1, z_permute(second, 1), z_permute(first, 3), piece3]
    (heads_out,) = vmem_call(
        "attend", attend_body, [doc_lengths, queries, kv], [SDS((ROWS, 128), BF)], flops=2 * 10**10
    )
    heads_cat, resid, scale_two, ffn_mine = middle(heads_out, in_mine, ffn_gain_all, w_out)
    (
        out_mine,
        resid_back,
        ffn_gain_part,
        mix_full,
        heads_back,
        ffn_input,
        up_back,
        down_own,
        down_came,
        gate_own,
        gate_came,
        _,
    ) = ffn(
        ffn_mine, grad_full, resid, scale_two, ffn_gain_all, w_out, w_gate, w_up, w_down, pieces
    )

    query_back, kv_back = vmem_call(
        "attend_back",
        attend_back_body,
        [doc_lengths, queries, kv, heads_back, cos_all[512:1536], sin_all[512:1536]],
        [SDS((ROWS, 128), BF), SDS((ROWS, 128), BF)],
        scratch=[pltpu.VMEM((1024, 128), F32)],
        flops=5 * 10**9,
    )
    (
        layer_output,
        input_grad,
        query_grad,
        kv_grad,
        output_proj_grad,
        gate_grad,
        up_grad,
        down_grad,
        gain_grads,
    ) = back(
        [
            query_back,
            kv_back,
            w_attn,
            heads_cat,
            out_mine,
            in_mine,
            resid_back,
            scale_mine,
            attn_gain[None, :],
            ffn_gain_part,
        ],
        [normed, mix_full, ffn_input, up_back, down_own, down_came, gate_own, gate_came],
    )
    kv_cols = jnp.moveaxis(kv_grad, 0, 1).reshape(32, 4, 2, 64)
    key_grad = kv_cols[:, :, 0, :].reshape(32, 256)
    value_grad = kv_cols[:, :, 1, :].reshape(32, 256)
    gain_grads = part(gain_grads, me.tok * 16, 16, 1)
    return (
        layer_output,
        input_grad,
        gain_grads[0:1],
        query_grad,
        key_grad,
        value_grad,
        output_proj_grad,
        gain_grads[1:2],
        gate_grad,
        up_grad,
        down_grad,
    )


def solution(mesh):
    in_specs = (
        P("tok", ("narrow", "wide")),
        P("tok", None),
        P(),
        P(None, ("narrow", "wide")),
        P(None, "narrow"),
        P(None, "narrow"),
        P(None, ("narrow", "wide")),
        P(("narrow", "wide")),
        P("narrow", "wide"),
        P("narrow", "wide"),
        P("wide", "narrow"),
        P("tok", ("narrow", "wide")),
    )
    out_specs = (
        P("tok", ("narrow", "wide")),
        P("tok", ("narrow", "wide")),
        P(("narrow", "wide"), "tok"),
        P("tok", ("narrow", "wide")),
        P(("tok", "wide"), "narrow"),
        P(("tok", "wide"), "narrow"),
        P("tok", ("narrow", "wide")),
        P(("narrow", "wide"), "tok"),
        P("narrow", "tok", "wide"),
        P("narrow", "tok", "wide"),
        P("wide", "tok", "narrow"),
    )
    return jax.shard_map(
        per_device, mesh=mesh, in_specs=in_specs, out_specs=out_specs, check_vma=False
    )
```

```python
import functools
import math

import jax
import jax.numpy as jnp
import numpy as np
from jax import lax
from jax.experimental import pallas as pl
from jax.experimental.pallas import tpu as pltpu
from jax.sharding import PartitionSpec as P

HEADS = 32
KV_HEADS = 8
HEAD_DIM = 64
GROUP = 128
EPS = 1e-05
THETA = 500000.0
FACTOR = 32.0
LOW_FACTOR = 1.0
HIGH_FACTOR = 4.0
INITIAL = 8192.0
NEG = -1e30

D = 2048
ROWS = 1536
CHUNK = 384
SUB = 96
SHORT = 512
BF = jnp.bfloat16
F32 = jnp.float32
MESH = pl.DeviceIdType.MESH
SDS = jax.ShapeDtypeStruct

HERE = (0, 0, 0, 0, 0)
XOFF = [(0, 0, 0, 0, 0), (0, 0, 1, 0, 0), (0, 0, 0, 0, 1), (0, 0, 1, 0, 1)]
YOFF = [(0, 0, 0, d, 0) for d in range(4)]
PLANE = [(0, 0, a, b, e) for b in range(4) for a in range(2) for e in range(2)]
SIBLING = (1, 0, 0, 0, 0)
TOKS = [(a, b, 0, 0, 0) for b in range(4) for a in range(2)]


class Place:
    def __init__(self, core, z, xl, y, xh):
        self.core, self.z, self.xl, self.y, self.xh = core, z, xl, y, xh
        self.tok = z * 2 + core
        self.wide = y * 2 + xh
        self.block = xl * 8 + self.wide
        self.chunk = xl * 2 + xh

    def at(self, off):
        return Place(
            (self.core + off[0]) % 2,
            (self.z + off[1]) % 4,
            (self.xl + off[2]) % 2,
            (self.y + off[3]) % 4,
            (self.xh + off[4]) % 2,
        )

    def device(self):
        return (self.tok, self.xl, self.wide)


def whereami():
    tok = lax.axis_index("tok")
    wide = lax.axis_index("wide")
    return Place(tok % 2, tok // 2, lax.axis_index("narrow"), wide // 2, wide % 2)


def rows(start, size):
    return pl.ds(pl.multiple_of(start, size), size)


def lanes(index, size=128):
    return pl.ds(pl.multiple_of(index * size, size), size)


def block_probs(q_ref, kv_ref, start, i, stack):
    n = 256 * (i + 1)
    keys = kv_ref[rows_256(start, n), 0:64]
    scores = lax.dot_general(
        keys, stack, (((1,), (1,)), ((), ())), preferred_element_type=F32
    ) * (HEAD_DIM**-0.5)
    last = scores[n - 256 :, :]
    key_id = lax.broadcasted_iota(jnp.int32, (256, 512), 0)
    query_id = lax.broadcasted_iota(jnp.int32, (256, 512), 1) % 256
    last = jnp.where(key_id <= query_id, last, NEG)
    if n > 256:
        scores = jnp.concatenate([scores[: n - 256, :], last], axis=0)
    else:
        scores = last
    raised = jnp.exp(scores - jnp.max(scores, axis=0, keepdims=True))
    return keys, raised, jnp.sum(raised, axis=0, keepdims=True)


def rows_256(start, size):
    return pl.ds(pl.multiple_of(start, 256), size)


def starts_of(len_ref):
    long_first = len_ref[0, 0] > SHORT
    long_start = jnp.where(long_first, 0, SHORT)
    short_start = jnp.where(long_first, 2 * SHORT, 0)
    return ((long_start, 4), (short_start, 2))


def both(block):
    return jnp.concatenate([block[:, 0:64], block[:, 64:128]], axis=0)


def attend_body(len_ref, q_ref, kv_ref, out_ref):
    for start, blocks in starts_of(len_ref):
        for i in range(blocks):
            mine = rows_256(start + 256 * i, 256)
            stack = both(q_ref[mine, :])
            keys, raised, mass = block_probs(q_ref, kv_ref, start, i, stack)
            soft = (raised * (1.0 / mass)).astype(BF)
            values = kv_ref[rows_256(start, 256 * (i + 1)), 64:128]
            mixed = lax.dot_general(
                soft, values, (((0,), (0,)), ((), ())), preferred_element_type=F32
            )
            out_ref[mine, :] = jnp.concatenate([mixed[:256], mixed[256:]], axis=1).astype(BF)


def unrope(tensor, cosine, sine):
    lane = lax.broadcasted_iota(jnp.int32, tensor.shape, 1)
    first = (lane % 64) < 32
    swapped = jnp.where(first, pltpu.roll(tensor, 96, 1), -pltpu.roll(tensor, 32, 1))
    return tensor * cosine + swapped * sine


def vmem_call(name, body, ins, outs, scratch=(), flops=0):
    return pl.pallas_call(
        body,
        name=name,
        out_shape=outs,
        in_specs=[pl.BlockSpec(memory_space=pltpu.SMEM)]
        + [pl.BlockSpec(memory_space=pltpu.VMEM)] * (len(ins) - 1),
        out_specs=[pl.BlockSpec(memory_space=pltpu.VMEM)] * len(outs),
        scratch_shapes=list(scratch),
        compiler_params=pltpu.CompilerParams(vmem_limit_bytes=48 * 2**20),
        cost_estimate=pl.CostEstimate(flops=flops, bytes_accessed=2**20, transcendentals=0),
    )(*ins)


def masked_scores(keys, query, i, length):
    n = keys.shape[0]
    scores = contract_cols(keys, query) * (HEAD_DIM**-0.5)
    key_id = lax.broadcasted_iota(jnp.int32, (256, 256), 0)
    query_id = lax.broadcasted_iota(jnp.int32, (256, 256), 1)
    parts = [jnp.where(key_id <= query_id, scores[n - 256 :, :], NEG)]
    middle = 0
    if i >= 2:
        cut = SHORT if i < 4 else 2 * SHORT
        middle = SHORT
        parts.insert(0, jnp.where(length == cut, NEG, scores[:SHORT, :]))
    if n - 256 > middle:
        parts.insert(len(parts) - 1, scores[middle : n - 256, :])
    return jnp.concatenate(parts, axis=0) if len(parts) > 1 else parts[0]


def back_body(
    len_ref,
    q_ref,
    kv_ref,
    heads_back,
    cos_ref,
    sin_ref,
    w_attn,
    heads_cat,
    out_mine,
    in_mine,
    resid_back,
    scale_ref,
    gain_ref,
    ffn_gain_part,
    normed,
    mix_full,
    down_own,
    down_came,
    gate_own,
    gate_came,
    up_own,
    up_late,
    up_pass,
    layer_output,
    input_grad,
    query_grad,
    kv_grad,
    out_grad,
    gate_grad,
    up_grad,
    down_grad,
    gain_grad,
    dq_ref,
    dkv_ref,
    dkv_acc,
    down_in,
    gate_in,
    up_in,
    late_in,
    pass_in,
    up_last,
    down_sum,
    gate_sum,
    up_sum,
    down_z,
    gate_x,
    up_x,
    cat_back,
    norm_send,
    norm_recv,
    in_grad,
    gain_parts,
    gain_plane,
    gain_mine,
    gain_toks,
    o_terms,
    o_core,
    o_x,
    o_sum,
    o_z,
    q_terms,
    q_core,
    q_x,
    q_sum,
    q_z,
    k_terms,
    k_core,
    k_x,
    k_sum,
    k_z,
    k_last,
    send_sem,
    recv_sem,
    local_sem,
):
    me = whereami()
    wire = Wire(me, send_sem, recv_sem)
    loads = []
    for src, dst in (
        (up_late, late_in),
        (up_pass, pass_in),
        (gate_own, gate_in.at[0]),
        (gate_came, gate_in.at[1:3]),
        (down_own, down_in.at[0]),
        (down_came, down_in.at[1:3]),
        (up_own, up_in),
    ):
        loads.append(pltpu.make_async_copy(src, dst, local_sem.at[len(loads)]))
        loads[-1].start()
    meet(me, PLANE[1:] + TOKS[1:])
    sent = []

    for copy in loads[0:2]:
        copy.wait()
    up_moves = [
        wire.send(ZOFF[1], late_in.at[0, 4:8], up_last.at[0, 4:8]),
        wire.send(ZOFF[3], late_in.at[1, 0:4], up_last.at[1, 0:4]),
    ]

    length = len_ref[0:1, 0:1]
    dkv_acc[...] = jnp.zeros(dkv_acc.shape, F32)
    for i in range(6):
        low, high = 0 if i < 4 else SHORT, 256 * (i + 1)
        here = slice(256 * i, high)
        keys, values = kv_ref[low:high, 0:64], kv_ref[low:high, 64:128]
        parts = []
        for head in (slice(0, 64), slice(64, 128)):
            query, value_back = q_ref[here, head], heads_back[here, head]
            scores = masked_scores(keys, query, i, length)
            raised = jnp.exp(scores - jnp.max(scores, axis=0, keepdims=True))
            soft = raised * (1.0 / jnp.sum(raised, axis=0, keepdims=True))
            prob_back = contract_cols(values, value_back)
            inner = jnp.sum(soft * prob_back, axis=0, keepdims=True)
            score_back = (soft * (prob_back - inner)).astype(BF)
            parts.append(contract_rows(score_back, keys) * (HEAD_DIM**-0.5))
            dk = multiply(score_back, query) * (HEAD_DIM**-0.5)
            dv = multiply(soft.astype(BF), value_back)
            dkv_acc[low:high, :] += jnp.concatenate([dk, dv], axis=1)
        dq = jnp.concatenate(parts, axis=1)
        dq_ref[here, :] = unrope(dq, cos_ref[here, :], sin_ref[here, :]).astype(BF)
    acc = dkv_acc[...]
    lane = lax.broadcasted_iota(jnp.int32, acc.shape, 1)
    turned = unrope(acc, cos_ref[...], sin_ref[...])
    dkv_ref[...] = jnp.where(lane < 64, turned, acc).astype(BF)

    spot = rows(me.chunk * CHUNK, CHUNK)
    moves = []
    for k in (1, 2, 3):
        there = rows(me.at(XOFF[k]).chunk * CHUNK, CHUNK)
        for ref, col in ((dq_ref, 0), (dkv_ref, 512)):
            moves.append(
                wire.send(
                    XOFF[k], ref.at[there, :], cat_back.at[:, col + k * 128 : col + k * 128 + 128]
                )
            )
    cat_back[:, 0:128] = dq_ref[spot, :]
    cat_back[:, 512:640] = dkv_ref[spot, :]

    mine = rows(me.chunk * CHUNK + me.y * SUB, SUB)
    leaving = [
        wire.send(off, out_mine.at[:, lanes(me.at(off).block)], layer_output.at[mine, :])
        for off in PLANE[1:]
    ]
    layer_output[mine, :] = out_mine[:, lanes(me.block)]

    add_to(late_in.at[0, 0:4], pass_in.at[0])
    up_moves.append(wire.send(ZOFF[1], late_in.at[0, 0:4], up_last.at[0, 0:4]))
    add_to(late_in.at[1, 4:8], pass_in.at[1])
    up_moves.append(wire.send(ZOFF[3], late_in.at[1, 4:8], up_last.at[1, 4:8]))

    def fold(ref, out):
        for n in range(out.shape[0]):
            value = ref[0, n].astype(F32)
            for k in range(1, ref.shape[0]):
                value = value + ref[k, n].astype(F32)
            out[n] = value.astype(BF)

    def x_blocks(ref, came):
        moves = []
        for k in (1, 2, 3):
            e, dxl = XOFF[k][4], XOFF[k][2]
            src = ref.at[dxl * 4 : dxl * 4 + 4, :, :, e * 1024 : e * 1024 + 1024]
            moves.append(wire.send(XOFF[k], src, came.at[k - 1]))
        return moves

    for copy in loads[2:]:
        copy.wait()
    fold(gate_in, gate_sum)
    gate_moves = x_blocks(gate_sum, gate_x)

    for z in range(4):
        block = contract_rows(mix_full[:, z * 512 : z * 512 + 512], heads_cat[...])
        o_terms[z] = block.astype(BF).reshape(2, 256, 512)
    o_pair = wire.send(SIBLING, o_terms.at[:, 1 - me.core], o_core)

    def add_core(copy, terms, came):
        copy.wait_recv()
        terms[:, me.core] = (terms[:, me.core].astype(F32) + came[...].astype(F32)).astype(BF)

    finish(moves)
    for h in range(4):
        cols = slice(h * 512, h * 512 + 512)
        term = contract_cols(cat_back[:, 0:768], w_attn[cols, :]) + contract_cols(
            cat_back[:, 768:1024], w_attn[cols, 512:768]
        )
        norm_send[:, cols] = term.astype(BF)
    norm_moves = [
        wire.send(YOFF[d], norm_send.at[rows(me.at(YOFF[d]).y * SUB, SUB), :], norm_recv.at[d - 1])
        for d in (1, 2, 3)
    ]

    add_core(o_pair, o_terms, o_core)
    o_moves = [
        wire.send(ZOFF[d], o_terms.at[(me.z + d) % 4, me.core], o_z.at[d - 1]) for d in (1, 2, 3)
    ]

    for z in range(4):
        block = contract_rows(normed[:, z * 512 : z * 512 + 512], cat_back[:, 0:512])
        q_terms[z] = block.astype(BF).reshape(2, 256, 512)
    q_pair = wire.send(SIBLING, q_terms.at[:, 1 - me.core], q_core)
    for z in range(4):
        left = normed[:, z * 512 : z * 512 + 512]
        block = contract_rows(left, cat_back[:, 512:768]) + contract_rows(
            left, cat_back[:, 768:1024]
        )
        k_terms[z] = block.astype(BF).reshape(2, 4, 2, 32, 256)
    k_pair = wire.send(SIBLING, k_terms.at[:, 1 - me.core], k_core)

    def kv_block(k):
        e, dxl = XOFF[k][4], XOFF[k][2]
        return k_terms.at[:, me.core, :, (me.xh + e) % 2, :, dxl * 128 : dxl * 128 + 128]

    add_core(k_pair, k_terms, k_core)
    k_moves = [wire.send(XOFF[k], kv_block(k), k_x.at[k - 1]) for k in (1, 2, 3)]
    add_core(q_pair, q_terms, q_core)
    q_moves = [
        wire.send(ZOFF[d], q_terms.at[(me.z + d) % 4, me.core], q_z.at[d - 1]) for d in (1, 2, 3)
    ]

    fold(down_in, down_sum)
    down_moves = [
        wire.send(ZOFF[d], down_sum.at[:, :, (me.z + d) % 4], down_z.at[d - 1]) for d in (1, 2, 3)
    ]

    def gathered(moves, own, came):
        for copy in moves:
            copy.wait_recv()
        sent.extend(moves)
        value = own.astype(F32)
        for d in range(came.shape[0]):
            value = value + came[d].astype(F32)
        return value

    for copy in up_moves:
        copy.wait_recv()
    sent.extend(up_moves)
    for n in range(8):
        value = up_in[n].astype(F32) + up_last[0, n].astype(F32)
        up_sum[n] = (value + up_last[1, n].astype(F32)).astype(BF)
    up_moves = x_blocks(up_sum, up_x)

    def over_x(ref, came):
        return [
            wire.send(XOFF[k], ref.at[:, k * 128 : k * 128 + 128], came.at[k - 1]) for k in (1, 2, 3)
        ]

    o_sum[...] = gathered(o_moves, o_terms[me.z, me.core], o_z).astype(BF)
    o_moves = over_x(o_sum, o_x)

    finish(norm_moves)
    here = rows(me.y * SUB, SUB)
    back = norm_send[here, :].astype(F32)
    for d in range(3):
        back = back + norm_recv[d].astype(F32)
    scale = scale_ref[...]
    enter = in_mine[...].astype(F32)
    weighed = back * enter
    inner = jnp.sum(weighed * gain_ref[...], axis=1, keepdims=True)
    gain_parts[0:1, :] = jnp.sum(weighed * scale, axis=0, keepdims=True)
    gain_parts[1:2, :] = ffn_gain_part[...]
    gain_parts[2:8, :] = jnp.zeros((6, D), F32)
    pull = scale * scale * scale * inner / D
    in_grad[...] = (resid_back[...] + scale * gain_ref[...] * back - enter * pull).astype(BF)
    for off in PLANE[1:]:
        there = lanes(me.at(off).block)
        leaving.append(wire.send(off, in_grad.at[:, there], input_grad.at[mine, :]))
        leaving.append(wire.send(off, gain_parts.at[:, there], gain_plane.at[me.block]))
    input_grad[mine, :] = in_grad[:, lanes(me.block)]
    gain_plane[me.block] = gain_parts[:, lanes(me.block)]

    k_sum[...] = gathered(k_moves, k_terms[:, me.core, :, me.xh, :, 0:128], k_x).astype(BF)
    k_moves = [wire.send(ZOFF[d], k_sum.at[(me.z + d) % 4], k_z.at[d - 1]) for d in (1, 2, 3)]
    q_sum[...] = gathered(q_moves, q_terms[me.z, me.core], q_z).astype(BF)
    q_moves = over_x(q_sum, q_x)

    shape = (8, 16, 1024)
    own = down_sum[:, :, me.z].reshape(shape)
    down_grad[...] = gathered(down_moves, own, down_z.reshape(3, *shape))
    own = gate_sum[0:4, :, :, 0:1024].reshape(shape)
    gate_grad[...] = gathered(gate_moves, own, gate_x.reshape(3, *shape))

    out_grad[...] = gathered(o_moves, o_sum[:, 0:128], o_x)
    query_grad[...] = gathered(q_moves, q_sum[:, 0:128], q_x)
    k_last[...] = gathered(k_moves, k_sum[me.z], k_z)
    y_moves = [wire.send(YOFF[d], k_last.at[me.at(YOFF[d]).y], kv_grad.at[me.y]) for d in (1, 2, 3)]
    kv_grad[me.y] = k_last[me.y]
    for copy in leaving:
        copy.wait_recv()
    sent.extend(leaving)
    gain_mine[...] = jnp.sum(gain_plane[...], axis=0)
    tok_moves = [wire.send(off, gain_mine, gain_toks.at[me.tok]) for off in TOKS[1:]]
    gain_toks[me.tok] = gain_mine[...]
    own = up_sum[0:4, :, :, 0:1024].reshape(shape)
    up_grad[...] = gathered(up_moves, own, up_x.reshape(3, *shape))
    finish(y_moves + tok_moves)
    gain_grad[...] = jnp.sum(gain_toks[...], axis=0)
    for copy in sent:
        copy.wait_send()
    o_pair.wait_send()
    q_pair.wait_send()
    k_pair.wait_send()


def back(vmem_ins, hbm_ins):
    vm = pl.BlockSpec(memory_space=pltpu.VMEM)
    hbm = pl.BlockSpec(memory_space=pl.ANY)
    outs = [
        SDS((ROWS, 128), BF),
        SDS((ROWS, 128), BF),
        SDS((256, 128), F32),
        SDS((4, 32, 128), F32),
        SDS((256, 128), F32),
        SDS((8, 16, 1024), F32),
        SDS((8, 16, 1024), F32),
        SDS((8, 16, 1024), F32),
        SDS((8, 128), F32),
    ]
    v = pltpu.VMEM
    return pl.pallas_call(
        back_body,
        name="back",
        out_shape=outs,
        in_specs=[vm] * len(vmem_ins) + [hbm] * len(hbm_ins),
        out_specs=[vm] * len(outs),
        scratch_shapes=[
            v((ROWS, 128), BF),
            v((ROWS, 128), BF),
            v((ROWS, 128), F32),
            v((3, 4, 2, 4, 16, 1024), BF),
            v((3, 8, 2, 16, 2048), BF),
            v((8, 2, 16, 2048), BF),
            v((2, 8, 2, 16, 2048), BF),
            v((2, 4, 2, 16, 2048), BF),
            v((2, 8, 2, 16, 2048), BF),
            v((4, 2, 4, 16, 1024), BF),
            v((8, 2, 16, 2048), BF),
            v((8, 2, 16, 2048), BF),
            v((3, 4, 2, 16, 1024), BF),
            v((3, 4, 2, 16, 1024), BF),
            v((3, 4, 2, 16, 1024), BF),
            v((CHUNK, 1024), BF),
            v((CHUNK, D), BF),
            v((3, SUB, D), BF),
            v((SUB, D), BF),
            v((8, D), F32),
            v((16, 8, 128), F32),
            v((8, 128), F32),
            v((8, 8, 128), F32),
        ]
        + [
            v((4, 2, 256, 512), BF),
            v((4, 256, 512), BF),
            v((3, 256, 128), BF),
            v((256, 512), BF),
            v((3, 256, 512), BF),
            v((4, 2, 256, 512), BF),
            v((4, 256, 512), BF),
            v((3, 256, 128), BF),
            v((256, 512), BF),
            v((3, 256, 512), BF),
            v((4, 2, 4, 2, 32, 256), BF),
            v((4, 4, 2, 32, 256), BF),
            v((3, 4, 4, 32, 128), BF),
            v((4, 4, 32, 128), BF),
            v((3, 4, 32, 128), BF),
            v((4, 32, 128), F32),
            pltpu.SemaphoreType.DMA((104,)),
            pltpu.SemaphoreType.DMA((104,)),
            pltpu.SemaphoreType.DMA((7,)),
        ],
        compiler_params=pltpu.CompilerParams(
            collective_id=15, has_side_effects=True, vmem_limit_bytes=56 * 2**20
        ),
        cost_estimate=pl.CostEstimate(flops=10**10, bytes_accessed=30 * 2**20, transcendentals=0),
    )(*vmem_ins, *hbm_ins)


def rope_table():
    halfway = HEAD_DIM // 2
    k = np.arange(halfway, dtype=np.float32)
    inverse = np.exp(-2.0 * k / HEAD_DIM * math.log(THETA)).astype(np.float32)
    wavelen = (2.0 * math.pi / inverse).astype(np.float32)
    scaled = inverse / np.float32(FACTOR)
    smooth = (INITIAL / wavelen - LOW_FACTOR) / (HIGH_FACTOR - LOW_FACTOR)
    middle = (1.0 - smooth) * scaled + smooth * inverse
    frequency = np.where(
        wavelen < INITIAL / HIGH_FACTOR,
        inverse,
        np.where(wavelen > INITIAL / LOW_FACTOR, scaled, middle),
    ).astype(np.float32)
    positions = np.concatenate([np.arange(512), np.arange(1024), np.arange(512)]).astype(np.float32)
    angles = (positions[:, None] * frequency[None, :]).astype(np.float32).astype(np.float64)
    return (
        np.tile(np.cos(angles).astype(np.float32), (1, 4)),
        np.tile(np.sin(angles).astype(np.float32), (1, 4)),
    )


def z_permute(value, d):
    return lax.ppermute(value, "tok", [(i, (i + 2 * d) % 8) for i in range(8)])


def part(array, start, size, axis):
    return lax.dynamic_slice_in_dim(array, start, size, axis)


def contract_rows(left_side, right_side):
    return lax.dot_general(
        left_side, right_side, (((0,), (0,)), ((), ())), preferred_element_type=F32
    )


def contract_cols(left_side, right_side):
    return lax.dot_general(
        left_side, right_side, (((1,), (1,)), ((), ())), preferred_element_type=F32
    )


def multiply(left_side, right_side):
    return jnp.dot(left_side, right_side, preferred_element_type=F32)


class Wire:
    def __init__(self, me, send_sem, recv_sem):
        self.me, self.send_sem, self.recv_sem, self.used = me, send_sem, recv_sem, 0

    def send(self, off, src, dst):
        copy = pltpu.make_async_remote_copy(
            src_ref=src,
            dst_ref=dst,
            send_sem=self.send_sem.at[self.used],
            recv_sem=self.recv_sem.at[self.used],
            device_id=self.me.at(off).device(),
            device_id_type=MESH,
        )
        copy.start()
        self.used += 1
        return copy


def meet(me, offsets):
    barrier = pltpu.get_barrier_semaphore()
    for off in offsets:
        back = tuple(-v for v in off)
        pl.semaphore_signal(barrier, inc=1, device_id=me.at(back).device(), device_id_type=MESH)
    pl.semaphore_wait(barrier, len(offsets))


def finish(copies):
    for copy in copies:
        copy.wait()


ZOFF = [(0, d, 0, 0, 0) for d in range(4)]


def weights_body(pieces, came, send_sem, recv_sem):
    me = whereami()
    wire = Wire(me, send_sem, recv_sem)
    meet(me, [XOFF[1], XOFF[3]])
    first = [wire.send(XOFF[k], pieces, came.at[:, k - 1]) for k in (1, 3)]
    first[0].wait_recv()
    second = [wire.send(XOFF[3], came.at[0, 0], came.at[0, 1])]
    first[1].wait_recv()
    second.append(wire.send(XOFF[1], came.at[1, 2], came.at[1, 1]))
    for copy in first:
        copy.wait_send()
    finish(second)


def weights_over_x(pieces):
    return pl.pallas_call(
        weights_body,
        name="weights",
        out_shape=SDS((2, 3, 3, 64, 1024), BF),
        in_specs=[pl.BlockSpec(memory_space=pl.ANY)],
        out_specs=pl.BlockSpec(memory_space=pl.ANY),
        scratch_shapes=[pltpu.SemaphoreType.DMA((4,)), pltpu.SemaphoreType.DMA((4,))],
        compiler_params=pltpu.CompilerParams(collective_id=13, has_side_effects=True),
    )(pieces)


def split_rows(count, size):
    return [slice(i * size, i * size + size) for i in range(count)]


def front_body(
    gain_row,
    attn_gain,
    cos_ref,
    sin_ref,
    hidden,
    w_q,
    w_kv,
    out_grad,
    w_o,
    q,
    kv,
    w_attn,
    normed,
    in_mine,
    scale_mine,
    gains,
    grad_full,
    w_cat,
    full,
    lin,
    scales,
    send_sem,
    recv_sem,
    local_sem,
):
    me = whereami()
    wire = Wire(me, send_sem, recv_sem)
    chunk = rows(me.chunk * CHUNK, CHUNK)
    near = []

    def take(src, dst):
        near.append(pltpu.make_async_copy(src, dst, local_sem.at[len(near)]))
        near[-1].start()

    take(w_q, w_attn.at[:, 0:128])
    take(w_kv, w_attn.at[:, 512:640])
    take(w_o, w_cat.at[:, 0:128])
    take(hidden.at[chunk, :], full.at[:, lanes(me.block)])
    take(out_grad.at[chunk, :], grad_full.at[:, lanes(me.wide)])
    gains[me.block] = gain_row[...]
    meet(me, PLANE[1:] + [SIBLING])

    def chunk_of(off):
        return rows(me.at(off).chunk * CHUNK, CHUNK)

    def spread(src, dst, column):
        return [wire.send(XOFF[k], src.at[chunk_of(XOFF[k]), :], dst.at[:, column(k)]) for k in (1, 2, 3)]

    enter = spread(hidden, full, lambda k: lanes(me.block))
    half = rows(me.core * 1024, 1024)
    blocks = [w_attn.at[half, k * 128 : k * 128 + 128] for k in (1, 2, 3)]
    over_x = [wire.send(XOFF[k], w_q.at[half, :], blocks[k - 1]) for k in (1, 2, 3)]
    blocks.append(w_attn.at[half, 640:768])
    over_x.append(wire.send(XOFF[1], w_kv.at[half, :], blocks[3]))
    others = [wire.send(off, gain_row, gains.at[me.block]) for off in PLANE[1:]]
    grads = spread(out_grad, grad_full, lambda k: lanes(XOFF[k][2] * 8 + me.wide))
    out_blocks = [w_cat.at[half, k * 128 : k * 128 + 128] for k in (1, 2, 3)]
    out_x = [wire.send(XOFF[k], w_o.at[half, :], out_blocks[k - 1]) for k in (1, 2, 3)]

    def pass_on(ref):
        out = []
        for h in range(2):
            cols = lanes(h * 4 + me.y, 256)
            out += [wire.send(off, ref.at[:, cols], ref.at[:, cols]) for off in YOFF[1:]]
        return out

    for copy in near:
        copy.wait()
    for copy in enter:
        copy.wait_recv()
    over_y = pass_on(full)
    over_core = []
    for copy, block in zip(over_x, blocks):
        copy.wait_recv()
        over_core.append(wire.send(SIBLING, block, block))
    for copy in grads:
        copy.wait_recv()
    others += pass_on(grad_full)
    for copy in over_y:
        copy.wait_recv()
    for part_rows in split_rows(4, SUB):
        value = full[part_rows, :].astype(F32)
        scale = lax.rsqrt(jnp.mean(value * value, axis=1, keepdims=True) + EPS)
        scales[part_rows, :] = scale
        normed[part_rows, :] = (value * scale * attn_gain[...]).astype(BF)
    for copy in over_core:
        copy.wait_recv()
    lane = lax.broadcasted_iota(jnp.int32, (CHUNK, 128), 1)
    for k in range(6):
        cols = slice(k * 128, k * 128 + 128)
        block = multiply(normed[...], w_attn[:, cols])
        swapped = jnp.where(
            (lane % 64) < 32, -pltpu.roll(block, 96, 1), pltpu.roll(block, 32, 1)
        )
        turned = block * cos_ref[...] + swapped * sin_ref[...]
        if k >= 4:
            turned = jnp.where(lane < 64, turned, block)
        lin[:, cols] = turned.astype(BF)
    moves = []
    for k in (1, 2, 3):
        kv_col = 512 + 128 * XOFF[k][2]
        moves.append(wire.send(XOFF[k], lin.at[:, k * 128 : k * 128 + 128], q.at[chunk, :]))
        moves.append(wire.send(XOFF[k], lin.at[:, kv_col : kv_col + 128], kv.at[chunk, :]))
    q[chunk, :] = lin[:, 0:128]
    kv[chunk, :] = lin[:, 512:640]
    for copy, block in zip(out_x, out_blocks):
        copy.wait_recv()
        over_core.append(wire.send(SIBLING, block, block))
        others.append(over_core[-1])
    here = rows(me.y * SUB, SUB)
    in_mine[...] = full[here, :]
    scale_mine[...] = scales[here, :]
    for copy in over_x + enter + grads + over_y + out_x + over_core[:4]:
        copy.wait_send()
    finish(others + moves)


def front(gain_row, attn_gain, cos_here, sin_here, hidden, w_q, w_kv, out_grad, w_o):
    vm = pl.BlockSpec(memory_space=pltpu.VMEM)
    hbm = pl.BlockSpec(memory_space=pl.ANY)
    outs = [
        SDS((ROWS, 128), BF),
        SDS((ROWS, 128), BF),
        SDS((D, 768), BF),
        SDS((CHUNK, D), BF),
        SDS((SUB, D), BF),
        SDS((SUB, 1), F32),
        SDS((16, 8, 128), F32),
        SDS((CHUNK, D), BF),
        SDS((D, 512), BF),
    ]
    return pl.pallas_call(
        front_body,
        name="front",
        out_shape=outs,
        in_specs=[vm] * 4 + [hbm] * 5,
        out_specs=[vm] * len(outs),
        scratch_shapes=[
            pltpu.VMEM((CHUNK, D), BF),
            pltpu.VMEM((CHUNK, 768), BF),
            pltpu.VMEM((CHUNK, 1), F32),
            pltpu.SemaphoreType.DMA((64,)),
            pltpu.SemaphoreType.DMA((64,)),
            pltpu.SemaphoreType.DMA((5,)),
        ],
        compiler_params=pltpu.CompilerParams(
            collective_id=0, has_side_effects=True, vmem_limit_bytes=40 * 2**20
        ),
        cost_estimate=pl.CostEstimate(flops=2 * 10**9, bytes_accessed=2**23, transcendentals=0),
    )(gain_row, attn_gain, cos_here, sin_here, hidden, w_q, w_kv, out_grad, w_o)


def middle_body(
    heads,
    in_mine,
    gain,
    w_cat,
    heads_cat,
    resid,
    scale_out,
    ffn_mine,
    term_send,
    term_recv,
    send_sem,
    recv_sem,
):
    me = whereami()
    wire = Wire(me, send_sem, recv_sem)
    meet(me, XOFF[1:] + YOFF[1:])
    moves = [
        wire.send(
            XOFF[k],
            heads.at[rows(me.at(XOFF[k]).chunk * CHUNK, CHUNK), :],
            heads_cat.at[:, k * 128 : k * 128 + 128],
        )
        for k in (1, 2, 3)
    ]
    heads_cat[:, 0:128] = heads[rows(me.chunk * CHUNK, CHUNK), :]
    finish(moves)
    sums = []
    for h in range(2):
        for p in range(2):
            cols = slice(h * 1024 + p * 512, h * 1024 + p * 512 + 512)
            term_send[:, cols] = contract_cols(heads_cat[...], w_cat[cols, :]).astype(BF)
        cols = slice(h * 1024, h * 1024 + 1024)
        for d in (1, 2, 3):
            there = rows(me.at(YOFF[d]).y * SUB, SUB)
            sums.append(
                wire.send(YOFF[d], term_send.at[there, cols], term_recv.at[d - 1, :, cols])
            )
    finish(sums)
    value = in_mine[...].astype(F32) + term_send[rows(me.y * SUB, SUB), :].astype(F32)
    for d in range(3):
        value = value + term_recv[d].astype(F32)
    resid[...] = value
    scale = lax.rsqrt(jnp.mean(value * value, axis=1, keepdims=True) + EPS)
    scale_out[...] = scale
    ffn_mine[...] = (value * scale * gain[...]).astype(BF)


def middle(heads, in_mine, gain, w_cat):
    vm = pl.BlockSpec(memory_space=pltpu.VMEM)
    outs = [SDS((CHUNK, 512), BF), SDS((SUB, D), F32), SDS((SUB, 1), F32), SDS((SUB, D), BF)]
    return pl.pallas_call(
        middle_body,
        name="middle",
        out_shape=outs,
        in_specs=[vm] * 4,
        out_specs=[vm] * len(outs),
        scratch_shapes=[
            pltpu.VMEM((CHUNK, D), BF),
            pltpu.VMEM((3, SUB, D), BF),
            pltpu.SemaphoreType.DMA((9,)),
            pltpu.SemaphoreType.DMA((9,)),
        ],
        compiler_params=pltpu.CompilerParams(
            collective_id=1, has_side_effects=True, vmem_limit_bytes=32 * 2**20
        ),
        cost_estimate=pl.CostEstimate(flops=10**9, bytes_accessed=2**23, transcendentals=0),
    )(heads, in_mine, gain, w_cat)


class PairSum:
    def __init__(self, me, left, right, own, came, stage, send_sem, recv_sem):
        self.me, self.left, self.right, self.own, self.came = me, left, right, own, came
        self.stage, self.send_sem, self.recv_sem = stage, send_sem, recv_sem

    def copy(self, i):
        return pltpu.make_async_remote_copy(
            src_ref=self.stage.at[i % 3, :, :, 1 - self.me.core],
            dst_ref=self.came.at[i],
            send_sem=self.send_sem.at[i],
            recv_sem=self.recv_sem.at[i],
            device_id=self.me.at(SIBLING).device(),
            device_id_type=MESH,
        )

    def multiply(self, first, last):
        def step(i, _):
            cols = pl.ds(pl.multiple_of(i * 256, 256), 256)

            @pl.when(i >= first + 3)
            def _():
                self.copy(i - 3).wait_send()

            block = contract_rows(self.left[:, cols], self.right[...])
            self.stage[i % 3] = block.astype(BF).reshape(2, 4, 2, 16, 2048)
            self.own[i] = self.stage[i % 3, :, :, self.me.core]
            self.copy(i).start()
            return 0

        lax.fori_loop(first, last, step, 0)
        for i in range(last - 3, last):
            self.copy(i).wait_send()

    def add(self, first, last):
        def step(i, _):
            self.copy(i).wait_recv()
            self.own[i] = (self.own[i].astype(F32) + self.came[i].astype(F32)).astype(BF)
            return 0

        lax.fori_loop(first, last, step, 0)


def add_to(target, came):
    for i in range(came.shape[0]):
        target[i] = (target[i].astype(F32) + came[i].astype(F32)).astype(BF)


def ffn_body(
    mine_ref,
    grad_ref,
    resid_ref,
    scale_ref,
    gain_ref,
    w_out_ref,
    own_gate,
    own_up,
    own_down,
    piece0,
    piece1,
    piece2_first,
    piece2_second,
    piece3,
    out_mine,
    resid_back,
    gain_part,
    mix_full,
    heads_back,
    down_own,
    down_came,
    gate_own,
    gate_came,
    up_own,
    up_late,
    up_pass,
    other_core,
    turned,
    ffn_in,
    act,
    gate_back,
    up_back,
    gate_tile,
    up_tile,
    down_tile,
    down_acc,
    ffn_acc,
    down_send,
    ffn_send,
    down_recv,
    ffn_recv,
    mix_mine,
    back_cat,
    down_terms,
    gate_terms,
    up_terms,
    stage,
    came,
    down_pass,
    gate_pass,
    send_sem,
    recv_sem,
    core_send,
    core_recv,
    tile_sem,
    local_sem,
    ack,
):
    me = whereami()
    wire = Wire(me, send_sem, recv_sem)
    half = [lanes(me.xl, 1024), lanes(1 - me.xl, 1024)]
    here = rows(me.y * SUB, SUB)

    pieces = (piece0, piece1, None, piece3)
    opposite = (piece2_first, piece2_second)

    def tile_copies(e, q, slot):
        copies, groups = [], []
        cols = pl.ds(pl.multiple_of(q * 256, 256), 256)

        def copy(src, dst):
            sem = tile_sem.at[slot, len(copies) + len(groups)]
            return pltpu.make_async_copy(src, dst, sem)

        for dxl in range(2):
            k = e * 2 + dxl
            for j, (own, tile) in enumerate(((own_gate, gate_tile), (own_up, up_tile))):
                if k == 0:
                    copies.append(copy(own.at[:, :, :, :, cols], tile.at[slot, dxl]))
                    continue
                for d, piece in enumerate(pieces):
                    spot = tile.at[slot, dxl, (me.z - d + 4) % 4, me.core]
                    if piece is not None:
                        copies.append(copy(piece.at[:, k - 1, j, :, cols], spot))
                        continue
                    for h in range(2):
                        copies.append(copy(opposite[h].at[k - 1, j, :, cols], spot.at[h]))
                spot = tile.at[slot, dxl, :, 1 - me.core]
                copies.append(copy(other_core.at[:, :, k - 1, j, :, cols], spot))
            here = slice(dxl * 1024, dxl * 1024 + 1024)
            if k == 0:
                copies.append(copy(own_down.at[q], down_tile.at[slot, :, :, :, here]))
                continue
            spot = down_tile.at[slot, 1 - me.core, :, :, here]
            copies.append(copy(other_core.at[q, :, k - 1, 2], spot))
            for h in range(2):
                spot = down_tile.at[slot, me.core, h, :, here]
                groups.append(
                    [
                        copy(opposite[h].at[k - 1, 2] if p is None else p.at[h, k - 1, 2], spot)
                        for p in pieces
                    ]
                )
        return copies, groups

    def fetch(e, q, slot):
        copies, groups = tile_copies(e, q, slot)
        for copy in copies:
            copy.start()
        for group in groups:
            for d, copy in enumerate(group):
                pl.when((me.z - q + 4) % 4 == d)(copy.start)

    def arrive(e, q, slot):
        copies, groups = tile_copies(e, q, slot)
        for copy in copies + [group[0] for group in groups]:
            copy.wait()

    meet(me, YOFF[1:] + XOFF[1:] + ZOFF[1:] + [SIBLING])
    for h in range(2):
        turned[:, h * 1024 : h * 1024 + 1024] = mine_ref[:, half[h]]
    gathers = [wire.send(off, turned, ffn_in.at[here, :]) for off in YOFF[1:]]
    shares = []
    for k in range(3):
        shares.append([])
        for d, piece in enumerate(pieces):
            spot = other_core.at[(me.z - d + 4) % 4, :, k]
            if piece is not None:
                shares[k].append(wire.send(SIBLING, piece.at[:, k], spot))
                continue
            for h in range(2):
                shares[k].append(wire.send(SIBLING, opposite[h].at[k], spot.at[h]))
    ffn_in[here, :] = turned[...]
    down_acc[...] = jnp.zeros(down_acc.shape, F32)
    ffn_acc[...] = jnp.zeros(ffn_acc.shape, F32)
    finish(shares[0])
    fetch(0, 0, 0)
    finish(gathers)

    sums = []
    for left, right, own in (
        (act, grad_ref, down_terms),
        (ffn_in, gate_back, gate_terms),
        (ffn_in, up_back, up_terms),
    ):
        j = len(sums)
        sums.append(PairSum(me, left, right, own, came, stage, core_send.at[j], core_recv.at[j]))
    down_sum, gate_sum, up_sum = sums

    def came_free():
        pl.semaphore_signal(ack, inc=1, device_id=me.at(SIBLING).device(), device_id_type=MESH)
        pl.semaphore_wait(ack, 1)

    for e in range(2):

        if e == 0:
            finish(shares[1] + shares[2])

        def step(q, _, e=e):
            slot = q % 2

            @pl.when(q < 3)
            def _():
                fetch(e, q + 1, 1 - slot)

            if e == 0:

                @pl.when(q == 3)
                def _():
                    fetch(1, 0, 0)

            arrive(e, q, slot)
            cols = pl.ds(pl.multiple_of(e * 1024 + q * 256, 256), 256)
            w_g = gate_tile[slot].reshape(2048, 256)
            w_u = up_tile[slot].reshape(2048, 256)
            w_d = down_tile[slot].reshape(256, 2048)
            gate = multiply(ffn_in[...], w_g)
            up = multiply(ffn_in[...], w_u)
            act_back = contract_cols(grad_ref[...], w_d)
            sigmoid = jax.nn.sigmoid(gate)
            silu = gate * sigmoid
            act_here = (silu * up).astype(BF)
            act[:, cols] = act_here
            down_acc[...] += multiply(act_here, w_d)
            g_back = (act_back * up * sigmoid * (1.0 + gate * (1.0 - sigmoid))).astype(BF)
            u_back = (act_back * silu).astype(BF)
            gate_back[:, cols] = g_back
            up_back[:, cols] = u_back
            ffn_acc[...] += contract_cols(g_back, w_g) + contract_cols(u_back, w_u)
            return 0

        lax.fori_loop(0, 4, step, 0)
        if e == 0:
            down_sum.multiply(0, 4)

    ffn_send[...] = ffn_acc[...].astype(BF)
    ffn_moves = [
        wire.send(YOFF[d], ffn_send.at[rows(me.at(YOFF[d]).y * SUB, SUB), :], ffn_recv.at[d - 1])
        for d in (1, 2, 3)
    ]
    down_sum.multiply(4, 8)


    def down_block(k, h=None):
        e, dxl = XOFF[k][4], XOFF[k][2]
        pairs = slice(e * 4, e * 4 + 4) if h is None else slice(e * 4 + h * 2, e * 4 + h * 2 + 2)
        return down_terms.at[pairs, :, :, :, dxl * 1024 : dxl * 1024 + 1024]

    down_sum.add(0, 8)
    x_moves = [
        wire.send(XOFF[1], down_block(2, 0), down_pass.at[0]),
        wire.send(XOFF[3], down_block(2, 1), down_pass.at[1]),
        wire.send(XOFF[1], down_block(1, 0), down_came.at[0, 0:2]),
        wire.send(XOFF[3], down_block(3, 1), down_came.at[1, 2:4]),
    ]
    near = []

    def keep(src, dst):
        near.append(pltpu.make_async_copy(src, dst, local_sem.at[len(near)]))
        near[-1].start()

    keep(down_block(0), down_own)

    def z_block(terms, d, h=None):
        pairs = slice(0, 8) if h is None else slice(h * 4, h * 4 + 4)
        return terms.at[pairs, :, (me.z + d) % 4]

    came_free()
    gate_sum.multiply(0, 8)
    gate_sum.add(0, 4)
    z_moves = [
        wire.send(ZOFF[1], z_block(gate_terms, 2, 0), gate_pass.at[0]),
        wire.send(ZOFF[3], z_block(gate_terms, 3, 0), gate_came.at[1, 0:4]),
    ]
    gate_sum.add(4, 8)
    z_moves += [
        wire.send(ZOFF[3], z_block(gate_terms, 2, 1), gate_pass.at[1]),
        wire.send(ZOFF[1], z_block(gate_terms, 1, 1), gate_came.at[0, 4:8]),
    ]
    keep(z_block(gate_terms, 0), gate_own)

    finish(ffn_moves)

    def summed(send, recv, h):
        cols = slice(h * 1024, h * 1024 + 1024)
        out = send[here, cols].astype(F32)
        for d in range(3):
            out = out + recv[d, :, cols].astype(F32)
        return out

    scale = scale_ref[...]
    inner = jnp.zeros((SUB, 1), F32)
    for h in range(2):
        back = summed(ffn_send, ffn_recv, h)
        weighed = back * resid_ref[:, half[h]]
        inner = inner + jnp.sum(weighed * gain_ref[:, half[h]], axis=1, keepdims=True)
        gain_part[:, half[h]] = jnp.sum(weighed * scale, axis=0, keepdims=True)
    pull = scale * scale * scale * inner / D
    for h in range(2):
        back = summed(ffn_send, ffn_recv, h)
        grad = grad_ref[here, h * 1024 : h * 1024 + 1024].astype(F32)
        total_back = grad + scale * gain_ref[:, half[h]] * back - resid_ref[:, half[h]] * pull
        resid_back[:, half[h]] = total_back
        mix_mine[:, half[h]] = total_back.astype(BF)
    mix_full[here, :] = mix_mine[...]
    mix_moves = [wire.send(off, mix_mine, mix_full.at[here, :]) for off in YOFF[1:]]

    down_send[...] = down_acc[...].astype(BF)
    down_moves = [
        wire.send(YOFF[d], down_send.at[rows(me.at(YOFF[d]).y * SUB, SUB), :], down_recv.at[d - 1])
        for d in (1, 2, 3)
    ]
    x_moves[0].wait_recv()
    add_to(down_block(3, 0), down_pass.at[0])
    x_late = [wire.send(XOFF[3], down_block(3, 0), down_came.at[1, 0:2])]
    x_moves[1].wait_recv()
    add_to(down_block(1, 1), down_pass.at[1])
    x_late.append(wire.send(XOFF[1], down_block(1, 1), down_came.at[0, 2:4]))
    came_free()
    up_sum.multiply(0, 8)
    z_moves[0].wait_recv()
    add_to(z_block(gate_terms, 1, 0), gate_pass.at[0])
    z_late = [wire.send(ZOFF[1], z_block(gate_terms, 1, 0), gate_came.at[0, 0:4])]
    z_moves[2].wait_recv()
    add_to(z_block(gate_terms, 3, 1), gate_pass.at[1])
    z_late.append(wire.send(ZOFF[3], z_block(gate_terms, 3, 1), gate_came.at[1, 4:8]))
    up_sum.add(0, 8)
    z_late += [
        wire.send(ZOFF[1], z_block(up_terms, 2, 0), up_pass.at[0]),
        wire.send(ZOFF[3], z_block(up_terms, 2, 1), up_pass.at[1]),
    ]
    keep(z_block(up_terms, 0), up_own)
    keep(z_block(up_terms, 1), up_late.at[0])
    keep(z_block(up_terms, 3), up_late.at[1])

    finish(mix_moves)
    back_cat[...] = multiply(mix_full[...], w_out_ref[...]).astype(BF)
    spot = rows(me.chunk * CHUNK, CHUNK)
    head_moves = [
        wire.send(XOFF[k], back_cat.at[:, k * 128 : k * 128 + 128], heads_back.at[spot, :])
        for k in (1, 2, 3)
    ]
    heads_back[spot, :] = back_cat[:, 0:128]
    finish(down_moves)
    for h in range(2):
        out_mine[:, half[h]] = (resid_ref[:, half[h]] + summed(down_send, down_recv, h)).astype(BF)
    for move in (x_moves[0], x_moves[1], z_moves[0], z_moves[2]):
        move.wait_send()
    finish(head_moves + x_moves[2:] + [z_moves[1], z_moves[3]] + x_late + z_late)
    for copy in near:
        copy.wait()


def ffn(ffn_mine, grad_full, resid, scale_two, gain, w_out, w_gate, w_up, w_down, pieces):
    vm = pl.BlockSpec(memory_space=pltpu.VMEM)
    hbm = pl.BlockSpec(memory_space=pl.ANY)
    return pl.pallas_call(
        ffn_body,
        name="ffn",
        out_shape=[
            SDS((SUB, D), BF),
            SDS((SUB, D), F32),
            SDS((1, D), F32),
            SDS((CHUNK, D), BF),
            SDS((ROWS, 128), BF),
            SDS((4, 2, 4, 16, 1024), BF),
            SDS((2, 4, 2, 4, 16, 1024), BF),
            SDS((8, 2, 16, 2048), BF),
            SDS((2, 8, 2, 16, 2048), BF),
            SDS((8, 2, 16, 2048), BF),
            SDS((2, 8, 2, 16, 2048), BF),
            SDS((2, 4, 2, 16, 2048), BF),
            SDS((4, 2, 3, 3, 64, 1024), BF),
        ],
        in_specs=[vm] * 6 + [hbm] * 8,
        out_specs=[vm] * 5 + [hbm] * 8,
        scratch_shapes=[
            pltpu.VMEM((SUB, D), BF),
            pltpu.VMEM((CHUNK, D), BF),
            pltpu.VMEM((CHUNK, D), BF),
            pltpu.VMEM((CHUNK, D), BF),
            pltpu.VMEM((CHUNK, D), BF),
            pltpu.VMEM((2, 2, 4, 2, 2, 64, 256), BF),
            pltpu.VMEM((2, 2, 4, 2, 2, 64, 256), BF),
            pltpu.VMEM((2, 2, 2, 64, 2048), BF),
            pltpu.VMEM((CHUNK, D), F32),
            pltpu.VMEM((CHUNK, D), F32),
            pltpu.VMEM((CHUNK, D), BF),
            pltpu.VMEM((CHUNK, D), BF),
            pltpu.VMEM((3, SUB, D), BF),
            pltpu.VMEM((3, SUB, D), BF),
            pltpu.VMEM((SUB, D), BF),
            pltpu.VMEM((CHUNK, 512), BF),
            pltpu.VMEM((8, 2, 4, 16, 2048), BF),
            pltpu.VMEM((8, 2, 4, 16, 2048), BF),
            pltpu.VMEM((8, 2, 4, 16, 2048), BF),
            pltpu.VMEM((3, 2, 4, 2, 16, 2048), BF),
            pltpu.VMEM((8, 2, 4, 16, 2048), BF),
            pltpu.VMEM((2, 2, 2, 4, 16, 1024), BF),
            pltpu.VMEM((2, 4, 2, 16, 2048), BF),
            pltpu.SemaphoreType.DMA((48,)),
            pltpu.SemaphoreType.DMA((48,)),
            pltpu.SemaphoreType.DMA((3, 8)),
            pltpu.SemaphoreType.DMA((3, 8)),
            pltpu.SemaphoreType.DMA((2, 32)),
            pltpu.SemaphoreType.DMA((6,)),
            pltpu.SemaphoreType.REGULAR,
        ],
        compiler_params=pltpu.CompilerParams(
            collective_id=14, has_side_effects=True, vmem_limit_bytes=60 * 2**20
        ),
        cost_estimate=pl.CostEstimate(flops=26 * 10**9, bytes_accessed=40 * 2**20, transcendentals=0),
    )(
        ffn_mine,
        grad_full,
        resid,
        scale_two,
        gain,
        w_out,
        w_gate.reshape(4, 2, 2, 64, 1024),
        w_up.reshape(4, 2, 2, 64, 1024),
        w_down.reshape(4, 2, 2, 64, 1024),
        *pieces,
    )


def per_device(
    layer_input,
    doc_lengths,
    attn_gain,
    w_query,
    w_key,
    w_value,
    w_output,
    ffn_gain,
    w_gate,
    w_up,
    w_down,
    output_grad,
):
    me = whereami()
    cos_np, sin_np = rope_table()
    cos_all, sin_all = jnp.asarray(cos_np), jnp.asarray(sin_np)
    long_first = doc_lengths[0, 0] > SHORT
    table_start = jnp.where(long_first, SHORT, 0) + me.chunk * CHUNK
    cos_here = part(cos_all, table_start, CHUNK, 0)
    sin_here = part(sin_all, table_start, CHUNK, 0)

    w_kv = jnp.concatenate(
        [part(w_key, me.y * 64, 64, 1), part(w_value, me.y * 64, 64, 1)], axis=1
    )
    pieces = jnp.stack([part(w, me.tok * 128, 128, 0) for w in (w_gate, w_up, w_down)])
    piece0 = weights_over_x(jnp.moveaxis(pieces.reshape(3, 2, 64, 1024), 1, 0))
    piece1, piece3 = z_permute(piece0, 1), z_permute(piece0, 3)
    queries, kv, w_attn, normed, in_mine, scale_mine, gains, grad_full, w_out = front(
        jnp.broadcast_to(ffn_gain[None, :], (8, 128)),
        attn_gain[None, :],
        cos_here,
        sin_here,
        layer_input,
        w_query,
        w_kv,
        output_grad,
        w_output,
    )
    ffn_gain_all = gains[:, 0, :].reshape(1, D)
    queries, second, first = lax.optimization_barrier((queries, piece1[0], piece3[1]))
    pieces = [piece0, piece1, z_permute(second, 1), z_permute(first, 3), piece3]
    (heads_out,) = vmem_call(
        "attend", attend_body, [doc_lengths, queries, kv], [SDS((ROWS, 128), BF)], flops=2 * 10**10
    )
    heads_cat, resid, scale_two, ffn_mine = middle(heads_out, in_mine, ffn_gain_all, w_out)
    (
        out_mine,
        resid_back,
        ffn_gain_part,
        mix_full,
        heads_back,
        *ffn_sums,
        _,
    ) = ffn(
        ffn_mine, grad_full, resid, scale_two, ffn_gain_all, w_out, w_gate, w_up, w_down, pieces
    )

    table = jnp.where(long_first, SHORT, 0)
    (
        layer_output,
        input_grad,
        query_grad,
        kv_grad,
        output_proj_grad,
        gate_grad,
        up_grad,
        down_grad,
        gain_grads,
    ) = back(
        [
            jnp.broadcast_to(doc_lengths[0, 0], (8, 128)),
            queries,
            kv,
            heads_back,
            part(cos_all, table, ROWS, 0),
            part(sin_all, table, ROWS, 0),
            w_attn,
            heads_cat,
            out_mine,
            in_mine,
            resid_back,
            scale_mine,
            attn_gain[None, :],
            ffn_gain_part,
            normed,
            mix_full,
        ],
        ffn_sums,
    )
    kv_cols = jnp.moveaxis(kv_grad, 0, 1).reshape(32, 4, 2, 64)
    key_grad = kv_cols[:, :, 0, :].reshape(32, 256)
    value_grad = kv_cols[:, :, 1, :].reshape(32, 256)
    gain_grads = part(gain_grads, me.tok * 16, 16, 1)
    return (
        layer_output,
        input_grad,
        gain_grads[0:1],
        query_grad,
        key_grad,
        value_grad,
        output_proj_grad,
        gain_grads[1:2],
        gate_grad,
        up_grad,
        down_grad,
    )


def solution(mesh):
    in_specs = (
        P("tok", ("narrow", "wide")),
        P("tok", None),
        P(),
        P(None, ("narrow", "wide")),
        P(None, "narrow"),
        P(None, "narrow"),
        P(None, ("narrow", "wide")),
        P(("narrow", "wide")),
        P("narrow", "wide"),
        P("narrow", "wide"),
        P("wide", "narrow"),
        P("tok", ("narrow", "wide")),
    )
    out_specs = (
        P("tok", ("narrow", "wide")),
        P("tok", ("narrow", "wide")),
        P(("narrow", "wide"), "tok"),
        P("tok", ("narrow", "wide")),
        P(("tok", "wide"), "narrow"),
        P(("tok", "wide"), "narrow"),
        P("tok", ("narrow", "wide")),
        P(("narrow", "wide"), "tok"),
        P("narrow", "tok", "wide"),
        P("narrow", "tok", "wide"),
        P("wide", "tok", "narrow"),
    )
    return jax.shard_map(
        per_device, mesh=mesh, in_specs=in_specs, out_specs=out_specs, check_vma=False
    )
```

```python
import functools
import math

import jax
import jax.numpy as jnp
import numpy as np
from jax import lax
from jax.experimental import pallas as pl
from jax.experimental.pallas import tpu as pltpu
from jax.sharding import PartitionSpec as P

HEADS = 32
KV_HEADS = 8
HEAD_DIM = 64
GROUP = 128
EPS = 1e-05
THETA = 500000.0
FACTOR = 32.0
LOW_FACTOR = 1.0
HIGH_FACTOR = 4.0
INITIAL = 8192.0
NEG = -1e30

D = 2048
ROWS = 1536
CHUNK = 384
SUB = 96
SHORT = 512
BF = jnp.bfloat16
F32 = jnp.float32
MESH = pl.DeviceIdType.MESH
SDS = jax.ShapeDtypeStruct

HERE = (0, 0, 0, 0, 0)
XOFF = [(0, 0, 0, 0, 0), (0, 0, 1, 0, 0), (0, 0, 0, 0, 1), (0, 0, 1, 0, 1)]
YOFF = [(0, 0, 0, d, 0) for d in range(4)]
PLANE = [(0, 0, a, b, e) for b in range(4) for a in range(2) for e in range(2)]
SIBLING = (1, 0, 0, 0, 0)
TOKS = [(a, b, 0, 0, 0) for b in range(4) for a in range(2)]


class Place:
    def __init__(self, core, z, xl, y, xh):
        self.core, self.z, self.xl, self.y, self.xh = core, z, xl, y, xh
        self.tok = z * 2 + core
        self.wide = y * 2 + xh
        self.block = xl * 8 + self.wide
        self.chunk = xl * 2 + xh

    def at(self, off):
        return Place(
            (self.core + off[0]) % 2,
            (self.z + off[1]) % 4,
            (self.xl + off[2]) % 2,
            (self.y + off[3]) % 4,
            (self.xh + off[4]) % 2,
        )

    def device(self):
        return (self.tok, self.xl, self.wide)


def whereami():
    tok = lax.axis_index("tok")
    wide = lax.axis_index("wide")
    return Place(tok % 2, tok // 2, lax.axis_index("narrow"), wide // 2, wide % 2)


def rows(start, size):
    return pl.ds(pl.multiple_of(start, size), size)


def lanes(index, size=128):
    return pl.ds(pl.multiple_of(index * size, size), size)


def block_probs(q_ref, kv_ref, start, i, stack):
    n = 256 * (i + 1)
    keys = kv_ref[rows_256(start, n), 0:64]
    scores = lax.dot_general(
        keys, stack, (((1,), (1,)), ((), ())), preferred_element_type=F32
    ) * (HEAD_DIM**-0.5)
    last = scores[n - 256 :, :]
    key_id = lax.broadcasted_iota(jnp.int32, (256, 512), 0)
    query_id = lax.broadcasted_iota(jnp.int32, (256, 512), 1) % 256
    last = jnp.where(key_id <= query_id, last, NEG)
    if n > 256:
        scores = jnp.concatenate([scores[: n - 256, :], last], axis=0)
    else:
        scores = last
    raised = jnp.exp(scores - jnp.max(scores, axis=0, keepdims=True))
    return keys, raised, jnp.sum(raised, axis=0, keepdims=True)


def rows_256(start, size):
    return pl.ds(pl.multiple_of(start, 256), size)


def starts_of(len_ref):
    long_first = len_ref[0, 0] > SHORT
    long_start = jnp.where(long_first, 0, SHORT)
    short_start = jnp.where(long_first, 2 * SHORT, 0)
    return ((long_start, 4), (short_start, 2))


def both(block):
    return jnp.concatenate([block[:, 0:64], block[:, 64:128]], axis=0)


def attend_body(len_ref, q_ref, kv_ref, out_ref):
    for start, blocks in starts_of(len_ref):
        for i in range(blocks):
            mine = rows_256(start + 256 * i, 256)
            stack = both(q_ref[mine, :])
            keys, raised, mass = block_probs(q_ref, kv_ref, start, i, stack)
            soft = (raised * (1.0 / mass)).astype(BF)
            values = kv_ref[rows_256(start, 256 * (i + 1)), 64:128]
            mixed = lax.dot_general(
                soft, values, (((0,), (0,)), ((), ())), preferred_element_type=F32
            )
            out_ref[mine, :] = jnp.concatenate([mixed[:256], mixed[256:]], axis=1).astype(BF)


def unrope(tensor, cosine, sine):
    lane = lax.broadcasted_iota(jnp.int32, tensor.shape, 1)
    first = (lane % 64) < 32
    swapped = jnp.where(first, pltpu.roll(tensor, 96, 1), -pltpu.roll(tensor, 32, 1))
    return tensor * cosine + swapped * sine


def vmem_call(name, body, ins, outs, scratch=(), flops=0):
    return pl.pallas_call(
        body,
        name=name,
        out_shape=outs,
        in_specs=[pl.BlockSpec(memory_space=pltpu.SMEM)]
        + [pl.BlockSpec(memory_space=pltpu.VMEM)] * (len(ins) - 1),
        out_specs=[pl.BlockSpec(memory_space=pltpu.VMEM)] * len(outs),
        scratch_shapes=list(scratch),
        compiler_params=pltpu.CompilerParams(vmem_limit_bytes=60 * 2**20),
        cost_estimate=pl.CostEstimate(flops=flops, bytes_accessed=2**20, transcendentals=0),
    )(*ins)


def masked_scores(keys, query, i, length):
    n = keys.shape[0]
    scores = contract_cols(keys, query) * (HEAD_DIM**-0.5)
    key_id = lax.broadcasted_iota(jnp.int32, (256, 256), 0)
    query_id = lax.broadcasted_iota(jnp.int32, (256, 256), 1)
    parts = [jnp.where(key_id <= query_id, scores[n - 256 :, :], NEG)]
    middle = 0
    if i >= 2:
        cut = SHORT if i < 4 else 2 * SHORT
        middle = SHORT
        parts.insert(0, jnp.where(length == cut, NEG, scores[:SHORT, :]))
    if n - 256 > middle:
        parts.insert(len(parts) - 1, scores[middle : n - 256, :])
    return jnp.concatenate(parts, axis=0) if len(parts) > 1 else parts[0]


def back_body(
    len_ref,
    q_ref,
    kv_ref,
    heads_back,
    out_mine,
    in_mine,
    resid_back,
    scale_ref,
    gain_ref,
    ffn_gain_part,
    table_in,
    w_attn_in,
    heads_in,
    normed_in,
    mix_in,
    down_own,
    down_came,
    gate_own,
    gate_came,
    up_own,
    up_late,
    up_pass,
    layer_output,
    input_grad,
    query_grad,
    kv_grad,
    out_grad,
    gate_grad,
    up_grad,
    down_grad,
    gain_grad,
    table,
    w_attn,
    heads_cat,
    normed,
    mix_full,
    dq_ref,
    dkv_ref,
    dkv_acc,
    down_in,
    gate_in,
    up_in,
    late_in,
    pass_in,
    up_last,
    down_sum,
    gate_sum,
    up_sum,
    down_z,
    gate_x,
    up_x,
    cat_back,
    norm_send,
    norm_recv,
    in_grad,
    gain_parts,
    gain_plane,
    gain_mine,
    gain_toks,
    o_terms,
    o_core,
    o_x,
    o_sum,
    o_z,
    q_terms,
    q_core,
    q_x,
    q_sum,
    q_z,
    k_terms,
    k_core,
    k_x,
    k_sum,
    k_z,
    k_last,
    send_sem,
    recv_sem,
    local_sem,
):
    me = whereami()
    wire = Wire(me, send_sem, recv_sem)
    loads = []
    for src, dst in (
        (up_late, late_in),
        (up_pass, pass_in),
        (gate_own, gate_in.at[0]),
        (gate_came, gate_in.at[1:3]),
        (down_own, down_in.at[0]),
        (down_came, down_in.at[1:3]),
        (up_own, up_in),
        (table_in, table),
        (mix_in, mix_full),
        (heads_in, heads_cat),
        (w_attn_in, w_attn),
        (normed_in, normed),
    ):
        loads.append(pltpu.make_async_copy(src, dst, local_sem.at[len(loads)]))
        loads[-1].start()
    meet(me, PLANE[1:] + TOKS[1:])
    sent = []

    for copy in loads[0:2]:
        copy.wait()
    up_moves = [
        wire.send(ZOFF[1], late_in.at[0, 4:8], up_last.at[0, 4:8]),
        wire.send(ZOFF[3], late_in.at[1, 0:4], up_last.at[1, 0:4]),
    ]

    length = len_ref[0:1, 0:1]
    loads[7].wait()

    def turns(row, size):
        first, later = slice(row, row + size), slice(row + SHORT, row + SHORT + size)
        return [jnp.where(length == SHORT, table[j, first], table[j, later]) for j in range(2)]

    dkv_acc[...] = jnp.zeros(dkv_acc.shape, F32)
    for i in range(6):
        low, high = 0 if i < 4 else SHORT, 256 * (i + 1)
        here = slice(256 * i, high)
        keys, values = kv_ref[low:high, 0:64], kv_ref[low:high, 64:128]
        parts = []
        for head in (slice(0, 64), slice(64, 128)):
            query, value_back = q_ref[here, head], heads_back[here, head]
            scores = masked_scores(keys, query, i, length)
            raised = jnp.exp(scores - jnp.max(scores, axis=0, keepdims=True))
            soft = raised * (1.0 / jnp.sum(raised, axis=0, keepdims=True))
            prob_back = contract_cols(values, value_back)
            inner = jnp.sum(soft * prob_back, axis=0, keepdims=True)
            score_back = (soft * (prob_back - inner)).astype(BF)
            parts.append(contract_rows(score_back, keys) * (HEAD_DIM**-0.5))
            dk = multiply(score_back, query) * (HEAD_DIM**-0.5)
            dv = multiply(soft.astype(BF), value_back)
            dkv_acc[low:high, :] += jnp.concatenate([dk, dv], axis=1)
        dq = jnp.concatenate(parts, axis=1)
        dq_ref[here, :] = unrope(dq, *turns(256 * i, 256)).astype(BF)
    lane = lax.broadcasted_iota(jnp.int32, (256, 128), 1)
    for here in split_rows(6, 256):
        acc = dkv_acc[here, :]
        turned = unrope(acc, *turns(here.start, 256))
        dkv_ref[here, :] = jnp.where(lane < 64, turned, acc).astype(BF)

    spot = rows(me.chunk * CHUNK, CHUNK)
    moves = []
    for k in (1, 2, 3):
        there = rows(me.at(XOFF[k]).chunk * CHUNK, CHUNK)
        for ref, col in ((dq_ref, 0), (dkv_ref, 512)):
            moves.append(
                wire.send(
                    XOFF[k], ref.at[there, :], cat_back.at[:, col + k * 128 : col + k * 128 + 128]
                )
            )
    cat_back[:, 0:128] = dq_ref[spot, :]
    cat_back[:, 512:640] = dkv_ref[spot, :]

    mine = rows(me.chunk * CHUNK + me.y * SUB, SUB)
    leaving = [
        wire.send(off, out_mine.at[:, lanes(me.at(off).block)], layer_output.at[mine, :])
        for off in PLANE[1:]
    ]
    layer_output[mine, :] = out_mine[:, lanes(me.block)]

    add_to(late_in.at[0, 0:4], pass_in.at[0])
    up_moves.append(wire.send(ZOFF[1], late_in.at[0, 0:4], up_last.at[0, 0:4]))
    add_to(late_in.at[1, 4:8], pass_in.at[1])
    up_moves.append(wire.send(ZOFF[3], late_in.at[1, 4:8], up_last.at[1, 4:8]))

    def fold(ref, out):
        for n in range(out.shape[0]):
            value = ref[0, n].astype(F32)
            for k in range(1, ref.shape[0]):
                value = value + ref[k, n].astype(F32)
            out[n] = value.astype(BF)

    def x_blocks(ref, came):
        moves = []
        for k in (1, 2, 3):
            e, dxl = XOFF[k][4], XOFF[k][2]
            src = ref.at[dxl * 4 : dxl * 4 + 4, :, :, e * 1024 : e * 1024 + 1024]
            moves.append(wire.send(XOFF[k], src, came.at[k - 1]))
        return moves

    for copy in loads[2:7] + loads[8:]:
        copy.wait()
    fold(gate_in, gate_sum)
    gate_moves = x_blocks(gate_sum, gate_x)

    for z in range(4):
        block = contract_rows(mix_full[:, z * 512 : z * 512 + 512], heads_cat[...])
        o_terms[z] = block.astype(BF).reshape(2, 256, 512)
    o_pair = wire.send(SIBLING, o_terms.at[:, 1 - me.core], o_core)

    def add_core(copy, terms, came):
        copy.wait_recv()
        terms[:, me.core] = (terms[:, me.core].astype(F32) + came[...].astype(F32)).astype(BF)

    finish(moves)
    for h in range(4):
        cols = slice(h * 512, h * 512 + 512)
        term = contract_cols(cat_back[:, 0:768], w_attn[cols, :]) + contract_cols(
            cat_back[:, 768:1024], w_attn[cols, 512:768]
        )
        norm_send[:, cols] = term.astype(BF)
    norm_moves = [
        wire.send(YOFF[d], norm_send.at[rows(me.at(YOFF[d]).y * SUB, SUB), :], norm_recv.at[d - 1])
        for d in (1, 2, 3)
    ]

    add_core(o_pair, o_terms, o_core)
    o_moves = [
        wire.send(ZOFF[d], o_terms.at[(me.z + d) % 4, me.core], o_z.at[d - 1]) for d in (1, 2, 3)
    ]

    for z in range(4):
        block = contract_rows(normed[:, z * 512 : z * 512 + 512], cat_back[:, 0:512])
        q_terms[z] = block.astype(BF).reshape(2, 256, 512)
    q_pair = wire.send(SIBLING, q_terms.at[:, 1 - me.core], q_core)
    for z in range(4):
        left = normed[:, z * 512 : z * 512 + 512]
        block = contract_rows(left, cat_back[:, 512:768]) + contract_rows(
            left, cat_back[:, 768:1024]
        )
        k_terms[z] = block.astype(BF).reshape(2, 4, 2, 32, 256)
    k_pair = wire.send(SIBLING, k_terms.at[:, 1 - me.core], k_core)

    def kv_block(k):
        e, dxl = XOFF[k][4], XOFF[k][2]
        return k_terms.at[:, me.core, :, (me.xh + e) % 2, :, dxl * 128 : dxl * 128 + 128]

    add_core(k_pair, k_terms, k_core)
    k_moves = [wire.send(XOFF[k], kv_block(k), k_x.at[k - 1]) for k in (1, 2, 3)]
    add_core(q_pair, q_terms, q_core)
    q_moves = [
        wire.send(ZOFF[d], q_terms.at[(me.z + d) % 4, me.core], q_z.at[d - 1]) for d in (1, 2, 3)
    ]

    fold(down_in, down_sum)
    down_moves = [
        wire.send(ZOFF[d], down_sum.at[:, :, (me.z + d) % 4], down_z.at[d - 1]) for d in (1, 2, 3)
    ]

    def gathered(moves, own, came):
        for copy in moves:
            copy.wait_recv()
        sent.extend(moves)
        value = own.astype(F32)
        for d in range(came.shape[0]):
            value = value + came[d].astype(F32)
        return value

    for copy in up_moves:
        copy.wait_recv()
    sent.extend(up_moves)
    for n in range(8):
        value = up_in[n].astype(F32) + up_last[0, n].astype(F32)
        up_sum[n] = (value + up_last[1, n].astype(F32)).astype(BF)
    up_moves = x_blocks(up_sum, up_x)

    def over_x(ref, came):
        return [
            wire.send(XOFF[k], ref.at[:, k * 128 : k * 128 + 128], came.at[k - 1]) for k in (1, 2, 3)
        ]

    o_sum[...] = gathered(o_moves, o_terms[me.z, me.core], o_z).astype(BF)
    o_moves = over_x(o_sum, o_x)

    finish(norm_moves)
    here = rows(me.y * SUB, SUB)
    back = norm_send[here, :].astype(F32)
    for d in range(3):
        back = back + norm_recv[d].astype(F32)
    scale = scale_ref[...]
    enter = in_mine[...].astype(F32)
    weighed = back * enter
    inner = jnp.sum(weighed * gain_ref[...], axis=1, keepdims=True)
    gain_parts[0:1, :] = jnp.sum(weighed * scale, axis=0, keepdims=True)
    gain_parts[1:2, :] = ffn_gain_part[...]
    gain_parts[2:8, :] = jnp.zeros((6, D), F32)
    pull = scale * scale * scale * inner / D
    in_grad[...] = (resid_back[...] + scale * gain_ref[...] * back - enter * pull).astype(BF)
    for off in PLANE[1:]:
        there = lanes(me.at(off).block)
        leaving.append(wire.send(off, in_grad.at[:, there], input_grad.at[mine, :]))
        leaving.append(wire.send(off, gain_parts.at[:, there], gain_plane.at[me.block]))
    input_grad[mine, :] = in_grad[:, lanes(me.block)]
    gain_plane[me.block] = gain_parts[:, lanes(me.block)]

    k_sum[...] = gathered(k_moves, k_terms[:, me.core, :, me.xh, :, 0:128], k_x).astype(BF)
    k_moves = [wire.send(ZOFF[d], k_sum.at[(me.z + d) % 4], k_z.at[d - 1]) for d in (1, 2, 3)]
    q_sum[...] = gathered(q_moves, q_terms[me.z, me.core], q_z).astype(BF)
    q_moves = over_x(q_sum, q_x)

    shape = (8, 16, 1024)
    own = down_sum[:, :, me.z].reshape(shape)
    down_grad[...] = gathered(down_moves, own, down_z.reshape(3, *shape))
    own = gate_sum[0:4, :, :, 0:1024].reshape(shape)
    gate_grad[...] = gathered(gate_moves, own, gate_x.reshape(3, *shape))

    out_grad[...] = gathered(o_moves, o_sum[:, 0:128], o_x)
    query_grad[...] = gathered(q_moves, q_sum[:, 0:128], q_x)
    k_last[...] = gathered(k_moves, k_sum[me.z], k_z)
    y_moves = [wire.send(YOFF[d], k_last.at[me.at(YOFF[d]).y], kv_grad.at[me.y]) for d in (1, 2, 3)]
    kv_grad[me.y] = k_last[me.y]
    for copy in leaving:
        copy.wait_recv()
    sent.extend(leaving)
    gain_mine[...] = jnp.sum(gain_plane[...], axis=0)
    tok_moves = [wire.send(off, gain_mine, gain_toks.at[me.tok]) for off in TOKS[1:]]
    gain_toks[me.tok] = gain_mine[...]
    own = up_sum[0:4, :, :, 0:1024].reshape(shape)
    up_grad[...] = gathered(up_moves, own, up_x.reshape(3, *shape))
    finish(y_moves + tok_moves)
    gain_grad[...] = jnp.sum(gain_toks[...], axis=0)
    for copy in sent:
        copy.wait_send()
    o_pair.wait_send()
    q_pair.wait_send()
    k_pair.wait_send()


def back(vmem_ins, hbm_ins):
    vm = pl.BlockSpec(memory_space=pltpu.VMEM)
    hbm = pl.BlockSpec(memory_space=pltpu.HBM)
    outs = [
        SDS((ROWS, 128), BF),
        SDS((ROWS, 128), BF),
        SDS((256, 128), F32),
        SDS((4, 32, 128), F32),
        SDS((256, 128), F32),
        SDS((8, 16, 1024), F32),
        SDS((8, 16, 1024), F32),
        SDS((8, 16, 1024), F32),
        SDS((8, 128), F32),
    ]
    v = pltpu.VMEM
    return pl.pallas_call(
        back_body,
        name="back",
        out_shape=outs,
        in_specs=[vm] * len(vmem_ins) + [hbm] * len(hbm_ins),
        out_specs=[vm] * len(outs),
        scratch_shapes=[
            v((2, 2048, 128), F32),
            v((D, 768), BF),
            v((CHUNK, 512), BF),
            v((CHUNK, D), BF),
            v((CHUNK, D), BF),
            v((ROWS, 128), BF),
            v((ROWS, 128), BF),
            v((ROWS, 128), F32),
            v((3, 4, 2, 4, 16, 1024), BF),
            v((3, 8, 2, 16, 2048), BF),
            v((8, 2, 16, 2048), BF),
            v((2, 8, 2, 16, 2048), BF),
            v((2, 4, 2, 16, 2048), BF),
            v((2, 8, 2, 16, 2048), BF),
            v((4, 2, 4, 16, 1024), BF),
            v((8, 2, 16, 2048), BF),
            v((8, 2, 16, 2048), BF),
            v((3, 4, 2, 16, 1024), BF),
            v((3, 4, 2, 16, 1024), BF),
            v((3, 4, 2, 16, 1024), BF),
            v((CHUNK, 1024), BF),
            v((CHUNK, D), BF),
            v((3, SUB, D), BF),
            v((SUB, D), BF),
            v((8, D), F32),
            v((16, 8, 128), F32),
            v((8, 128), F32),
            v((8, 8, 128), F32),
        ]
        + [
            v((4, 2, 256, 512), BF),
            v((4, 256, 512), BF),
            v((3, 256, 128), BF),
            v((256, 512), BF),
            v((3, 256, 512), BF),
            v((4, 2, 256, 512), BF),
            v((4, 256, 512), BF),
            v((3, 256, 128), BF),
            v((256, 512), BF),
            v((3, 256, 512), BF),
            v((4, 2, 4, 2, 32, 256), BF),
            v((4, 4, 2, 32, 256), BF),
            v((3, 4, 4, 32, 128), BF),
            v((4, 4, 32, 128), BF),
            v((3, 4, 32, 128), BF),
            v((4, 32, 128), F32),
            pltpu.SemaphoreType.DMA((104,)),
            pltpu.SemaphoreType.DMA((104,)),
            pltpu.SemaphoreType.DMA((12,)),
        ],
        compiler_params=pltpu.CompilerParams(
            collective_id=15, has_side_effects=True, vmem_limit_bytes=60 * 2**20
        ),
        cost_estimate=pl.CostEstimate(flops=10**10, bytes_accessed=30 * 2**20, transcendentals=0),
    )(*vmem_ins, *hbm_ins)


def rope_table():
    halfway = HEAD_DIM // 2
    k = np.arange(halfway, dtype=np.float32)
    inverse = np.exp(-2.0 * k / HEAD_DIM * math.log(THETA)).astype(np.float32)
    wavelen = (2.0 * math.pi / inverse).astype(np.float32)
    scaled = inverse / np.float32(FACTOR)
    smooth = (INITIAL / wavelen - LOW_FACTOR) / (HIGH_FACTOR - LOW_FACTOR)
    middle = (1.0 - smooth) * scaled + smooth * inverse
    frequency = np.where(
        wavelen < INITIAL / HIGH_FACTOR,
        inverse,
        np.where(wavelen > INITIAL / LOW_FACTOR, scaled, middle),
    ).astype(np.float32)
    positions = np.concatenate([np.arange(512), np.arange(1024), np.arange(512)]).astype(np.float32)
    angles = (positions[:, None] * frequency[None, :]).astype(np.float32).astype(np.float64)
    return (
        np.tile(np.cos(angles).astype(np.float32), (1, 4)),
        np.tile(np.sin(angles).astype(np.float32), (1, 4)),
    )


def part(array, start, size, axis):
    return lax.dynamic_slice_in_dim(array, start, size, axis)


def contract_rows(left_side, right_side):
    return lax.dot_general(
        left_side, right_side, (((0,), (0,)), ((), ())), preferred_element_type=F32
    )


def contract_cols(left_side, right_side):
    return lax.dot_general(
        left_side, right_side, (((1,), (1,)), ((), ())), preferred_element_type=F32
    )


def multiply(left_side, right_side):
    return jnp.dot(left_side, right_side, preferred_element_type=F32)


class Wire:
    def __init__(self, me, send_sem, recv_sem):
        self.me, self.send_sem, self.recv_sem, self.used = me, send_sem, recv_sem, 0

    def send(self, off, src, dst):
        copy = pltpu.make_async_remote_copy(
            src_ref=src,
            dst_ref=dst,
            send_sem=self.send_sem.at[self.used],
            recv_sem=self.recv_sem.at[self.used],
            device_id=self.me.at(off).device(),
            device_id_type=MESH,
        )
        copy.start()
        self.used += 1
        return copy


def meet(me, offsets):
    barrier = pltpu.get_barrier_semaphore()
    for off in offsets:
        back = tuple(-v for v in off)
        pl.semaphore_signal(barrier, inc=1, device_id=me.at(back).device(), device_id_type=MESH)
    pl.semaphore_wait(barrier, len(offsets))


def finish(copies):
    for copy in copies:
        copy.wait()


ZOFF = [(0, d, 0, 0, 0) for d in range(4)]


def split_rows(count, size):
    return [slice(i * size, i * size + size) for i in range(count)]


def front_body(
    gain_row,
    attn_gain,
    table,
    len_ref,
    hidden,
    w_q,
    w_kv,
    out_grad,
    w_o,
    pieces,
    q,
    kv,
    in_mine,
    scale_mine,
    gains,
    grad_full,
    w_cat,
    w_attn_out,
    normed_out,
    piece0,
    piece1,
    piece3,
    w_attn,
    normed,
    full,
    lin,
    scales,
    send_sem,
    recv_sem,
    local_sem,
):
    me = whereami()
    wire = Wire(me, send_sem, recv_sem)
    chunk = rows(me.chunk * CHUNK, CHUNK)
    near = []

    def take(src, dst):
        near.append(pltpu.make_async_copy(src, dst, local_sem.at[len(near)]))
        near[-1].start()

    take(w_q, w_attn.at[:, 0:128])
    take(w_kv, w_attn.at[:, 512:640])
    take(w_o, w_cat.at[:, 0:128])
    take(hidden.at[chunk, :], full.at[:, lanes(me.block)])
    take(out_grad.at[chunk, :], grad_full.at[:, lanes(me.wide)])
    gains[me.block] = gain_row[...]
    meet(me, PLANE[1:] + [SIBLING, ZOFF[1], ZOFF[3]])

    def chunk_of(off):
        return rows(me.at(off).chunk * CHUNK, CHUNK)

    def spread(src, dst, column):
        return [wire.send(XOFF[k], src.at[chunk_of(XOFF[k]), :], dst.at[:, column(k)]) for k in (1, 2, 3)]

    enter = spread(hidden, full, lambda k: lanes(me.block))
    ring = [wire.send(XOFF[k], pieces, piece0.at[:, k - 1]) for k in (1, 3)]
    half = rows(me.core * 1024, 1024)
    blocks = [w_attn.at[half, k * 128 : k * 128 + 128] for k in (1, 2, 3)]
    over_x = [wire.send(XOFF[k], w_q.at[half, :], blocks[k - 1]) for k in (1, 2, 3)]
    blocks.append(w_attn.at[half, 640:768])
    over_x.append(wire.send(XOFF[1], w_kv.at[half, :], blocks[3]))
    others = [wire.send(off, gain_row, gains.at[me.block]) for off in PLANE[1:]]

    def pass_on(ref):
        out = []
        for h in range(2):
            cols = lanes(h * 4 + me.y, 256)
            out += [wire.send(off, ref.at[:, cols], ref.at[:, cols]) for off in YOFF[1:]]
        return out

    def over_z(k):
        return [
            wire.send(ZOFF[1], piece0.at[:, k - 1], piece1.at[:, k - 1]),
            wire.send(ZOFF[3], piece0.at[:, k - 1], piece3.at[:, k - 1]),
        ]

    for copy in near:
        copy.wait()
    for copy in enter:
        copy.wait_recv()
    over_y = pass_on(full)
    ring[0].wait_recv()
    ring_pass = [wire.send(XOFF[3], piece0.at[0, 0], piece0.at[0, 1])]
    others += over_z(1)
    ring[1].wait_recv()
    ring_pass.append(wire.send(XOFF[1], piece0.at[1, 2], piece0.at[1, 1]))
    others += over_z(3)
    grads = spread(out_grad, grad_full, lambda k: lanes(XOFF[k][2] * 8 + me.wide))
    over_core = []
    for copy, block in zip(over_x, blocks):
        copy.wait_recv()
        over_core.append(wire.send(SIBLING, block, block))
    for copy in over_y:
        copy.wait_recv()
    for part_rows in split_rows(4, SUB):
        value = full[part_rows, :].astype(F32)
        scale = lax.rsqrt(jnp.mean(value * value, axis=1, keepdims=True) + EPS)
        scales[part_rows, :] = scale
        normed[part_rows, :] = (value * scale * attn_gain[...]).astype(BF)
    for copy in over_core:
        copy.wait_recv()
    lane = lax.broadcasted_iota(jnp.int32, (CHUNK, 128), 1)
    first, later = rows(me.chunk * CHUNK, CHUNK), pl.ds(me.chunk * CHUNK + SHORT, CHUNK)
    short_first = len_ref[0:1, 0:1] == SHORT
    cosine, sine = [jnp.where(short_first, table[j, first], table[j, later]) for j in range(2)]
    for j in range(3):
        pair = multiply(normed[...], w_attn[:, j * 256 : j * 256 + 256])
        for k in (2 * j, 2 * j + 1):
            block = pair[:, k % 2 * 128 : k % 2 * 128 + 128]
            swapped = jnp.where(
                (lane % 64) < 32, -pltpu.roll(block, 96, 1), pltpu.roll(block, 32, 1)
            )
            turned = block * cosine + swapped * sine
            if k >= 4:
                turned = jnp.where(lane < 64, turned, block)
            lin[:, k * 128 : k * 128 + 128] = turned.astype(BF)
    moves = []
    for k in (1, 2, 3):
        kv_col = 512 + 128 * XOFF[k][2]
        moves.append(wire.send(XOFF[k], lin.at[:, k * 128 : k * 128 + 128], q.at[chunk, :]))
        moves.append(wire.send(XOFF[k], lin.at[:, kv_col : kv_col + 128], kv.at[chunk, :]))
    out_blocks = [w_cat.at[half, k * 128 : k * 128 + 128] for k in (1, 2, 3)]
    out_x = [wire.send(XOFF[k], w_o.at[half, :], out_blocks[k - 1]) for k in (1, 2, 3)]
    q[chunk, :] = lin[:, 0:128]
    kv[chunk, :] = lin[:, 512:640]
    for copy in ring_pass:
        copy.wait_recv()
    others += over_z(2)
    for copy in grads:
        copy.wait_recv()
    others += pass_on(grad_full)
    for copy, block in zip(out_x, out_blocks):
        copy.wait_recv()
        over_core.append(wire.send(SIBLING, block, block))
        others.append(over_core[-1])
    take(w_attn, w_attn_out)
    take(normed, normed_out)
    here = rows(me.y * SUB, SUB)
    in_mine[...] = full[here, :]
    scale_mine[...] = scales[here, :]
    for copy in over_x + enter + ring + ring_pass + grads + over_y + out_x + over_core[:4]:
        copy.wait_send()
    finish(others + moves + near[-2:])


def front(gain_row, attn_gain, table, lengths, hidden, w_q, w_kv, out_grad, w_o, pieces):
    vm = pl.BlockSpec(memory_space=pltpu.VMEM)
    hbm = pl.BlockSpec(memory_space=pltpu.HBM)
    outs = [
        SDS((ROWS, 128), BF),
        SDS((ROWS, 128), BF),
        SDS((SUB, D), BF),
        SDS((SUB, 1), F32),
        SDS((16, 8, 128), F32),
        SDS((CHUNK, D), BF),
        SDS((D, 512), BF),
        SDS((D, 768), BF),
        SDS((CHUNK, D), BF),
        SDS((2, 3, 3, 64, 1024), BF),
        SDS((2, 3, 3, 64, 1024), BF),
        SDS((2, 3, 3, 64, 1024), BF),
    ]
    return pl.pallas_call(
        front_body,
        name="front",
        out_shape=outs,
        in_specs=[vm] * 4 + [hbm] * 6,
        out_specs=[vm] * 7 + [hbm] * 5,
        scratch_shapes=[
            pltpu.VMEM((D, 768), BF),
            pltpu.VMEM((CHUNK, D), BF),
            pltpu.VMEM((CHUNK, D), BF),
            pltpu.VMEM((CHUNK, 768), BF),
            pltpu.VMEM((CHUNK, 1), F32),
            pltpu.SemaphoreType.DMA((72,)),
            pltpu.SemaphoreType.DMA((72,)),
            pltpu.SemaphoreType.DMA((7,)),
        ],
        compiler_params=pltpu.CompilerParams(
            collective_id=0, has_side_effects=True, vmem_limit_bytes=60 * 2**20
        ),
        cost_estimate=pl.CostEstimate(flops=2 * 10**9, bytes_accessed=2**23, transcendentals=0),
    )(gain_row, attn_gain, table, lengths, hidden, w_q, w_kv, out_grad, w_o, pieces)


def middle_body(
    heads,
    in_mine,
    gain,
    w_cat,
    piece1,
    piece3,
    heads_cat,
    resid,
    scale_out,
    ffn_mine,
    piece2_first,
    piece2_second,
    term_send,
    term_recv,
    send_sem,
    recv_sem,
):
    me = whereami()
    wire = Wire(me, send_sem, recv_sem)
    meet(me, XOFF[1:] + YOFF[1:] + [ZOFF[1], ZOFF[3]])
    weights = [
        wire.send(ZOFF[1], piece1.at[0, 0], piece2_first),
        wire.send(ZOFF[3], piece3.at[1, 0], piece2_second),
    ]
    moves = [
        wire.send(
            XOFF[k],
            heads.at[rows(me.at(XOFF[k]).chunk * CHUNK, CHUNK), :],
            heads_cat.at[:, k * 128 : k * 128 + 128],
        )
        for k in (1, 2, 3)
    ]
    heads_cat[:, 0:128] = heads[rows(me.chunk * CHUNK, CHUNK), :]
    finish(moves)
    sums = []
    for h in range(2):
        for p in range(2):
            cols = slice(h * 1024 + p * 512, h * 1024 + p * 512 + 512)
            term_send[:, cols] = contract_cols(heads_cat[...], w_cat[cols, :]).astype(BF)
        cols = slice(h * 1024, h * 1024 + 1024)
        for d in (1, 2, 3):
            there = rows(me.at(YOFF[d]).y * SUB, SUB)
            sums.append(
                wire.send(YOFF[d], term_send.at[there, cols], term_recv.at[d - 1, :, cols])
            )
    finish(sums)
    value = in_mine[...].astype(F32) + term_send[rows(me.y * SUB, SUB), :].astype(F32)
    for d in range(3):
        value = value + term_recv[d].astype(F32)
    resid[...] = value
    scale = lax.rsqrt(jnp.mean(value * value, axis=1, keepdims=True) + EPS)
    scale_out[...] = scale
    ffn_mine[...] = (value * scale * gain[...]).astype(BF)
    finish(weights)


def middle(heads, in_mine, gain, w_cat, piece1, piece3):
    vm = pl.BlockSpec(memory_space=pltpu.VMEM)
    hbm = pl.BlockSpec(memory_space=pltpu.HBM)
    outs = [SDS((CHUNK, 512), BF), SDS((SUB, D), F32), SDS((SUB, 1), F32), SDS((SUB, D), BF)]
    outs += [SDS((3, 64, 1024), BF)] * 2
    return pl.pallas_call(
        middle_body,
        name="middle",
        out_shape=outs,
        in_specs=[vm] * 4 + [hbm] * 2,
        out_specs=[vm] * 4 + [hbm] * 2,
        scratch_shapes=[
            pltpu.VMEM((CHUNK, D), BF),
            pltpu.VMEM((3, SUB, D), BF),
            pltpu.SemaphoreType.DMA((13,)),
            pltpu.SemaphoreType.DMA((13,)),
        ],
        compiler_params=pltpu.CompilerParams(
            collective_id=1, has_side_effects=True, vmem_limit_bytes=60 * 2**20
        ),
        cost_estimate=pl.CostEstimate(flops=10**9, bytes_accessed=2**23, transcendentals=0),
    )(heads, in_mine, gain, w_cat, piece1, piece3)


class PairSum:
    def __init__(self, me, left, right, own, came, stage, send_sem, recv_sem):
        self.me, self.left, self.right, self.own, self.came = me, left, right, own, came
        self.stage, self.send_sem, self.recv_sem = stage, send_sem, recv_sem

    def copy(self, i):
        return pltpu.make_async_remote_copy(
            src_ref=self.stage.at[i % 3, :, :, 1 - self.me.core],
            dst_ref=self.came.at[i],
            send_sem=self.send_sem.at[i],
            recv_sem=self.recv_sem.at[i],
            device_id=self.me.at(SIBLING).device(),
            device_id_type=MESH,
        )

    def multiply(self, first, last):
        def step(i, _):
            cols = pl.ds(pl.multiple_of(i * 256, 256), 256)

            @pl.when(i >= first + 3)
            def _():
                self.copy(i - 3).wait_send()

            block = contract_rows(self.left[:, cols], self.right[...])
            self.stage[i % 3] = block.astype(BF).reshape(2, 4, 2, 16, 2048)
            self.own[i] = self.stage[i % 3, :, :, self.me.core]
            self.copy(i).start()
            return 0

        lax.fori_loop(first, last, step, 0)
        for i in range(last - 3, last):
            self.copy(i).wait_send()

    def add(self, first, last):
        def step(i, _):
            self.copy(i).wait_recv()
            self.own[i] = (self.own[i].astype(F32) + self.came[i].astype(F32)).astype(BF)
            return 0

        lax.fori_loop(first, last, step, 0)


def add_to(target, came):
    for i in range(came.shape[0]):
        target[i] = (target[i].astype(F32) + came[i].astype(F32)).astype(BF)


def ffn_body(
    mine_ref,
    grad_ref,
    resid_ref,
    scale_ref,
    gain_ref,
    w_out_ref,
    own_gate,
    own_up,
    own_down,
    piece0,
    piece1,
    piece2_first,
    piece2_second,
    piece3,
    out_mine,
    resid_back,
    gain_part,
    mix_full,
    heads_back,
    down_own,
    down_came,
    gate_own,
    gate_came,
    up_own,
    up_late,
    up_pass,
    other_core,
    rest_first,
    rest_second,
    turned,
    ffn_in,
    act,
    gate_back,
    up_back,
    gate_tile,
    up_tile,
    down_tile,
    down_acc,
    ffn_acc,
    down_send,
    ffn_send,
    down_recv,
    ffn_recv,
    mix_mine,
    back_cat,
    down_terms,
    gate_terms,
    up_terms,
    stage,
    came,
    down_pass,
    gate_pass,
    send_sem,
    recv_sem,
    core_send,
    core_recv,
    tile_sem,
    local_sem,
    ack,
):
    me = whereami()
    wire = Wire(me, send_sem, recv_sem)
    half = [lanes(me.xl, 1024), lanes(1 - me.xl, 1024)]
    here = rows(me.y * SUB, SUB)

    def piece(d, k):
        return {0: piece0, 1: piece1, 3: piece3}[d].at[:, k - 1]

    rest = (rest_first, rest_second)

    def opposite(h, k):
        return (piece2_first, piece2_second)[h] if k == 1 else rest[h].at[k - 2]


    def tile_copies(e, q, slot):
        copies, groups = [], []
        cols = pl.ds(pl.multiple_of(q * 256, 256), 256)

        def copy(src, dst):
            sem = tile_sem.at[slot, len(copies) + len(groups)]
            return pltpu.make_async_copy(src, dst, sem)

        for dxl in range(2):
            k = e * 2 + dxl
            for j, (own, tile) in enumerate(((own_gate, gate_tile), (own_up, up_tile))):
                if k == 0:
                    copies.append(copy(own.at[:, :, :, :, cols], tile.at[slot, dxl]))
                    continue
                for d in range(4):
                    spot = tile.at[slot, dxl, (me.z - d + 4) % 4, me.core]
                    if d != 2:
                        copies.append(copy(piece(d, k).at[:, j, :, cols], spot))
                        continue
                    for h in range(2):
                        copies.append(copy(opposite(h, k).at[j, :, cols], spot.at[h]))
                spot = tile.at[slot, dxl, :, 1 - me.core]
                copies.append(copy(other_core.at[:, :, k - 1, j, :, cols], spot))
            here = slice(dxl * 1024, dxl * 1024 + 1024)
            if k == 0:
                copies.append(copy(own_down.at[q], down_tile.at[slot, :, :, :, here]))
                continue
            spot = down_tile.at[slot, 1 - me.core, :, :, here]
            copies.append(copy(other_core.at[q, :, k - 1, 2], spot))
            for h in range(2):
                spot = down_tile.at[slot, me.core, h, :, here]
                groups.append(
                    [
                        copy(opposite(h, k).at[2] if d == 2 else piece(d, k).at[h, 2], spot)
                        for d in range(4)
                    ]
                )
        return copies, groups

    def fetch(e, q, slot):
        copies, groups = tile_copies(e, q, slot)
        for copy in copies:
            copy.start()
        for group in groups:
            for d, copy in enumerate(group):
                pl.when((me.z - q + 4) % 4 == d)(copy.start)

    def arrive(e, q, slot):
        copies, groups = tile_copies(e, q, slot)
        for copy in copies + [group[0] for group in groups]:
            copy.wait()

    meet(me, YOFF[1:] + XOFF[1:] + ZOFF[1:] + [SIBLING])
    for h in range(2):
        turned[:, h * 1024 : h * 1024 + 1024] = mine_ref[:, half[h]]
    gathers = [wire.send(off, turned, ffn_in.at[here, :]) for off in YOFF[1:]]
    passed = []
    for k in (2, 3):
        passed.append(wire.send(ZOFF[1], piece(1, k).at[0], rest_first.at[k - 2]))
        passed.append(wire.send(ZOFF[3], piece(3, k).at[1], rest_second.at[k - 2]))

    def share(k, parts):
        moves = []
        for d in parts:
            spot = other_core.at[(me.z - d + 4) % 4, :, k - 1]
            if d != 2:
                moves.append(wire.send(SIBLING, piece(d, k), spot))
                continue
            for h in range(2):
                moves.append(wire.send(SIBLING, opposite(h, k), spot.at[h]))
        return moves

    shares = share(1, range(4))
    late_shares = share(2, (0, 1, 3)) + share(3, (0, 1, 3))
    ffn_in[here, :] = turned[...]
    down_acc[...] = jnp.zeros(down_acc.shape, F32)
    ffn_acc[...] = jnp.zeros(ffn_acc.shape, F32)
    finish(shares)
    fetch(0, 0, 0)
    finish(gathers)
    finish(passed)
    late_shares += share(2, (2,)) + share(3, (2,))

    sums = []
    for left, right, own in (
        (act, grad_ref, down_terms),
        (ffn_in, gate_back, gate_terms),
        (ffn_in, up_back, up_terms),
    ):
        j = len(sums)
        sums.append(PairSum(me, left, right, own, came, stage, core_send.at[j], core_recv.at[j]))
    down_sum, gate_sum, up_sum = sums

    def came_free():
        pl.semaphore_signal(ack, inc=1, device_id=me.at(SIBLING).device(), device_id_type=MESH)
        pl.semaphore_wait(ack, 1)

    for e in range(2):

        def step(q, _, e=e):
            slot = q % 2

            @pl.when(q < 3)
            def _():
                fetch(e, q + 1, 1 - slot)

            arrive(e, q, slot)
            cols = pl.ds(pl.multiple_of(e * 1024 + q * 256, 256), 256)
            w_g = gate_tile[slot].reshape(2048, 256)
            w_u = up_tile[slot].reshape(2048, 256)
            w_d = down_tile[slot].reshape(256, 2048)
            gate = multiply(ffn_in[...], w_g)
            up = multiply(ffn_in[...], w_u)
            act_back = contract_cols(grad_ref[...], w_d)
            sigmoid = jax.nn.sigmoid(gate)
            silu = gate * sigmoid
            act_here = (silu * up).astype(BF)
            act[:, cols] = act_here
            down_acc[...] += multiply(act_here, w_d)
            g_back = (act_back * up * sigmoid * (1.0 + gate * (1.0 - sigmoid))).astype(BF)
            u_back = (act_back * silu).astype(BF)
            gate_back[:, cols] = g_back
            up_back[:, cols] = u_back
            ffn_acc[...] += contract_cols(g_back, w_g) + contract_cols(u_back, w_u)
            return 0

        lax.fori_loop(0, 4, step, 0)
        if e == 0:
            finish(late_shares)
            fetch(1, 0, 0)
            down_sum.multiply(0, 4)

    ffn_send[...] = ffn_acc[...].astype(BF)
    ffn_moves = [
        wire.send(YOFF[d], ffn_send.at[rows(me.at(YOFF[d]).y * SUB, SUB), :], ffn_recv.at[d - 1])
        for d in (1, 2, 3)
    ]
    down_sum.multiply(4, 8)


    def down_block(k, h=None):
        e, dxl = XOFF[k][4], XOFF[k][2]
        pairs = slice(e * 4, e * 4 + 4) if h is None else slice(e * 4 + h * 2, e * 4 + h * 2 + 2)
        return down_terms.at[pairs, :, :, :, dxl * 1024 : dxl * 1024 + 1024]

    down_sum.add(0, 8)
    x_moves = [
        wire.send(XOFF[1], down_block(2, 0), down_pass.at[0]),
        wire.send(XOFF[3], down_block(2, 1), down_pass.at[1]),
        wire.send(XOFF[1], down_block(1, 0), down_came.at[0, 0:2]),
        wire.send(XOFF[3], down_block(3, 1), down_came.at[1, 2:4]),
    ]
    near = []

    def keep(src, dst):
        near.append(pltpu.make_async_copy(src, dst, local_sem.at[len(near)]))
        near[-1].start()

    keep(down_block(0), down_own)

    def z_block(terms, d, h=None):
        pairs = slice(0, 8) if h is None else slice(h * 4, h * 4 + 4)
        return terms.at[pairs, :, (me.z + d) % 4]

    came_free()
    gate_sum.multiply(0, 8)
    gate_sum.add(0, 4)
    z_moves = [
        wire.send(ZOFF[1], z_block(gate_terms, 2, 0), gate_pass.at[0]),
        wire.send(ZOFF[3], z_block(gate_terms, 3, 0), gate_came.at[1, 0:4]),
    ]
    gate_sum.add(4, 8)
    z_moves += [
        wire.send(ZOFF[3], z_block(gate_terms, 2, 1), gate_pass.at[1]),
        wire.send(ZOFF[1], z_block(gate_terms, 1, 1), gate_came.at[0, 4:8]),
    ]
    keep(z_block(gate_terms, 0), gate_own)

    finish(ffn_moves)

    def summed(send, recv, h):
        cols = slice(h * 1024, h * 1024 + 1024)
        out = send[here, cols].astype(F32)
        for d in range(3):
            out = out + recv[d, :, cols].astype(F32)
        return out

    scale = scale_ref[...]
    inner = jnp.zeros((SUB, 1), F32)
    for h in range(2):
        back = summed(ffn_send, ffn_recv, h)
        weighed = back * resid_ref[:, half[h]]
        inner = inner + jnp.sum(weighed * gain_ref[:, half[h]], axis=1, keepdims=True)
        gain_part[:, half[h]] = jnp.sum(weighed * scale, axis=0, keepdims=True)
    pull = scale * scale * scale * inner / D
    for h in range(2):
        back = summed(ffn_send, ffn_recv, h)
        grad = grad_ref[here, h * 1024 : h * 1024 + 1024].astype(F32)
        total_back = grad + scale * gain_ref[:, half[h]] * back - resid_ref[:, half[h]] * pull
        resid_back[:, half[h]] = total_back
        mix_mine[:, half[h]] = total_back.astype(BF)
    mix_full[here, :] = mix_mine[...]
    mix_moves = [wire.send(off, mix_mine, mix_full.at[here, :]) for off in YOFF[1:]]

    down_send[...] = down_acc[...].astype(BF)
    down_moves = [
        wire.send(YOFF[d], down_send.at[rows(me.at(YOFF[d]).y * SUB, SUB), :], down_recv.at[d - 1])
        for d in (1, 2, 3)
    ]
    x_moves[0].wait_recv()
    add_to(down_block(3, 0), down_pass.at[0])
    x_late = [wire.send(XOFF[3], down_block(3, 0), down_came.at[1, 0:2])]
    x_moves[1].wait_recv()
    add_to(down_block(1, 1), down_pass.at[1])
    x_late.append(wire.send(XOFF[1], down_block(1, 1), down_came.at[0, 2:4]))
    came_free()
    up_sum.multiply(0, 8)
    z_moves[0].wait_recv()
    add_to(z_block(gate_terms, 1, 0), gate_pass.at[0])
    z_late = [wire.send(ZOFF[1], z_block(gate_terms, 1, 0), gate_came.at[0, 0:4])]
    z_moves[2].wait_recv()
    add_to(z_block(gate_terms, 3, 1), gate_pass.at[1])
    z_late.append(wire.send(ZOFF[3], z_block(gate_terms, 3, 1), gate_came.at[1, 4:8]))
    up_sum.add(0, 8)
    z_late += [
        wire.send(ZOFF[1], z_block(up_terms, 2, 0), up_pass.at[0]),
        wire.send(ZOFF[3], z_block(up_terms, 2, 1), up_pass.at[1]),
    ]
    keep(z_block(up_terms, 0), up_own)
    keep(z_block(up_terms, 1), up_late.at[0])
    keep(z_block(up_terms, 3), up_late.at[1])

    finish(mix_moves)
    back_cat[...] = multiply(mix_full[...], w_out_ref[...]).astype(BF)
    spot = rows(me.chunk * CHUNK, CHUNK)
    head_moves = [
        wire.send(XOFF[k], back_cat.at[:, k * 128 : k * 128 + 128], heads_back.at[spot, :])
        for k in (1, 2, 3)
    ]
    heads_back[spot, :] = back_cat[:, 0:128]
    finish(down_moves)
    for h in range(2):
        out_mine[:, half[h]] = (resid_ref[:, half[h]] + summed(down_send, down_recv, h)).astype(BF)
    for move in (x_moves[0], x_moves[1], z_moves[0], z_moves[2]):
        move.wait_send()
    finish(head_moves + x_moves[2:] + [z_moves[1], z_moves[3]] + x_late + z_late)
    for copy in near:
        copy.wait()


def ffn(ffn_mine, grad_full, resid, scale_two, gain, w_out, w_gate, w_up, w_down, pieces):
    vm = pl.BlockSpec(memory_space=pltpu.VMEM)
    hbm = pl.BlockSpec(memory_space=pltpu.HBM)
    return pl.pallas_call(
        ffn_body,
        name="ffn",
        out_shape=[
            SDS((SUB, D), BF),
            SDS((SUB, D), F32),
            SDS((1, D), F32),
            SDS((CHUNK, D), BF),
            SDS((ROWS, 128), BF),
            SDS((4, 2, 4, 16, 1024), BF),
            SDS((2, 4, 2, 4, 16, 1024), BF),
            SDS((8, 2, 16, 2048), BF),
            SDS((2, 8, 2, 16, 2048), BF),
            SDS((8, 2, 16, 2048), BF),
            SDS((2, 8, 2, 16, 2048), BF),
            SDS((2, 4, 2, 16, 2048), BF),
            SDS((4, 2, 3, 3, 64, 1024), BF),
            SDS((2, 3, 64, 1024), BF),
            SDS((2, 3, 64, 1024), BF),
        ],
        in_specs=[vm] * 6 + [hbm] * 8,
        out_specs=[vm] * 5 + [hbm] * 10,
        scratch_shapes=[
            pltpu.VMEM((SUB, D), BF),
            pltpu.VMEM((CHUNK, D), BF),
            pltpu.VMEM((CHUNK, D), BF),
            pltpu.VMEM((CHUNK, D), BF),
            pltpu.VMEM((CHUNK, D), BF),
            pltpu.VMEM((2, 2, 4, 2, 2, 64, 256), BF),
            pltpu.VMEM((2, 2, 4, 2, 2, 64, 256), BF),
            pltpu.VMEM((2, 2, 2, 64, 2048), BF),
            pltpu.VMEM((CHUNK, D), F32),
            pltpu.VMEM((CHUNK, D), F32),
            pltpu.VMEM((CHUNK, D), BF),
            pltpu.VMEM((CHUNK, D), BF),
            pltpu.VMEM((3, SUB, D), BF),
            pltpu.VMEM((3, SUB, D), BF),
            pltpu.VMEM((SUB, D), BF),
            pltpu.VMEM((CHUNK, 512), BF),
            pltpu.VMEM((8, 2, 4, 16, 2048), BF),
            pltpu.VMEM((8, 2, 4, 16, 2048), BF),
            pltpu.VMEM((8, 2, 4, 16, 2048), BF),
            pltpu.VMEM((3, 2, 4, 2, 16, 2048), BF),
            pltpu.VMEM((8, 2, 4, 16, 2048), BF),
            pltpu.VMEM((2, 2, 2, 4, 16, 1024), BF),
            pltpu.VMEM((2, 4, 2, 16, 2048), BF),
            pltpu.SemaphoreType.DMA((64,)),
            pltpu.SemaphoreType.DMA((64,)),
            pltpu.SemaphoreType.DMA((3, 8)),
            pltpu.SemaphoreType.DMA((3, 8)),
            pltpu.SemaphoreType.DMA((2, 32)),
            pltpu.SemaphoreType.DMA((6,)),
            pltpu.SemaphoreType.REGULAR,
        ],
        compiler_params=pltpu.CompilerParams(
            collective_id=14, has_side_effects=True, vmem_limit_bytes=60 * 2**20
        ),
        cost_estimate=pl.CostEstimate(flops=26 * 10**9, bytes_accessed=40 * 2**20, transcendentals=0),
    )(
        ffn_mine,
        grad_full,
        resid,
        scale_two,
        gain,
        w_out,
        w_gate.reshape(4, 2, 2, 64, 1024),
        w_up.reshape(4, 2, 2, 64, 1024),
        w_down.reshape(4, 2, 2, 64, 1024),
        *pieces,
    )


def per_device(
    layer_input,
    doc_lengths,
    attn_gain,
    w_query,
    w_key,
    w_value,
    w_output,
    ffn_gain,
    w_gate,
    w_up,
    w_down,
    output_grad,
):
    me = whereami()
    cos_np, sin_np = rope_table()
    table_all = jnp.asarray(np.stack([cos_np, sin_np]))
    lengths = jnp.broadcast_to(doc_lengths[0, 0], (8, 128))

    w_kv = jnp.concatenate(
        [part(w_key, me.y * 64, 64, 1), part(w_value, me.y * 64, 64, 1)], axis=1
    )
    pieces = jnp.stack([part(w, me.tok * 128, 128, 0) for w in (w_gate, w_up, w_down)])
    pieces = jnp.moveaxis(pieces.reshape(3, 2, 64, 1024), 1, 0)
    queries, kv, in_mine, scale_mine, gains, grad_full, w_out, w_attn, normed, *passed = front(
        jnp.broadcast_to(ffn_gain[None, :], (8, 128)),
        attn_gain[None, :],
        table_all,
        lengths,
        layer_input,
        w_query,
        w_kv,
        output_grad,
        w_output,
        pieces,
    )
    ffn_gain_all = gains[:, 0, :].reshape(1, D)
    (heads_out,) = vmem_call(
        "attend", attend_body, [doc_lengths, queries, kv], [SDS((ROWS, 128), BF)], flops=2 * 10**10
    )
    heads_cat, resid, scale_two, ffn_mine, *opposite = middle(
        heads_out, in_mine, ffn_gain_all, w_out, *passed[1:]
    )
    pieces = [*passed[:2], *opposite, passed[2]]
    (
        out_mine,
        resid_back,
        ffn_gain_part,
        mix_full,
        heads_back,
        *ffn_sums,
        _,
        _,
        _,
    ) = ffn(
        ffn_mine, grad_full, resid, scale_two, ffn_gain_all, w_out, w_gate, w_up, w_down, pieces
    )

    (
        layer_output,
        input_grad,
        query_grad,
        kv_grad,
        output_proj_grad,
        gate_grad,
        up_grad,
        down_grad,
        gain_grads,
    ) = back(
        [
            lengths,
            queries,
            kv,
            heads_back,
            out_mine,
            in_mine,
            resid_back,
            scale_mine,
            attn_gain[None, :],
            ffn_gain_part,
        ],
        [table_all, w_attn, heads_cat, normed, mix_full, *ffn_sums],
    )
    kv_cols = jnp.moveaxis(kv_grad, 0, 1).reshape(32, 4, 2, 64)
    key_grad = kv_cols[:, :, 0, :].reshape(32, 256)
    value_grad = kv_cols[:, :, 1, :].reshape(32, 256)
    gain_grads = part(gain_grads, me.tok * 16, 16, 1)
    return (
        layer_output,
        input_grad,
        gain_grads[0:1],
        query_grad,
        key_grad,
        value_grad,
        output_proj_grad,
        gain_grads[1:2],
        gate_grad,
        up_grad,
        down_grad,
    )


def solution(mesh):
    in_specs = (
        P("tok", ("narrow", "wide")),
        P("tok", None),
        P(),
        P(None, ("narrow", "wide")),
        P(None, "narrow"),
        P(None, "narrow"),
        P(None, ("narrow", "wide")),
        P(("narrow", "wide")),
        P("narrow", "wide"),
        P("narrow", "wide"),
        P("wide", "narrow"),
        P("tok", ("narrow", "wide")),
    )
    out_specs = (
        P("tok", ("narrow", "wide")),
        P("tok", ("narrow", "wide")),
        P(("narrow", "wide"), "tok"),
        P("tok", ("narrow", "wide")),
        P(("tok", "wide"), "narrow"),
        P(("tok", "wide"), "narrow"),
        P("tok", ("narrow", "wide")),
        P(("narrow", "wide"), "tok"),
        P("narrow", "tok", "wide"),
        P("narrow", "tok", "wide"),
        P("wide", "tok", "narrow"),
    )
    return jax.shard_map(
        per_device, mesh=mesh, in_specs=in_specs, out_specs=out_specs, check_vma=False
    )
```

```python
import functools
import math

import jax
import jax.numpy as jnp
import numpy as np
from jax import lax
from jax.experimental import pallas as pl
from jax.experimental.pallas import tpu as pltpu
from jax.sharding import PartitionSpec as P

HEADS = 32
KV_HEADS = 8
HEAD_DIM = 64
GROUP = 128
EPS = 1e-05
THETA = 500000.0
FACTOR = 32.0
LOW_FACTOR = 1.0
HIGH_FACTOR = 4.0
INITIAL = 8192.0
NEG = -1e30

D = 2048
ROWS = 1536
CHUNK = 384
SUB = 96
SHORT = 512
BF = jnp.bfloat16
F32 = jnp.float32
MESH = pl.DeviceIdType.MESH
SDS = jax.ShapeDtypeStruct

HERE = (0, 0, 0, 0, 0)
XOFF = [(0, 0, 0, 0, 0), (0, 0, 1, 0, 0), (0, 0, 0, 0, 1), (0, 0, 1, 0, 1)]
YOFF = [(0, 0, 0, d, 0) for d in range(4)]
PLANE = [(0, 0, a, b, e) for b in range(4) for a in range(2) for e in range(2)]
SIBLING = (1, 0, 0, 0, 0)
TOKS = [(a, b, 0, 0, 0) for b in range(4) for a in range(2)]


class Place:
    def __init__(self, core, z, xl, y, xh):
        self.core, self.z, self.xl, self.y, self.xh = core, z, xl, y, xh
        self.tok = z * 2 + core
        self.wide = y * 2 + xh
        self.block = xl * 8 + self.wide
        self.chunk = xl * 2 + xh

    def at(self, off):
        return Place(
            (self.core + off[0]) % 2,
            (self.z + off[1]) % 4,
            (self.xl + off[2]) % 2,
            (self.y + off[3]) % 4,
            (self.xh + off[4]) % 2,
        )

    def device(self):
        return (self.tok, self.xl, self.wide)


def whereami():
    tok = lax.axis_index("tok")
    wide = lax.axis_index("wide")
    return Place(tok % 2, tok // 2, lax.axis_index("narrow"), wide // 2, wide % 2)


def rows(start, size):
    return pl.ds(pl.multiple_of(start, size), size)


def lanes(index, size=128):
    return pl.ds(pl.multiple_of(index * size, size), size)


def block_probs(q_ref, kv_ref, start, i, stack):
    n = 256 * (i + 1)
    keys = kv_ref[rows_256(start, n), 0:64]
    scores = lax.dot_general(
        keys, stack, (((1,), (1,)), ((), ())), preferred_element_type=F32
    ) * (HEAD_DIM**-0.5)
    last = scores[n - 256 :, :]
    key_id = lax.broadcasted_iota(jnp.int32, (256, 512), 0)
    query_id = lax.broadcasted_iota(jnp.int32, (256, 512), 1) % 256
    last = jnp.where(key_id <= query_id, last, NEG)
    if n > 256:
        scores = jnp.concatenate([scores[: n - 256, :], last], axis=0)
    else:
        scores = last
    raised = jnp.exp(scores - jnp.max(scores, axis=0, keepdims=True))
    return keys, raised, jnp.sum(raised, axis=0, keepdims=True)


def rows_256(start, size):
    return pl.ds(pl.multiple_of(start, 256), size)


def starts_of(len_ref):
    long_first = len_ref[0, 0] > SHORT
    long_start = jnp.where(long_first, 0, SHORT)
    short_start = jnp.where(long_first, 2 * SHORT, 0)
    return ((long_start, 4), (short_start, 2))


def both(block):
    return jnp.concatenate([block[:, 0:64], block[:, 64:128]], axis=0)


def attend_body(len_ref, q_ref, kv_ref, out_ref):
    for start, blocks in starts_of(len_ref):
        for i in range(blocks):
            mine = rows_256(start + 256 * i, 256)
            stack = both(q_ref[mine, :])
            keys, raised, mass = block_probs(q_ref, kv_ref, start, i, stack)
            soft = (raised * (1.0 / mass)).astype(BF)
            values = kv_ref[rows_256(start, 256 * (i + 1)), 64:128]
            mixed = lax.dot_general(
                soft, values, (((0,), (0,)), ((), ())), preferred_element_type=F32
            )
            out_ref[mine, :] = jnp.concatenate([mixed[:256], mixed[256:]], axis=1).astype(BF)


def unrope(tensor, cosine, sine):
    lane = lax.broadcasted_iota(jnp.int32, tensor.shape, 1)
    first = (lane % 64) < 32
    swapped = jnp.where(first, pltpu.roll(tensor, 96, 1), -pltpu.roll(tensor, 32, 1))
    return tensor * cosine + swapped * sine


def vmem_call(name, body, ins, outs, scratch=(), flops=0):
    return pl.pallas_call(
        body,
        name=name,
        out_shape=outs,
        in_specs=[pl.BlockSpec(memory_space=pltpu.SMEM)]
        + [pl.BlockSpec(memory_space=pltpu.VMEM)] * (len(ins) - 1),
        out_specs=[pl.BlockSpec(memory_space=pltpu.VMEM)] * len(outs),
        scratch_shapes=list(scratch),
        compiler_params=pltpu.CompilerParams(vmem_limit_bytes=60 * 2**20),
        cost_estimate=pl.CostEstimate(flops=flops, bytes_accessed=2**20, transcendentals=0),
    )(*ins)


def masked_scores(keys, query, i, length):
    n = keys.shape[0]
    scores = contract_cols(keys, query) * (HEAD_DIM**-0.5)
    key_id = lax.broadcasted_iota(jnp.int32, (256, 256), 0)
    query_id = lax.broadcasted_iota(jnp.int32, (256, 256), 1)
    parts = [jnp.where(key_id <= query_id, scores[n - 256 :, :], NEG)]
    middle = 0
    if i >= 2:
        cut = SHORT if i < 4 else 2 * SHORT
        middle = SHORT
        parts.insert(0, jnp.where(length == cut, NEG, scores[:SHORT, :]))
    if n - 256 > middle:
        parts.insert(len(parts) - 1, scores[middle : n - 256, :])
    return jnp.concatenate(parts, axis=0) if len(parts) > 1 else parts[0]


def back_body(
    len_ref,
    q_ref,
    kv_ref,
    heads_back,
    out_mine,
    in_mine,
    resid_back,
    scale_ref,
    gain_ref,
    ffn_gain_part,
    table_in,
    w_attn_in,
    heads_in,
    normed_in,
    mix_in,
    down_own,
    down_came,
    gate_own,
    gate_came,
    up_own,
    up_late,
    up_pass,
    layer_output,
    input_grad,
    query_grad,
    kv_grad,
    out_grad,
    gate_grad,
    up_grad,
    down_grad,
    gain_grad,
    table,
    w_attn,
    heads_cat,
    normed,
    mix_full,
    dq_ref,
    dkv_ref,
    dkv_acc,
    down_in,
    gate_in,
    up_in,
    late_in,
    pass_in,
    up_last,
    down_sum,
    gate_sum,
    up_sum,
    down_z,
    gate_x,
    up_x,
    cat_back,
    norm_send,
    norm_recv,
    in_grad,
    gain_parts,
    gain_plane,
    gain_mine,
    gain_toks,
    o_terms,
    o_core,
    o_x,
    o_sum,
    o_z,
    q_terms,
    q_core,
    q_x,
    q_sum,
    q_z,
    k_terms,
    k_core,
    k_x,
    k_sum,
    k_z,
    k_last,
    send_sem,
    recv_sem,
    local_sem,
):
    me = whereami()
    wire = Wire(me, send_sem, recv_sem)
    loads = []
    for src, dst in (
        (up_late, late_in),
        (up_pass, pass_in),
        (gate_own, gate_in.at[0]),
        (gate_came, gate_in.at[1:3]),
        (down_own, down_in.at[0]),
        (down_came, down_in.at[1:3]),
        (up_own, up_in),
        (table_in, table),
        (mix_in, mix_full),
        (heads_in, heads_cat),
        (w_attn_in, w_attn),
        (normed_in, normed),
    ):
        loads.append(pltpu.make_async_copy(src, dst, local_sem.at[len(loads)]))
        loads[-1].start()
    meet(me, PLANE[1:] + TOKS[1:])
    sent = []

    for copy in loads[0:2]:
        copy.wait()
    up_moves = [
        wire.send(ZOFF[1], late_in.at[0, 4:8], up_last.at[0, 4:8]),
        wire.send(ZOFF[3], late_in.at[1, 0:4], up_last.at[1, 0:4]),
    ]

    length = len_ref[0:1, 0:1]
    loads[7].wait()

    def turns(row, size):
        first, later = slice(row, row + size), slice(row + SHORT, row + SHORT + size)
        return [jnp.where(length == SHORT, table[j, first], table[j, later]) for j in range(2)]

    dkv_acc[...] = jnp.zeros(dkv_acc.shape, F32)
    for i in range(6):
        low, high = 0 if i < 4 else SHORT, 256 * (i + 1)
        here = slice(256 * i, high)
        keys, values = kv_ref[low:high, 0:64], kv_ref[low:high, 64:128]
        parts = []
        for head in (slice(0, 64), slice(64, 128)):
            query, value_back = q_ref[here, head], heads_back[here, head]
            scores = masked_scores(keys, query, i, length)
            raised = jnp.exp(scores - jnp.max(scores, axis=0, keepdims=True))
            soft = raised * (1.0 / jnp.sum(raised, axis=0, keepdims=True))
            prob_back = contract_cols(values, value_back)
            inner = jnp.sum(soft * prob_back, axis=0, keepdims=True)
            score_back = (soft * (prob_back - inner)).astype(BF)
            parts.append(contract_rows(score_back, keys) * (HEAD_DIM**-0.5))
            dk = multiply(score_back, query) * (HEAD_DIM**-0.5)
            dv = multiply(soft.astype(BF), value_back)
            dkv_acc[low:high, :] += jnp.concatenate([dk, dv], axis=1)
        dq = jnp.concatenate(parts, axis=1)
        dq_ref[here, :] = unrope(dq, *turns(256 * i, 256)).astype(BF)
    lane = lax.broadcasted_iota(jnp.int32, (256, 128), 1)
    for here in split_rows(6, 256):
        acc = dkv_acc[here, :]
        turned = unrope(acc, *turns(here.start, 256))
        dkv_ref[here, :] = jnp.where(lane < 64, turned, acc).astype(BF)

    spot = rows(me.chunk * CHUNK, CHUNK)
    moves = []
    for k in (1, 2, 3):
        there = rows(me.at(XOFF[k]).chunk * CHUNK, CHUNK)
        for ref, col in ((dq_ref, 0), (dkv_ref, 512)):
            moves.append(
                wire.send(
                    XOFF[k], ref.at[there, :], cat_back.at[:, col + k * 128 : col + k * 128 + 128]
                )
            )
    cat_back[:, 0:128] = dq_ref[spot, :]
    cat_back[:, 512:640] = dkv_ref[spot, :]

    mine = rows(me.chunk * CHUNK + me.y * SUB, SUB)
    leaving = [
        wire.send(off, out_mine.at[:, lanes(me.at(off).block)], layer_output.at[mine, :])
        for off in PLANE[1:]
    ]
    layer_output[mine, :] = out_mine[:, lanes(me.block)]

    add_to(late_in.at[0, 0:4], pass_in.at[0])
    up_moves.append(wire.send(ZOFF[1], late_in.at[0, 0:4], up_last.at[0, 0:4]))
    add_to(late_in.at[1, 4:8], pass_in.at[1])
    up_moves.append(wire.send(ZOFF[3], late_in.at[1, 4:8], up_last.at[1, 4:8]))

    def fold(ref, out):
        for n in range(out.shape[0]):
            value = ref[0, n].astype(F32)
            for k in range(1, ref.shape[0]):
                value = value + ref[k, n].astype(F32)
            out[n] = value.astype(BF)

    def x_blocks(ref, came):
        moves = []
        for k in (1, 2, 3):
            e, dxl = XOFF[k][4], XOFF[k][2]
            src = ref.at[dxl * 4 : dxl * 4 + 4, :, :, e * 1024 : e * 1024 + 1024]
            moves.append(wire.send(XOFF[k], src, came.at[k - 1]))
        return moves

    for copy in loads[2:7] + loads[8:]:
        copy.wait()
    fold(gate_in, gate_sum)
    gate_moves = x_blocks(gate_sum, gate_x)

    for z in range(4):
        block = contract_rows(mix_full[:, z * 512 : z * 512 + 512], heads_cat[...])
        o_terms[z] = block.astype(BF).reshape(2, 256, 512)
    o_pair = wire.send(SIBLING, o_terms.at[:, 1 - me.core], o_core)

    def add_core(copy, terms, came):
        copy.wait_recv()
        terms[:, me.core] = (terms[:, me.core].astype(F32) + came[...].astype(F32)).astype(BF)

    finish(moves)
    for h in range(4):
        cols = slice(h * 512, h * 512 + 512)
        term = contract_cols(cat_back[:, 0:768], w_attn[cols, :]) + contract_cols(
            cat_back[:, 768:1024], w_attn[cols, 512:768]
        )
        norm_send[:, cols] = term.astype(BF)
    norm_moves = [
        wire.send(YOFF[d], norm_send.at[rows(me.at(YOFF[d]).y * SUB, SUB), :], norm_recv.at[d - 1])
        for d in (1, 2, 3)
    ]

    add_core(o_pair, o_terms, o_core)
    o_moves = [
        wire.send(ZOFF[d], o_terms.at[(me.z + d) % 4, me.core], o_z.at[d - 1]) for d in (1, 2, 3)
    ]

    for z in range(4):
        block = contract_rows(normed[:, z * 512 : z * 512 + 512], cat_back[:, 0:512])
        q_terms[z] = block.astype(BF).reshape(2, 256, 512)
    q_pair = wire.send(SIBLING, q_terms.at[:, 1 - me.core], q_core)
    for z in range(4):
        left = normed[:, z * 512 : z * 512 + 512]
        block = contract_rows(left, cat_back[:, 512:768]) + contract_rows(
            left, cat_back[:, 768:1024]
        )
        k_terms[z] = block.astype(BF).reshape(2, 4, 2, 32, 256)
    k_pair = wire.send(SIBLING, k_terms.at[:, 1 - me.core], k_core)

    def kv_block(k):
        e, dxl = XOFF[k][4], XOFF[k][2]
        return k_terms.at[:, me.core, :, (me.xh + e) % 2, :, dxl * 128 : dxl * 128 + 128]

    add_core(k_pair, k_terms, k_core)
    k_moves = [wire.send(XOFF[k], kv_block(k), k_x.at[k - 1]) for k in (1, 2, 3)]
    add_core(q_pair, q_terms, q_core)
    q_moves = [
        wire.send(ZOFF[d], q_terms.at[(me.z + d) % 4, me.core], q_z.at[d - 1]) for d in (1, 2, 3)
    ]

    fold(down_in, down_sum)
    down_moves = [
        wire.send(ZOFF[d], down_sum.at[:, :, (me.z + d) % 4], down_z.at[d - 1]) for d in (1, 2, 3)
    ]

    def gathered(moves, own, came):
        for copy in moves:
            copy.wait_recv()
        sent.extend(moves)
        value = own.astype(F32)
        for d in range(came.shape[0]):
            value = value + came[d].astype(F32)
        return value

    for copy in up_moves:
        copy.wait_recv()
    sent.extend(up_moves)
    for n in range(8):
        value = up_in[n].astype(F32) + up_last[0, n].astype(F32)
        up_sum[n] = (value + up_last[1, n].astype(F32)).astype(BF)
    up_moves = x_blocks(up_sum, up_x)

    def over_x(ref, came):
        return [
            wire.send(XOFF[k], ref.at[:, k * 128 : k * 128 + 128], came.at[k - 1]) for k in (1, 2, 3)
        ]

    o_sum[...] = gathered(o_moves, o_terms[me.z, me.core], o_z).astype(BF)
    o_moves = over_x(o_sum, o_x)

    finish(norm_moves)
    here = rows(me.y * SUB, SUB)
    back = norm_send[here, :].astype(F32)
    for d in range(3):
        back = back + norm_recv[d].astype(F32)
    scale = scale_ref[...]
    enter = in_mine[...].astype(F32)
    weighed = back * enter
    inner = jnp.sum(weighed * gain_ref[...], axis=1, keepdims=True)
    gain_parts[0:1, :] = jnp.sum(weighed * scale, axis=0, keepdims=True)
    gain_parts[1:2, :] = ffn_gain_part[...]
    gain_parts[2:8, :] = jnp.zeros((6, D), F32)
    pull = scale * scale * scale * inner / D
    in_grad[...] = (resid_back[...] + scale * gain_ref[...] * back - enter * pull).astype(BF)
    for off in PLANE[1:]:
        there = lanes(me.at(off).block)
        leaving.append(wire.send(off, in_grad.at[:, there], input_grad.at[mine, :]))
        leaving.append(wire.send(off, gain_parts.at[:, there], gain_plane.at[me.block]))
    input_grad[mine, :] = in_grad[:, lanes(me.block)]
    gain_plane[me.block] = gain_parts[:, lanes(me.block)]

    k_sum[...] = gathered(k_moves, k_terms[:, me.core, :, me.xh, :, 0:128], k_x).astype(BF)
    k_moves = [wire.send(ZOFF[d], k_sum.at[(me.z + d) % 4], k_z.at[d - 1]) for d in (1, 2, 3)]
    q_sum[...] = gathered(q_moves, q_terms[me.z, me.core], q_z).astype(BF)
    q_moves = over_x(q_sum, q_x)

    shape = (8, 16, 1024)
    own = down_sum[:, :, me.z].reshape(shape)
    down_grad[...] = gathered(down_moves, own, down_z.reshape(3, *shape))
    own = gate_sum[0:4, :, :, 0:1024].reshape(shape)
    gate_grad[...] = gathered(gate_moves, own, gate_x.reshape(3, *shape))

    out_grad[...] = gathered(o_moves, o_sum[:, 0:128], o_x)
    query_grad[...] = gathered(q_moves, q_sum[:, 0:128], q_x)
    k_last[...] = gathered(k_moves, k_sum[me.z], k_z)
    y_moves = [wire.send(YOFF[d], k_last.at[me.at(YOFF[d]).y], kv_grad.at[me.y]) for d in (1, 2, 3)]
    kv_grad[me.y] = k_last[me.y]
    for copy in leaving:
        copy.wait_recv()
    sent.extend(leaving)
    gain_mine[...] = jnp.sum(gain_plane[...], axis=0)
    tok_moves = [wire.send(off, gain_mine, gain_toks.at[me.tok]) for off in TOKS[1:]]
    gain_toks[me.tok] = gain_mine[...]
    own = up_sum[0:4, :, :, 0:1024].reshape(shape)
    up_grad[...] = gathered(up_moves, own, up_x.reshape(3, *shape))
    finish(y_moves + tok_moves)
    gain_grad[...] = jnp.sum(gain_toks[...], axis=0)
    for copy in sent:
        copy.wait_send()
    o_pair.wait_send()
    q_pair.wait_send()
    k_pair.wait_send()


def back(vmem_ins, hbm_ins):
    vm = pl.BlockSpec(memory_space=pltpu.VMEM)
    hbm = pl.BlockSpec(memory_space=pltpu.HBM)
    outs = [
        SDS((ROWS, 128), BF),
        SDS((ROWS, 128), BF),
        SDS((256, 128), F32),
        SDS((4, 32, 128), F32),
        SDS((256, 128), F32),
        SDS((8, 16, 1024), F32),
        SDS((8, 16, 1024), F32),
        SDS((8, 16, 1024), F32),
        SDS((8, 128), F32),
    ]
    v = pltpu.VMEM
    return pl.pallas_call(
        back_body,
        name="back",
        out_shape=outs,
        in_specs=[vm] * len(vmem_ins) + [hbm] * len(hbm_ins),
        out_specs=[vm] * len(outs),
        scratch_shapes=[
            v((2, 2048, 128), F32),
            v((D, 768), BF),
            v((CHUNK, 512), BF),
            v((CHUNK, D), BF),
            v((CHUNK, D), BF),
            v((ROWS, 128), BF),
            v((ROWS, 128), BF),
            v((ROWS, 128), F32),
            v((3, 4, 2, 4, 16, 1024), BF),
            v((3, 8, 2, 16, 2048), BF),
            v((8, 2, 16, 2048), BF),
            v((2, 8, 2, 16, 2048), BF),
            v((2, 4, 2, 16, 2048), BF),
            v((2, 8, 2, 16, 2048), BF),
            v((4, 2, 4, 16, 1024), BF),
            v((8, 2, 16, 2048), BF),
            v((8, 2, 16, 2048), BF),
            v((3, 4, 2, 16, 1024), BF),
            v((3, 4, 2, 16, 1024), BF),
            v((3, 4, 2, 16, 1024), BF),
            v((CHUNK, 1024), BF),
            v((CHUNK, D), BF),
            v((3, SUB, D), BF),
            v((SUB, D), BF),
            v((8, D), F32),
            v((16, 8, 128), F32),
            v((8, 128), F32),
            v((8, 8, 128), F32),
        ]
        + [
            v((4, 2, 256, 512), BF),
            v((4, 256, 512), BF),
            v((3, 256, 128), BF),
            v((256, 512), BF),
            v((3, 256, 512), BF),
            v((4, 2, 256, 512), BF),
            v((4, 256, 512), BF),
            v((3, 256, 128), BF),
            v((256, 512), BF),
            v((3, 256, 512), BF),
            v((4, 2, 4, 2, 32, 256), BF),
            v((4, 4, 2, 32, 256), BF),
            v((3, 4, 4, 32, 128), BF),
            v((4, 4, 32, 128), BF),
            v((3, 4, 32, 128), BF),
            v((4, 32, 128), F32),
            pltpu.SemaphoreType.DMA((104,)),
            pltpu.SemaphoreType.DMA((104,)),
            pltpu.SemaphoreType.DMA((12,)),
        ],
        compiler_params=pltpu.CompilerParams(
            collective_id=15, has_side_effects=True, vmem_limit_bytes=60 * 2**20
        ),
        cost_estimate=pl.CostEstimate(flops=10**10, bytes_accessed=30 * 2**20, transcendentals=0),
    )(*vmem_ins, *hbm_ins)


def rope_table():
    halfway = HEAD_DIM // 2
    k = np.arange(halfway, dtype=np.float32)
    inverse = np.exp(-2.0 * k / HEAD_DIM * math.log(THETA)).astype(np.float32)
    wavelen = (2.0 * math.pi / inverse).astype(np.float32)
    scaled = inverse / np.float32(FACTOR)
    smooth = (INITIAL / wavelen - LOW_FACTOR) / (HIGH_FACTOR - LOW_FACTOR)
    middle = (1.0 - smooth) * scaled + smooth * inverse
    frequency = np.where(
        wavelen < INITIAL / HIGH_FACTOR,
        inverse,
        np.where(wavelen > INITIAL / LOW_FACTOR, scaled, middle),
    ).astype(np.float32)
    positions = np.concatenate([np.arange(512), np.arange(1024), np.arange(512)]).astype(np.float32)
    angles = (positions[:, None] * frequency[None, :]).astype(np.float32).astype(np.float64)
    return (
        np.tile(np.cos(angles).astype(np.float32), (1, 4)),
        np.tile(np.sin(angles).astype(np.float32), (1, 4)),
    )


def part(array, start, size, axis):
    return lax.dynamic_slice_in_dim(array, start, size, axis)


def contract_rows(left_side, right_side):
    return lax.dot_general(
        left_side, right_side, (((0,), (0,)), ((), ())), preferred_element_type=F32
    )


def contract_cols(left_side, right_side):
    return lax.dot_general(
        left_side, right_side, (((1,), (1,)), ((), ())), preferred_element_type=F32
    )


def multiply(left_side, right_side):
    return jnp.dot(left_side, right_side, preferred_element_type=F32)


class Wire:
    def __init__(self, me, send_sem, recv_sem):
        self.me, self.send_sem, self.recv_sem, self.used = me, send_sem, recv_sem, 0

    def send(self, off, src, dst):
        copy = pltpu.make_async_remote_copy(
            src_ref=src,
            dst_ref=dst,
            send_sem=self.send_sem.at[self.used],
            recv_sem=self.recv_sem.at[self.used],
            device_id=self.me.at(off).device(),
            device_id_type=MESH,
        )
        copy.start()
        self.used += 1
        return copy


def meet(me, offsets):
    barrier = pltpu.get_barrier_semaphore()
    for off in offsets:
        back = tuple(-v for v in off)
        pl.semaphore_signal(barrier, inc=1, device_id=me.at(back).device(), device_id_type=MESH)
    pl.semaphore_wait(barrier, len(offsets))


def finish(copies):
    for copy in copies:
        copy.wait()


ZOFF = [(0, d, 0, 0, 0) for d in range(4)]


def split_rows(count, size):
    return [slice(i * size, i * size + size) for i in range(count)]


def front_body(
    gain_row,
    attn_gain,
    table,
    len_ref,
    hidden,
    w_q,
    w_kv,
    out_grad,
    w_o,
    gate,
    up,
    down,
    q,
    kv,
    in_mine,
    scale_mine,
    gains,
    grad_full,
    w_cat,
    w_attn_out,
    normed_out,
    piece0,
    piece1,
    piece3,
    w_attn,
    normed,
    full,
    lin,
    scales,
    send_sem,
    recv_sem,
    local_sem,
):
    me = whereami()
    wire = Wire(me, send_sem, recv_sem)
    chunk = rows(me.chunk * CHUNK, CHUNK)
    near = []

    def take(src, dst):
        near.append(pltpu.make_async_copy(src, dst, local_sem.at[len(near)]))
        near[-1].start()

    take(w_q, w_attn.at[:, 0:128])
    take(w_kv, w_attn.at[:, 512:640])
    take(w_o, w_cat.at[:, 0:128])
    take(hidden.at[chunk, :], full.at[:, lanes(me.block)])
    take(out_grad.at[chunk, :], grad_full.at[:, lanes(me.wide)])
    gains[me.block] = gain_row[...]
    meet(me, PLANE[1:] + [SIBLING, ZOFF[1], ZOFF[3]])

    def chunk_of(off):
        return rows(me.at(off).chunk * CHUNK, CHUNK)

    def spread(src, dst, column):
        return [wire.send(XOFF[k], src.at[chunk_of(XOFF[k]), :], dst.at[:, column(k)]) for k in (1, 2, 3)]

    enter = spread(hidden, full, lambda k: lanes(me.block))
    ring = [
        wire.send(XOFF[k], weight.at[me.tok], piece0.at[:, k - 1, j])
        for k in (1, 3)
        for j, weight in enumerate((gate, up, down))
    ]
    half = rows(me.core * 1024, 1024)
    blocks = [w_attn.at[half, k * 128 : k * 128 + 128] for k in (1, 2, 3)]
    over_x = [wire.send(XOFF[k], w_q.at[half, :], blocks[k - 1]) for k in (1, 2, 3)]
    blocks.append(w_attn.at[half, 640:768])
    over_x.append(wire.send(XOFF[1], w_kv.at[half, :], blocks[3]))
    others = [wire.send(off, gain_row, gains.at[me.block]) for off in PLANE[1:]]

    def pass_on(ref):
        out = []
        for h in range(2):
            cols = lanes(h * 4 + me.y, 256)
            out += [wire.send(off, ref.at[:, cols], ref.at[:, cols]) for off in YOFF[1:]]
        return out

    def over_z(k):
        return [
            wire.send(ZOFF[1], piece0.at[:, k - 1], piece1.at[:, k - 1]),
            wire.send(ZOFF[3], piece0.at[:, k - 1], piece3.at[:, k - 1]),
        ]

    for copy in near:
        copy.wait()
    for copy in enter:
        copy.wait_recv()
    over_y = pass_on(full)
    for copy in ring[:3]:
        copy.wait_recv()
    ring_pass = [wire.send(XOFF[3], piece0.at[0, 0], piece0.at[0, 1])]
    others += over_z(1)
    for copy in ring[3:]:
        copy.wait_recv()
    ring_pass.append(wire.send(XOFF[1], piece0.at[1, 2], piece0.at[1, 1]))
    others += over_z(3)
    grads = spread(out_grad, grad_full, lambda k: lanes(XOFF[k][2] * 8 + me.wide))
    over_core = []
    for copy, block in zip(over_x, blocks):
        copy.wait_recv()
        over_core.append(wire.send(SIBLING, block, block))
    for copy in over_y:
        copy.wait_recv()
    for part_rows in split_rows(4, SUB):
        value = full[part_rows, :].astype(F32)
        scale = lax.rsqrt(jnp.mean(value * value, axis=1, keepdims=True) + EPS)
        scales[part_rows, :] = scale
        normed[part_rows, :] = (value * scale * attn_gain[...]).astype(BF)
    for copy in over_core:
        copy.wait_recv()
    lane = lax.broadcasted_iota(jnp.int32, (CHUNK, 128), 1)
    first, later = rows(me.chunk * CHUNK, CHUNK), pl.ds(me.chunk * CHUNK + SHORT, CHUNK)
    short_first = len_ref[0:1, 0:1] == SHORT
    cosine, sine = [jnp.where(short_first, table[j, first], table[j, later]) for j in range(2)]
    for j in range(3):
        pair = multiply(normed[...], w_attn[:, j * 256 : j * 256 + 256])
        for k in (2 * j, 2 * j + 1):
            block = pair[:, k % 2 * 128 : k % 2 * 128 + 128]
            swapped = jnp.where(
                (lane % 64) < 32, -pltpu.roll(block, 96, 1), pltpu.roll(block, 32, 1)
            )
            turned = block * cosine + swapped * sine
            if k >= 4:
                turned = jnp.where(lane < 64, turned, block)
            lin[:, k * 128 : k * 128 + 128] = turned.astype(BF)
    moves = []
    for k in (1, 2, 3):
        kv_col = 512 + 128 * XOFF[k][2]
        moves.append(wire.send(XOFF[k], lin.at[:, k * 128 : k * 128 + 128], q.at[chunk, :]))
        moves.append(wire.send(XOFF[k], lin.at[:, kv_col : kv_col + 128], kv.at[chunk, :]))
    out_blocks = [w_cat.at[half, k * 128 : k * 128 + 128] for k in (1, 2, 3)]
    out_x = [wire.send(XOFF[k], w_o.at[half, :], out_blocks[k - 1]) for k in (1, 2, 3)]
    q[chunk, :] = lin[:, 0:128]
    kv[chunk, :] = lin[:, 512:640]
    for copy in ring_pass:
        copy.wait_recv()
    others += over_z(2)
    for copy in grads:
        copy.wait_recv()
    others += pass_on(grad_full)
    for copy, block in zip(out_x, out_blocks):
        copy.wait_recv()
        over_core.append(wire.send(SIBLING, block, block))
        others.append(over_core[-1])
    take(w_attn, w_attn_out)
    take(normed, normed_out)
    here = rows(me.y * SUB, SUB)
    in_mine[...] = full[here, :]
    scale_mine[...] = scales[here, :]
    for copy in over_x + enter + ring + ring_pass + grads + over_y + out_x + over_core[:4]:
        copy.wait_send()
    finish(others + moves + near[-2:])


def front(gain_row, attn_gain, table, lengths, hidden, w_q, w_kv, out_grad, w_o, *weights):
    vm = pl.BlockSpec(memory_space=pltpu.VMEM)
    hbm = pl.BlockSpec(memory_space=pltpu.HBM)
    outs = [
        SDS((ROWS, 128), BF),
        SDS((ROWS, 128), BF),
        SDS((SUB, D), BF),
        SDS((SUB, 1), F32),
        SDS((16, 1, 128), F32),
        SDS((CHUNK, D), BF),
        SDS((D, 512), BF),
        SDS((D, 768), BF),
        SDS((CHUNK, D), BF),
        SDS((2, 3, 3, 64, 1024), BF),
        SDS((2, 3, 3, 64, 1024), BF),
        SDS((2, 3, 3, 64, 1024), BF),
    ]
    return pl.pallas_call(
        front_body,
        name="front",
        out_shape=outs,
        in_specs=[vm] * 4 + [hbm] * 8,
        out_specs=[vm] * 7 + [hbm] * 5,
        scratch_shapes=[
            pltpu.VMEM((D, 768), BF),
            pltpu.VMEM((CHUNK, D), BF),
            pltpu.VMEM((CHUNK, D), BF),
            pltpu.VMEM((CHUNK, 768), BF),
            pltpu.VMEM((CHUNK, 1), F32),
            pltpu.SemaphoreType.DMA((80,)),
            pltpu.SemaphoreType.DMA((80,)),
            pltpu.SemaphoreType.DMA((7,)),
        ],
        compiler_params=pltpu.CompilerParams(
            collective_id=0, has_side_effects=True, vmem_limit_bytes=60 * 2**20
        ),
        cost_estimate=pl.CostEstimate(flops=2 * 10**9, bytes_accessed=2**23, transcendentals=0),
    )(
        gain_row,
        attn_gain,
        table,
        lengths,
        hidden,
        w_q,
        w_kv,
        out_grad,
        w_o,
        *[weight.reshape(8, 2, 64, 1024) for weight in weights],
    )


def middle_body(
    heads,
    in_mine,
    gains,
    w_cat,
    piece1,
    piece3,
    heads_cat,
    resid,
    scale_out,
    ffn_mine,
    piece2_first,
    piece2_second,
    term_send,
    term_recv,
    send_sem,
    recv_sem,
):
    me = whereami()
    wire = Wire(me, send_sem, recv_sem)
    meet(me, XOFF[1:] + YOFF[1:] + [ZOFF[1], ZOFF[3]])
    weights = [
        wire.send(ZOFF[1], piece1.at[0, 0], piece2_first),
        wire.send(ZOFF[3], piece3.at[1, 0], piece2_second),
    ]
    moves = [
        wire.send(
            XOFF[k],
            heads.at[rows(me.at(XOFF[k]).chunk * CHUNK, CHUNK), :],
            heads_cat.at[:, k * 128 : k * 128 + 128],
        )
        for k in (1, 2, 3)
    ]
    heads_cat[:, 0:128] = heads[rows(me.chunk * CHUNK, CHUNK), :]
    finish(moves)
    sums = []
    for h in range(2):
        for p in range(2):
            cols = slice(h * 1024 + p * 512, h * 1024 + p * 512 + 512)
            term_send[:, cols] = contract_cols(heads_cat[...], w_cat[cols, :]).astype(BF)
        cols = slice(h * 1024, h * 1024 + 1024)
        for d in (1, 2, 3):
            there = rows(me.at(YOFF[d]).y * SUB, SUB)
            sums.append(
                wire.send(YOFF[d], term_send.at[there, cols], term_recv.at[d - 1, :, cols])
            )
    finish(sums)
    value = in_mine[...].astype(F32) + term_send[rows(me.y * SUB, SUB), :].astype(F32)
    for d in range(3):
        value = value + term_recv[d].astype(F32)
    resid[...] = value
    scale = lax.rsqrt(jnp.mean(value * value, axis=1, keepdims=True) + EPS)
    scale_out[...] = scale
    gain = jnp.concatenate([gains[b] for b in range(16)], axis=1)
    ffn_mine[...] = (value * scale * gain).astype(BF)
    finish(weights)


def middle(heads, in_mine, gain, w_cat, piece1, piece3):
    vm = pl.BlockSpec(memory_space=pltpu.VMEM)
    hbm = pl.BlockSpec(memory_space=pltpu.HBM)
    outs = [SDS((CHUNK, 512), BF), SDS((SUB, D), F32), SDS((SUB, 1), F32), SDS((SUB, D), BF)]
    outs += [SDS((3, 64, 1024), BF)] * 2
    return pl.pallas_call(
        middle_body,
        name="middle",
        out_shape=outs,
        in_specs=[vm] * 4 + [hbm] * 2,
        out_specs=[vm] * 4 + [hbm] * 2,
        scratch_shapes=[
            pltpu.VMEM((CHUNK, D), BF),
            pltpu.VMEM((3, SUB, D), BF),
            pltpu.SemaphoreType.DMA((13,)),
            pltpu.SemaphoreType.DMA((13,)),
        ],
        compiler_params=pltpu.CompilerParams(
            collective_id=1, has_side_effects=True, vmem_limit_bytes=60 * 2**20
        ),
        cost_estimate=pl.CostEstimate(flops=10**9, bytes_accessed=2**23, transcendentals=0),
    )(heads, in_mine, gain, w_cat, piece1, piece3)


class PairSum:
    def __init__(self, me, left, right, own, came, stage, send_sem, recv_sem):
        self.me, self.left, self.right, self.own, self.came = me, left, right, own, came
        self.stage, self.send_sem, self.recv_sem = stage, send_sem, recv_sem

    def copy(self, i):
        return pltpu.make_async_remote_copy(
            src_ref=self.stage.at[i % 3, :, :, 1 - self.me.core],
            dst_ref=self.came.at[i],
            send_sem=self.send_sem.at[i],
            recv_sem=self.recv_sem.at[i],
            device_id=self.me.at(SIBLING).device(),
            device_id_type=MESH,
        )

    def multiply(self, first, last):
        def step(i, _):
            cols = pl.ds(pl.multiple_of(i * 256, 256), 256)

            @pl.when(i >= first + 3)
            def _():
                self.copy(i - 3).wait_send()

            block = contract_rows(self.left[:, cols], self.right[...])
            self.stage[i % 3] = block.astype(BF).reshape(2, 4, 2, 16, 2048)
            self.own[i] = self.stage[i % 3, :, :, self.me.core]
            self.copy(i).start()
            return 0

        lax.fori_loop(first, last, step, 0)
        for i in range(last - 3, last):
            self.copy(i).wait_send()

    def add(self, first, last):
        def step(i, _):
            self.copy(i).wait_recv()
            self.own[i] = (self.own[i].astype(F32) + self.came[i].astype(F32)).astype(BF)
            return 0

        lax.fori_loop(first, last, step, 0)


def add_to(target, came):
    for i in range(came.shape[0]):
        target[i] = (target[i].astype(F32) + came[i].astype(F32)).astype(BF)


def ffn_body(
    mine_ref,
    grad_ref,
    resid_ref,
    scale_ref,
    gains,
    w_out_ref,
    own_gate,
    own_up,
    own_down,
    piece0,
    piece1,
    piece2_first,
    piece2_second,
    piece3,
    out_mine,
    resid_back,
    gain_part,
    mix_full,
    heads_back,
    down_own,
    down_came,
    gate_own,
    gate_came,
    up_own,
    up_late,
    up_pass,
    other_core,
    rest_first,
    rest_second,
    gain_ref,
    turned,
    ffn_in,
    act,
    gate_back,
    up_back,
    gate_tile,
    up_tile,
    down_tile,
    down_acc,
    ffn_acc,
    down_send,
    ffn_send,
    down_recv,
    ffn_recv,
    mix_mine,
    back_cat,
    down_terms,
    gate_terms,
    up_terms,
    stage,
    came,
    down_pass,
    gate_pass,
    send_sem,
    recv_sem,
    core_send,
    core_recv,
    tile_sem,
    local_sem,
    ack,
):
    me = whereami()
    wire = Wire(me, send_sem, recv_sem)
    half = [lanes(me.xl, 1024), lanes(1 - me.xl, 1024)]
    here = rows(me.y * SUB, SUB)

    def piece(d, k):
        return {0: piece0, 1: piece1, 3: piece3}[d].at[:, k - 1]

    rest = (rest_first, rest_second)

    def opposite(h, k):
        return (piece2_first, piece2_second)[h] if k == 1 else rest[h].at[k - 2]


    def tile_copies(e, q, slot):
        copies, groups = [], []
        cols = pl.ds(pl.multiple_of(q * 256, 256), 256)

        def copy(src, dst):
            sem = tile_sem.at[slot, len(copies) + len(groups)]
            return pltpu.make_async_copy(src, dst, sem)

        for dxl in range(2):
            k = e * 2 + dxl
            for j, (own, tile) in enumerate(((own_gate, gate_tile), (own_up, up_tile))):
                if k == 0:
                    copies.append(copy(own.at[:, :, :, :, cols], tile.at[slot, dxl]))
                    continue
                for d in range(4):
                    spot = tile.at[slot, dxl, (me.z - d + 4) % 4, me.core]
                    if d != 2:
                        copies.append(copy(piece(d, k).at[:, j, :, cols], spot))
                        continue
                    for h in range(2):
                        copies.append(copy(opposite(h, k).at[j, :, cols], spot.at[h]))
                spot = tile.at[slot, dxl, :, 1 - me.core]
                copies.append(copy(other_core.at[:, :, k - 1, j, :, cols], spot))
            here = slice(dxl * 1024, dxl * 1024 + 1024)
            if k == 0:
                copies.append(copy(own_down.at[q], down_tile.at[slot, :, :, :, here]))
                continue
            spot = down_tile.at[slot, 1 - me.core, :, :, here]
            copies.append(copy(other_core.at[q, :, k - 1, 2], spot))
            for h in range(2):
                spot = down_tile.at[slot, me.core, h, :, here]
                groups.append(
                    [
                        copy(opposite(h, k).at[2] if d == 2 else piece(d, k).at[h, 2], spot)
                        for d in range(4)
                    ]
                )
        return copies, groups

    def fetch(e, q, slot):
        copies, groups = tile_copies(e, q, slot)
        for copy in copies:
            copy.start()
        for group in groups:
            for d, copy in enumerate(group):
                pl.when((me.z - q + 4) % 4 == d)(copy.start)

    def arrive(e, q, slot):
        copies, groups = tile_copies(e, q, slot)
        for copy in copies + [group[0] for group in groups]:
            copy.wait()

    meet(me, YOFF[1:] + XOFF[1:] + ZOFF[1:] + [SIBLING])
    for h in range(2):
        turned[:, h * 1024 : h * 1024 + 1024] = mine_ref[:, half[h]]
    gathers = [wire.send(off, turned, ffn_in.at[here, :]) for off in YOFF[1:]]
    passed = []
    for k in (2, 3):
        passed.append(wire.send(ZOFF[1], piece(1, k).at[0], rest_first.at[k - 2]))
        passed.append(wire.send(ZOFF[3], piece(3, k).at[1], rest_second.at[k - 2]))

    def share(k, parts):
        moves = []
        for d in parts:
            spot = other_core.at[(me.z - d + 4) % 4, :, k - 1]
            if d != 2:
                moves.append(wire.send(SIBLING, piece(d, k), spot))
                continue
            for h in range(2):
                moves.append(wire.send(SIBLING, opposite(h, k), spot.at[h]))
        return moves

    shares = share(1, range(4))
    late_shares = share(2, (0, 1, 3)) + share(3, (0, 1, 3))
    ffn_in[here, :] = turned[...]
    down_acc[...] = jnp.zeros(down_acc.shape, F32)
    ffn_acc[...] = jnp.zeros(ffn_acc.shape, F32)
    finish(shares)
    fetch(0, 0, 0)
    for b in range(16):
        gain_ref[:, b * 128 : b * 128 + 128] = gains[b]
    finish(gathers)
    finish(passed)
    late_shares += share(2, (2,)) + share(3, (2,))

    sums = []
    for left, right, own in (
        (act, grad_ref, down_terms),
        (ffn_in, gate_back, gate_terms),
        (ffn_in, up_back, up_terms),
    ):
        j = len(sums)
        sums.append(PairSum(me, left, right, own, came, stage, core_send.at[j], core_recv.at[j]))
    down_sum, gate_sum, up_sum = sums

    def came_free():
        pl.semaphore_signal(ack, inc=1, device_id=me.at(SIBLING).device(), device_id_type=MESH)
        pl.semaphore_wait(ack, 1)

    for e in range(2):

        def step(q, _, e=e):
            slot = q % 2

            @pl.when(q < 3)
            def _():
                fetch(e, q + 1, 1 - slot)

            arrive(e, q, slot)
            cols = pl.ds(pl.multiple_of(e * 1024 + q * 256, 256), 256)
            w_g = gate_tile[slot].reshape(2048, 256)
            w_u = up_tile[slot].reshape(2048, 256)
            w_d = down_tile[slot].reshape(256, 2048)
            gate = multiply(ffn_in[...], w_g)
            up = multiply(ffn_in[...], w_u)
            act_back = contract_cols(grad_ref[...], w_d)
            sigmoid = jax.nn.sigmoid(gate)
            silu = gate * sigmoid
            act_here = (silu * up).astype(BF)
            act[:, cols] = act_here
            down_acc[...] += multiply(act_here, w_d)
            g_back = (act_back * up * sigmoid * (1.0 + gate * (1.0 - sigmoid))).astype(BF)
            u_back = (act_back * silu).astype(BF)
            gate_back[:, cols] = g_back
            up_back[:, cols] = u_back
            ffn_acc[...] += contract_cols(g_back, w_g) + contract_cols(u_back, w_u)
            return 0

        lax.fori_loop(0, 4, step, 0)
        if e == 0:
            finish(late_shares)
            fetch(1, 0, 0)
            down_sum.multiply(0, 4)

    ffn_send[...] = ffn_acc[...].astype(BF)
    ffn_moves = [
        wire.send(YOFF[d], ffn_send.at[rows(me.at(YOFF[d]).y * SUB, SUB), :], ffn_recv.at[d - 1])
        for d in (1, 2, 3)
    ]
    down_sum.multiply(4, 8)


    def down_block(k, h=None):
        e, dxl = XOFF[k][4], XOFF[k][2]
        pairs = slice(e * 4, e * 4 + 4) if h is None else slice(e * 4 + h * 2, e * 4 + h * 2 + 2)
        return down_terms.at[pairs, :, :, :, dxl * 1024 : dxl * 1024 + 1024]

    down_sum.add(0, 8)
    x_moves = [
        wire.send(XOFF[1], down_block(2, 0), down_pass.at[0]),
        wire.send(XOFF[3], down_block(2, 1), down_pass.at[1]),
        wire.send(XOFF[1], down_block(1, 0), down_came.at[0, 0:2]),
        wire.send(XOFF[3], down_block(3, 1), down_came.at[1, 2:4]),
    ]
    near = []

    def keep(src, dst):
        near.append(pltpu.make_async_copy(src, dst, local_sem.at[len(near)]))
        near[-1].start()

    keep(down_block(0), down_own)

    def z_block(terms, d, h=None):
        pairs = slice(0, 8) if h is None else slice(h * 4, h * 4 + 4)
        return terms.at[pairs, :, (me.z + d) % 4]

    came_free()
    gate_sum.multiply(0, 8)
    gate_sum.add(0, 4)
    z_moves = [
        wire.send(ZOFF[1], z_block(gate_terms, 2, 0), gate_pass.at[0]),
        wire.send(ZOFF[3], z_block(gate_terms, 3, 0), gate_came.at[1, 0:4]),
    ]
    gate_sum.add(4, 8)
    z_moves += [
        wire.send(ZOFF[3], z_block(gate_terms, 2, 1), gate_pass.at[1]),
        wire.send(ZOFF[1], z_block(gate_terms, 1, 1), gate_came.at[0, 4:8]),
    ]
    keep(z_block(gate_terms, 0), gate_own)

    finish(ffn_moves)

    def summed(send, recv, h):
        cols = slice(h * 1024, h * 1024 + 1024)
        out = send[here, cols].astype(F32)
        for d in range(3):
            out = out + recv[d, :, cols].astype(F32)
        return out

    scale = scale_ref[...]
    inner = jnp.zeros((SUB, 1), F32)
    for h in range(2):
        back = summed(ffn_send, ffn_recv, h)
        weighed = back * resid_ref[:, half[h]]
        inner = inner + jnp.sum(weighed * gain_ref[:, half[h]], axis=1, keepdims=True)
        gain_part[:, half[h]] = jnp.sum(weighed * scale, axis=0, keepdims=True)
    pull = scale * scale * scale * inner / D
    for h in range(2):
        back = summed(ffn_send, ffn_recv, h)
        grad = grad_ref[here, h * 1024 : h * 1024 + 1024].astype(F32)
        total_back = grad + scale * gain_ref[:, half[h]] * back - resid_ref[:, half[h]] * pull
        resid_back[:, half[h]] = total_back
        mix_mine[:, half[h]] = total_back.astype(BF)
    mix_full[here, :] = mix_mine[...]
    mix_moves = [wire.send(off, mix_mine, mix_full.at[here, :]) for off in YOFF[1:]]

    down_send[...] = down_acc[...].astype(BF)
    down_moves = [
        wire.send(YOFF[d], down_send.at[rows(me.at(YOFF[d]).y * SUB, SUB), :], down_recv.at[d - 1])
        for d in (1, 2, 3)
    ]
    x_moves[0].wait_recv()
    add_to(down_block(3, 0), down_pass.at[0])
    x_late = [wire.send(XOFF[3], down_block(3, 0), down_came.at[1, 0:2])]
    x_moves[1].wait_recv()
    add_to(down_block(1, 1), down_pass.at[1])
    x_late.append(wire.send(XOFF[1], down_block(1, 1), down_came.at[0, 2:4]))
    came_free()
    up_sum.multiply(0, 8)
    z_moves[0].wait_recv()
    add_to(z_block(gate_terms, 1, 0), gate_pass.at[0])
    z_late = [wire.send(ZOFF[1], z_block(gate_terms, 1, 0), gate_came.at[0, 0:4])]
    z_moves[2].wait_recv()
    add_to(z_block(gate_terms, 3, 1), gate_pass.at[1])
    z_late.append(wire.send(ZOFF[3], z_block(gate_terms, 3, 1), gate_came.at[1, 4:8]))
    up_sum.add(0, 8)
    z_late += [
        wire.send(ZOFF[1], z_block(up_terms, 2, 0), up_pass.at[0]),
        wire.send(ZOFF[3], z_block(up_terms, 2, 1), up_pass.at[1]),
    ]
    keep(z_block(up_terms, 0), up_own)
    keep(z_block(up_terms, 1), up_late.at[0])
    keep(z_block(up_terms, 3), up_late.at[1])

    finish(mix_moves)
    back_cat[...] = multiply(mix_full[...], w_out_ref[...]).astype(BF)
    spot = rows(me.chunk * CHUNK, CHUNK)
    head_moves = [
        wire.send(XOFF[k], back_cat.at[:, k * 128 : k * 128 + 128], heads_back.at[spot, :])
        for k in (1, 2, 3)
    ]
    heads_back[spot, :] = back_cat[:, 0:128]
    finish(down_moves)
    for h in range(2):
        out_mine[:, half[h]] = (resid_ref[:, half[h]] + summed(down_send, down_recv, h)).astype(BF)
    for move in (x_moves[0], x_moves[1], z_moves[0], z_moves[2]):
        move.wait_send()
    finish(head_moves + x_moves[2:] + [z_moves[1], z_moves[3]] + x_late + z_late)
    for copy in near:
        copy.wait()


def ffn(ffn_mine, grad_full, resid, scale_two, gain, w_out, w_gate, w_up, w_down, pieces):
    vm = pl.BlockSpec(memory_space=pltpu.VMEM)
    hbm = pl.BlockSpec(memory_space=pltpu.HBM)
    return pl.pallas_call(
        ffn_body,
        name="ffn",
        out_shape=[
            SDS((SUB, D), BF),
            SDS((SUB, D), F32),
            SDS((1, D), F32),
            SDS((CHUNK, D), BF),
            SDS((ROWS, 128), BF),
            SDS((4, 2, 4, 16, 1024), BF),
            SDS((2, 4, 2, 4, 16, 1024), BF),
            SDS((8, 2, 16, 2048), BF),
            SDS((2, 8, 2, 16, 2048), BF),
            SDS((8, 2, 16, 2048), BF),
            SDS((2, 8, 2, 16, 2048), BF),
            SDS((2, 4, 2, 16, 2048), BF),
            SDS((4, 2, 3, 3, 64, 1024), BF),
            SDS((2, 3, 64, 1024), BF),
            SDS((2, 3, 64, 1024), BF),
        ],
        in_specs=[vm] * 6 + [hbm] * 8,
        out_specs=[vm] * 5 + [hbm] * 10,
        scratch_shapes=[
            pltpu.VMEM((1, D), F32),
            pltpu.VMEM((SUB, D), BF),
            pltpu.VMEM((CHUNK, D), BF),
            pltpu.VMEM((CHUNK, D), BF),
            pltpu.VMEM((CHUNK, D), BF),
            pltpu.VMEM((CHUNK, D), BF),
            pltpu.VMEM((2, 2, 4, 2, 2, 64, 256), BF),
            pltpu.VMEM((2, 2, 4, 2, 2, 64, 256), BF),
            pltpu.VMEM((2, 2, 2, 64, 2048), BF),
            pltpu.VMEM((CHUNK, D), F32),
            pltpu.VMEM((CHUNK, D), F32),
            pltpu.VMEM((CHUNK, D), BF),
            pltpu.VMEM((CHUNK, D), BF),
            pltpu.VMEM((3, SUB, D), BF),
            pltpu.VMEM((3, SUB, D), BF),
            pltpu.VMEM((SUB, D), BF),
            pltpu.VMEM((CHUNK, 512), BF),
            pltpu.VMEM((8, 2, 4, 16, 2048), BF),
            pltpu.VMEM((8, 2, 4, 16, 2048), BF),
            pltpu.VMEM((8, 2, 4, 16, 2048), BF),
            pltpu.VMEM((3, 2, 4, 2, 16, 2048), BF),
            pltpu.VMEM((8, 2, 4, 16, 2048), BF),
            pltpu.VMEM((2, 2, 2, 4, 16, 1024), BF),
            pltpu.VMEM((2, 4, 2, 16, 2048), BF),
            pltpu.SemaphoreType.DMA((64,)),
            pltpu.SemaphoreType.DMA((64,)),
            pltpu.SemaphoreType.DMA((3, 8)),
            pltpu.SemaphoreType.DMA((3, 8)),
            pltpu.SemaphoreType.DMA((2, 32)),
            pltpu.SemaphoreType.DMA((6,)),
            pltpu.SemaphoreType.REGULAR,
        ],
        compiler_params=pltpu.CompilerParams(
            collective_id=14, has_side_effects=True, vmem_limit_bytes=60 * 2**20
        ),
        cost_estimate=pl.CostEstimate(flops=26 * 10**9, bytes_accessed=40 * 2**20, transcendentals=0),
    )(
        ffn_mine,
        grad_full,
        resid,
        scale_two,
        gain,
        w_out,
        w_gate.reshape(4, 2, 2, 64, 1024),
        w_up.reshape(4, 2, 2, 64, 1024),
        w_down.reshape(4, 2, 2, 64, 1024),
        *pieces,
    )


def per_device(
    layer_input,
    doc_lengths,
    attn_gain,
    w_query,
    w_key,
    w_value,
    w_output,
    ffn_gain,
    w_gate,
    w_up,
    w_down,
    output_grad,
):
    me = whereami()
    cos_np, sin_np = rope_table()
    table_all = jnp.asarray(np.stack([cos_np, sin_np]))

    w_kv = jnp.concatenate(
        [part(w_key, me.y * 64, 64, 1), part(w_value, me.y * 64, 64, 1)], axis=1
    )
    queries, kv, in_mine, scale_mine, gains, grad_full, w_out, w_attn, normed, *passed = front(
        ffn_gain[None, :],
        attn_gain[None, :],
        table_all,
        doc_lengths,
        layer_input,
        w_query,
        w_kv,
        output_grad,
        w_output,
        w_gate,
        w_up,
        w_down,
    )
    (heads_out,) = vmem_call(
        "attend", attend_body, [doc_lengths, queries, kv], [SDS((ROWS, 128), BF)], flops=2 * 10**10
    )
    heads_cat, resid, scale_two, ffn_mine, *opposite = middle(
        heads_out, in_mine, gains, w_out, *passed[1:]
    )
    pieces = [*passed[:2], *opposite, passed[2]]
    (
        out_mine,
        resid_back,
        ffn_gain_part,
        mix_full,
        heads_back,
        *ffn_sums,
        _,
        _,
        _,
    ) = ffn(
        ffn_mine, grad_full, resid, scale_two, gains, w_out, w_gate, w_up, w_down, pieces
    )

    (
        layer_output,
        input_grad,
        query_grad,
        kv_grad,
        output_proj_grad,
        gate_grad,
        up_grad,
        down_grad,
        gain_grads,
    ) = back(
        [
            doc_lengths,
            queries,
            kv,
            heads_back,
            out_mine,
            in_mine,
            resid_back,
            scale_mine,
            attn_gain[None, :],
            ffn_gain_part,
        ],
        [table_all, w_attn, heads_cat, normed, mix_full, *ffn_sums],
    )
    kv_cols = jnp.moveaxis(kv_grad, 0, 1).reshape(32, 4, 2, 64)
    key_grad = kv_cols[:, :, 0, :].reshape(32, 256)
    value_grad = kv_cols[:, :, 1, :].reshape(32, 256)
    gain_grads = part(gain_grads, me.tok * 16, 16, 1)
    return (
        layer_output,
        input_grad,
        gain_grads[0:1],
        query_grad,
        key_grad,
        value_grad,
        output_proj_grad,
        gain_grads[1:2],
        gate_grad,
        up_grad,
        down_grad,
    )


def solution(mesh):
    in_specs = (
        P("tok", ("narrow", "wide")),
        P("tok", None),
        P(),
        P(None, ("narrow", "wide")),
        P(None, "narrow"),
        P(None, "narrow"),
        P(None, ("narrow", "wide")),
        P(("narrow", "wide")),
        P("narrow", "wide"),
        P("narrow", "wide"),
        P("wide", "narrow"),
        P("tok", ("narrow", "wide")),
    )
    out_specs = (
        P("tok", ("narrow", "wide")),
        P("tok", ("narrow", "wide")),
        P(("narrow", "wide"), "tok"),
        P("tok", ("narrow", "wide")),
        P(("tok", "wide"), "narrow"),
        P(("tok", "wide"), "narrow"),
        P("tok", ("narrow", "wide")),
        P(("narrow", "wide"), "tok"),
        P("narrow", "tok", "wide"),
        P("narrow", "tok", "wide"),
        P("wide", "tok", "narrow"),
    )
    return jax.shard_map(
        per_device, mesh=mesh, in_specs=in_specs, out_specs=out_specs, check_vma=False
    )
```

```python
import functools
import math

import jax
import jax.numpy as jnp
import numpy as np
from jax import lax
from jax.experimental import pallas as pl
from jax.experimental.pallas import tpu as pltpu
from jax.sharding import PartitionSpec as P

HEADS = 32
KV_HEADS = 8
HEAD_DIM = 64
GROUP = 128
EPS = 1e-05
THETA = 500000.0
FACTOR = 32.0
LOW_FACTOR = 1.0
HIGH_FACTOR = 4.0
INITIAL = 8192.0
NEG = -1e30

D = 2048
ROWS = 1536
CHUNK = 384
SUB = 96
SHORT = 512
BF = jnp.bfloat16
F32 = jnp.float32
MESH = pl.DeviceIdType.MESH
SDS = jax.ShapeDtypeStruct

HERE = (0, 0, 0, 0, 0)
XOFF = [(0, 0, 0, 0, 0), (0, 0, 1, 0, 0), (0, 0, 0, 0, 1), (0, 0, 1, 0, 1)]
YOFF = [(0, 0, 0, d, 0) for d in range(4)]
PLANE = [(0, 0, a, b, e) for b in range(4) for a in range(2) for e in range(2)]
SIBLING = (1, 0, 0, 0, 0)
TOKS = [(a, b, 0, 0, 0) for b in range(4) for a in range(2)]


class Place:
    def __init__(self, core, z, xl, y, xh):
        self.core, self.z, self.xl, self.y, self.xh = core, z, xl, y, xh
        self.tok = z * 2 + core
        self.wide = y * 2 + xh
        self.block = xl * 8 + self.wide
        self.chunk = xl * 2 + xh

    def at(self, off):
        return Place(
            (self.core + off[0]) % 2,
            (self.z + off[1]) % 4,
            (self.xl + off[2]) % 2,
            (self.y + off[3]) % 4,
            (self.xh + off[4]) % 2,
        )

    def device(self):
        return (self.tok, self.xl, self.wide)


def whereami():
    tok = lax.axis_index("tok")
    wide = lax.axis_index("wide")
    return Place(tok % 2, tok // 2, lax.axis_index("narrow"), wide // 2, wide % 2)


def rows(start, size):
    return pl.ds(pl.multiple_of(start, size), size)


def lanes(index, size=128):
    return pl.ds(pl.multiple_of(index * size, size), size)


def block_probs(q_ref, kv_ref, start, i, stack):
    n = 256 * (i + 1)
    keys = kv_ref[rows_256(start, n), 0:64]
    scores = lax.dot_general(
        keys, stack, (((1,), (1,)), ((), ())), preferred_element_type=F32
    ) * (HEAD_DIM**-0.5)
    last = scores[n - 256 :, :]
    key_id = lax.broadcasted_iota(jnp.int32, (256, 512), 0)
    query_id = lax.broadcasted_iota(jnp.int32, (256, 512), 1) % 256
    last = jnp.where(key_id <= query_id, last, NEG)
    if n > 256:
        scores = jnp.concatenate([scores[: n - 256, :], last], axis=0)
    else:
        scores = last
    raised = jnp.exp(scores - jnp.max(scores, axis=0, keepdims=True))
    return keys, raised, jnp.sum(raised, axis=0, keepdims=True)


def rows_256(start, size):
    return pl.ds(pl.multiple_of(start, 256), size)


def starts_of(len_ref):
    long_first = len_ref[0, 0] > SHORT
    long_start = jnp.where(long_first, 0, SHORT)
    short_start = jnp.where(long_first, 2 * SHORT, 0)
    return ((long_start, 4), (short_start, 2))


def both(block):
    return jnp.concatenate([block[:, 0:64], block[:, 64:128]], axis=0)


def attend_body(len_ref, q_ref, kv_ref, out_ref):
    for start, blocks in starts_of(len_ref):
        for i in range(blocks):
            mine = rows_256(start + 256 * i, 256)
            stack = both(q_ref[mine, :])
            keys, raised, mass = block_probs(q_ref, kv_ref, start, i, stack)
            soft = (raised * (1.0 / mass)).astype(BF)
            values = kv_ref[rows_256(start, 256 * (i + 1)), 64:128]
            mixed = lax.dot_general(
                soft, values, (((0,), (0,)), ((), ())), preferred_element_type=F32
            )
            out_ref[mine, :] = jnp.concatenate([mixed[:256], mixed[256:]], axis=1).astype(BF)


def unrope(tensor, cosine, sine):
    lane = lax.broadcasted_iota(jnp.int32, tensor.shape, 1)
    first = (lane % 64) < 32
    swapped = jnp.where(first, pltpu.roll(tensor, 96, 1), -pltpu.roll(tensor, 32, 1))
    return tensor * cosine + swapped * sine


def vmem_call(name, body, ins, outs, scratch=(), flops=0):
    return pl.pallas_call(
        body,
        name=name,
        out_shape=outs,
        in_specs=[pl.BlockSpec(memory_space=pltpu.SMEM)]
        + [pl.BlockSpec(memory_space=pltpu.VMEM)] * (len(ins) - 1),
        out_specs=[pl.BlockSpec(memory_space=pltpu.VMEM)] * len(outs),
        scratch_shapes=list(scratch),
        compiler_params=pltpu.CompilerParams(vmem_limit_bytes=60 * 2**20),
        cost_estimate=pl.CostEstimate(flops=flops, bytes_accessed=2**20, transcendentals=0),
    )(*ins)


def masked_scores(keys, query, i, length):
    n = keys.shape[0]
    scores = contract_cols(keys, query) * (HEAD_DIM**-0.5)
    key_id = lax.broadcasted_iota(jnp.int32, (256, 256), 0)
    query_id = lax.broadcasted_iota(jnp.int32, (256, 256), 1)
    parts = [jnp.where(key_id <= query_id, scores[n - 256 :, :], NEG)]
    middle = 0
    if i >= 2:
        cut = SHORT if i < 4 else 2 * SHORT
        middle = SHORT
        parts.insert(0, jnp.where(length == cut, NEG, scores[:SHORT, :]))
    if n - 256 > middle:
        parts.insert(len(parts) - 1, scores[middle : n - 256, :])
    return jnp.concatenate(parts, axis=0) if len(parts) > 1 else parts[0]


def back_body(
    len_ref,
    q_ref,
    kv_ref,
    heads_back,
    out_mine,
    in_mine,
    resid_back,
    scale_ref,
    gain_ref,
    ffn_gain_part,
    table_in,
    w_attn_in,
    heads_in,
    normed_in,
    mix_in,
    down_own,
    down_came,
    gate_own,
    gate_came,
    up_own,
    up_late,
    up_pass,
    layer_output,
    input_grad,
    query_grad,
    kv_grad,
    out_grad,
    gate_grad,
    up_grad,
    down_grad,
    gain_grad,
    table,
    w_attn,
    heads_cat,
    normed,
    mix_full,
    dq_ref,
    dkv_ref,
    dkv_acc,
    down_in,
    gate_in,
    up_in,
    late_in,
    pass_in,
    up_last,
    down_sum,
    gate_sum,
    up_sum,
    down_z,
    gate_x,
    up_x,
    cat_back,
    norm_send,
    norm_recv,
    in_grad,
    gain_parts,
    gain_plane,
    gain_mine,
    gain_toks,
    o_terms,
    o_core,
    o_x,
    o_sum,
    o_z,
    q_terms,
    q_core,
    q_x,
    q_sum,
    q_z,
    k_terms,
    k_core,
    k_x,
    k_sum,
    k_z,
    k_last,
    send_sem,
    recv_sem,
    local_sem,
):
    me = whereami()
    wire = Wire(me, send_sem, recv_sem)
    loads = []
    for src, dst in (
        (up_late, late_in),
        (up_pass, pass_in),
        (gate_own, gate_in.at[0]),
        (gate_came, gate_in.at[1:3]),
        (down_own, down_in.at[0]),
        (down_came, down_in.at[1:3]),
        (up_own, up_in),
        (table_in, table),
        (mix_in, mix_full),
        (heads_in, heads_cat),
        (w_attn_in, w_attn),
        (normed_in, normed),
    ):
        loads.append(pltpu.make_async_copy(src, dst, local_sem.at[len(loads)]))
        loads[-1].start()
    meet(me, PLANE[1:] + TOKS[1:])
    sent = []

    for copy in loads[0:2]:
        copy.wait()
    up_moves = [
        wire.send(ZOFF[1], late_in.at[0, 4:8], up_last.at[0, 4:8]),
        wire.send(ZOFF[3], late_in.at[1, 0:4], up_last.at[1, 0:4]),
    ]

    length = len_ref[0:1, 0:1]
    loads[7].wait()

    def turns(row, size):
        first, later = slice(row, row + size), slice(row + SHORT, row + SHORT + size)
        return [jnp.where(length == SHORT, table[j, first], table[j, later]) for j in range(2)]

    dkv_acc[...] = jnp.zeros(dkv_acc.shape, F32)
    for i in range(6):
        low, high = 0 if i < 4 else SHORT, 256 * (i + 1)
        here = slice(256 * i, high)
        keys, values = kv_ref[low:high, 0:64], kv_ref[low:high, 64:128]
        parts = []
        for head in (slice(0, 64), slice(64, 128)):
            query, value_back = q_ref[here, head], heads_back[here, head]
            scores = masked_scores(keys, query, i, length)
            raised = jnp.exp(scores - jnp.max(scores, axis=0, keepdims=True))
            soft = raised * (1.0 / jnp.sum(raised, axis=0, keepdims=True))
            prob_back = contract_cols(values, value_back)
            inner = jnp.sum(soft * prob_back, axis=0, keepdims=True)
            score_back = (soft * (prob_back - inner)).astype(BF)
            parts.append(contract_rows(score_back, keys) * (HEAD_DIM**-0.5))
            dk = multiply(score_back, query) * (HEAD_DIM**-0.5)
            dv = multiply(soft.astype(BF), value_back)
            dkv_acc[low:high, :] += jnp.concatenate([dk, dv], axis=1)
        dq = jnp.concatenate(parts, axis=1)
        dq_ref[here, :] = unrope(dq, *turns(256 * i, 256)).astype(BF)
    lane = lax.broadcasted_iota(jnp.int32, (256, 128), 1)
    for here in split_rows(6, 256):
        acc = dkv_acc[here, :]
        turned = unrope(acc, *turns(here.start, 256))
        dkv_ref[here, :] = jnp.where(lane < 64, turned, acc).astype(BF)

    spot = rows(me.chunk * CHUNK, CHUNK)
    moves = []
    for k in (1, 2, 3):
        there = rows(me.at(XOFF[k]).chunk * CHUNK, CHUNK)
        for ref, col in ((dq_ref, 0), (dkv_ref, 512)):
            moves.append(
                wire.send(
                    XOFF[k], ref.at[there, :], cat_back.at[:, col + k * 128 : col + k * 128 + 128]
                )
            )
    cat_back[:, 0:128] = dq_ref[spot, :]
    cat_back[:, 512:640] = dkv_ref[spot, :]

    mine = rows(me.chunk * CHUNK + me.y * SUB, SUB)
    leaving = [
        wire.send(off, out_mine.at[:, lanes(me.at(off).block)], layer_output.at[mine, :])
        for off in PLANE[1:]
    ]
    layer_output[mine, :] = out_mine[:, lanes(me.block)]

    add_to(late_in.at[0, 0:4], pass_in.at[0])
    up_moves.append(wire.send(ZOFF[1], late_in.at[0, 0:4], up_last.at[0, 0:4]))
    add_to(late_in.at[1, 4:8], pass_in.at[1])
    up_moves.append(wire.send(ZOFF[3], late_in.at[1, 4:8], up_last.at[1, 4:8]))

    def fold(ref, out):
        for n in range(out.shape[0]):
            value = ref[0, n].astype(F32)
            for k in range(1, ref.shape[0]):
                value = value + ref[k, n].astype(F32)
            out[n] = value.astype(BF)

    def x_blocks(ref, came):
        moves = []
        for k in (1, 2, 3):
            e, dxl = XOFF[k][4], XOFF[k][2]
            src = ref.at[dxl * 4 : dxl * 4 + 4, :, :, e * 1024 : e * 1024 + 1024]
            moves.append(wire.send(XOFF[k], src, came.at[k - 1]))
        return moves

    for copy in loads[2:7] + loads[8:]:
        copy.wait()
    fold(gate_in, gate_sum)
    gate_moves = x_blocks(gate_sum, gate_x)

    for z in range(4):
        block = contract_rows(mix_full[:, z * 512 : z * 512 + 512], heads_cat[...])
        o_terms[z] = block.astype(BF).reshape(2, 256, 512)
    o_pair = wire.send(SIBLING, o_terms.at[:, 1 - me.core], o_core)

    def add_core(copy, terms, came):
        copy.wait_recv()
        terms[:, me.core] = (terms[:, me.core].astype(F32) + came[...].astype(F32)).astype(BF)

    finish(moves)
    for h in range(4):
        cols = slice(h * 512, h * 512 + 512)
        term = contract_cols(cat_back[:, 0:768], w_attn[cols, :]) + contract_cols(
            cat_back[:, 768:1024], w_attn[cols, 512:768]
        )
        norm_send[:, cols] = term.astype(BF)
    norm_moves = [
        wire.send(YOFF[d], norm_send.at[rows(me.at(YOFF[d]).y * SUB, SUB), :], norm_recv.at[d - 1])
        for d in (1, 2, 3)
    ]

    add_core(o_pair, o_terms, o_core)
    o_moves = [
        wire.send(ZOFF[d], o_terms.at[(me.z + d) % 4, me.core], o_z.at[d - 1]) for d in (1, 2, 3)
    ]

    for z in range(4):
        block = contract_rows(normed[:, z * 512 : z * 512 + 512], cat_back[:, 0:512])
        q_terms[z] = block.astype(BF).reshape(2, 256, 512)
    q_pair = wire.send(SIBLING, q_terms.at[:, 1 - me.core], q_core)
    for z in range(4):
        left = normed[:, z * 512 : z * 512 + 512]
        block = contract_rows(left, cat_back[:, 512:768]) + contract_rows(
            left, cat_back[:, 768:1024]
        )
        k_terms[z] = block.astype(BF).reshape(2, 4, 2, 32, 256)
    k_pair = wire.send(SIBLING, k_terms.at[:, 1 - me.core], k_core)

    def kv_block(k):
        e, dxl = XOFF[k][4], XOFF[k][2]
        return k_terms.at[:, me.core, :, (me.xh + e) % 2, :, dxl * 128 : dxl * 128 + 128]

    add_core(k_pair, k_terms, k_core)
    k_moves = [wire.send(XOFF[k], kv_block(k), k_x.at[k - 1]) for k in (1, 2, 3)]
    add_core(q_pair, q_terms, q_core)
    q_moves = [
        wire.send(ZOFF[d], q_terms.at[(me.z + d) % 4, me.core], q_z.at[d - 1]) for d in (1, 2, 3)
    ]

    fold(down_in, down_sum)
    down_moves = [
        wire.send(ZOFF[d], down_sum.at[:, :, (me.z + d) % 4], down_z.at[d - 1]) for d in (1, 2, 3)
    ]

    def gathered(moves, own, came):
        for copy in moves:
            copy.wait_recv()
        sent.extend(moves)
        value = own.astype(F32)
        for d in range(came.shape[0]):
            value = value + came[d].astype(F32)
        return value

    for copy in up_moves:
        copy.wait_recv()
    sent.extend(up_moves)
    for n in range(8):
        value = up_in[n].astype(F32) + up_last[0, n].astype(F32)
        up_sum[n] = (value + up_last[1, n].astype(F32)).astype(BF)
    up_moves = x_blocks(up_sum, up_x)

    def over_x(ref, came):
        return [
            wire.send(XOFF[k], ref.at[:, k * 128 : k * 128 + 128], came.at[k - 1]) for k in (1, 2, 3)
        ]

    o_sum[...] = gathered(o_moves, o_terms[me.z, me.core], o_z).astype(BF)
    o_moves = over_x(o_sum, o_x)

    finish(norm_moves)
    here = rows(me.y * SUB, SUB)
    back = norm_send[here, :].astype(F32)
    for d in range(3):
        back = back + norm_recv[d].astype(F32)
    scale = scale_ref[...]
    enter = in_mine[...].astype(F32)
    weighed = back * enter
    inner = jnp.sum(weighed * gain_ref[...], axis=1, keepdims=True)
    gain_parts[0:1, :] = jnp.sum(weighed * scale, axis=0, keepdims=True)
    gain_parts[1:2, :] = ffn_gain_part[...]
    gain_parts[2:8, :] = jnp.zeros((6, D), F32)
    pull = scale * scale * scale * inner / D
    in_grad[...] = (resid_back[...] + scale * gain_ref[...] * back - enter * pull).astype(BF)
    for off in PLANE[1:]:
        there = lanes(me.at(off).block)
        leaving.append(wire.send(off, in_grad.at[:, there], input_grad.at[mine, :]))
        leaving.append(wire.send(off, gain_parts.at[:, there], gain_plane.at[me.block]))
    input_grad[mine, :] = in_grad[:, lanes(me.block)]
    gain_plane[me.block] = gain_parts[:, lanes(me.block)]

    k_sum[...] = gathered(k_moves, k_terms[:, me.core, :, me.xh, :, 0:128], k_x).astype(BF)
    k_moves = [wire.send(ZOFF[d], k_sum.at[(me.z + d) % 4], k_z.at[d - 1]) for d in (1, 2, 3)]
    q_sum[...] = gathered(q_moves, q_terms[me.z, me.core], q_z).astype(BF)
    q_moves = over_x(q_sum, q_x)

    shape = (8, 16, 1024)
    own = down_sum[:, :, me.z].reshape(shape)
    down_grad[...] = gathered(down_moves, own, down_z.reshape(3, *shape))
    own = gate_sum[0:4, :, :, 0:1024].reshape(shape)
    gate_grad[...] = gathered(gate_moves, own, gate_x.reshape(3, *shape))

    out_grad[...] = gathered(o_moves, o_sum[:, 0:128], o_x)
    query_grad[...] = gathered(q_moves, q_sum[:, 0:128], q_x)
    k_last[...] = gathered(k_moves, k_sum[me.z], k_z)
    y_moves = [wire.send(YOFF[d], k_last.at[me.at(YOFF[d]).y], kv_grad.at[me.y]) for d in (1, 2, 3)]
    kv_grad[me.y] = k_last[me.y]
    for copy in leaving:
        copy.wait_recv()
    sent.extend(leaving)
    gain_mine[...] = jnp.sum(gain_plane[...], axis=0)
    tok_moves = [wire.send(off, gain_mine, gain_toks.at[me.tok]) for off in TOKS[1:]]
    gain_toks[me.tok] = gain_mine[...]
    own = up_sum[0:4, :, :, 0:1024].reshape(shape)
    up_grad[...] = gathered(up_moves, own, up_x.reshape(3, *shape))
    finish(y_moves + tok_moves)
    gain_grad[...] = jnp.sum(gain_toks[...], axis=0)
    for copy in sent:
        copy.wait_send()
    o_pair.wait_send()
    q_pair.wait_send()
    k_pair.wait_send()


def back(vmem_ins, hbm_ins):
    vm = pl.BlockSpec(memory_space=pltpu.VMEM)
    hbm = pl.BlockSpec(memory_space=pltpu.HBM)
    outs = [
        SDS((ROWS, 128), BF),
        SDS((ROWS, 128), BF),
        SDS((256, 128), F32),
        SDS((4, 32, 128), F32),
        SDS((256, 128), F32),
        SDS((8, 16, 1024), F32),
        SDS((8, 16, 1024), F32),
        SDS((8, 16, 1024), F32),
        SDS((8, 128), F32),
    ]
    v = pltpu.VMEM
    return pl.pallas_call(
        back_body,
        name="back",
        out_shape=outs,
        in_specs=[vm] * len(vmem_ins) + [hbm] * len(hbm_ins),
        out_specs=[vm] * len(outs),
        scratch_shapes=[
            v((2, 2048, 128), F32),
            v((D, 768), BF),
            v((CHUNK, 512), BF),
            v((CHUNK, D), BF),
            v((CHUNK, D), BF),
            v((ROWS, 128), BF),
            v((ROWS, 128), BF),
            v((ROWS, 128), F32),
            v((3, 4, 2, 4, 16, 1024), BF),
            v((3, 8, 2, 16, 2048), BF),
            v((8, 2, 16, 2048), BF),
            v((2, 8, 2, 16, 2048), BF),
            v((2, 4, 2, 16, 2048), BF),
            v((2, 8, 2, 16, 2048), BF),
            v((4, 2, 4, 16, 1024), BF),
            v((8, 2, 16, 2048), BF),
            v((8, 2, 16, 2048), BF),
            v((3, 4, 2, 16, 1024), BF),
            v((3, 4, 2, 16, 1024), BF),
            v((3, 4, 2, 16, 1024), BF),
            v((CHUNK, 1024), BF),
            v((CHUNK, D), BF),
            v((3, SUB, D), BF),
            v((SUB, D), BF),
            v((8, D), F32),
            v((16, 8, 128), F32),
            v((8, 128), F32),
            v((8, 8, 128), F32),
        ]
        + [
            v((4, 2, 256, 512), BF),
            v((4, 256, 512), BF),
            v((3, 256, 128), BF),
            v((256, 512), BF),
            v((3, 256, 512), BF),
            v((4, 2, 256, 512), BF),
            v((4, 256, 512), BF),
            v((3, 256, 128), BF),
            v((256, 512), BF),
            v((3, 256, 512), BF),
            v((4, 2, 4, 2, 32, 256), BF),
            v((4, 4, 2, 32, 256), BF),
            v((3, 4, 4, 32, 128), BF),
            v((4, 4, 32, 128), BF),
            v((3, 4, 32, 128), BF),
            v((4, 32, 128), F32),
            pltpu.SemaphoreType.DMA((104,)),
            pltpu.SemaphoreType.DMA((104,)),
            pltpu.SemaphoreType.DMA((12,)),
        ],
        compiler_params=pltpu.CompilerParams(
            collective_id=15, has_side_effects=True, vmem_limit_bytes=60 * 2**20
        ),
        cost_estimate=pl.CostEstimate(flops=10**10, bytes_accessed=30 * 2**20, transcendentals=0),
    )(*vmem_ins, *hbm_ins)


def rope_table():
    halfway = HEAD_DIM // 2
    k = np.arange(halfway, dtype=np.float32)
    inverse = np.exp(-2.0 * k / HEAD_DIM * math.log(THETA)).astype(np.float32)
    wavelen = (2.0 * math.pi / inverse).astype(np.float32)
    scaled = inverse / np.float32(FACTOR)
    smooth = (INITIAL / wavelen - LOW_FACTOR) / (HIGH_FACTOR - LOW_FACTOR)
    middle = (1.0 - smooth) * scaled + smooth * inverse
    frequency = np.where(
        wavelen < INITIAL / HIGH_FACTOR,
        inverse,
        np.where(wavelen > INITIAL / LOW_FACTOR, scaled, middle),
    ).astype(np.float32)
    positions = np.concatenate([np.arange(512), np.arange(1024), np.arange(512)]).astype(np.float32)
    angles = (positions[:, None] * frequency[None, :]).astype(np.float32).astype(np.float64)
    return (
        np.tile(np.cos(angles).astype(np.float32), (1, 4)),
        np.tile(np.sin(angles).astype(np.float32), (1, 4)),
    )


def part(array, start, size, axis):
    return lax.dynamic_slice_in_dim(array, start, size, axis)


def contract_rows(left_side, right_side):
    return lax.dot_general(
        left_side, right_side, (((0,), (0,)), ((), ())), preferred_element_type=F32
    )


def contract_cols(left_side, right_side):
    return lax.dot_general(
        left_side, right_side, (((1,), (1,)), ((), ())), preferred_element_type=F32
    )


def multiply(left_side, right_side):
    return jnp.dot(left_side, right_side, preferred_element_type=F32)


class Wire:
    def __init__(self, me, send_sem, recv_sem):
        self.me, self.send_sem, self.recv_sem, self.used = me, send_sem, recv_sem, 0

    def send(self, off, src, dst):
        copy = pltpu.make_async_remote_copy(
            src_ref=src,
            dst_ref=dst,
            send_sem=self.send_sem.at[self.used],
            recv_sem=self.recv_sem.at[self.used],
            device_id=self.me.at(off).device(),
            device_id_type=MESH,
        )
        copy.start()
        self.used += 1
        return copy


def meet(me, offsets):
    barrier = pltpu.get_barrier_semaphore()
    for off in offsets:
        back = tuple(-v for v in off)
        pl.semaphore_signal(barrier, inc=1, device_id=me.at(back).device(), device_id_type=MESH)
    pl.semaphore_wait(barrier, len(offsets))


def finish(copies):
    for copy in copies:
        copy.wait()


ZOFF = [(0, d, 0, 0, 0) for d in range(4)]


def split_rows(count, size):
    return [slice(i * size, i * size + size) for i in range(count)]


def front_body(
    gain_row,
    attn_gain,
    table,
    len_ref,
    hidden,
    w_q,
    w_key,
    w_value,
    out_grad,
    w_o,
    gate,
    up,
    down,
    q,
    kv,
    in_mine,
    scale_mine,
    gains,
    grad_full,
    w_cat,
    w_attn_out,
    normed_out,
    piece0,
    piece1,
    piece3,
    kv_blocks,
    w_kv,
    w_attn,
    normed,
    full,
    lin,
    scales,
    send_sem,
    recv_sem,
    local_sem,
):
    me = whereami()
    wire = Wire(me, send_sem, recv_sem)
    chunk = rows(me.chunk * CHUNK, CHUNK)
    near = []

    def take(src, dst):
        near.append(pltpu.make_async_copy(src, dst, local_sem.at[len(near)]))
        near[-1].start()

    take(w_q, w_attn.at[:, 0:128])
    head_loads = [
        pltpu.make_async_copy(weight.at[:, lanes(me.y // 2)], kv_blocks.at[n], local_sem.at[6 + n])
        for n, weight in enumerate((w_key, w_value))
    ]
    for copy in head_loads:
        copy.start()
    take(w_o, w_cat.at[:, 0:128])
    take(hidden.at[chunk, :], full.at[:, lanes(me.block)])
    take(out_grad.at[chunk, :], grad_full.at[:, lanes(me.wide)])
    gains[me.block] = gain_row[...]
    meet(me, PLANE[1:] + [SIBLING, ZOFF[1], ZOFF[3]])

    def chunk_of(off):
        return rows(me.at(off).chunk * CHUNK, CHUNK)

    def spread(src, dst, column):
        return [wire.send(XOFF[k], src.at[chunk_of(XOFF[k]), :], dst.at[:, column(k)]) for k in (1, 2, 3)]

    enter = spread(hidden, full, lambda k: lanes(me.block))
    ring = [
        wire.send(XOFF[k], weight.at[me.tok], piece0.at[:, k - 1, j])
        for k in (1, 3)
        for j, weight in enumerate((gate, up, down))
    ]
    half = rows(me.core * 1024, 1024)
    blocks = [w_attn.at[half, k * 128 : k * 128 + 128] for k in (1, 2, 3)]
    over_x = [wire.send(XOFF[k], w_q.at[half, :], blocks[k - 1]) for k in (1, 2, 3)]
    blocks.append(w_attn.at[half, 640:768])
    for copy in head_loads:
        copy.wait()
    for odd in range(2):

        @pl.when(me.y % 2 == odd)
        def _(odd=odd):
            cols = slice(odd * 64, odd * 64 + 64)
            w_kv[...] = jnp.concatenate([kv_blocks[0, :, cols], kv_blocks[1, :, cols]], axis=1)

    w_attn[:, 512:640] = w_kv[...]
    over_x.append(wire.send(XOFF[1], w_kv.at[half, :], blocks[3]))
    others = [wire.send(off, gain_row, gains.at[me.block]) for off in PLANE[1:]]

    def pass_on(ref):
        out = []
        for h in range(2):
            cols = lanes(h * 4 + me.y, 256)
            out += [wire.send(off, ref.at[:, cols], ref.at[:, cols]) for off in YOFF[1:]]
        return out

    def over_z(k):
        return [
            wire.send(ZOFF[1], piece0.at[:, k - 1], piece1.at[:, k - 1]),
            wire.send(ZOFF[3], piece0.at[:, k - 1], piece3.at[:, k - 1]),
        ]

    for copy in near:
        copy.wait()
    for copy in enter:
        copy.wait_recv()
    over_y = pass_on(full)
    for copy in ring[:3]:
        copy.wait_recv()
    ring_pass = [wire.send(XOFF[3], piece0.at[0, 0], piece0.at[0, 1])]
    others += over_z(1)
    for copy in ring[3:]:
        copy.wait_recv()
    ring_pass.append(wire.send(XOFF[1], piece0.at[1, 2], piece0.at[1, 1]))
    others += over_z(3)
    grads = spread(out_grad, grad_full, lambda k: lanes(XOFF[k][2] * 8 + me.wide))
    over_core = []
    for copy, block in zip(over_x, blocks):
        copy.wait_recv()
        over_core.append(wire.send(SIBLING, block, block))
    for copy in over_y:
        copy.wait_recv()
    for part_rows in split_rows(4, SUB):
        value = full[part_rows, :].astype(F32)
        scale = lax.rsqrt(jnp.mean(value * value, axis=1, keepdims=True) + EPS)
        scales[part_rows, :] = scale
        normed[part_rows, :] = (value * scale * attn_gain[...]).astype(BF)
    for copy in over_core:
        copy.wait_recv()
    lane = lax.broadcasted_iota(jnp.int32, (CHUNK, 128), 1)
    first, later = rows(me.chunk * CHUNK, CHUNK), pl.ds(me.chunk * CHUNK + SHORT, CHUNK)
    short_first = len_ref[0:1, 0:1] == SHORT
    cosine, sine = [jnp.where(short_first, table[j, first], table[j, later]) for j in range(2)]
    for j in range(3):
        pair = multiply(normed[...], w_attn[:, j * 256 : j * 256 + 256])
        for k in (2 * j, 2 * j + 1):
            block = pair[:, k % 2 * 128 : k % 2 * 128 + 128]
            swapped = jnp.where(
                (lane % 64) < 32, -pltpu.roll(block, 96, 1), pltpu.roll(block, 32, 1)
            )
            turned = block * cosine + swapped * sine
            if k >= 4:
                turned = jnp.where(lane < 64, turned, block)
            lin[:, k * 128 : k * 128 + 128] = turned.astype(BF)
    moves = []
    for k in (1, 2, 3):
        kv_col = 512 + 128 * XOFF[k][2]
        moves.append(wire.send(XOFF[k], lin.at[:, k * 128 : k * 128 + 128], q.at[chunk, :]))
        moves.append(wire.send(XOFF[k], lin.at[:, kv_col : kv_col + 128], kv.at[chunk, :]))
    out_blocks = [w_cat.at[half, k * 128 : k * 128 + 128] for k in (1, 2, 3)]
    out_x = [wire.send(XOFF[k], w_o.at[half, :], out_blocks[k - 1]) for k in (1, 2, 3)]
    q[chunk, :] = lin[:, 0:128]
    kv[chunk, :] = lin[:, 512:640]
    for copy in ring_pass:
        copy.wait_recv()
    others += over_z(2)
    for copy in grads:
        copy.wait_recv()
    others += pass_on(grad_full)
    for copy, block in zip(out_x, out_blocks):
        copy.wait_recv()
        over_core.append(wire.send(SIBLING, block, block))
        others.append(over_core[-1])
    take(w_attn, w_attn_out)
    take(normed, normed_out)
    here = rows(me.y * SUB, SUB)
    in_mine[...] = full[here, :]
    scale_mine[...] = scales[here, :]
    for copy in over_x + enter + ring + ring_pass + grads + over_y + out_x + over_core[:4]:
        copy.wait_send()
    finish(others + moves + near[-2:])


def front(gain_row, attn_gain, table, lengths, hidden, w_q, w_key, w_value, out_grad, w_o, *weights):
    vm = pl.BlockSpec(memory_space=pltpu.VMEM)
    hbm = pl.BlockSpec(memory_space=pltpu.HBM)
    outs = [
        SDS((ROWS, 128), BF),
        SDS((ROWS, 128), BF),
        SDS((SUB, D), BF),
        SDS((SUB, 1), F32),
        SDS((16, 1, 128), F32),
        SDS((CHUNK, D), BF),
        SDS((D, 512), BF),
        SDS((D, 768), BF),
        SDS((CHUNK, D), BF),
        SDS((2, 3, 3, 64, 1024), BF),
        SDS((2, 3, 3, 64, 1024), BF),
        SDS((2, 3, 3, 64, 1024), BF),
    ]
    return pl.pallas_call(
        front_body,
        name="front",
        out_shape=outs,
        in_specs=[vm] * 4 + [hbm] * 9,
        out_specs=[vm] * 7 + [hbm] * 5,
        scratch_shapes=[
            pltpu.VMEM((2, D, 128), BF),
            pltpu.VMEM((D, 128), BF),
            pltpu.VMEM((D, 768), BF),
            pltpu.VMEM((CHUNK, D), BF),
            pltpu.VMEM((CHUNK, D), BF),
            pltpu.VMEM((CHUNK, 768), BF),
            pltpu.VMEM((CHUNK, 1), F32),
            pltpu.SemaphoreType.DMA((80,)),
            pltpu.SemaphoreType.DMA((80,)),
            pltpu.SemaphoreType.DMA((8,)),
        ],
        compiler_params=pltpu.CompilerParams(
            collective_id=0, has_side_effects=True, vmem_limit_bytes=60 * 2**20
        ),
        cost_estimate=pl.CostEstimate(flops=2 * 10**9, bytes_accessed=2**23, transcendentals=0),
    )(
        gain_row,
        attn_gain,
        table,
        lengths,
        hidden,
        w_q,
        w_key,
        w_value,
        out_grad,
        w_o,
        *[weight.reshape(8, 2, 64, 1024) for weight in weights],
    )


def middle_body(
    heads,
    in_mine,
    gains,
    w_cat,
    piece1,
    piece3,
    heads_cat,
    resid,
    scale_out,
    ffn_mine,
    piece2_first,
    piece2_second,
    term_send,
    term_recv,
    send_sem,
    recv_sem,
):
    me = whereami()
    wire = Wire(me, send_sem, recv_sem)
    meet(me, XOFF[1:] + YOFF[1:] + [ZOFF[1], ZOFF[3]])
    weights = [
        wire.send(ZOFF[1], piece1.at[0, 0], piece2_first),
        wire.send(ZOFF[3], piece3.at[1, 0], piece2_second),
    ]
    moves = [
        wire.send(
            XOFF[k],
            heads.at[rows(me.at(XOFF[k]).chunk * CHUNK, CHUNK), :],
            heads_cat.at[:, k * 128 : k * 128 + 128],
        )
        for k in (1, 2, 3)
    ]
    heads_cat[:, 0:128] = heads[rows(me.chunk * CHUNK, CHUNK), :]
    finish(moves)
    sums = []
    for h in range(2):
        for p in range(2):
            cols = slice(h * 1024 + p * 512, h * 1024 + p * 512 + 512)
            term_send[:, cols] = contract_cols(heads_cat[...], w_cat[cols, :]).astype(BF)
        cols = slice(h * 1024, h * 1024 + 1024)
        for d in (1, 2, 3):
            there = rows(me.at(YOFF[d]).y * SUB, SUB)
            sums.append(
                wire.send(YOFF[d], term_send.at[there, cols], term_recv.at[d - 1, :, cols])
            )
    finish(sums)
    value = in_mine[...].astype(F32) + term_send[rows(me.y * SUB, SUB), :].astype(F32)
    for d in range(3):
        value = value + term_recv[d].astype(F32)
    resid[...] = value
    scale = lax.rsqrt(jnp.mean(value * value, axis=1, keepdims=True) + EPS)
    scale_out[...] = scale
    gain = jnp.concatenate([gains[b] for b in range(16)], axis=1)
    ffn_mine[...] = (value * scale * gain).astype(BF)
    finish(weights)


def middle(heads, in_mine, gain, w_cat, piece1, piece3):
    vm = pl.BlockSpec(memory_space=pltpu.VMEM)
    hbm = pl.BlockSpec(memory_space=pltpu.HBM)
    outs = [SDS((CHUNK, 512), BF), SDS((SUB, D), F32), SDS((SUB, 1), F32), SDS((SUB, D), BF)]
    outs += [SDS((3, 64, 1024), BF)] * 2
    return pl.pallas_call(
        middle_body,
        name="middle",
        out_shape=outs,
        in_specs=[vm] * 4 + [hbm] * 2,
        out_specs=[vm] * 4 + [hbm] * 2,
        scratch_shapes=[
            pltpu.VMEM((CHUNK, D), BF),
            pltpu.VMEM((3, SUB, D), BF),
            pltpu.SemaphoreType.DMA((13,)),
            pltpu.SemaphoreType.DMA((13,)),
        ],
        compiler_params=pltpu.CompilerParams(
            collective_id=1, has_side_effects=True, vmem_limit_bytes=60 * 2**20
        ),
        cost_estimate=pl.CostEstimate(flops=10**9, bytes_accessed=2**23, transcendentals=0),
    )(heads, in_mine, gain, w_cat, piece1, piece3)


class PairSum:
    def __init__(self, me, left, right, own, came, stage, send_sem, recv_sem):
        self.me, self.left, self.right, self.own, self.came = me, left, right, own, came
        self.stage, self.send_sem, self.recv_sem = stage, send_sem, recv_sem

    def copy(self, i):
        return pltpu.make_async_remote_copy(
            src_ref=self.stage.at[i % 3, :, :, 1 - self.me.core],
            dst_ref=self.came.at[i],
            send_sem=self.send_sem.at[i],
            recv_sem=self.recv_sem.at[i],
            device_id=self.me.at(SIBLING).device(),
            device_id_type=MESH,
        )

    def multiply(self, first, last):
        def step(i, _):
            cols = pl.ds(pl.multiple_of(i * 256, 256), 256)

            @pl.when(i >= first + 3)
            def _():
                self.copy(i - 3).wait_send()

            block = contract_rows(self.left[:, cols], self.right[...])
            self.stage[i % 3] = block.astype(BF).reshape(2, 4, 2, 16, 2048)
            self.own[i] = self.stage[i % 3, :, :, self.me.core]
            self.copy(i).start()
            return 0

        lax.fori_loop(first, last, step, 0)
        for i in range(last - 3, last):
            self.copy(i).wait_send()

    def add(self, first, last):
        def step(i, _):
            self.copy(i).wait_recv()
            self.own[i] = (self.own[i].astype(F32) + self.came[i].astype(F32)).astype(BF)
            return 0

        lax.fori_loop(first, last, step, 0)


def add_to(target, came):
    for i in range(came.shape[0]):
        target[i] = (target[i].astype(F32) + came[i].astype(F32)).astype(BF)


def ffn_body(
    mine_ref,
    grad_ref,
    resid_ref,
    scale_ref,
    gains,
    w_out_ref,
    own_gate,
    own_up,
    own_down,
    piece0,
    piece1,
    piece2_first,
    piece2_second,
    piece3,
    out_mine,
    resid_back,
    gain_part,
    mix_full,
    heads_back,
    down_own,
    down_came,
    gate_own,
    gate_came,
    up_own,
    up_late,
    up_pass,
    other_core,
    rest_first,
    rest_second,
    gain_ref,
    turned,
    ffn_in,
    act,
    gate_back,
    up_back,
    gate_tile,
    up_tile,
    down_tile,
    down_acc,
    ffn_acc,
    down_send,
    ffn_send,
    down_recv,
    ffn_recv,
    mix_mine,
    back_cat,
    down_terms,
    gate_terms,
    up_terms,
    stage,
    came,
    down_pass,
    gate_pass,
    send_sem,
    recv_sem,
    core_send,
    core_recv,
    tile_sem,
    local_sem,
    ack,
):
    me = whereami()
    wire = Wire(me, send_sem, recv_sem)
    half = [lanes(me.xl, 1024), lanes(1 - me.xl, 1024)]
    here = rows(me.y * SUB, SUB)

    def piece(d, k):
        return {0: piece0, 1: piece1, 3: piece3}[d].at[:, k - 1]

    rest = (rest_first, rest_second)

    def opposite(h, k):
        return (piece2_first, piece2_second)[h] if k == 1 else rest[h].at[k - 2]


    def tile_copies(e, q, slot):
        copies, groups = [], []
        cols = pl.ds(pl.multiple_of(q * 256, 256), 256)

        def copy(src, dst):
            sem = tile_sem.at[slot, len(copies) + len(groups)]
            return pltpu.make_async_copy(src, dst, sem)

        for dxl in range(2):
            k = e * 2 + dxl
            for j, (own, tile) in enumerate(((own_gate, gate_tile), (own_up, up_tile))):
                if k == 0:
                    copies.append(copy(own.at[:, :, :, :, cols], tile.at[slot, dxl]))
                    continue
                for d in range(4):
                    spot = tile.at[slot, dxl, (me.z - d + 4) % 4, me.core]
                    if d != 2:
                        copies.append(copy(piece(d, k).at[:, j, :, cols], spot))
                        continue
                    for h in range(2):
                        copies.append(copy(opposite(h, k).at[j, :, cols], spot.at[h]))
                spot = tile.at[slot, dxl, :, 1 - me.core]
                copies.append(copy(other_core.at[:, :, k - 1, j, :, cols], spot))
            here = slice(dxl * 1024, dxl * 1024 + 1024)
            if k == 0:
                copies.append(copy(own_down.at[q], down_tile.at[slot, :, :, :, here]))
                continue
            spot = down_tile.at[slot, 1 - me.core, :, :, here]
            copies.append(copy(other_core.at[q, :, k - 1, 2], spot))
            for h in range(2):
                spot = down_tile.at[slot, me.core, h, :, here]
                groups.append(
                    [
                        copy(opposite(h, k).at[2] if d == 2 else piece(d, k).at[h, 2], spot)
                        for d in range(4)
                    ]
                )
        return copies, groups

    def fetch(e, q, slot):
        copies, groups = tile_copies(e, q, slot)
        for copy in copies:
            copy.start()
        for group in groups:
            for d, copy in enumerate(group):
                pl.when((me.z - q + 4) % 4 == d)(copy.start)

    def arrive(e, q, slot):
        copies, groups = tile_copies(e, q, slot)
        for copy in copies + [group[0] for group in groups]:
            copy.wait()

    meet(me, YOFF[1:] + XOFF[1:] + ZOFF[1:] + [SIBLING])
    for h in range(2):
        turned[:, h * 1024 : h * 1024 + 1024] = mine_ref[:, half[h]]
    gathers = [wire.send(off, turned, ffn_in.at[here, :]) for off in YOFF[1:]]
    passed = []
    for k in (2, 3):
        passed.append(wire.send(ZOFF[1], piece(1, k).at[0], rest_first.at[k - 2]))
        passed.append(wire.send(ZOFF[3], piece(3, k).at[1], rest_second.at[k - 2]))

    def share(k, parts):
        moves = []
        for d in parts:
            spot = other_core.at[(me.z - d + 4) % 4, :, k - 1]
            if d != 2:
                moves.append(wire.send(SIBLING, piece(d, k), spot))
                continue
            for h in range(2):
                moves.append(wire.send(SIBLING, opposite(h, k), spot.at[h]))
        return moves

    shares = share(1, range(4))
    late_shares = share(2, (0, 1, 3)) + share(3, (0, 1, 3))
    ffn_in[here, :] = turned[...]
    down_acc[...] = jnp.zeros(down_acc.shape, F32)
    ffn_acc[...] = jnp.zeros(ffn_acc.shape, F32)
    finish(shares)
    fetch(0, 0, 0)
    for b in range(16):
        gain_ref[:, b * 128 : b * 128 + 128] = gains[b]
    finish(gathers)
    finish(passed)
    late_shares += share(2, (2,)) + share(3, (2,))

    sums = []
    for left, right, own in (
        (act, grad_ref, down_terms),
        (ffn_in, gate_back, gate_terms),
        (ffn_in, up_back, up_terms),
    ):
        j = len(sums)
        sums.append(PairSum(me, left, right, own, came, stage, core_send.at[j], core_recv.at[j]))
    down_sum, gate_sum, up_sum = sums

    def came_free():
        pl.semaphore_signal(ack, inc=1, device_id=me.at(SIBLING).device(), device_id_type=MESH)
        pl.semaphore_wait(ack, 1)

    for e in range(2):

        def step(q, _, e=e):
            slot = q % 2

            @pl.when(q < 3)
            def _():
                fetch(e, q + 1, 1 - slot)

            arrive(e, q, slot)
            cols = pl.ds(pl.multiple_of(e * 1024 + q * 256, 256), 256)
            w_g = gate_tile[slot].reshape(2048, 256)
            w_u = up_tile[slot].reshape(2048, 256)
            w_d = down_tile[slot].reshape(256, 2048)
            gate = multiply(ffn_in[...], w_g)
            up = multiply(ffn_in[...], w_u)
            act_back = contract_cols(grad_ref[...], w_d)
            sigmoid = jax.nn.sigmoid(gate)
            silu = gate * sigmoid
            act_here = (silu * up).astype(BF)
            act[:, cols] = act_here
            down_acc[...] += multiply(act_here, w_d)
            g_back = (act_back * up * sigmoid * (1.0 + gate * (1.0 - sigmoid))).astype(BF)
            u_back = (act_back * silu).astype(BF)
            gate_back[:, cols] = g_back
            up_back[:, cols] = u_back
            ffn_acc[...] += contract_cols(g_back, w_g) + contract_cols(u_back, w_u)
            return 0

        lax.fori_loop(0, 4, step, 0)
        if e == 0:
            finish(late_shares)
            fetch(1, 0, 0)
            down_sum.multiply(0, 4)

    ffn_send[...] = ffn_acc[...].astype(BF)
    ffn_moves = [
        wire.send(YOFF[d], ffn_send.at[rows(me.at(YOFF[d]).y * SUB, SUB), :], ffn_recv.at[d - 1])
        for d in (1, 2, 3)
    ]
    down_sum.multiply(4, 8)


    def down_block(k, h=None):
        e, dxl = XOFF[k][4], XOFF[k][2]
        pairs = slice(e * 4, e * 4 + 4) if h is None else slice(e * 4 + h * 2, e * 4 + h * 2 + 2)
        return down_terms.at[pairs, :, :, :, dxl * 1024 : dxl * 1024 + 1024]

    down_sum.add(0, 8)
    x_moves = [
        wire.send(XOFF[1], down_block(2, 0), down_pass.at[0]),
        wire.send(XOFF[3], down_block(2, 1), down_pass.at[1]),
        wire.send(XOFF[1], down_block(1, 0), down_came.at[0, 0:2]),
        wire.send(XOFF[3], down_block(3, 1), down_came.at[1, 2:4]),
    ]
    near = []

    def keep(src, dst):
        near.append(pltpu.make_async_copy(src, dst, local_sem.at[len(near)]))
        near[-1].start()

    keep(down_block(0), down_own)

    def z_block(terms, d, h=None):
        pairs = slice(0, 8) if h is None else slice(h * 4, h * 4 + 4)
        return terms.at[pairs, :, (me.z + d) % 4]

    came_free()
    gate_sum.multiply(0, 8)
    gate_sum.add(0, 4)
    z_moves = [
        wire.send(ZOFF[1], z_block(gate_terms, 2, 0), gate_pass.at[0]),
        wire.send(ZOFF[3], z_block(gate_terms, 3, 0), gate_came.at[1, 0:4]),
    ]
    gate_sum.add(4, 8)
    z_moves += [
        wire.send(ZOFF[3], z_block(gate_terms, 2, 1), gate_pass.at[1]),
        wire.send(ZOFF[1], z_block(gate_terms, 1, 1), gate_came.at[0, 4:8]),
    ]
    keep(z_block(gate_terms, 0), gate_own)

    finish(ffn_moves)

    def summed(send, recv, h):
        cols = slice(h * 1024, h * 1024 + 1024)
        out = send[here, cols].astype(F32)
        for d in range(3):
            out = out + recv[d, :, cols].astype(F32)
        return out

    scale = scale_ref[...]
    inner = jnp.zeros((SUB, 1), F32)
    for h in range(2):
        back = summed(ffn_send, ffn_recv, h)
        weighed = back * resid_ref[:, half[h]]
        inner = inner + jnp.sum(weighed * gain_ref[:, half[h]], axis=1, keepdims=True)
        gain_part[:, half[h]] = jnp.sum(weighed * scale, axis=0, keepdims=True)
    pull = scale * scale * scale * inner / D
    for h in range(2):
        back = summed(ffn_send, ffn_recv, h)
        grad = grad_ref[here, h * 1024 : h * 1024 + 1024].astype(F32)
        total_back = grad + scale * gain_ref[:, half[h]] * back - resid_ref[:, half[h]] * pull
        resid_back[:, half[h]] = total_back
        mix_mine[:, half[h]] = total_back.astype(BF)
    mix_full[here, :] = mix_mine[...]
    mix_moves = [wire.send(off, mix_mine, mix_full.at[here, :]) for off in YOFF[1:]]

    down_send[...] = down_acc[...].astype(BF)
    down_moves = [
        wire.send(YOFF[d], down_send.at[rows(me.at(YOFF[d]).y * SUB, SUB), :], down_recv.at[d - 1])
        for d in (1, 2, 3)
    ]
    x_moves[0].wait_recv()
    add_to(down_block(3, 0), down_pass.at[0])
    x_late = [wire.send(XOFF[3], down_block(3, 0), down_came.at[1, 0:2])]
    x_moves[1].wait_recv()
    add_to(down_block(1, 1), down_pass.at[1])
    x_late.append(wire.send(XOFF[1], down_block(1, 1), down_came.at[0, 2:4]))
    came_free()
    up_sum.multiply(0, 8)
    z_moves[0].wait_recv()
    add_to(z_block(gate_terms, 1, 0), gate_pass.at[0])
    z_late = [wire.send(ZOFF[1], z_block(gate_terms, 1, 0), gate_came.at[0, 0:4])]
    z_moves[2].wait_recv()
    add_to(z_block(gate_terms, 3, 1), gate_pass.at[1])
    z_late.append(wire.send(ZOFF[3], z_block(gate_terms, 3, 1), gate_came.at[1, 4:8]))
    up_sum.add(0, 8)
    z_late += [
        wire.send(ZOFF[1], z_block(up_terms, 2, 0), up_pass.at[0]),
        wire.send(ZOFF[3], z_block(up_terms, 2, 1), up_pass.at[1]),
    ]
    keep(z_block(up_terms, 0), up_own)
    keep(z_block(up_terms, 1), up_late.at[0])
    keep(z_block(up_terms, 3), up_late.at[1])

    finish(mix_moves)
    back_cat[...] = multiply(mix_full[...], w_out_ref[...]).astype(BF)
    spot = rows(me.chunk * CHUNK, CHUNK)
    head_moves = [
        wire.send(XOFF[k], back_cat.at[:, k * 128 : k * 128 + 128], heads_back.at[spot, :])
        for k in (1, 2, 3)
    ]
    heads_back[spot, :] = back_cat[:, 0:128]
    finish(down_moves)
    for h in range(2):
        out_mine[:, half[h]] = (resid_ref[:, half[h]] + summed(down_send, down_recv, h)).astype(BF)
    for move in (x_moves[0], x_moves[1], z_moves[0], z_moves[2]):
        move.wait_send()
    finish(head_moves + x_moves[2:] + [z_moves[1], z_moves[3]] + x_late + z_late)
    for copy in near:
        copy.wait()


def ffn(ffn_mine, grad_full, resid, scale_two, gain, w_out, w_gate, w_up, w_down, pieces):
    vm = pl.BlockSpec(memory_space=pltpu.VMEM)
    hbm = pl.BlockSpec(memory_space=pltpu.HBM)
    return pl.pallas_call(
        ffn_body,
        name="ffn",
        out_shape=[
            SDS((SUB, D), BF),
            SDS((SUB, D), F32),
            SDS((1, D), F32),
            SDS((CHUNK, D), BF),
            SDS((ROWS, 128), BF),
            SDS((4, 2, 4, 16, 1024), BF),
            SDS((2, 4, 2, 4, 16, 1024), BF),
            SDS((8, 2, 16, 2048), BF),
            SDS((2, 8, 2, 16, 2048), BF),
            SDS((8, 2, 16, 2048), BF),
            SDS((2, 8, 2, 16, 2048), BF),
            SDS((2, 4, 2, 16, 2048), BF),
            SDS((4, 2, 3, 3, 64, 1024), BF),
            SDS((2, 3, 64, 1024), BF),
            SDS((2, 3, 64, 1024), BF),
        ],
        in_specs=[vm] * 6 + [hbm] * 8,
        out_specs=[vm] * 5 + [hbm] * 10,
        scratch_shapes=[
            pltpu.VMEM((1, D), F32),
            pltpu.VMEM((SUB, D), BF),
            pltpu.VMEM((CHUNK, D), BF),
            pltpu.VMEM((CHUNK, D), BF),
            pltpu.VMEM((CHUNK, D), BF),
            pltpu.VMEM((CHUNK, D), BF),
            pltpu.VMEM((2, 2, 4, 2, 2, 64, 256), BF),
            pltpu.VMEM((2, 2, 4, 2, 2, 64, 256), BF),
            pltpu.VMEM((2, 2, 2, 64, 2048), BF),
            pltpu.VMEM((CHUNK, D), F32),
            pltpu.VMEM((CHUNK, D), F32),
            pltpu.VMEM((CHUNK, D), BF),
            pltpu.VMEM((CHUNK, D), BF),
            pltpu.VMEM((3, SUB, D), BF),
            pltpu.VMEM((3, SUB, D), BF),
            pltpu.VMEM((SUB, D), BF),
            pltpu.VMEM((CHUNK, 512), BF),
            pltpu.VMEM((8, 2, 4, 16, 2048), BF),
            pltpu.VMEM((8, 2, 4, 16, 2048), BF),
            pltpu.VMEM((8, 2, 4, 16, 2048), BF),
            pltpu.VMEM((3, 2, 4, 2, 16, 2048), BF),
            pltpu.VMEM((8, 2, 4, 16, 2048), BF),
            pltpu.VMEM((2, 2, 2, 4, 16, 1024), BF),
            pltpu.VMEM((2, 4, 2, 16, 2048), BF),
            pltpu.SemaphoreType.DMA((64,)),
            pltpu.SemaphoreType.DMA((64,)),
            pltpu.SemaphoreType.DMA((3, 8)),
            pltpu.SemaphoreType.DMA((3, 8)),
            pltpu.SemaphoreType.DMA((2, 32)),
            pltpu.SemaphoreType.DMA((6,)),
            pltpu.SemaphoreType.REGULAR,
        ],
        compiler_params=pltpu.CompilerParams(
            collective_id=14, has_side_effects=True, vmem_limit_bytes=60 * 2**20
        ),
        cost_estimate=pl.CostEstimate(flops=26 * 10**9, bytes_accessed=40 * 2**20, transcendentals=0),
    )(
        ffn_mine,
        grad_full,
        resid,
        scale_two,
        gain,
        w_out,
        w_gate.reshape(4, 2, 2, 64, 1024),
        w_up.reshape(4, 2, 2, 64, 1024),
        w_down.reshape(4, 2, 2, 64, 1024),
        *pieces,
    )


def per_device(
    layer_input,
    doc_lengths,
    attn_gain,
    w_query,
    w_key,
    w_value,
    w_output,
    ffn_gain,
    w_gate,
    w_up,
    w_down,
    output_grad,
):
    me = whereami()
    cos_np, sin_np = rope_table()
    table_all = jnp.asarray(np.stack([cos_np, sin_np]))

    queries, kv, in_mine, scale_mine, gains, grad_full, w_out, w_attn, normed, *passed = front(
        ffn_gain[None, :],
        attn_gain[None, :],
        table_all,
        doc_lengths,
        layer_input,
        w_query,
        w_key,
        w_value,
        output_grad,
        w_output,
        w_gate,
        w_up,
        w_down,
    )
    (heads_out,) = vmem_call(
        "attend", attend_body, [doc_lengths, queries, kv], [SDS((ROWS, 128), BF)], flops=2 * 10**10
    )
    heads_cat, resid, scale_two, ffn_mine, *opposite = middle(
        heads_out, in_mine, gains, w_out, *passed[1:]
    )
    pieces = [*passed[:2], *opposite, passed[2]]
    (
        out_mine,
        resid_back,
        ffn_gain_part,
        mix_full,
        heads_back,
        *ffn_sums,
        _,
        _,
        _,
    ) = ffn(
        ffn_mine, grad_full, resid, scale_two, gains, w_out, w_gate, w_up, w_down, pieces
    )

    (
        layer_output,
        input_grad,
        query_grad,
        kv_grad,
        output_proj_grad,
        gate_grad,
        up_grad,
        down_grad,
        gain_grads,
    ) = back(
        [
            doc_lengths,
            queries,
            kv,
            heads_back,
            out_mine,
            in_mine,
            resid_back,
            scale_mine,
            attn_gain[None, :],
            ffn_gain_part,
        ],
        [table_all, w_attn, heads_cat, normed, mix_full, *ffn_sums],
    )
    kv_cols = jnp.moveaxis(kv_grad, 0, 1).reshape(32, 4, 2, 64)
    key_grad = kv_cols[:, :, 0, :].reshape(32, 256)
    value_grad = kv_cols[:, :, 1, :].reshape(32, 256)
    gain_grads = part(gain_grads, me.tok * 16, 16, 1)
    return (
        layer_output,
        input_grad,
        gain_grads[0:1],
        query_grad,
        key_grad,
        value_grad,
        output_proj_grad,
        gain_grads[1:2],
        gate_grad,
        up_grad,
        down_grad,
    )


def solution(mesh):
    in_specs = (
        P("tok", ("narrow", "wide")),
        P("tok", None),
        P(),
        P(None, ("narrow", "wide")),
        P(None, "narrow"),
        P(None, "narrow"),
        P(None, ("narrow", "wide")),
        P(("narrow", "wide")),
        P("narrow", "wide"),
        P("narrow", "wide"),
        P("wide", "narrow"),
        P("tok", ("narrow", "wide")),
    )
    out_specs = (
        P("tok", ("narrow", "wide")),
        P("tok", ("narrow", "wide")),
        P(("narrow", "wide"), "tok"),
        P("tok", ("narrow", "wide")),
        P(("tok", "wide"), "narrow"),
        P(("tok", "wide"), "narrow"),
        P("tok", ("narrow", "wide")),
        P(("narrow", "wide"), "tok"),
        P("narrow", "tok", "wide"),
        P("narrow", "tok", "wide"),
        P("wide", "tok", "narrow"),
    )
    return jax.shard_map(
        per_device, mesh=mesh, in_specs=in_specs, out_specs=out_specs, check_vma=False
    )
```
